32 devices in a mesh: dp: 4 (over y, x), tensor: 4 (over z), chip: 2 (over core).
Axes of the slice: x: 2, y: 2, z: 4, core: 2. Of those that a mesh axis runs over, the one named last changes fastest.
Arguments:
- residual: bfloat16 [8, 1024, 2048], P(('dp', 'chip'), 'tensor'), may hold values from -6 to 6
- cotangent: bfloat16 [8, 1024, 2048], P(('dp', 'chip'), 'tensor'), may hold values from -6 to 6
- lengths: int32 [8, 5], P(('dp', 'chip')), may hold values from 1 to 512, 1024 in all within a row
- owners: int32 [8], replicated, may hold values from 0 to 7, as said below
- step_count: int32 [1], replicated, may hold values from 1 to 20
- rates: float32 [8], replicated, as said below
- weight_decay: float32 [1], replicated, may hold values from 0.1 to 1
- ema_decay: float32 [1], replicated, may hold values from 0.5 to 0.95
- master: float32 [4, 8, 1574912], P('tensor', ('dp', 'chip')), as said below
- moment_one: float32 [4, 8, 1574912], P('tensor', ('dp', 'chip')), as said below
- moment_two: float32 [4, 8, 1574912], P('tensor', ('dp', 'chip')), as said below
- average: float32 [4, 8, 1574912], P('tensor', ('dp', 'chip')), as said below
Outputs:
- output: float32 [8, 1024, 2048], P(('dp', 'chip'), 'tensor')
- input_grad: float32 [8, 1024, 2048], P(('dp', 'chip'), 'tensor')
- new_master: float32 [4, 8, 1574912], P('tensor', ('dp', 'chip'))
- new_moment_one: float32 [4, 8, 1574912], P('tensor', ('dp', 'chip'))
- new_moment_two: float32 [4, 8, 1574912], P('tensor', ('dp', 'chip'))
- new_average: float32 [4, 8, 1574912], P('tensor', ('dp', 'chip'))
- reduced_grad: float32 [4, 8, 1574912], P('tensor', ('dp', 'chip'))
The draws below stay inside these ranges and needn't reach their ends.
Inputs may be any that keep to these rules, and one draw needn't show every extreme that they name: Row g lists the lengths of group g's sequences in order; they sum to 1024 and the longest is 512. `owners`: a permutation of 0 to 7. `master`: the entries of S are equal for every tensor index. `moment_one`: the entries of S are equal for every tensor index. `moment_two`: every entry is positive; the entries of S are equal for every tensor index. `average`: the entries of S are equal for every tensor index. `rates`: every rate is positive.
All inputs are finite; a program needn't handle non-finite values.
Results may differ from the reference program's by a relative error of at most 0.003.
The reference program's roundings to bfloat16 on the way count: a program that leaves them out, or rounds other values in their place, can miss the bound.
Values may be sent and summed in bfloat16 or wider, within the bound.
No kernel may reach another device: no remote copies, remote signals or barrier semaphores. Data moves between devices by JAX's collectives and lax.ppermute only.
A program may use at most 384 MiB of HBM per device.

```python
import math
import jax
import jax.numpy as jnp
import numpy as np
from jax import lax

D = 2048
H = 16
HD = 128
FF = 8192
ROT = 32
NSEQ = 5
KINDS = 8
TP_DEVS = 4
GROUPS = 8
HLOC = 4
DLOC = 512
FLOC = 2048
GTOK = 1024
LONG = 512
TOKENS = 8192
PDEV = 12598784
BUCKET = 1574912


def owner_order(key):
    return jax.random.permutation(jax.random.fold_in(key, 11), GROUPS).astype(jnp.int32)


def bound_list_drawn():
    widths = [D * 3 * DLOC, DLOC * D, D * FLOC, FLOC * D, 3 * DLOC, FLOC, 6 * D]
    bounds = [0]
    for part_width in widths:
        bounds.append(bounds[-1] + part_width)
    return bounds


def kind_of_position():
    bounds = bound_list_drawn()
    position = jnp.arange(GROUPS * BUCKET, dtype=jnp.int32)
    kind_index = jnp.zeros((GROUPS * BUCKET,), jnp.int32)
    for edge in bounds[1:]:
        kind_index = kind_index + (position >= edge).astype(jnp.int32)
    return kind_index


def spread_table():
    return jnp.array([D ** (-0.5), (GTOK / 8.0 / D) ** 0.5, D ** (-0.5), FF ** (-0.5), 0.3, 0.3, 0.3, 0.1], jnp.float32)


def grad_table():
    return TOKENS ** 0.5 * jnp.array([1.0, (GTOK / 8.0) ** (-0.5), 0.25, 0.6, 1.0, 0.25, 1.0, 1.0], jnp.float32)


def base_values(key, shape):
    return jax.random.truncated_normal(key, -2.5, 2.5, shape, jnp.float32)


def arrange(key, full_values, small_values):
    bounds = bound_list_drawn()
    shared = jnp.broadcast_to(small_values.reshape(1, 6 * D), (TP_DEVS, 6 * D))
    full_values = jnp.concatenate([full_values[:, :bounds[6]], shared, full_values[:, bounds[7]:]], axis=1)
    inverse = jnp.argsort(owner_order(key)).astype(jnp.int32)
    return jnp.take(full_values.reshape(TP_DEVS, GROUPS, BUCKET), inverse, axis=1)


def weight_like(key, salt):
    kinds = kind_of_position()
    full_values = base_values(jax.random.fold_in(key, salt), (TP_DEVS, GROUPS * BUCKET)) * spread_table()[kinds][None, :]
    offsets = jnp.array([1.0, 0.0, 1.0, 0.0, 0.0, 0.0], jnp.float32)[:, None]
    small_values = base_values(jax.random.fold_in(key, salt + 1), (6, D)) * 0.3 + offsets
    return arrange(key, full_values, small_values)


def signed_sizes(key, shape):
    signs = (2 * jax.random.randint(jax.random.fold_in(key, 1), shape, 0, 2) - 1).astype(jnp.float32)
    magnitude = jax.random.uniform(jax.random.fold_in(key, 2), shape, jnp.float32, 0.5, 1.5)
    return signs * magnitude


def draw_owners(key, part):
    return owner_order(key)


def draw_master(key, part):
    return weight_like(key, 21)


def draw_average(key, part):
    return weight_like(key, 31)


def draw_moment_one(key, part):
    kinds = kind_of_position()
    scales = grad_table()[kinds][None, :]
    full_values = signed_sizes(jax.random.fold_in(key, 41), (TP_DEVS, GROUPS * BUCKET)) * scales
    small_values = signed_sizes(jax.random.fold_in(key, 42), (6, D)) * grad_table()[6]
    return arrange(key, full_values, small_values)


def draw_moment_two(key, part):
    kinds = kind_of_position()
    scales = grad_table()[kinds][None, :]
    shape = (TP_DEVS, GROUPS * BUCKET)
    factor = jnp.exp(jax.random.uniform(jax.random.fold_in(key, 51), shape, jnp.float32, -0.6931, 2.0794))
    small_factor = jnp.exp(jax.random.uniform(jax.random.fold_in(key, 52), (6, D), jnp.float32, -0.6931, 2.0794))
    full_values = scales * scales * factor
    small_values = grad_table()[6] * grad_table()[6] * small_factor
    return arrange(key, full_values, small_values)


def draw_rates(key, part):
    return spread_table() * jax.random.uniform(jax.random.fold_in(key, 61), (KINDS,), jnp.float32, 0.5, 1.0)


def shard_levels(key, extent, cuts, smallest, largest):
    level, own = 1.0, jax.random.fold_in(key, 6)
    for dim, parts in cuts:
        heights = jnp.exp(jax.random.uniform(jax.random.fold_in(own, dim), (parts,), jnp.float32, smallest / len(cuts), largest / len(cuts)))
        level = level * jnp.repeat(heights, extent[dim] // parts).reshape([-1 if axis == dim else 1 for axis in range(len(extent))])
    return level


def split_up(number_of, total, bound, lean):
    portions = [(1 << 20) // math.isqrt(standing ** lean) + 1 for standing in range(2, number_of + 1)]
    spare, counts = total - bound - (number_of - 1), [1] * (number_of - 1)
    while spare > 0:
        free = [i for i in range(number_of - 1) if counts[i] < bound]
        mass, remaining = sum([portions[i] for i in free]), spare
        for i in free:
            more = min(bound - counts[i], max(1, remaining * portions[i] // mass), spare)
            counts[i] = counts[i] + more
            spare = spare - more
    return np.array([bound] + counts)


def uneven_parts(key, count, total, bound, lean):
    if count == 2:
        one = jax.random.randint(key, (), max(1, total - bound), min(bound, total - 1) + 1)
        return jnp.stack([one, total - one])
    sizes = jnp.asarray(split_up(count, total, bound, lean), jnp.int32)
    pairs = (count - 1) // 2
    donor, receiver = sizes[1:1 + 2 * pairs:2], sizes[2:2 + 2 * pairs:2]
    margin = jnp.minimum(donor - 1, bound - receiver)
    passed = jax.random.randint(jax.random.fold_in(key, 1), (pairs,), 0, 1 << 20) % (margin + 1)
    sizes = sizes.at[1:1 + 2 * pairs:2].set(donor - passed).at[2:2 + 2 * pairs:2].set(receiver + passed)
    return sizes[jax.random.permutation(jax.random.fold_in(key, 2), count)]


def centred(rng, shape, scale, most, cuts=(), kind=jnp.bfloat16):
    entries = jax.random.normal(rng, shape, jnp.float32) * scale
    if len(cuts) > 0:
        entries = shard_levels(rng, shape, cuts, -0.22, 0.18) * entries
    return jnp.clip(entries, min=-most, max=most).astype(kind)


def setup_inputs(seed: int = 0) -> dict:
    splits = jax.random.split(jax.random.key(seed), 13)
    residual = centred(splits[0], (GROUPS, GTOK, D), 1.0, 6.0, ((0, 8), (1, 4)))
    cotangent = centred(splits[1], (GROUPS, GTOK, D), 1.0, 6.0, ((0, 8), (1, 4)))
    lengths = jax.vmap(lambda own: uneven_parts(own, NSEQ, GTOK, LONG, 2))(jax.random.split(splits[2], GROUPS)).reshape((GROUPS, NSEQ)).astype(jnp.int32)
    owners = draw_owners(jax.random.fold_in(splits[12], 71), 0)
    step_count = jax.random.randint(splits[4], (1,), 1, 21).astype(jnp.int32)
    rates = draw_rates(jax.random.fold_in(splits[12], 71), 0)
    weight_decay = jnp.clip(jax.random.uniform(splits[6], (1,), jnp.float32, 0.1, 1.0), 0.1, 1.0)
    ema_decay = jnp.clip(jax.random.uniform(splits[7], (1,), jnp.float32, 0.5, 0.95), 0.5, 0.95)
    master = draw_master(jax.random.fold_in(splits[12], 71), 0)
    moment_one = draw_moment_one(jax.random.fold_in(splits[12], 71), 0)
    moment_two = draw_moment_two(jax.random.fold_in(splits[12], 71), 0)
    average = draw_average(jax.random.fold_in(splits[12], 71), 0)
    return dict(residual=residual, cotangent=cotangent, lengths=lengths, owners=owners, step_count=step_count, rates=rates, weight_decay=weight_decay, ema_decay=ema_decay, master=master, moment_one=moment_one, moment_two=moment_two, average=average)


@jax.custom_vjp
def low(v):
    return lax.optimization_barrier(v.astype(jnp.bfloat16)).astype(jnp.float32)

@jax.custom_vjp
def low_back(v):
    return v

def low_keep(v):
    return (low(v), None)

def low_pass(kept, grad):
    return (grad,)

def back_keep(v):
    return (v, None)

def back_low(kept, grad):
    return (low(grad),)
low.defvjp(low_keep, low_pass)
low_back.defvjp(back_keep, back_low)
highest = lax.Precision.HIGHEST
norm_epsilon = 1e-05
adam_epsilon = 1e-08
beta_one = 0.5
beta_two = 0.5
rope_base = 10000.0
masked_score = -1e+30

def matmul(left, right):
    return jnp.dot(left, right, preferred_element_type=jnp.float32, precision=highest)

def bound_list():
    widths = [D * 3 * DLOC, DLOC * D, D * FLOC, FLOC * D, 3 * DLOC, FLOC, 6 * D]
    bounds = [0]
    for part_width in widths:
        bounds.append(bounds[-1] + part_width)
    return bounds

def unpack(flat_params):
    bounds = bound_list()
    weight_set = {}
    weight_set['mixer_in'] = flat_params[:, bounds[0]:bounds[1]].reshape(TP_DEVS, D, 3 * DLOC).transpose(1, 0, 2).reshape(D, TP_DEVS * 3 * DLOC)
    weight_set['mixer_out'] = flat_params[:, bounds[1]:bounds[2]].reshape(TP_DEVS * DLOC, D)
    weight_set['expand'] = flat_params[:, bounds[2]:bounds[3]].reshape(TP_DEVS, D, FLOC).transpose(1, 0, 2).reshape(D, FF)
    weight_set['shrink'] = flat_params[:, bounds[3]:bounds[4]].reshape(FF, D)
    weight_set['mixer_bias'] = flat_params[:, bounds[4]:bounds[5]].reshape(TP_DEVS * 3 * DLOC)
    weight_set['expand_bias'] = flat_params[:, bounds[5]:bounds[6]].reshape(FF)
    weight_set['small_params'] = flat_params[0, bounds[6]:bounds[7]].reshape(6, D)
    return weight_set

def pack(weight_set):
    pieces = [weight_set['mixer_in'].reshape(D, TP_DEVS, 3 * DLOC).transpose(1, 0, 2).reshape(TP_DEVS, D * 3 * DLOC), weight_set['mixer_out'].reshape(TP_DEVS, DLOC * D), weight_set['expand'].reshape(D, TP_DEVS, FLOC).transpose(1, 0, 2).reshape(TP_DEVS, D * FLOC), weight_set['shrink'].reshape(TP_DEVS, FLOC * D), weight_set['mixer_bias'].reshape(TP_DEVS, 3 * DLOC), weight_set['expand_bias'].reshape(TP_DEVS, FLOC), jnp.broadcast_to(weight_set['small_params'].reshape(1, 6 * D), (TP_DEVS, 6 * D)), jnp.zeros((TP_DEVS, GROUPS * BUCKET - PDEV), jnp.float32)]
    return jnp.concatenate(pieces, axis=1)

def group_layout(seq_lengths, group_rows):
    seq_ends = jnp.cumsum(seq_lengths).astype(jnp.int32)
    starts = (seq_ends - seq_lengths).astype(jnp.int32)
    token_index = jnp.arange(group_rows, dtype=jnp.int32)
    segment = lax.optimization_barrier(jnp.sum((token_index[:, None] >= seq_ends[None, :]).astype(jnp.int32), axis=1)).astype(jnp.int32)
    chosen = (segment[:, None] == jnp.arange(seq_lengths.shape[0], dtype=jnp.int32)[None, :]).astype(jnp.int32)
    places = token_index - lax.optimization_barrier(jnp.sum(chosen * starts[None, :], axis=1)).astype(jnp.int32)
    return (segment, places.astype(jnp.float32))

def rotary_tables(places):
    half_rot = ROT // 2
    frequency = rope_base ** (-2.0 * jnp.arange(half_rot, dtype=jnp.float32) / ROT)
    angles = places[:, None] * frequency[None, :]
    return (jnp.cos(angles)[:, None, :], jnp.sin(angles)[:, None, :])

def rotate(values, cosine, sines):
    half_rot = ROT // 2
    first = values[..., :half_rot]
    second = values[..., half_rot:ROT]
    return jnp.concatenate([first * cosine - second * sines, second * cosine + first * sines, values[..., ROT:]], axis=-1)

def layer_norm(inputs, gain, shift):
    center = inputs - lax.optimization_barrier(jnp.mean(inputs, axis=-1, keepdims=True))
    scale = lax.rsqrt(lax.optimization_barrier(jnp.mean(center * center, axis=-1, keepdims=True)) + norm_epsilon)
    return center * scale * gain + shift

def attend(queries, keys, values, segment):
    block_rows = min(512, GTOK)
    block_count = GTOK // block_rows
    key_index = jnp.arange(GTOK, dtype=jnp.int32)
    score_scale = 1.0 / math.sqrt(HD)

    def one_block(index):
        start = index * block_rows
        query_block = lax.dynamic_slice_in_dim(queries, start, block_rows, 0)
        scores = jnp.einsum('qhd,khd->hqk', query_block, keys, precision=highest) * score_scale
        scores = low_back(scores)
        row_index = start + jnp.arange(block_rows, dtype=jnp.int32)
        row_segment = lax.dynamic_slice_in_dim(segment, start, block_rows, 0)
        allowed = (row_segment[:, None] == segment[None, :]) & (key_index[None, :] <= row_index[:, None])
        scores = jnp.where(allowed[None], scores, masked_score)
        row_top = lax.optimization_barrier(jnp.max(scores, axis=-1, keepdims=True))
        raised = jnp.exp(scores - row_top)
        soft_weights = raised / lax.optimization_barrier(jnp.sum(raised, axis=-1, keepdims=True))
        mixed = jnp.einsum('hqk,khd->qhd', low(soft_weights), values, precision=highest)
        return mixed.reshape(block_rows, H * HD)
    blocks = lax.map(jax.checkpoint(one_block), jnp.arange(block_count, dtype=jnp.int32))
    return blocks.reshape(GTOK, H * HD)

def block_forward(weight_set, inputs, segment, places):
    small_params = low(weight_set['small_params'])
    normed_one = low(layer_norm(inputs, small_params[0], small_params[1]))
    normed_two = low(layer_norm(inputs, small_params[2], small_params[3]))
    projected = low_back(matmul(normed_one, low(weight_set['mixer_in'])) + low(weight_set['mixer_bias']))
    projected = projected.reshape(GTOK, TP_DEVS, 3, HLOC, HD)
    cosine, sines = rotary_tables(places)
    queries = low(rotate(projected[:, :, 0].reshape(GTOK, H, HD), cosine, sines))
    keys = low(rotate(projected[:, :, 1].reshape(GTOK, H, HD), cosine, sines))
    values = low(projected[:, :, 2].reshape(GTOK, H, HD))
    context = low(low_back(attend(queries, keys, values, segment)))
    before = low_back(matmul(normed_two, low(weight_set['expand'])) + low(weight_set['expand_bias']))
    hidden = low(jax.nn.gelu(before, approximate=False))
    branches = matmul(context, low(weight_set['mixer_out'])) + matmul(hidden, low(weight_set['shrink']))
    return inputs + branches + small_params[4] + small_params[5]

def adam_update(weights, first, second, moving, gradient, step_rate, step_value, decay_rate, ema_keep):
    bias_one = 1.0 - jnp.power(beta_one, step_value)
    bias_two = 1.0 - jnp.power(beta_two, step_value)
    new_first = beta_one * first + (1.0 - beta_one) * gradient
    new_second = beta_two * second + (1.0 - beta_two) * gradient * gradient
    ratio = new_first / bias_one / (jnp.sqrt(new_second / bias_two) + adam_epsilon)
    new_weights = weights - step_rate * (ratio + decay_rate * weights)
    new_moving = ema_keep * moving + (1.0 - ema_keep) * new_weights
    return (new_weights, new_first, new_second, new_moving)

def reference(residual, cotangent, lengths, owners, step_count, rates, weight_decay, ema_decay, master, moment_one, moment_two, average):
    slots = jnp.arange(GROUPS, dtype=jnp.int32)
    inverse = lax.optimization_barrier(jnp.sum(slots[None, :] * (owners[None, :] == slots[:, None]).astype(jnp.int32), axis=1)).astype(jnp.int32)

    def to_flat(stored):
        return jnp.take(stored, owners, axis=1).reshape(TP_DEVS, GROUPS * BUCKET)

    def to_stored(flat_values):
        return jnp.take(flat_values.reshape(TP_DEVS, GROUPS, BUCKET), inverse, axis=1)
    flat_master = to_flat(master)
    weight_set = unpack(flat_master)
    zero_set = jax.tree.map(jnp.zeros_like, weight_set)

    def per_group(totals, items):
        group_in, group_grad, group_lengths = items
        segment, places = group_layout(group_lengths, GTOK)

        def forward(params_now, inputs):
            return block_forward(params_now, inputs, segment, places)
        result, pullback = jax.vjp(forward, weight_set, group_in.astype(jnp.float32))
        grad_set, grad_in = pullback(group_grad.astype(jnp.float32))
        totals = jax.tree.map(jnp.add, totals, grad_set)
        return (totals, (result, grad_in))
    totals, (output, input_grad) = lax.scan(per_group, zero_set, (residual, cotangent, lengths))
    flat_grad = pack(totals)
    bounds = bound_list()
    position = jnp.arange(GROUPS * BUCKET, dtype=jnp.int32)
    step_rate = jnp.zeros((GROUPS * BUCKET,), jnp.float32) + rates[0]
    for kind_index in range(1, 8):
        step_rate = jnp.where(position >= bounds[kind_index], rates[kind_index], step_rate)
    step_value = step_count[0].astype(jnp.float32)
    new_weights, new_first, new_second, new_moving = adam_update(flat_master, to_flat(moment_one), to_flat(moment_two), to_flat(average), flat_grad, step_rate[None, :], step_value, weight_decay[0], ema_decay[0])
    return (output, input_grad, to_stored(new_weights), to_stored(new_first), to_stored(new_second), to_stored(new_moving), to_stored(flat_grad))
```

```python
import functools
import math

import jax
import jax.numpy as jnp
from jax import lax
from jax.experimental import pallas as pl
from jax.experimental.pallas import tpu as pltpu
from jax.sharding import PartitionSpec as P

D = 2048
H = 16
HD = 128
FF = 8192
ROT = 32


norm_epsilon = 1e-05
adam_epsilon = 1e-08
beta_one = 0.5
beta_two = 0.5
rope_base = 10000.0
masked_score = -1e30


def matmul(left, right):
    return jnp.dot(left, right, preferred_element_type=jnp.float32)


def product_rows(left, right):
    return lax.dot_general(
        left, right, (((0,), (0,)), ((), ())), preferred_element_type=jnp.float32
    )


def product_back(left, right):
    return lax.dot_general(
        left, right, (((1,), (1,)), ((), ())), preferred_element_type=jnp.float32
    )


def bound_list(local_width, local_ff):
    widths = [
        D * 3 * local_width,
        local_width * D,
        D * local_ff,
        local_ff * D,
        3 * local_width,
        local_ff,
        6 * D,
    ]
    bounds = [0]
    for part_width in widths:
        bounds.append(bounds[-1] + part_width)
    return bounds


def group_layout(seq_lengths, group_rows):
    order = jnp.arange(seq_lengths.shape[0], dtype=jnp.int32)
    seq_ends = jnp.sum(
        jnp.where(order[None, :] <= order[:, None], seq_lengths[None, :], 0), axis=1
    )
    starts = seq_ends - seq_lengths
    token_index = jnp.arange(group_rows, dtype=jnp.int32)
    segment = jnp.sum((token_index[:, None] >= seq_ends[None, :]).astype(jnp.int32), axis=1)
    chosen = (
        segment[:, None] == jnp.arange(seq_lengths.shape[0], dtype=jnp.int32)[None, :]
    ).astype(jnp.int32)
    places = token_index - jnp.sum(chosen * starts[None, :], axis=1)
    return (segment, places.astype(jnp.float32))


def rotary_tables(places):
    half_rot = ROT // 2
    frequency = rope_base ** (-2.0 * jnp.arange(half_rot, dtype=jnp.float32) / ROT)
    angles = places[:, None] * frequency[None, :]
    return (jnp.cos(angles)[:, None, :], jnp.sin(angles)[:, None, :])


def rotate(values, cosine, sines):
    half_rot = ROT // 2
    first = values[..., :half_rot]
    second = values[..., half_rot:ROT]
    return jnp.concatenate(
        [first * cosine - second * sines, second * cosine + first * sines, values[..., ROT:]],
        axis=-1,
    )


def norm_stats(inputs):
    center = inputs - jnp.mean(inputs, axis=-1, keepdims=True)
    scale = lax.rsqrt(jnp.mean(center * center, axis=-1, keepdims=True) + norm_epsilon)
    return (center * scale, scale)


def norm_back(grad_norm, gain, unit_rows, scale):
    scaled = grad_norm * gain
    return scale * (
        scaled
        - jnp.mean(scaled, axis=-1, keepdims=True)
        - unit_rows * jnp.mean(scaled * unit_rows, axis=-1, keepdims=True)
    )


def adam_update(
    weights, first, second, moving, gradient, step_rate, step_value, decay_rate, ema_keep
):
    bias_one = 1.0 - jnp.power(beta_one, step_value)
    bias_two = 1.0 - jnp.power(beta_two, step_value)
    new_first = beta_one * first + (1.0 - beta_one) * gradient
    new_second = beta_two * second + (1.0 - beta_two) * gradient * gradient
    ratio = new_first / bias_one / (jnp.sqrt(new_second / bias_two) + adam_epsilon)
    new_weights = weights - step_rate * (ratio + decay_rate * weights)
    new_moving = ema_keep * moving + (1.0 - ema_keep) * new_weights
    return (new_weights, new_first, new_second, new_moving)


def on_device(
    residual,
    cotangent,
    lengths,
    owners,
    step_count,
    rates,
    weight_decay,
    ema_decay,
    master,
    moment_one,
    moment_two,
    average,
):
    tensor_count = lax.axis_size("tensor")
    group_count = lax.axis_size(("dp", "chip"))
    local_heads = H // tensor_count
    local_width = local_heads * HD
    local_ff = FF // tensor_count
    rows_here = residual.shape[1]
    group_rows = rows_here * tensor_count
    bucket_size = master.shape[2]
    bounds = bound_list(local_width, local_ff)
    slots = jnp.arange(group_count, dtype=jnp.int32)
    inverse = jnp.sum(
        slots[None, :] * (owners[None, :] == slots[:, None]).astype(jnp.int32), axis=1
    )
    gathered = lax.all_gather(master.astype(jnp.bfloat16), ("dp", "chip"), axis=1, tiled=True)
    flat_params = jnp.take(gathered[0], owners, axis=0).reshape(-1)
    mixer_in = flat_params[bounds[0] : bounds[1]].reshape(D, 3 * local_width)
    mixer_out = flat_params[bounds[1] : bounds[2]].reshape(local_width, D)
    expand_weight = flat_params[bounds[2] : bounds[3]].reshape(D, local_ff)
    shrink_weight = flat_params[bounds[3] : bounds[4]].reshape(local_ff, D)
    mixer_bias = flat_params[bounds[4] : bounds[5]].astype(jnp.float32)
    expand_bias = flat_params[bounds[5] : bounds[6]].astype(jnp.float32)
    small_params = flat_params[bounds[6] : bounds[7]].reshape(6, D).astype(jnp.float32)
    own_rows = residual[0].astype(jnp.float32)
    segment, places = group_layout(lengths[0], group_rows)
    cosine, sines = rotary_tables(places)
    own_unit, own_scale = norm_stats(own_rows)
    normed_one = (own_unit * small_params[0] + small_params[1]).astype(jnp.bfloat16)
    normed_two = (own_unit * small_params[2] + small_params[3]).astype(jnp.bfloat16)
    full_one, full_two = (
        lax.all_gather(normed_one, "tensor", axis=0, tiled=True),
        lax.all_gather(normed_two, "tensor", axis=0, tiled=True),
    )
    projected = matmul(full_one, mixer_in) + mixer_bias
    head_shape = (group_rows, local_heads, HD)
    queries = rotate(projected[:, :local_width].reshape(head_shape), cosine, sines).astype(
        jnp.bfloat16
    )
    keys = rotate(
        projected[:, local_width : 2 * local_width].reshape(head_shape), cosine, sines
    ).astype(jnp.bfloat16)
    values = projected[:, 2 * local_width :].reshape(head_shape).astype(jnp.bfloat16)
    block_rows = min(512, group_rows)
    block_count = group_rows // block_rows
    score_scale = 1.0 / math.sqrt(HD)
    key_index = jnp.arange(group_rows, dtype=jnp.int32)

    def block_scores(start):
        query_block = lax.dynamic_slice_in_dim(queries, start, block_rows, 0)
        scores = (
            jnp.einsum("qhd,khd->hqk", query_block, keys, preferred_element_type=jnp.float32)
            * score_scale
        )
        row_index = start + jnp.arange(block_rows, dtype=jnp.int32)
        row_segment = lax.dynamic_slice_in_dim(segment, start, block_rows, 0)
        allowed = (row_segment[:, None] == segment[None, :]) & (
            key_index[None, :] <= row_index[:, None]
        )
        return (query_block, jnp.where(allowed[None], scores, masked_score))

    def attend_block(index):
        query_block, scores = block_scores(index * block_rows)
        row_top = jnp.max(scores, axis=-1, keepdims=True)
        raised = jnp.exp(scores - row_top)
        totals = jnp.sum(raised, axis=-1, keepdims=True)
        soft_weights = (raised / totals).astype(jnp.bfloat16)
        mixed = jnp.einsum("hqk,khd->qhd", soft_weights, values, preferred_element_type=jnp.float32)
        return (mixed.reshape(block_rows, local_width), (row_top + jnp.log(totals))[..., 0])

    context_blocks, log_blocks = lax.map(attend_block, jnp.arange(block_count, dtype=jnp.int32))
    context = context_blocks.reshape(group_rows, local_width).astype(jnp.bfloat16)
    before = matmul(full_two, expand_weight) + expand_bias
    hidden = jax.nn.gelu(before, approximate=False).astype(jnp.bfloat16)
    branches = lax.psum_scatter(
        matmul(context, mixer_out) + matmul(hidden, shrink_weight),
        "tensor",
        scatter_dimension=0,
        tiled=True,
    )
    output = own_rows + branches + small_params[4] + small_params[5]
    grad_own = cotangent[0].astype(jnp.float32)
    grad_rows = lax.all_gather(cotangent[0], "tensor", axis=0, tiled=True)
    grad_mixer_out = product_rows(context, grad_rows)
    grad_shrink = product_rows(hidden, grad_rows)
    grad_context = product_back(grad_rows, mixer_out).astype(jnp.bfloat16)
    grad_hidden = product_back(grad_rows, shrink_weight)
    gelu_pull = jax.vjp(lambda inner: jax.nn.gelu(inner, approximate=False), before)[1]
    grad_before = gelu_pull(grad_hidden)[0].astype(jnp.bfloat16)
    grad_expand = product_rows(full_two, grad_before)
    grad_expand_bias = jnp.sum(grad_before.astype(jnp.float32), axis=0)
    partial_two = product_back(grad_before, expand_weight)

    def attention_back(carry, index):
        grad_keys, grad_values = carry
        start = index * block_rows
        query_block, scores = block_scores(start)
        log_rows = lax.dynamic_index_in_dim(log_blocks, index, 0, keepdims=False)
        soft_weights = jnp.exp(scores - log_rows[..., None])
        grad_block = lax.dynamic_slice_in_dim(grad_context, start, block_rows, 0).reshape(
            block_rows, local_heads, HD
        )
        grad_weights = jnp.einsum(
            "qhd,khd->hqk", grad_block, values, preferred_element_type=jnp.float32
        )
        delta = jnp.sum(soft_weights * grad_weights, axis=-1, keepdims=True)
        grad_scores = (soft_weights * (grad_weights - delta)).astype(jnp.bfloat16)
        grad_query = (
            jnp.einsum("hqk,khd->qhd", grad_scores, keys, preferred_element_type=jnp.float32)
            * score_scale
        )
        grad_keys = (
            grad_keys
            + jnp.einsum(
                "hqk,qhd->khd", grad_scores, query_block, preferred_element_type=jnp.float32
            )
            * score_scale
        )
        grad_values = grad_values + jnp.einsum(
            "hqk,qhd->khd",
            soft_weights.astype(jnp.bfloat16),
            grad_block,
            preferred_element_type=jnp.float32,
        )
        return ((grad_keys, grad_values), grad_query)

    zero_heads = jnp.zeros(head_shape, jnp.float32)
    (grad_keys, grad_values), grad_query = lax.scan(
        attention_back, (zero_heads, zero_heads), jnp.arange(block_count, dtype=jnp.int32)
    )
    grad_query = grad_query.reshape(head_shape)
    grad_projected = jnp.concatenate(
        [
            rotate(grad_query, cosine, -sines).reshape(group_rows, local_width),
            rotate(grad_keys, cosine, -sines).reshape(group_rows, local_width),
            grad_values.reshape(group_rows, local_width),
        ],
        axis=1,
    ).astype(jnp.bfloat16)
    grad_mixer_in = product_rows(full_one, grad_projected)
    grad_mixer_bias = jnp.sum(grad_projected.astype(jnp.float32), axis=0)
    partial_one = product_back(grad_projected, mixer_in)
    bias_grad = jnp.sum(grad_own, axis=0)
    grad_one, grad_two = (
        lax.psum_scatter(partial_one, "tensor", scatter_dimension=0, tiled=True),
        lax.psum_scatter(partial_two, "tensor", scatter_dimension=0, tiled=True),
    )
    norm_grads = [
        jnp.sum(grad_one * own_unit, axis=0),
        jnp.sum(grad_one, axis=0),
        jnp.sum(grad_two * own_unit, axis=0),
        jnp.sum(grad_two, axis=0),
    ]
    input_grad = (
        grad_own
        + norm_back(grad_one, small_params[0], own_unit, own_scale)
        + norm_back(grad_two, small_params[2], own_unit, own_scale)
    )
    small_grad = jnp.stack(norm_grads + [bias_grad, bias_grad])
    small_grad = lax.psum(small_grad, "tensor")
    flat_grad = jnp.concatenate(
        [
            grad_mixer_in.reshape(-1),
            grad_mixer_out.reshape(-1),
            grad_expand.reshape(-1),
            grad_shrink.reshape(-1),
            grad_mixer_bias,
            grad_expand_bias,
            small_grad.reshape(-1),
            jnp.zeros((group_count * bucket_size - bounds[7],), jnp.float32),
        ]
    )
    stored_grad = jnp.take(flat_grad.reshape(group_count, bucket_size), inverse, axis=0)
    reduced = lax.psum_scatter(stored_grad, ("dp", "chip"), scatter_dimension=0, tiled=True)[0]
    my_bucket = inverse[lax.axis_index(("dp", "chip"))]
    position = my_bucket * bucket_size + jnp.arange(bucket_size, dtype=jnp.int32)
    step_rate = jnp.zeros((bucket_size,), jnp.float32) + rates[0]
    for kind_index in range(1, 8):
        step_rate = jnp.where(position >= bounds[kind_index], rates[kind_index], step_rate)
    step_value = step_count[0].astype(jnp.float32)
    new_weights, new_first, new_second, new_moving = adam_update(
        master[0, 0],
        moment_one[0, 0],
        moment_two[0, 0],
        average[0, 0],
        reduced,
        step_rate,
        step_value,
        weight_decay[0],
        ema_decay[0],
    )
    return (
        output[None],
        input_grad[None],
        new_weights[None, None],
        new_first[None, None],
        new_second[None, None],
        new_moving[None, None],
        reduced[None, None],
    )


LANES = 128
TROWS = 16


def fits(mesh):
    return mesh.shape["dp"] == 4 and mesh.shape["chip"] == 2 and mesh.shape["tensor"] == 4


def device_program(mesh):
    return on_device_fast if fits(mesh) else on_device


CHUNKS = 4
BROWS = 768
QROWS = 1024
FRONT = 128
BACK = 256
FLAT = 12304
HBM = pl.ANY


def params(limit_mb, **more):
    return pltpu.CompilerParams(vmem_limit_bytes=limit_mb * 1024 * 1024, **more)


def pack_kernel(bucket_ref, flat_ref, *refs):
    outs, padded, sem = refs[:CHUNKS], refs[CHUNKS], refs[CHUNKS + 1]
    bucket = bucket_ref[0]
    load = pltpu.make_async_copy(flat_ref, padded.at[pl.ds(FRONT, FLAT)], sem)
    load.start()
    padded[pl.ds(0, FRONT)] = jnp.zeros((FRONT, LANES), jnp.float32)
    padded[pl.ds(FRONT + FLAT, BACK)] = jnp.zeros((BACK, LANES), jnp.float32)
    load.wait()
    wide, narrow = 16 // CHUNKS, 12 // CHUNKS

    def take(start, stride):
        return padded[pl.ds(start, 16, stride=stride), :].astype(jnp.bfloat16)

    @pl.when(bucket >= 2)
    def _():
        def step(tile, carry):
            row = pl.multiple_of(tile * 16, 16)
            for panel in range(16):
                outs[panel // wide][pl.ds((panel % wide) * BROWS + row, 16), :] = take(
                    (row - bucket) * 16 + panel + FRONT, 16
                )
            return carry

        lax.fori_loop(0, BROWS // 16, step, 0)

    @pl.when(bucket < 2)
    def _():
        def step(tile, carry):
            row = pl.multiple_of(tile * 16, 16)
            for panel in range(12):
                outs[panel // narrow][pl.ds((panel % narrow) * QROWS + row, 16), :] = take(
                    row * 12 + panel - 16 * bucket + FRONT, 12
                )
            return carry

        lax.fori_loop(0, QROWS // 16, step, 0)

    main = wide * BROWS

    @pl.when(bucket >= 1)
    def _():
        for panel in range(16):
            outs[panel // wide][pl.ds(main + (panel % wide) * TROWS, TROWS), :] = take(
                (BROWS - bucket) * 16 + panel + FRONT, 16
            )

    @pl.when(bucket == 0)
    def _():
        for part in range(CHUNKS):
            for panel in range(wide):
                source = part * narrow + min(panel, narrow - 1)
                outs[part][pl.ds(main + panel * TROWS, TROWS), :] = take(
                    QROWS * 12 + source + FRONT, 12
                )


def chunk_rows():
    return (16 // CHUNKS) * (BROWS + TROWS)


def pack(bucket, flat):
    return pl.pallas_call(
        pack_kernel,
        out_shape=[jax.ShapeDtypeStruct((chunk_rows(), LANES), jnp.bfloat16)] * CHUNKS,
        in_specs=[pl.BlockSpec(memory_space=pltpu.SMEM), pl.BlockSpec(memory_space=HBM)],
        out_specs=[pl.BlockSpec(memory_space=pltpu.VMEM)] * CHUNKS,
        scratch_shapes=[
            pltpu.VMEM((FRONT + FLAT + BACK, LANES), jnp.float32),
            pltpu.SemaphoreType.DMA,
        ],
        compiler_params=params(24),
        name="pack_params",
    )(bucket, flat)


PLACES = {
    0: (("in", 0, 1024, 0),),
    1: (("in", 1024, 1024, 0),),
    2: (("out", 0, 512, 0), ("up", 0, 256, 512)),
    3: (("up", 256, 768, 0),),
    4: (("up", 1024, 768, 0),),
    5: (("up", 1792, 256, 0), ("down", 0, 512, 256)),
    6: (("down", 512, 768, 0),),
    7: (("down", 1280, 768, 0),),
}
NAMES = ("in", "out", "up", "down", "bias")


def panels_of(bucket):
    return (12 if bucket < 2 else 16) // CHUNKS


MATRICES = {
    "in": (2048, 1536),
    "out": (512, 2048),
    "up": (2048, 2048),
    "down": (2048, 2048),
    "bias": (TROWS, 2048),
}


def head_of(bucket):
    if bucket == 8:
        return ("bias", 0)
    name, first, _, _ = PLACES[bucket][0]
    return (name, first)


def columns(panel):
    return pl.ds(panel * LANES, LANES)


def unpack_kernel(part, bucket_ref, *refs):
    sources = refs[:8]
    staged, load_sems, store_sems = refs[-3:]
    outs = dict(zip(NAMES, refs[-8:-3], strict=True))
    main = (16 // CHUNKS) * BROWS
    loads = [
        pltpu.make_async_copy(sources[k], staged.at[bucket_ref[k]], load_sems.at[k])
        for k in range(8)
    ]
    for load in loads:
        load.start()
    for load in loads:
        load.wait()
    stores = []

    def store(bucket, row, name, first, rows, panel):
        wide = panels_of(bucket)
        stores.append(
            pltpu.make_async_copy(
                staged.at[bucket, pl.ds(row, rows)],
                outs[name].at[pl.ds(first, rows), columns(part * wide + panel)],
                store_sems.at[len(stores)],
            )
        )
        stores[-1].start()

    for bucket in range(8):
        span = QROWS if bucket < 2 else BROWS
        for panel in range(panels_of(bucket)):
            if bucket:
                head = pl.ds(panel * span, TROWS)
                tail = pl.ds(main + panel * TROWS, TROWS)
                staged[bucket, head, :] = staged[bucket, head, :] + staged[bucket - 1, tail, :]
            for name, first, rows, offset in PLACES[bucket]:
                store(bucket, panel * span + offset, name, first, rows, panel)
    for panel in range(16 // CHUNKS):
        store(7, main + panel * TROWS, "bias", 0, TROWS, panel)
    for put in stores:
        put.wait()


def unpack(part, buckets, sources, before):
    copies = sum(len(PLACES[b]) * panels_of(b) for b in range(8)) + 16 // CHUNKS
    return pl.pallas_call(
        functools.partial(unpack_kernel, part),
        out_shape=[jax.ShapeDtypeStruct(MATRICES[name], jnp.bfloat16) for name in NAMES],
        in_specs=[pl.BlockSpec(memory_space=pltpu.SMEM)]
        + [pl.BlockSpec(memory_space=HBM)] * (8 + len(before)),
        out_specs=[pl.BlockSpec(memory_space=HBM)] * 5,
        input_output_aliases={9 + at: at for at in range(len(before))},
        scratch_shapes=[
            pltpu.VMEM((8, chunk_rows(), LANES), jnp.bfloat16),
            pltpu.SemaphoreType.DMA((8,)),
            pltpu.SemaphoreType.DMA((copies,)),
        ],
        compiler_params=params(16),
        name="unpack_params",
    )(buckets, *sources, *before)


GRAD_ROWS = 256
IN_STEPS, OUT_STEPS, UP_STEPS, DOWN_STEPS = 8, 2, 8, 8
GRAD_STEPS = IN_STEPS + OUT_STEPS + UP_STEPS + DOWN_STEPS


def weight_grad_kernel(table, *refs):
    lefts, rights = refs[:8], refs[8:14]
    sent, kept, wide32, wide16, tail32, tail16, sems, tail_sem = refs[14:]
    step = pl.program_id(0)
    main = (16 // CHUNKS) * BROWS

    def bucket_of(at):
        return jnp.where(at < IN_STEPS, at // 4, (at - 2) // 3)

    def copies(at, act):
        slot = lax.rem(at, 2)
        bucket = bucket_of(at)
        inner = at < IN_STEPS
        goes, place = table[1 + bucket], table[9 + bucket]
        for panels, span, mine in ((3, QROWS, inner), (4, BROWS, jnp.logical_not(inner))):
            offset = pl.multiple_of(
                (lax.rem(at, 4) if span == QROWS else lax.rem(at - 2, 3)) * GRAD_ROWS, GRAD_ROWS
            )
            for away, stage, target in ((1, wide16, sent), (0, wide32, kept)):

                @pl.when(jnp.logical_and(mine, goes == away))
                def _(panels=panels, span=span, offset=offset, stage=stage, target=target):
                    for panel in range(panels):
                        act(
                            pltpu.make_async_copy(
                                stage.at[slot, pl.ds(panel * GRAD_ROWS, GRAD_ROWS)],
                                target.at[place, pl.ds(panel * span + offset, GRAD_ROWS)],
                                sems.at[slot, panel],
                            )
                        )

    @pl.when(step >= 2)
    def _():
        copies(step - 2, lambda copy: copy.wait())

    @pl.when(step == 0)
    def _():
        tail32[...] = jnp.zeros_like(tail32)
        tail16[...] = jnp.zeros_like(tail16)

    def block(pair, right, panels, first):
        left_own, left_other = lefts[2 * pair], lefts[2 * pair + 1]
        right_own, right_other = rights[2 * right], rights[2 * right + 1]
        value = product_rows(left_own[...], right_own[...]) + product_rows(
            left_other[...], right_other[...]
        )
        slot = lax.rem(step, 2)
        for panel in range(panels):
            part = value[:, panel * LANES : (panel + 1) * LANES]
            rows = pl.ds(panel * GRAD_ROWS, GRAD_ROWS)
            wide32[slot, rows, :] = part
            wide16[slot, rows, :] = part.astype(jnp.bfloat16)

        @pl.when(first)
        def _():
            before = jnp.maximum(bucket_of(step) - 1, 0)
            for panel in range(panels):
                part = value[:TROWS, panel * LANES : (panel + 1) * LANES]
                rows = pl.ds(panel * TROWS, TROWS)
                tail32[before, rows, :] = part
                tail16[before, rows, :] = part.astype(jnp.bfloat16)

    third = lax.rem(step - 2, 3) == 0
    edges = (0, IN_STEPS, IN_STEPS + OUT_STEPS, IN_STEPS + OUT_STEPS + UP_STEPS, GRAD_STEPS)
    for pair, right in enumerate((0, 1, 2, 1)):

        @pl.when(jnp.logical_and(step >= edges[pair], step < edges[pair + 1]))
        def _(pair=pair, right=right):
            block(pair, right, 3 if pair == 0 else 4, step == 4 if pair == 0 else third)

    copies(step, lambda copy: copy.start())

    @pl.when(step == GRAD_STEPS - 1)
    def _():
        def tails(act):
            for bucket in range(8):
                for away, stage, target in ((1, tail16, sent), (0, tail32, kept)):

                    @pl.when(table[1 + bucket] == away)
                    def _(bucket=bucket, stage=stage, target=target):
                        act(
                            pltpu.make_async_copy(
                                stage.at[bucket],
                                target.at[table[9 + bucket], pl.ds(main, stage.shape[1])],
                                tail_sem.at[bucket],
                            )
                        )

        tails(lambda copy: copy.start())
        copies(step - 1, lambda copy: copy.wait())
        copies(step, lambda copy: copy.wait())
        tails(lambda copy: copy.wait())


def weight_grads(part, table, lefts, rights):
    tokens = lefts[0].shape[0]

    def columns_at(first, count):
        return pl.BlockSpec(
            (tokens, GRAD_ROWS), lambda i, table: (0, jnp.clip(i - first, 0, count - 1))
        )

    firsts = (0, IN_STEPS, IN_STEPS + OUT_STEPS, IN_STEPS + OUT_STEPS + UP_STEPS)
    left_specs = [
        columns_at(first, count)
        for first, count in zip(firsts, (IN_STEPS, OUT_STEPS, UP_STEPS, DOWN_STEPS), strict=True)
        for _ in range(2)
    ]
    right_specs = []
    for width in (384, 512, 512):
        right_specs.append(
            pl.BlockSpec((tokens, width), lambda i, table: (0, 2 * table[0] + part))
        )
        right_specs.append(pl.BlockSpec((tokens, width), lambda i, table: (0, part)))
    rows = chunk_rows()
    return pl.pallas_call(
        weight_grad_kernel,
        out_shape=[
            jax.ShapeDtypeStruct((4, rows, LANES), jnp.bfloat16),
            jax.ShapeDtypeStruct((4, rows, LANES), jnp.float32),
        ],
        grid_spec=pltpu.PrefetchScalarGridSpec(
            num_scalar_prefetch=1,
            grid=(GRAD_STEPS,),
            in_specs=left_specs + right_specs,
            out_specs=[pl.BlockSpec(memory_space=HBM)] * 2,
            scratch_shapes=[
                pltpu.VMEM((2, 4 * GRAD_ROWS, LANES), jnp.float32),
                pltpu.VMEM((2, 4 * GRAD_ROWS, LANES), jnp.bfloat16),
                pltpu.VMEM((8, 4 * TROWS, LANES), jnp.float32),
                pltpu.VMEM((8, 4 * TROWS, LANES), jnp.bfloat16),
                pltpu.SemaphoreType.DMA((2, 4)),
                pltpu.SemaphoreType.DMA((8,)),
            ],
        ),
        compiler_params=params(48),
        name="weight_grads",
    )(table, *lefts, *rights)


def place_rows_kernel(index_ref, *refs):
    pieces, out, sems = refs[:7], refs[7], refs[8]
    rows = pieces[0].shape[0]
    here = index_ref[0]

    def each(act):
        for at, piece in enumerate(pieces):
            target = here + at - 3

            @pl.when(jnp.logical_and(target >= 0, target <= 3))
            def _(at=at, piece=piece, target=target):
                spot = pl.ds(pl.multiple_of(jnp.clip(target, 0, 3) * rows, rows), rows)
                act(pltpu.make_async_copy(piece, out.at[spot], sems.at[at]))

    each(lambda copy: copy.start())
    each(lambda copy: copy.wait())


def place_rows(index, pieces):
    rows, width = pieces[0].shape
    return pl.pallas_call(
        place_rows_kernel,
        out_shape=jax.ShapeDtypeStruct((4 * rows, width), pieces[0].dtype),
        in_specs=[pl.BlockSpec(memory_space=pltpu.SMEM)] + [pl.BlockSpec(memory_space=HBM)] * 7,
        out_specs=pl.BlockSpec(memory_space=pltpu.VMEM),
        scratch_shapes=[pltpu.SemaphoreType.DMA((7,))],
        compiler_params=params(12),
        name="place_rows",
    )(index, *pieces)


ADAM_ROWS = 1024


def adam_kernel(table, scalar_ref, rate_ref, *refs):
    pieces, small = refs[:4], refs[4]
    weights, first, second, moving = refs[5:9]
    new_weights, new_first, new_second, new_moving, reduced = refs[9:14]
    held, flat, sems = refs[14:]
    bucket, core = table[0], table[1]
    wide, narrow = 16 // CHUNKS, 12 // CHUNKS
    main = wide * BROWS

    @pl.when(pl.program_id(0) == 0)
    def _():
        loads = []
        for at, piece in enumerate(pieces):
            half = core if at < 2 else 1 - core
            loads.append(
                pltpu.make_async_copy(piece, held.at[2 * half + at % 2], sems.at[at])
            )
            loads[-1].start()
        for load in loads:
            load.wait()

        def put(part, row, start, stride):
            flat[pl.ds(start, 16, stride=stride), :] = held[part, pl.ds(row, 16), :]

        @pl.when(bucket >= 2)
        def _():
            def step(tile, carry):
                row = pl.multiple_of(tile * 16, 16)
                for panel in range(16):
                    put(
                        panel // wide,
                        (panel % wide) * BROWS + row,
                        (row - bucket) * 16 + panel + FRONT,
                        16,
                    )
                return carry

            lax.fori_loop(0, BROWS // 16, step, 0)

        @pl.when(bucket < 2)
        def _():
            def step(tile, carry):
                row = pl.multiple_of(tile * 16, 16)
                for panel in range(12):
                    put(
                        panel // narrow,
                        (panel % narrow) * QROWS + row,
                        row * 12 + panel - 16 * bucket + FRONT,
                        12,
                    )
                return carry

            lax.fori_loop(0, QROWS // 16, step, 0)

        @pl.when(bucket >= 1)
        def _():
            for panel in range(16):
                put(
                    panel // wide,
                    main + (panel % wide) * TROWS,
                    (BROWS - bucket) * 16 + panel + FRONT,
                    16,
                )

        @pl.when(bucket == 0)
        def _():
            for panel in range(12):
                put(
                    panel // narrow,
                    main + (panel % narrow) * TROWS,
                    QROWS * 12 + panel + FRONT,
                    12,
                )

        @pl.when(bucket == 7)
        def _():
            flat[pl.ds(FRONT + FLAT - LANES, LANES), :] = small[...]

    start = pl.program_id(0) * ADAM_ROWS
    gradient = flat[pl.ds(pl.multiple_of(FRONT + start, 8), ADAM_ROWS), :]
    row = bucket * FLAT + start + lax.broadcasted_iota(jnp.int32, (ADAM_ROWS, LANES), 0)
    rate = jnp.full((ADAM_ROWS, LANES), rate_ref[0], jnp.float32)
    for kind, bound in enumerate(bound_list(512, 2048)[1:]):
        rate = jnp.where(row >= bound // LANES, rate_ref[kind + 1], rate)
    reduced[...] = gradient
    bias_one, bias_two, decay, keep = (scalar_ref[at] for at in range(4))
    one = beta_one * first[...] + (1.0 - beta_one) * gradient
    two = beta_two * second[...] + (1.0 - beta_two) * gradient * gradient
    old = weights[...]
    ratio = one / bias_one / (jnp.sqrt(two / bias_two) + adam_epsilon)
    fresh = old - rate * (ratio + decay * old)
    new_weights[...] = fresh
    new_first[...] = one
    new_second[...] = two
    new_moving[...] = keep * moving[...] + (1.0 - keep) * fresh


def adam(table, scalars, rates, pieces, small, state):
    steps = -(-FLAT // ADAM_ROWS)
    block = pl.BlockSpec((ADAM_ROWS, LANES), lambda i: (i, 0))
    return pl.pallas_call(
        adam_kernel,
        grid=(steps,),
        out_shape=[jax.ShapeDtypeStruct((FLAT, LANES), jnp.float32)] * 5,
        in_specs=[pl.BlockSpec(memory_space=pltpu.SMEM)] * 3
        + [pl.BlockSpec(memory_space=HBM)] * 4
        + [pl.BlockSpec(memory_space=pltpu.VMEM)]
        + [block] * 4,
        out_specs=[block] * 5,
        scratch_shapes=[
            pltpu.VMEM((4, chunk_rows(), LANES), jnp.float32),
            pltpu.VMEM((FRONT + steps * ADAM_ROWS, LANES), jnp.float32),
            pltpu.SemaphoreType.DMA((4,)),
        ],
        compiler_params=params(40),
        name="adam",
    )(table, scalars, rates, *pieces, small, *state)


FF_BLOCK = 256


def hidden_kernel(normed, up, up_bias, hidden, slope):
    before = matmul(normed[...], up[...]) + up_bias[...]
    half = 0.5 + 0.5 * lax.erf(before * math.sqrt(0.5))
    hidden[...] = (before * half).astype(jnp.bfloat16)
    slope[...] = half + before * jnp.exp(-0.5 * before * before) * (1.0 / math.sqrt(2.0 * math.pi))


def hidden_layer(normed, up, up_bias):
    rows, units = normed.shape[0], up.shape[1]
    block = pl.BlockSpec((rows, FF_BLOCK), lambda i: (0, i))
    return pl.pallas_call(
        hidden_kernel,
        grid=(units // FF_BLOCK,),
        out_shape=[
            jax.ShapeDtypeStruct((rows, units), jnp.bfloat16),
            jax.ShapeDtypeStruct((rows, units), jnp.float32),
        ],
        in_specs=[
            pl.BlockSpec(memory_space=pltpu.VMEM),
            pl.BlockSpec((D, FF_BLOCK), lambda i: (0, i)),
            pl.BlockSpec((1, FF_BLOCK), lambda i: (0, i)),
        ],
        out_specs=[block, block],
        compiler_params=params(40),
        name="hidden_layer",
    )(normed, up, up_bias)


def hidden_back_kernel(grads, down, slope, grad_before, grad_bias):
    rounded = (slope[...] * product_back(grads[...], down[...])).astype(jnp.bfloat16)
    grad_before[...] = rounded
    grad_bias[...] = jnp.sum(rounded.astype(jnp.float32), axis=0, keepdims=True)


def hidden_back(grads, down, slope):
    rows, units = slope.shape
    block = pl.BlockSpec((rows, FF_BLOCK), lambda i: (0, i))
    return pl.pallas_call(
        hidden_back_kernel,
        grid=(units // FF_BLOCK,),
        out_shape=[
            jax.ShapeDtypeStruct((rows, units), jnp.bfloat16),
            jax.ShapeDtypeStruct((1, units), jnp.float32),
        ],
        in_specs=[
            pl.BlockSpec(memory_space=pltpu.VMEM),
            pl.BlockSpec((FF_BLOCK, D), lambda i: (i, 0)),
            block,
        ],
        out_specs=[block, pl.BlockSpec((1, FF_BLOCK), lambda i: (0, i))],
        compiler_params=params(40),
        name="hidden_back",
    )(grads, down, slope)


QUERY_BLOCK = 256


def turn(values, tables, sign):
    plain, lower, upper = tables
    half_rot = ROT // 2
    return (
        values * plain
        + pltpu.roll(values, HD - half_rot, 1) * (sign * lower)
        + pltpu.roll(values, half_rot, 1) * (sign * upper)
    )


def block_scores(query, keys, begins, first):
    scores = product_back(query, keys) * (1.0 / math.sqrt(HD))
    row_index = first + lax.broadcasted_iota(jnp.int32, scores.shape, 0)
    key_index = lax.broadcasted_iota(jnp.int32, scores.shape, 1)
    allowed = (key_index <= row_index) & (key_index >= begins)
    return jnp.where(allowed, scores, masked_score)


def head_columns(width, head):
    return [pl.ds(pl.multiple_of(part * width + head * HD, HD), HD) for part in range(3)]


def attend_kernel(projected, bias, plain, lower, upper, begins, context, turned, logs):
    rows, width = context.shape

    def one_head(head, carry):
        cols = head_columns(width, head)
        tables = (plain[...], lower[...], upper[...])
        raw = [projected[:, col] + bias[:, col] for col in cols]
        queries = turn(raw[0], tables, 1.0).astype(jnp.bfloat16)
        keys = turn(raw[1], tables, 1.0).astype(jnp.bfloat16)
        values = raw[2].astype(jnp.bfloat16)
        for col, value in zip(cols, (queries, keys, values), strict=True):
            turned[:, col] = value
        for first in range(0, rows, QUERY_BLOCK):
            last = first + QUERY_BLOCK
            mine = slice(first, last)
            scores = block_scores(queries[mine], keys[:last], begins[mine, :], first)
            top = jnp.max(scores, axis=-1, keepdims=True)
            raised = jnp.exp(scores - top)
            total = jnp.sum(raised, axis=-1, keepdims=True)
            rounded = (raised / total).astype(jnp.bfloat16)
            context[mine, cols[0]] = matmul(rounded, values[:last]).astype(jnp.bfloat16)
            logs[head, mine, :] = top + jnp.log(total)
        return carry

    lax.fori_loop(0, width // HD, one_head, 0)


def attend(projected, bias, tables, begins):
    rows, width = projected.shape[0], projected.shape[1] // 3
    whole = pl.BlockSpec(memory_space=pltpu.VMEM)
    return pl.pallas_call(
        attend_kernel,
        out_shape=[
            jax.ShapeDtypeStruct((rows, width), jnp.bfloat16),
            jax.ShapeDtypeStruct((rows, 3 * width), jnp.bfloat16),
            jax.ShapeDtypeStruct((width // HD, rows, 1), jnp.float32),
        ],
        in_specs=[whole] * 6,
        out_specs=[whole] * 3,
        compiler_params=params(48),
        name="attend",
    )(projected, bias, *tables, begins)


def attend_back_kernel(
    turned, logs, plain, lower, upper, begins, grad_context, grad_projected, key_sum, value_sum
):
    rows, width = grad_context.shape
    score_scale = 1.0 / math.sqrt(HD)

    def one_head(head, carry):
        cols = head_columns(width, head)
        queries, keys, values = (turned[:, col] for col in cols)
        key_sum[...] = jnp.zeros_like(key_sum)
        value_sum[...] = jnp.zeros_like(value_sum)
        for first in range(0, rows, QUERY_BLOCK):
            last = first + QUERY_BLOCK
            mine = slice(first, last)
            query = queries[mine]
            scores = block_scores(query, keys[:last], begins[mine, :], first)
            soft = jnp.exp(scores - logs[head, mine, :])
            grad_mine = grad_context[mine, cols[0]]
            grad_soft = product_back(grad_mine, values[:last])
            delta = jnp.sum(soft * grad_soft, axis=-1, keepdims=True)
            grad_scores = (soft * (grad_soft - delta)).astype(jnp.bfloat16)
            grad_query = matmul(grad_scores, keys[:last]) * score_scale
            tables = (plain[mine, :], lower[mine, :], upper[mine, :])
            grad_projected[mine, cols[0]] = turn(grad_query, tables, -1.0).astype(jnp.bfloat16)
            key_sum[:last, :] += product_rows(grad_scores, query)
            value_sum[:last, :] += product_rows(soft.astype(jnp.bfloat16), grad_mine)
        tables = (plain[...], lower[...], upper[...])
        grad_projected[:, cols[1]] = turn(key_sum[...] * score_scale, tables, -1.0).astype(
            jnp.bfloat16
        )
        grad_projected[:, cols[2]] = value_sum[...].astype(jnp.bfloat16)
        return carry

    lax.fori_loop(0, width // HD, one_head, 0)


def attend_back(turned, logs, tables, begins, grad_context):
    rows, width = grad_context.shape
    whole = pl.BlockSpec(memory_space=pltpu.VMEM)
    return pl.pallas_call(
        attend_back_kernel,
        out_shape=jax.ShapeDtypeStruct((rows, 3 * width), jnp.bfloat16),
        in_specs=[whole] * 7,
        out_specs=whole,
        scratch_shapes=[pltpu.VMEM((rows, HD), jnp.float32)] * 2,
        compiler_params=params(48),
        name="attend_back",
    )(turned, logs, *tables, begins, grad_context)


def rope_tables(places):
    half_rot = ROT // 2
    frequency = rope_base ** (-2.0 * jnp.arange(half_rot, dtype=jnp.float32) / ROT)
    angles = places[:, None] * frequency[None, :]
    cosine, sines = jnp.cos(angles), jnp.sin(angles)
    rest = jnp.zeros((places.shape[0], HD - ROT), jnp.float32)
    none = jnp.zeros_like(sines)
    return (
        jnp.concatenate([cosine, cosine, rest + 1.0], axis=1),
        jnp.concatenate([-sines, none, rest], axis=1),
        jnp.concatenate([none, sines, rest], axis=1),
    )


def along_x(value):
    return lax.ppermute(value, "dp", [(i, i ^ 1) for i in range(4)])


def along_y(value):
    return lax.ppermute(value, "dp", [(i, i ^ 2) for i in range(4)])


def across(value):
    return lax.ppermute(value, "chip", [(0, 1), (1, 0)])


def spread_rows(value):
    ups, downs = [value], [value]
    for hop in range(3):
        ups.append(lax.ppermute(ups[-1], "tensor", [(i, i + 1) for i in range(hop, 3)]))
        downs.append(lax.ppermute(downs[-1], "tensor", [(i + 1, i) for i in range(3 - hop)]))
    return [ups[3], ups[2], ups[1], value, downs[1], downs[2], downs[3]]


def sum_rows(partial, here):
    rows = partial.shape[0] // 4

    def block(index):
        return lax.dynamic_slice_in_dim(partial, jnp.clip(index, 0, 3) * rows, rows, 0)

    up = down = None
    for hop in range(1, 4):
        up_value, down_value = block(here + 4 - hop), block(here - 4 + hop)
        if up is not None:
            up_value = up_value + up.astype(jnp.float32)
            down_value = down_value + down.astype(jnp.float32)
        up = lax.ppermute(
            up_value.astype(jnp.bfloat16), "tensor", [(i, i + 1) for i in range(hop)]
        )
        down = lax.ppermute(
            down_value.astype(jnp.bfloat16), "tensor", [(i, i - 1) for i in range(4 - hop, 4)]
        )
    return block(here) + (up.astype(jnp.float32) + down.astype(jnp.float32))


def on_device_fast(
    residual,
    cotangent,
    lengths,
    owners,
    step_count,
    rates,
    weight_decay,
    ema_decay,
    master,
    moment_one,
    moment_two,
    average,
):
    local_width = HD * H // lax.axis_size("tensor")
    group_rows = residual.shape[1] * lax.axis_size("tensor")
    slots = jnp.arange(8, dtype=jnp.int32)
    inverse = jnp.sum(
        slots[None, :] * (owners[None, :] == slots[:, None]).astype(jnp.int32), axis=1
    )
    data_index, core, here = lax.axis_index("dp"), lax.axis_index("chip"), lax.axis_index("tensor")
    partners = jnp.stack([(data_index ^ j) * 2 + (core ^ c) for c in range(2) for j in range(4)])
    buckets = jnp.sum(
        jnp.where(partners[:, None] == slots[None, :], inverse[None, :], 0), axis=1
    ).astype(jnp.int32)
    partner_of = jnp.sum(
        jnp.where(buckets[None, :] == slots[:, None], slots[None, :], 0), axis=1
    )
    hop, other = partner_of % 4, partner_of // 4
    grad_tables = [
        jnp.concatenate([core[None], hop % 2, (hop // 2) * 2 + other]).astype(jnp.int32),
        jnp.concatenate([core[None], hop // 2, (hop % 2) * 2 + other]).astype(jnp.int32),
    ]

    row_pieces = spread_rows(residual[0])
    grad_pieces = spread_rows(cotangent[0])
    packed = pack(buckets[:1], master.reshape(FLAT, LANES))
    weights = []
    for part, own in enumerate(packed):
        from_x, from_y = along_x(own), along_y(own)
        diagonal = along_x(from_y) if part % 2 == 0 else along_y(from_x)
        mine = [own, from_x, from_y, diagonal]
        weights = unpack(part, buckets, mine + [across(value) for value in mine], weights)
    mixer_in, mixer_out, expand_weight, shrink_weight, biases = weights
    flat_bias = biases[:8].reshape(-1).astype(jnp.float32)
    mixer_bias = flat_bias[: 3 * local_width]
    expand_bias = flat_bias[3 * local_width : 3 * local_width + D]
    small_params = flat_bias[3 * local_width + D : 3 * local_width + 7 * D].reshape(6, D)

    index = here[None].astype(jnp.int32)
    full_rows = place_rows(index, row_pieces)
    other_rows = across(full_rows)
    grad_rows = place_rows(index, grad_pieces)
    half_width = D // 2
    other_grads = across(lax.dynamic_slice_in_dim(grad_rows, (1 - core) * half_width, half_width, 1))

    own_rows = residual[0].astype(jnp.float32)
    own_unit, own_scale = norm_stats(own_rows)

    def norms(rows):
        unit, _ = norm_stats(rows.astype(jnp.float32))
        return (
            (unit * small_params[0] + small_params[1]).astype(jnp.bfloat16),
            (unit * small_params[2] + small_params[3]).astype(jnp.bfloat16),
        )

    full_one, full_two = norms(full_rows)
    other_one, other_two = norms(other_rows)

    order = jnp.arange(lengths.shape[1], dtype=jnp.int32)
    seq_ends = jnp.sum(jnp.where(order[None, :] <= order[:, None], lengths[0][None, :], 0), axis=1)
    token_index = jnp.arange(group_rows, dtype=jnp.int32)
    passed = (token_index[:, None] >= seq_ends[None, :]).astype(jnp.int32)
    begins = jnp.sum(passed * lengths[0][None, :], axis=1)
    tables = rope_tables((token_index - begins).astype(jnp.float32))
    begins = begins[:, None]

    projected = matmul(full_one, mixer_in)
    context, turned, logs = attend(projected, mixer_bias[None], tables, begins)
    hidden, slope = hidden_layer(full_two, expand_weight, expand_bias[None])
    other_context, other_hidden = across(context), across(hidden)
    branches = sum_rows(matmul(context, mixer_out) + matmul(hidden, shrink_weight), here)
    output = own_rows + branches + small_params[4] + small_params[5]

    grad_before, grad_expand_bias = hidden_back(grad_rows, shrink_weight, slope)
    other_before = across(
        lax.dynamic_slice_in_dim(grad_before, (1 - core) * half_width, half_width, 1)
    )
    grad_context = product_back(grad_rows, mixer_out).astype(jnp.bfloat16)
    grad_projected = attend_back(turned, logs, tables, begins, grad_context)
    half_in = 3 * local_width // 2
    other_projected = across(
        lax.dynamic_slice_in_dim(grad_projected, (1 - core) * half_in, half_in, 1)
    )

    lefts = [
        full_one, other_one, context, other_context, full_two, other_two, hidden, other_hidden
    ]
    rights = [grad_projected, other_projected, grad_rows, other_grads, grad_before, other_before]
    pieces = []
    for part, (first, second) in enumerate(((along_x, along_y), (along_y, along_x))):
        sent, kept = weight_grads(part, grad_tables[part], lefts, rights)
        came = first(sent)
        passed_on = second((kept[2:] + came[2:].astype(jnp.float32)).astype(jnp.bfloat16))
        total = kept[:2] + came[:2].astype(jnp.float32) + passed_on.astype(jnp.float32)
        pieces.append((total[0], across(total[1])))
    pieces = [pieces[0][0], pieces[1][0], pieces[0][1], pieces[1][1]]

    partial_one = product_back(grad_projected, mixer_in)
    partial_two = product_back(grad_before, expand_weight)
    unit_rows, _ = norm_stats(full_rows.astype(jnp.float32))
    norm_grads = jnp.stack(
        [
            jnp.sum(partial_one * unit_rows, axis=0),
            jnp.sum(partial_one, axis=0),
            jnp.sum(partial_two * unit_rows, axis=0),
            jnp.sum(partial_two, axis=0),
        ]
    )
    scaled = sum_rows(partial_one * small_params[0] + partial_two * small_params[2], here)
    grad_own = cotangent[0].astype(jnp.float32)
    input_grad = grad_own + own_scale * (
        scaled
        - jnp.mean(scaled, axis=-1, keepdims=True)
        - own_unit * jnp.mean(scaled * own_unit, axis=-1, keepdims=True)
    )
    seen = jnp.stack(spread_rows(norm_grads))
    ordered = lax.dynamic_slice_in_dim(seen, 3 - here, 4, 0)
    norm_grads = ((ordered[0] + ordered[1]) + ordered[2]) + ordered[3]
    bias_grad = jnp.sum(grad_rows.astype(jnp.float32), axis=0)
    small = jnp.concatenate(
        [
            jnp.sum(grad_projected.astype(jnp.float32), axis=0),
            grad_expand_bias[0],
            norm_grads.reshape(-1),
            bias_grad,
            bias_grad,
            jnp.zeros((8 * D - 3 * local_width - 7 * D,), jnp.float32),
        ]
    ).reshape(LANES, LANES)
    for move in (across, along_x, along_y):
        small = small + move(small)

    step_value = step_count[0].astype(jnp.float32)
    scalars = jnp.stack(
        [
            1.0 - jnp.power(beta_one, step_value),
            1.0 - jnp.power(beta_two, step_value),
            weight_decay[0],
            ema_decay[0],
        ]
    )
    state = [v.reshape(FLAT, LANES) for v in (master, moment_one, moment_two, average)]
    table = jnp.stack([buckets[0], core.astype(jnp.int32)])
    results = adam(table, scalars, rates, pieces, small, state)
    return (output[None], input_grad[None], *[v.reshape(master.shape) for v in results])


def solution(mesh):
    placed = (
        P(("dp", "chip"), "tensor", None),
        P(("dp", "chip"), "tensor", None),
        P(("dp", "chip"), None),
        P(),
        P(),
        P(),
        P(),
        P(),
        P("tensor", ("dp", "chip"), None),
        P("tensor", ("dp", "chip"), None),
        P("tensor", ("dp", "chip"), None),
        P("tensor", ("dp", "chip"), None),
    )
    return jax.shard_map(
        device_program(mesh),
        mesh=mesh,
        in_specs=placed,
        out_specs=(
            P(("dp", "chip"), "tensor", None),
            P(("dp", "chip"), "tensor", None),
            P("tensor", ("dp", "chip"), None),
            P("tensor", ("dp", "chip"), None),
            P("tensor", ("dp", "chip"), None),
            P("tensor", ("dp", "chip"), None),
            P("tensor", ("dp", "chip"), None),
        ),
        check_vma=False,
    )
```

```python
import functools
import math

import jax
import jax.numpy as jnp
from jax import lax
from jax.experimental import pallas as pl
from jax.experimental.pallas import tpu as pltpu
from jax.sharding import PartitionSpec as P

D = 2048
H = 16
HD = 128
FF = 8192
ROT = 32


norm_epsilon = 1e-05
adam_epsilon = 1e-08
beta_one = 0.5
beta_two = 0.5
rope_base = 10000.0
masked_score = -1e30


def matmul(left, right):
    return jnp.dot(left, right, preferred_element_type=jnp.float32)


def product_rows(left, right):
    return lax.dot_general(
        left, right, (((0,), (0,)), ((), ())), preferred_element_type=jnp.float32
    )


def product_back(left, right):
    return lax.dot_general(
        left, right, (((1,), (1,)), ((), ())), preferred_element_type=jnp.float32
    )


def bound_list(local_width, local_ff):
    widths = [
        D * 3 * local_width,
        local_width * D,
        D * local_ff,
        local_ff * D,
        3 * local_width,
        local_ff,
        6 * D,
    ]
    bounds = [0]
    for part_width in widths:
        bounds.append(bounds[-1] + part_width)
    return bounds


def group_layout(seq_lengths, group_rows):
    order = jnp.arange(seq_lengths.shape[0], dtype=jnp.int32)
    seq_ends = jnp.sum(
        jnp.where(order[None, :] <= order[:, None], seq_lengths[None, :], 0), axis=1
    )
    starts = seq_ends - seq_lengths
    token_index = jnp.arange(group_rows, dtype=jnp.int32)
    segment = jnp.sum((token_index[:, None] >= seq_ends[None, :]).astype(jnp.int32), axis=1)
    chosen = (
        segment[:, None] == jnp.arange(seq_lengths.shape[0], dtype=jnp.int32)[None, :]
    ).astype(jnp.int32)
    places = token_index - jnp.sum(chosen * starts[None, :], axis=1)
    return (segment, places.astype(jnp.float32))


def rotary_tables(places):
    half_rot = ROT // 2
    frequency = rope_base ** (-2.0 * jnp.arange(half_rot, dtype=jnp.float32) / ROT)
    angles = places[:, None] * frequency[None, :]
    return (jnp.cos(angles)[:, None, :], jnp.sin(angles)[:, None, :])


def rotate(values, cosine, sines):
    half_rot = ROT // 2
    first = values[..., :half_rot]
    second = values[..., half_rot:ROT]
    return jnp.concatenate(
        [first * cosine - second * sines, second * cosine + first * sines, values[..., ROT:]],
        axis=-1,
    )


def norm_stats(inputs):
    center = inputs - jnp.mean(inputs, axis=-1, keepdims=True)
    scale = lax.rsqrt(jnp.mean(center * center, axis=-1, keepdims=True) + norm_epsilon)
    return (center * scale, scale)


def norm_back(grad_norm, gain, unit_rows, scale):
    scaled = grad_norm * gain
    return scale * (
        scaled
        - jnp.mean(scaled, axis=-1, keepdims=True)
        - unit_rows * jnp.mean(scaled * unit_rows, axis=-1, keepdims=True)
    )


def adam_update(
    weights, first, second, moving, gradient, step_rate, step_value, decay_rate, ema_keep
):
    bias_one = 1.0 - jnp.power(beta_one, step_value)
    bias_two = 1.0 - jnp.power(beta_two, step_value)
    new_first = beta_one * first + (1.0 - beta_one) * gradient
    new_second = beta_two * second + (1.0 - beta_two) * gradient * gradient
    ratio = new_first / bias_one / (jnp.sqrt(new_second / bias_two) + adam_epsilon)
    new_weights = weights - step_rate * (ratio + decay_rate * weights)
    new_moving = ema_keep * moving + (1.0 - ema_keep) * new_weights
    return (new_weights, new_first, new_second, new_moving)


def on_device(
    residual,
    cotangent,
    lengths,
    owners,
    step_count,
    rates,
    weight_decay,
    ema_decay,
    master,
    moment_one,
    moment_two,
    average,
):
    tensor_count = lax.axis_size("tensor")
    group_count = lax.axis_size(("dp", "chip"))
    local_heads = H // tensor_count
    local_width = local_heads * HD
    local_ff = FF // tensor_count
    rows_here = residual.shape[1]
    group_rows = rows_here * tensor_count
    bucket_size = master.shape[2]
    bounds = bound_list(local_width, local_ff)
    slots = jnp.arange(group_count, dtype=jnp.int32)
    inverse = jnp.sum(
        slots[None, :] * (owners[None, :] == slots[:, None]).astype(jnp.int32), axis=1
    )
    gathered = lax.all_gather(master.astype(jnp.bfloat16), ("dp", "chip"), axis=1, tiled=True)
    flat_params = jnp.take(gathered[0], owners, axis=0).reshape(-1)
    mixer_in = flat_params[bounds[0] : bounds[1]].reshape(D, 3 * local_width)
    mixer_out = flat_params[bounds[1] : bounds[2]].reshape(local_width, D)
    expand_weight = flat_params[bounds[2] : bounds[3]].reshape(D, local_ff)
    shrink_weight = flat_params[bounds[3] : bounds[4]].reshape(local_ff, D)
    mixer_bias = flat_params[bounds[4] : bounds[5]].astype(jnp.float32)
    expand_bias = flat_params[bounds[5] : bounds[6]].astype(jnp.float32)
    small_params = flat_params[bounds[6] : bounds[7]].reshape(6, D).astype(jnp.float32)
    own_rows = residual[0].astype(jnp.float32)
    segment, places = group_layout(lengths[0], group_rows)
    cosine, sines = rotary_tables(places)
    own_unit, own_scale = norm_stats(own_rows)
    normed_one = (own_unit * small_params[0] + small_params[1]).astype(jnp.bfloat16)
    normed_two = (own_unit * small_params[2] + small_params[3]).astype(jnp.bfloat16)
    full_one, full_two = (
        lax.all_gather(normed_one, "tensor", axis=0, tiled=True),
        lax.all_gather(normed_two, "tensor", axis=0, tiled=True),
    )
    projected = matmul(full_one, mixer_in) + mixer_bias
    head_shape = (group_rows, local_heads, HD)
    queries = rotate(projected[:, :local_width].reshape(head_shape), cosine, sines).astype(
        jnp.bfloat16
    )
    keys = rotate(
        projected[:, local_width : 2 * local_width].reshape(head_shape), cosine, sines
    ).astype(jnp.bfloat16)
    values = projected[:, 2 * local_width :].reshape(head_shape).astype(jnp.bfloat16)
    block_rows = min(512, group_rows)
    block_count = group_rows // block_rows
    score_scale = 1.0 / math.sqrt(HD)
    key_index = jnp.arange(group_rows, dtype=jnp.int32)

    def block_scores(start):
        query_block = lax.dynamic_slice_in_dim(queries, start, block_rows, 0)
        scores = (
            jnp.einsum("qhd,khd->hqk", query_block, keys, preferred_element_type=jnp.float32)
            * score_scale
        )
        row_index = start + jnp.arange(block_rows, dtype=jnp.int32)
        row_segment = lax.dynamic_slice_in_dim(segment, start, block_rows, 0)
        allowed = (row_segment[:, None] == segment[None, :]) & (
            key_index[None, :] <= row_index[:, None]
        )
        return (query_block, jnp.where(allowed[None], scores, masked_score))

    def attend_block(index):
        query_block, scores = block_scores(index * block_rows)
        row_top = jnp.max(scores, axis=-1, keepdims=True)
        raised = jnp.exp(scores - row_top)
        totals = jnp.sum(raised, axis=-1, keepdims=True)
        soft_weights = (raised / totals).astype(jnp.bfloat16)
        mixed = jnp.einsum("hqk,khd->qhd", soft_weights, values, preferred_element_type=jnp.float32)
        return (mixed.reshape(block_rows, local_width), (row_top + jnp.log(totals))[..., 0])

    context_blocks, log_blocks = lax.map(attend_block, jnp.arange(block_count, dtype=jnp.int32))
    context = context_blocks.reshape(group_rows, local_width).astype(jnp.bfloat16)
    before = matmul(full_two, expand_weight) + expand_bias
    hidden = jax.nn.gelu(before, approximate=False).astype(jnp.bfloat16)
    branches = lax.psum_scatter(
        matmul(context, mixer_out) + matmul(hidden, shrink_weight),
        "tensor",
        scatter_dimension=0,
        tiled=True,
    )
    output = own_rows + branches + small_params[4] + small_params[5]
    grad_own = cotangent[0].astype(jnp.float32)
    grad_rows = lax.all_gather(cotangent[0], "tensor", axis=0, tiled=True)
    grad_mixer_out = product_rows(context, grad_rows)
    grad_shrink = product_rows(hidden, grad_rows)
    grad_context = product_back(grad_rows, mixer_out).astype(jnp.bfloat16)
    grad_hidden = product_back(grad_rows, shrink_weight)
    gelu_pull = jax.vjp(lambda inner: jax.nn.gelu(inner, approximate=False), before)[1]
    grad_before = gelu_pull(grad_hidden)[0].astype(jnp.bfloat16)
    grad_expand = product_rows(full_two, grad_before)
    grad_expand_bias = jnp.sum(grad_before.astype(jnp.float32), axis=0)
    partial_two = product_back(grad_before, expand_weight)

    def attention_back(carry, index):
        grad_keys, grad_values = carry
        start = index * block_rows
        query_block, scores = block_scores(start)
        log_rows = lax.dynamic_index_in_dim(log_blocks, index, 0, keepdims=False)
        soft_weights = jnp.exp(scores - log_rows[..., None])
        grad_block = lax.dynamic_slice_in_dim(grad_context, start, block_rows, 0).reshape(
            block_rows, local_heads, HD
        )
        grad_weights = jnp.einsum(
            "qhd,khd->hqk", grad_block, values, preferred_element_type=jnp.float32
        )
        delta = jnp.sum(soft_weights * grad_weights, axis=-1, keepdims=True)
        grad_scores = (soft_weights * (grad_weights - delta)).astype(jnp.bfloat16)
        grad_query = (
            jnp.einsum("hqk,khd->qhd", grad_scores, keys, preferred_element_type=jnp.float32)
            * score_scale
        )
        grad_keys = (
            grad_keys
            + jnp.einsum(
                "hqk,qhd->khd", grad_scores, query_block, preferred_element_type=jnp.float32
            )
            * score_scale
        )
        grad_values = grad_values + jnp.einsum(
            "hqk,qhd->khd",
            soft_weights.astype(jnp.bfloat16),
            grad_block,
            preferred_element_type=jnp.float32,
        )
        return ((grad_keys, grad_values), grad_query)

    zero_heads = jnp.zeros(head_shape, jnp.float32)
    (grad_keys, grad_values), grad_query = lax.scan(
        attention_back, (zero_heads, zero_heads), jnp.arange(block_count, dtype=jnp.int32)
    )
    grad_query = grad_query.reshape(head_shape)
    grad_projected = jnp.concatenate(
        [
            rotate(grad_query, cosine, -sines).reshape(group_rows, local_width),
            rotate(grad_keys, cosine, -sines).reshape(group_rows, local_width),
            grad_values.reshape(group_rows, local_width),
        ],
        axis=1,
    ).astype(jnp.bfloat16)
    grad_mixer_in = product_rows(full_one, grad_projected)
    grad_mixer_bias = jnp.sum(grad_projected.astype(jnp.float32), axis=0)
    partial_one = product_back(grad_projected, mixer_in)
    bias_grad = jnp.sum(grad_own, axis=0)
    grad_one, grad_two = (
        lax.psum_scatter(partial_one, "tensor", scatter_dimension=0, tiled=True),
        lax.psum_scatter(partial_two, "tensor", scatter_dimension=0, tiled=True),
    )
    norm_grads = [
        jnp.sum(grad_one * own_unit, axis=0),
        jnp.sum(grad_one, axis=0),
        jnp.sum(grad_two * own_unit, axis=0),
        jnp.sum(grad_two, axis=0),
    ]
    input_grad = (
        grad_own
        + norm_back(grad_one, small_params[0], own_unit, own_scale)
        + norm_back(grad_two, small_params[2], own_unit, own_scale)
    )
    small_grad = jnp.stack(norm_grads + [bias_grad, bias_grad])
    small_grad = lax.psum(small_grad, "tensor")
    flat_grad = jnp.concatenate(
        [
            grad_mixer_in.reshape(-1),
            grad_mixer_out.reshape(-1),
            grad_expand.reshape(-1),
            grad_shrink.reshape(-1),
            grad_mixer_bias,
            grad_expand_bias,
            small_grad.reshape(-1),
            jnp.zeros((group_count * bucket_size - bounds[7],), jnp.float32),
        ]
    )
    stored_grad = jnp.take(flat_grad.reshape(group_count, bucket_size), inverse, axis=0)
    reduced = lax.psum_scatter(stored_grad, ("dp", "chip"), scatter_dimension=0, tiled=True)[0]
    my_bucket = inverse[lax.axis_index(("dp", "chip"))]
    position = my_bucket * bucket_size + jnp.arange(bucket_size, dtype=jnp.int32)
    step_rate = jnp.zeros((bucket_size,), jnp.float32) + rates[0]
    for kind_index in range(1, 8):
        step_rate = jnp.where(position >= bounds[kind_index], rates[kind_index], step_rate)
    step_value = step_count[0].astype(jnp.float32)
    new_weights, new_first, new_second, new_moving = adam_update(
        master[0, 0],
        moment_one[0, 0],
        moment_two[0, 0],
        average[0, 0],
        reduced,
        step_rate,
        step_value,
        weight_decay[0],
        ema_decay[0],
    )
    return (
        output[None],
        input_grad[None],
        new_weights[None, None],
        new_first[None, None],
        new_second[None, None],
        new_moving[None, None],
        reduced[None, None],
    )


LANES = 128
TROWS = 16


def fits(mesh):
    return mesh.shape["dp"] == 4 and mesh.shape["chip"] == 2 and mesh.shape["tensor"] == 4


def device_program(mesh):
    return on_device_fast if fits(mesh) else on_device


CHUNKS = 4
BROWS = 768
QROWS = 1024
FRONT = 128
BACK = 256
FLAT = 12304
HBM = pltpu.HBM


def params(limit_mb, **more):
    return pltpu.CompilerParams(vmem_limit_bytes=limit_mb * 1024 * 1024, **more)


def pack_kernel(bucket_ref, flat_ref, *refs):
    outs, padded, sem = refs[:CHUNKS], refs[CHUNKS], refs[CHUNKS + 1]
    bucket = bucket_ref[0]
    load = pltpu.make_async_copy(flat_ref, padded.at[pl.ds(FRONT, FLAT)], sem)
    load.start()
    padded[pl.ds(0, FRONT)] = jnp.zeros((FRONT, LANES), jnp.float32)
    padded[pl.ds(FRONT + FLAT, BACK)] = jnp.zeros((BACK, LANES), jnp.float32)
    load.wait()
    wide, narrow = 16 // CHUNKS, 12 // CHUNKS

    def take(start, stride):
        return padded[pl.ds(start, 16, stride=stride), :].astype(jnp.bfloat16)

    @pl.when(bucket >= 2)
    def _():
        def step(tile, carry):
            row = pl.multiple_of(tile * 16, 16)
            for panel in range(16):
                outs[panel // wide][pl.ds((panel % wide) * BROWS + row, 16), :] = take(
                    (row - bucket) * 16 + panel + FRONT, 16
                )
            return carry

        lax.fori_loop(0, BROWS // 16, step, 0)

    @pl.when(bucket < 2)
    def _():
        def step(tile, carry):
            row = pl.multiple_of(tile * 16, 16)
            for panel in range(12):
                outs[panel // narrow][pl.ds((panel % narrow) * QROWS + row, 16), :] = take(
                    row * 12 + panel - 16 * bucket + FRONT, 12
                )
            return carry

        lax.fori_loop(0, QROWS // 16, step, 0)

    main = wide * BROWS

    @pl.when(bucket >= 1)
    def _():
        for panel in range(16):
            outs[0][pl.ds(main + panel * TROWS, TROWS), :] = take(
                (BROWS - bucket) * 16 + panel + FRONT, 16
            )

    @pl.when(bucket == 0)
    def _():
        for panel in range(16):
            outs[0][pl.ds(main + panel * TROWS, TROWS), :] = take(
                QROWS * 12 + min(panel, 11) + FRONT, 12
            )


def chunk_rows():
    return (16 // CHUNKS) * (BROWS + TROWS)


def pack(bucket, flat):
    return pl.pallas_call(
        pack_kernel,
        out_shape=[
            jax.ShapeDtypeStruct(
                ((16 // CHUNKS) * BROWS + (0 if part else 16 * TROWS), LANES), jnp.bfloat16
            )
            for part in range(CHUNKS)
        ],
        in_specs=[pl.BlockSpec(memory_space=pltpu.SMEM), pl.BlockSpec(memory_space=HBM)],
        out_specs=[pl.BlockSpec(memory_space=pltpu.VMEM)] * CHUNKS,
        scratch_shapes=[
            pltpu.VMEM((FRONT + FLAT + BACK, LANES), jnp.float32),
            pltpu.SemaphoreType.DMA,
        ],
        compiler_params=params(60),
        name="pack_params",
    )(bucket, flat)


PLACES = {
    0: (("in", 0, 1024, 0),),
    1: (("in", 1024, 1024, 0),),
    2: (("out", 0, 512, 0), ("up", 0, 256, 512)),
    3: (("up", 256, 768, 0),),
    4: (("up", 1024, 768, 0),),
    5: (("up", 1792, 256, 0), ("down", 0, 512, 256)),
    6: (("down", 512, 768, 0),),
    7: (("down", 1280, 768, 0),),
}
NAMES = ("in", "out", "up", "down", "bias")


def panels_of(bucket):
    return (12 if bucket < 2 else 16) // CHUNKS


MATRICES = {
    "in": (2048, 1536),
    "out": (512, 2048),
    "up": (2048, 2048),
    "down": (2048, 2048),
    "bias": (TROWS, 2048),
}


def head_of(bucket):
    if bucket == 8:
        return ("bias", 0)
    name, first, _, _ = PLACES[bucket][0]
    return (name, first)


def columns(panel):
    return pl.ds(panel * LANES, LANES)


def unpack_kernel(part, bucket_ref, *refs):
    sources = refs[:8]
    staged, tails, load_sems, tail_sem, store_sems = refs[-5:]
    matrices = refs[-11:-5] if part == 0 else refs[-9:-5]
    outs = dict(zip(NAMES[: len(matrices)], matrices, strict=False))
    main = (16 // CHUNKS) * BROWS
    loads = [
        pltpu.make_async_copy(
            sources[k].at[pl.ds(0, main)], staged.at[bucket_ref[k]], load_sems.at[k]
        )
        for k in range(8)
    ]
    if part == 0:
        for k in range(8):
            pltpu.make_async_copy(
                sources[k].at[pl.ds(main, 16 * TROWS)], tails.at[bucket_ref[k]], tail_sem
            ).start()
        take_tails = pltpu.make_async_copy(tails, tails, tail_sem)
    else:
        take_tails = pltpu.make_async_copy(refs[8], tails, tail_sem)
        take_tails.start()
    for load in loads:
        load.start()
    take_tails.wait()
    for load in loads:
        load.wait()
    stores = []

    def store(source, target):
        stores.append(pltpu.make_async_copy(source, target, store_sems.at[len(stores)]))
        stores[-1].start()

    if part == 0:
        store(tails, matrices[5])
        for panel in range(16):
            store(
                tails.at[7, pl.ds(panel * TROWS, TROWS)],
                outs["bias"].at[pl.ds(0, TROWS), columns(panel)],
            )
    for bucket in range(8):
        span = QROWS if bucket < 2 else BROWS
        wide = panels_of(bucket)
        for panel in range(wide):
            if bucket:
                head = pl.ds(panel * span, TROWS)
                tail = pl.ds((part * wide + panel) * TROWS, TROWS)
                staged[bucket, head, :] = staged[bucket, head, :] + tails[bucket - 1, tail, :]
            for name, first, rows, offset in PLACES[bucket]:
                store(
                    staged.at[bucket, pl.ds(panel * span + offset, rows)],
                    outs[name].at[pl.ds(first, rows), columns(part * wide + panel)],
                )
    for put in stores:
        put.wait()


def unpack(part, buckets, sources, before):
    copies = sum(len(PLACES[b]) * panels_of(b) for b in range(8)) + (0 if part else 17)
    names = NAMES[:4] if part else NAMES
    tails = jax.ShapeDtypeStruct((8, 16 * TROWS, LANES), jnp.bfloat16)
    shapes = [jax.ShapeDtypeStruct(MATRICES[name], jnp.bfloat16) for name in names]
    results = pl.pallas_call(
        functools.partial(unpack_kernel, part),
        out_shape=shapes if part else [*shapes, tails],
        in_specs=[pl.BlockSpec(memory_space=pltpu.SMEM)]
        + [pl.BlockSpec(memory_space=HBM)] * (8 + (5 if part else 0)),
        out_specs=[pl.BlockSpec(memory_space=HBM)] * (4 if part else 6),
        input_output_aliases={10 + at: at for at in range(4)} if part else {},
        scratch_shapes=[
            pltpu.VMEM((8, (16 // CHUNKS) * BROWS, LANES), jnp.bfloat16),
            pltpu.VMEM(tails.shape, tails.dtype),
            pltpu.SemaphoreType.DMA((8,)),
            pltpu.SemaphoreType.DMA,
            pltpu.SemaphoreType.DMA((copies,)),
        ],
        compiler_params=params(60),
        name="unpack_params",
    )(buckets, *sources, *((before[5], *before[:4]) if part else ()))
    return [*results, *before[4:]] if part else results


GRAD_ROWS = 256
PAIR = 2 * GRAD_ROWS
IN_STEPS, OUT_STEPS, UP_STEPS, DOWN_STEPS = 4, 1, 4, 4
GRAD_EDGES = (0, 4, 5, 9, 13)
GRAD_STEPS = 13
KEPT, NEAR, FAR = 0, 1, 2


def weight_grad_kernel(table, *refs):
    lefts, rights, outs = refs[:8], refs[8:14], refs[14:20]
    wide32, wide16, tail32, tail16, sems, tail_sem = refs[20:]
    step = pl.program_id(0)
    main = (16 // CHUNKS) * BROWS

    def bucket_of(block):
        return jnp.where(block < 2 * IN_STEPS, block // 4, (block - 2) // 3)

    def target(part, bucket):
        kind, place = table[1 + 16 * part + bucket], table[9 + 16 * part + bucket]
        return [
            (kind == KEPT, False, outs[3 * part + 2].at[place]),
            (kind == NEAR, True, outs[3 * part].at[jnp.minimum(place, 1)]),
            (kind == FAR, True, outs[3 * part + 1].at[jnp.minimum(place, 1)]),
        ]

    def copies(at, act):
        slot = lax.rem(at, 2)
        for half in range(2):
            block = 2 * at + half
            bucket = bucket_of(block)
            inner = block < 2 * IN_STEPS
            for panels, span, mine in ((3, QROWS, inner), (4, BROWS, jnp.logical_not(inner))):
                offset = pl.multiple_of(
                    (lax.rem(block, 4) if span == QROWS else lax.rem(block - 2, 3)) * GRAD_ROWS,
                    GRAD_ROWS,
                )
                for part in range(2):
                    for which, (is_it, short, place) in enumerate(target(part, bucket)):

                        @pl.when(jnp.logical_and(mine, is_it))
                        def _(
                            panels=panels, span=span, offset=offset, part=part, short=short,
                            place=place, half=half,
                        ):
                            stage = wide16 if short else wide32
                            for panel in range(panels):
                                act(
                                    pltpu.make_async_copy(
                                        stage.at[
                                            slot, part, half, pl.ds(panel * GRAD_ROWS, GRAD_ROWS)
                                        ],
                                        place.at[pl.ds(panel * span + offset, GRAD_ROWS)],
                                        sems.at[slot, part, half, panel],
                                    )
                                )

    @pl.when(step >= 2)
    def _():
        copies(step - 2, lambda copy: copy.wait())

    @pl.when(step == 0)
    def _():
        tail32[...] = jnp.zeros_like(tail32)
        tail16[...] = jnp.zeros_like(tail16)

    def multiply(pair, right, panels):
        value = product_rows(lefts[2 * pair][...], rights[2 * right][...]) + product_rows(
            lefts[2 * pair + 1][...], rights[2 * right + 1][...]
        )
        slot = lax.rem(step, 2)
        for half in range(2):
            block = 2 * step + half
            before = jnp.maximum(bucket_of(block) - 1, 0)
            first = block == 4 if pair == 0 else lax.rem(block - 2, 3) == 0
            for part in range(2):
                for panel in range(panels):
                    left = (part * panels + panel) * LANES
                    tile = value[half * GRAD_ROWS : (half + 1) * GRAD_ROWS, left : left + LANES]
                    rows = pl.ds(panel * GRAD_ROWS, GRAD_ROWS)
                    wide32[slot, part, half, rows, :] = tile
                    wide16[slot, part, half, rows, :] = tile.astype(jnp.bfloat16)

            @pl.when(first)
            def _(half=half, before=before):
                for part in range(2):
                    for panel in range(panels):
                        left = (part * panels + panel) * LANES
                        tile = value[
                            half * GRAD_ROWS : half * GRAD_ROWS + TROWS, left : left + LANES
                        ]
                        rows = pl.ds(panel * TROWS, TROWS)
                        tail32[part, before, rows, :] = tile
                        tail16[part, before, rows, :] = tile.astype(jnp.bfloat16)

    for pair, right in enumerate((0, 1, 2, 1)):

        @pl.when(jnp.logical_and(step >= GRAD_EDGES[pair], step < GRAD_EDGES[pair + 1]))
        def _(pair=pair, right=right):
            multiply(pair, right, 3 if pair == 0 else 4)

    copies(step, lambda copy: copy.start())

    @pl.when(step == GRAD_STEPS - 1)
    def _():
        def tails(act):
            for part in range(2):
                for bucket in range(8):
                    for is_it, short, place in target(part, bucket):

                        @pl.when(is_it)
                        def _(part=part, bucket=bucket, short=short, place=place):
                            stage = tail16 if short else tail32
                            act(
                                pltpu.make_async_copy(
                                    stage.at[part, bucket],
                                    place.at[pl.ds(main, stage.shape[2])],
                                    tail_sem.at[part, bucket],
                                )
                            )

        tails(lambda copy: copy.start())
        copies(step - 1, lambda copy: copy.wait())
        copies(step, lambda copy: copy.wait())
        tails(lambda copy: copy.wait())


def weight_grads(table, lefts, rights):
    tokens = lefts[0].shape[0]

    def columns_at(first, count):
        return pl.BlockSpec(
            (tokens, PAIR), lambda i, table: (0, jnp.clip(i - first, 0, count - 1))
        )

    left_specs = [
        columns_at(first, last - first)
        for first, last in zip(GRAD_EDGES, GRAD_EDGES[1:], strict=False)
        for _ in range(2)
    ]
    right_specs = []
    for own, other in zip(rights[::2], rights[1::2], strict=True):
        if own.shape == other.shape:
            right_specs.append(pl.BlockSpec(other.shape, lambda i, table: (0, 0)))
        else:
            right_specs.append(pl.BlockSpec(other.shape, lambda i, table: (0, table[0])))
        right_specs.append(pl.BlockSpec(other.shape, lambda i, table: (0, 0)))
    rows = chunk_rows()
    short = jax.ShapeDtypeStruct((2, rows, LANES), jnp.bfloat16)
    return pl.pallas_call(
        weight_grad_kernel,
        out_shape=[short, short, jax.ShapeDtypeStruct((4, rows, LANES), jnp.float32)] * 2,
        grid_spec=pltpu.PrefetchScalarGridSpec(
            num_scalar_prefetch=1,
            grid=(GRAD_STEPS,),
            in_specs=left_specs + right_specs,
            out_specs=[pl.BlockSpec(memory_space=HBM)] * 6,
            scratch_shapes=[
                pltpu.VMEM((2, 2, 2, 4 * GRAD_ROWS, LANES), jnp.float32),
                pltpu.VMEM((2, 2, 2, 4 * GRAD_ROWS, LANES), jnp.bfloat16),
                pltpu.VMEM((2, 8, 4 * TROWS, LANES), jnp.float32),
                pltpu.VMEM((2, 8, 4 * TROWS, LANES), jnp.bfloat16),
                pltpu.SemaphoreType.DMA((2, 2, 2, 4)),
                pltpu.SemaphoreType.DMA((2, 8)),
            ],
        ),
        compiler_params=params(60),
        name="weight_grads",
    )(table, *lefts, *rights)


NORM_COLUMNS = 512


def norm_grad_kernel(
    core, grad_projected, mixer_in, own_before, own_up, rest_before, rest_up, rows, centre, scale,
    gains, partial, sums,
):
    one = product_back(grad_projected[...], mixer_in[...])
    two = product_back(own_before[...], own_up[...]) + product_back(rest_before[...], rest_up[...])
    unit = (rows[...].astype(jnp.float32) - centre[...]) * scale[...]
    partial[...] = one * gains[0:1, :] + two * gains[1:2, :]
    for at, value in enumerate((one * unit, one, two * unit, two)):
        sums[at : at + 1, :] = jnp.sum(value, axis=0, keepdims=True)


def norm_grad(core, grad_projected, mixer_in, own_before, rest_before, up, rows, centre, scale, gains):
    tokens = rows.shape[0]
    half = up.shape[1] // 2

    def whole(value):
        return pl.BlockSpec(value.shape, lambda i, core: (0, 0))

    block = pl.BlockSpec((tokens, NORM_COLUMNS), lambda i, core: (0, i))
    return pl.pallas_call(
        norm_grad_kernel,
        out_shape=[
            jax.ShapeDtypeStruct((tokens, D), jnp.float32),
            jax.ShapeDtypeStruct((4, D), jnp.float32),
        ],
        grid_spec=pltpu.PrefetchScalarGridSpec(
            num_scalar_prefetch=1,
            grid=(D // NORM_COLUMNS,),
            in_specs=[
                whole(grad_projected),
                pl.BlockSpec((NORM_COLUMNS, mixer_in.shape[1]), lambda i, core: (i, 0)),
                whole(own_before),
                pl.BlockSpec((NORM_COLUMNS, half), lambda i, core: (i, core[0])),
                whole(rest_before),
                pl.BlockSpec((NORM_COLUMNS, half), lambda i, core: (i, 1 - core[0])),
                block,
                whole(centre),
                whole(scale),
                pl.BlockSpec((2, NORM_COLUMNS), lambda i, core: (0, i)),
            ],
            out_specs=[block, pl.BlockSpec((4, NORM_COLUMNS), lambda i, core: (0, i))],
        ),
        compiler_params=params(60),
        name="norm_grad",
    )(core, grad_projected, mixer_in, own_before, up, rest_before, up, rows, centre, scale, gains)


ADAM_ROWS = 1024


def adam_kernel(table, scalar_ref, rate_ref, *refs):
    pieces, small = refs[:4], refs[4]
    weights, first, second, moving = refs[5:9]
    new_weights, new_first, new_second, new_moving, reduced = refs[9:14]
    held, flat, sems = refs[14:]
    bucket, core = table[0], table[1]
    wide, narrow = 16 // CHUNKS, 12 // CHUNKS
    main = wide * BROWS

    @pl.when(pl.program_id(0) == 0)
    def _():
        loads = []
        for at, piece in enumerate(pieces):
            half = core if at < 2 else 1 - core
            loads.append(
                pltpu.make_async_copy(piece, held.at[2 * half + at % 2], sems.at[at])
            )
            loads[-1].start()
        for load in loads:
            load.wait()

        def put(part, row, start, stride):
            flat[pl.ds(start, 16, stride=stride), :] = held[part, pl.ds(row, 16), :]

        @pl.when(bucket >= 2)
        def _():
            def step(tile, carry):
                row = pl.multiple_of(tile * 16, 16)
                for panel in range(16):
                    put(
                        panel // wide,
                        (panel % wide) * BROWS + row,
                        (row - bucket) * 16 + panel + FRONT,
                        16,
                    )
                return carry

            lax.fori_loop(0, BROWS // 16, step, 0)

        @pl.when(bucket < 2)
        def _():
            def step(tile, carry):
                row = pl.multiple_of(tile * 16, 16)
                for panel in range(12):
                    put(
                        panel // narrow,
                        (panel % narrow) * QROWS + row,
                        row * 12 + panel - 16 * bucket + FRONT,
                        12,
                    )
                return carry

            lax.fori_loop(0, QROWS // 16, step, 0)

        @pl.when(bucket >= 1)
        def _():
            for panel in range(16):
                put(
                    panel // wide,
                    main + (panel % wide) * TROWS,
                    (BROWS - bucket) * 16 + panel + FRONT,
                    16,
                )

        @pl.when(bucket == 0)
        def _():
            for panel in range(12):
                put(
                    panel // narrow,
                    main + (panel % narrow) * TROWS,
                    QROWS * 12 + panel + FRONT,
                    12,
                )

        @pl.when(bucket == 7)
        def _():
            flat[pl.ds(FRONT + FLAT - LANES, LANES), :] = small[...]

    start = pl.program_id(0) * ADAM_ROWS
    gradient = flat[pl.ds(pl.multiple_of(FRONT + start, 8), ADAM_ROWS), :]
    row = bucket * FLAT + start + lax.broadcasted_iota(jnp.int32, (ADAM_ROWS, LANES), 0)
    rate = jnp.full((ADAM_ROWS, LANES), rate_ref[0], jnp.float32)
    for kind, bound in enumerate(bound_list(512, 2048)[1:]):
        rate = jnp.where(row >= bound // LANES, rate_ref[kind + 1], rate)
    reduced[...] = gradient
    bias_one, bias_two, decay, keep = (scalar_ref[at] for at in range(4))
    one = beta_one * first[...] + (1.0 - beta_one) * gradient
    two = beta_two * second[...] + (1.0 - beta_two) * gradient * gradient
    old = weights[...]
    ratio = one / bias_one / (jnp.sqrt(two / bias_two) + adam_epsilon)
    fresh = old - rate * (ratio + decay * old)
    new_weights[...] = fresh
    new_first[...] = one
    new_second[...] = two
    new_moving[...] = keep * moving[...] + (1.0 - keep) * fresh


def adam(table, scalars, rates, pieces, small, state):
    steps = -(-FLAT // ADAM_ROWS)
    block = pl.BlockSpec((ADAM_ROWS, LANES), lambda i: (i, 0))
    return pl.pallas_call(
        adam_kernel,
        grid=(steps,),
        out_shape=[jax.ShapeDtypeStruct((FLAT, LANES), jnp.float32)] * 5,
        in_specs=[pl.BlockSpec(memory_space=pltpu.SMEM)] * 3
        + [pl.BlockSpec(memory_space=HBM)] * 4
        + [pl.BlockSpec(memory_space=pltpu.VMEM)]
        + [block] * 4,
        out_specs=[block] * 5,
        scratch_shapes=[
            pltpu.VMEM((4, chunk_rows(), LANES), jnp.float32),
            pltpu.VMEM((FRONT + steps * ADAM_ROWS, LANES), jnp.float32),
            pltpu.SemaphoreType.DMA((4,)),
        ],
        compiler_params=params(60),
        name="adam",
    )(table, scalars, rates, *pieces, small, *state)


FF_BLOCK = 256


def hidden_kernel(normed, up, up_bias, *refs):
    hidden, slope = refs[-2:]
    before = matmul(normed[...], up[...]) + up_bias[...]
    half = 0.5 + 0.5 * lax.erf(before * math.sqrt(0.5))
    hidden[...] = (before * half).astype(jnp.bfloat16)
    slope[...] = half + before * jnp.exp(-0.5 * before * before) * (1.0 / math.sqrt(2.0 * math.pi))


def hidden_layer(half, normed, up, up_bias, before):
    rows, units = normed.shape[0], up.shape[1]
    steps = units // FF_BLOCK // 2
    block = pl.BlockSpec((rows, FF_BLOCK), lambda i: (0, i + half * steps))
    return pl.pallas_call(
        hidden_kernel,
        grid=(steps,),
        out_shape=[
            jax.ShapeDtypeStruct((rows, units), jnp.bfloat16),
            jax.ShapeDtypeStruct((rows, units), jnp.float32),
        ],
        in_specs=[
            pl.BlockSpec(memory_space=pltpu.VMEM),
            pl.BlockSpec((D, FF_BLOCK), lambda i: (0, i + half * steps)),
            pl.BlockSpec((1, FF_BLOCK), lambda i: (0, i + half * steps)),
        ]
        + [pl.BlockSpec(memory_space=HBM)] * len(before),
        out_specs=[block, block],
        input_output_aliases={3 + at: at for at in range(len(before))},
        compiler_params=params(60),
        name="hidden_layer",
    )(normed, up, up_bias, *before)


def hidden_back_kernel(half, grads, down, slope, grad_before, grad_bias):
    rounded = (slope[...] * product_back(grads[...], down[...])).astype(jnp.bfloat16)
    grad_before[...] = rounded
    grad_bias[...] = jnp.sum(rounded.astype(jnp.float32), axis=0, keepdims=True)


def hidden_back(half, grads, down, slope):
    rows, units = slope.shape
    steps = units // FF_BLOCK // 2
    return pl.pallas_call(
        hidden_back_kernel,
        out_shape=[
            jax.ShapeDtypeStruct((rows, units // 2), jnp.bfloat16),
            jax.ShapeDtypeStruct((1, units // 2), jnp.float32),
        ],
        grid_spec=pltpu.PrefetchScalarGridSpec(
            num_scalar_prefetch=1,
            grid=(steps,),
            in_specs=[
                pl.BlockSpec((rows, D), lambda i, half: (0, 0)),
                pl.BlockSpec((FF_BLOCK, D), lambda i, half: (half[0] * steps + i, 0)),
                pl.BlockSpec((rows, FF_BLOCK), lambda i, half: (0, half[0] * steps + i)),
            ],
            out_specs=[
                pl.BlockSpec((rows, FF_BLOCK), lambda i, half: (0, i)),
                pl.BlockSpec((1, FF_BLOCK), lambda i, half: (0, i)),
            ],
        ),
        compiler_params=params(60),
        name="hidden_back",
    )(half, grads, down, slope)


QUERY_BLOCK = 256


def turn(values, tables, sign):
    plain, lower, upper = tables
    half_rot = ROT // 2
    return (
        values * plain
        + pltpu.roll(values, HD - half_rot, 1) * (sign * lower)
        + pltpu.roll(values, half_rot, 1) * (sign * upper)
    )


def block_scores(query, keys, begins, first):
    scores = product_back(query, keys) * (1.0 / math.sqrt(HD))
    row_index = first + lax.broadcasted_iota(jnp.int32, scores.shape, 0)
    key_index = lax.broadcasted_iota(jnp.int32, scores.shape, 1)
    allowed = (key_index <= row_index) & (key_index >= begins)
    return jnp.where(allowed, scores, masked_score)


def head_columns(width, head):
    return [pl.ds(pl.multiple_of(part * width + head * HD, HD), HD) for part in range(3)]


def attend_kernel(projected, bias, plain, lower, upper, begins, context, turned, logs):
    rows, width = context.shape

    def one_head(head, carry):
        cols = head_columns(width, head)
        tables = (plain[...], lower[...], upper[...])
        raw = [projected[:, col] + bias[:, col] for col in cols]
        queries = turn(raw[0], tables, 1.0).astype(jnp.bfloat16)
        keys = turn(raw[1], tables, 1.0).astype(jnp.bfloat16)
        values = raw[2].astype(jnp.bfloat16)
        for col, value in zip(cols, (queries, keys, values), strict=True):
            turned[:, col] = value
        for first in range(0, rows, QUERY_BLOCK):
            last = first + QUERY_BLOCK
            mine = slice(first, last)
            scores = block_scores(queries[mine], keys[:last], begins[mine, :], first)
            top = jnp.max(scores, axis=-1, keepdims=True)
            raised = jnp.exp(scores - top)
            total = jnp.sum(raised, axis=-1, keepdims=True)
            rounded = (raised / total).astype(jnp.bfloat16)
            context[mine, cols[0]] = matmul(rounded, values[:last]).astype(jnp.bfloat16)
            logs[head, mine, :] = top + jnp.log(total)
        return carry

    lax.fori_loop(0, width // HD, one_head, 0)


def attend(projected, bias, tables, begins):
    rows, width = projected.shape[0], projected.shape[1] // 3
    whole = pl.BlockSpec(memory_space=pltpu.VMEM)
    return pl.pallas_call(
        attend_kernel,
        out_shape=[
            jax.ShapeDtypeStruct((rows, width), jnp.bfloat16),
            jax.ShapeDtypeStruct((rows, 3 * width), jnp.bfloat16),
            jax.ShapeDtypeStruct((width // HD, rows, 1), jnp.float32),
        ],
        in_specs=[whole] * 6,
        out_specs=[whole] * 3,
        compiler_params=params(60),
        name="attend",
    )(projected, bias, *tables, begins)


def attend_back_kernel(
    turned, logs, plain, lower, upper, begins, grad_context, grad_projected, key_sum, value_sum
):
    rows, width = grad_context.shape
    score_scale = 1.0 / math.sqrt(HD)

    def one_head(head, carry):
        cols = head_columns(width, head)
        queries, keys, values = (turned[:, col] for col in cols)
        key_sum[...] = jnp.zeros_like(key_sum)
        value_sum[...] = jnp.zeros_like(value_sum)
        for first in range(0, rows, QUERY_BLOCK):
            last = first + QUERY_BLOCK
            mine = slice(first, last)
            query = queries[mine]
            scores = block_scores(query, keys[:last], begins[mine, :], first)
            soft = jnp.exp(scores - logs[head, mine, :])
            grad_mine = grad_context[mine, cols[0]]
            grad_soft = product_back(grad_mine, values[:last])
            delta = jnp.sum(soft * grad_soft, axis=-1, keepdims=True)
            grad_scores = (soft * (grad_soft - delta)).astype(jnp.bfloat16)
            grad_query = matmul(grad_scores, keys[:last]) * score_scale
            tables = (plain[mine, :], lower[mine, :], upper[mine, :])
            grad_projected[mine, cols[0]] = turn(grad_query, tables, -1.0).astype(jnp.bfloat16)
            key_sum[:last, :] += product_rows(grad_scores, query)
            value_sum[:last, :] += product_rows(soft.astype(jnp.bfloat16), grad_mine)
        tables = (plain[...], lower[...], upper[...])
        grad_projected[:, cols[1]] = turn(key_sum[...] * score_scale, tables, -1.0).astype(
            jnp.bfloat16
        )
        grad_projected[:, cols[2]] = value_sum[...].astype(jnp.bfloat16)
        return carry

    lax.fori_loop(0, width // HD, one_head, 0)


def attend_back(turned, logs, tables, begins, grad_context):
    rows, width = grad_context.shape
    whole = pl.BlockSpec(memory_space=pltpu.VMEM)
    return pl.pallas_call(
        attend_back_kernel,
        out_shape=jax.ShapeDtypeStruct((rows, 3 * width), jnp.bfloat16),
        in_specs=[whole] * 7,
        out_specs=whole,
        scratch_shapes=[pltpu.VMEM((rows, HD), jnp.float32)] * 2,
        compiler_params=params(60),
        name="attend_back",
    )(turned, logs, *tables, begins, grad_context)


def rope_tables(places):
    half_rot = ROT // 2
    frequency = rope_base ** (-2.0 * jnp.arange(half_rot, dtype=jnp.float32) / ROT)
    angles = places[:, None] * frequency[None, :]
    cosine, sines = jnp.cos(angles), jnp.sin(angles)
    rest = jnp.zeros((places.shape[0], HD - ROT), jnp.float32)
    none = jnp.zeros_like(sines)
    return (
        jnp.concatenate([cosine, cosine, rest + 1.0], axis=1),
        jnp.concatenate([-sines, none, rest], axis=1),
        jnp.concatenate([none, sines, rest], axis=1),
    )


def along_x(value):
    return lax.ppermute(value, "dp", [(i, i ^ 1) for i in range(4)])


def along_y(value):
    return lax.ppermute(value, "dp", [(i, i ^ 2) for i in range(4)])


def along_line(value, bit):
    return lax.ppermute(value, "tensor", [(i, i ^ bit) for i in range(4)])


def across(value):
    return lax.ppermute(value, "chip", [(0, 1), (1, 0)])


def line_block(partial, index):
    rows = partial.shape[0] // 4
    return lax.dynamic_slice_in_dim(partial, jnp.clip(index, 0, 3) * rows, rows, 0)


def line_hop(partial, here, hop, came):
    up, down = line_block(partial, here + 4 - hop), line_block(partial, here - 4 + hop)
    if came is not None:
        up = up + came[0].astype(jnp.float32)
        down = down + came[1].astype(jnp.float32)
    ups, downs = [(i, i + 1) for i in range(hop)], [(i, i - 1) for i in range(4 - hop, 4)]
    return (
        lax.ppermute(up.astype(jnp.bfloat16), "tensor", ups),
        lax.ppermute(down.astype(jnp.bfloat16), "tensor", downs),
    )


def on_device_fast(
    residual,
    cotangent,
    lengths,
    owners,
    step_count,
    rates,
    weight_decay,
    ema_decay,
    master,
    moment_one,
    moment_two,
    average,
):
    local_width = HD * H // lax.axis_size("tensor")
    group_rows = residual.shape[1] * lax.axis_size("tensor")
    slots = jnp.arange(8, dtype=jnp.int32)
    inverse = jnp.sum(
        slots[None, :] * (owners[None, :] == slots[:, None]).astype(jnp.int32), axis=1
    )
    data_index, core, here = lax.axis_index("dp"), lax.axis_index("chip"), lax.axis_index("tensor")
    partners = jnp.stack([(data_index ^ j) * 2 + (core ^ c) for c in range(2) for j in range(4)])
    buckets = jnp.sum(
        jnp.where(partners[:, None] == slots[None, :], inverse[None, :], 0), axis=1
    ).astype(jnp.int32)
    partner_of = jnp.sum(
        jnp.where(buckets[None, :] == slots[:, None], slots[None, :], 0), axis=1
    )
    hop, other = partner_of % 4, partner_of // 4
    grad_table = [core[None]]
    for first, second in ((hop % 2, hop // 2), (hop // 2, hop % 2)):
        grad_table.append(first * (1 + second))
        grad_table.append(other + 2 * second * (1 - first))
    grad_table = jnp.concatenate(grad_table).astype(jnp.int32)

    full_rows = lax.all_gather(residual[0], "tensor", axis=0, tiled=True)
    grad_rows = lax.all_gather(cotangent[0], "tensor", axis=0, tiled=True)
    own_rows = residual[0].astype(jnp.float32)
    own_unit, own_scale = norm_stats(own_rows)

    def moments(rows):
        float_rows = rows.astype(jnp.float32)
        centre = jnp.mean(float_rows, axis=-1, keepdims=True)
        spread = jnp.mean((float_rows - centre) * (float_rows - centre), axis=-1, keepdims=True)
        return centre, lax.rsqrt(spread + norm_epsilon)

    def norms(rows, centre, scale, small_params):
        unit = (rows.astype(jnp.float32) - centre) * scale
        return (
            (unit * small_params[0] + small_params[1]).astype(jnp.bfloat16),
            (unit * small_params[2] + small_params[3]).astype(jnp.bfloat16),
        )

    def order(*values):
        return lax.optimization_barrier(values)

    def both(values, move):
        return [move(value) for value in values]

    packed = pack(buckets[:1], master.reshape(FLAT, LANES))
    one, two = packed[:2], packed[2:]
    one_x, one_y, one_own = order(both(one, along_x), both(one, along_y), both(one, across))

    far = [along_x(one_y[0]), along_y(one_x[1])]
    near = both([*one_x, *one_y], across)
    far, near, two = order(far, near, two)

    two_x, two_y, far_other = both(two, along_x), both(two, along_y), both(far, across)
    two_own = both(two, across)
    weights = []
    for part in range(2):
        sources = [one[part], one_x[part], one_y[part], far[part]]
        sources += [one_own[part], near[part], near[2 + part], far_other[part]]
        weights = unpack(part, buckets, sources, weights)
    flat_bias = weights[4][:8].reshape(-1).astype(jnp.float32)
    mixer_bias = flat_bias[: 3 * local_width]
    expand_bias = flat_bias[3 * local_width : 3 * local_width + D]
    small_params = flat_bias[3 * local_width + D : 3 * local_width + 7 * D].reshape(6, D)
    centre, scale = moments(full_rows)
    full_one, full_two = norms(full_rows, centre, scale, small_params)
    other_rows = across(full_rows)
    two_x, two_y, two_own, weights, full_one, full_two, other_rows = order(
        two_x, two_y, two_own, weights, full_one, full_two, other_rows
    )

    far = [along_x(two_y[0]), along_y(two_x[1])]
    near = both([*two_x, *two_y], across)
    hidden_half = hidden_layer(0, full_two, weights[2], expand_bias[None], ())
    other_one, other_two = norms(other_rows, *moments(other_rows), small_params)
    far, near, hidden_half, weights, other_one, other_two = order(
        far, near, hidden_half, weights, other_one, other_two
    )

    far_other = both(far, across)
    for part in range(2):
        sources = [two[part], two_x[part], two_y[part], far[part]]
        sources += [two_own[part], near[part], near[2 + part], far_other[part]]
        weights = unpack(2 + part, buckets, sources, weights)
    mixer_in, mixer_out, expand_weight, shrink_weight = weights[:4]

    half_width = D // 2
    other_grads = across(lax.dynamic_slice_in_dim(grad_rows, (1 - core) * half_width, half_width, 1))

    rank = jnp.arange(lengths.shape[1], dtype=jnp.int32)
    seq_ends = jnp.sum(jnp.where(rank[None, :] <= rank[:, None], lengths[0][None, :], 0), axis=1)
    token_index = jnp.arange(group_rows, dtype=jnp.int32)
    passed = (token_index[:, None] >= seq_ends[None, :]).astype(jnp.int32)
    begins = jnp.sum(passed * lengths[0][None, :], axis=1)
    tables = rope_tables((token_index - begins).astype(jnp.float32))
    begins = begins[:, None]

    projected = matmul(full_one, mixer_in)
    context, turned, logs = attend(projected, mixer_bias[None], tables, begins)
    hidden, slope = hidden_layer(1, full_two, expand_weight, expand_bias[None], hidden_half)
    other_context, other_hidden = across(context), across(hidden)
    branches = matmul(context, mixer_out) + matmul(hidden, shrink_weight)
    branches, turned = order(branches, turned)
    branches = lax.psum_scatter(branches, "tensor", scatter_dimension=0, tiled=True)
    output = own_rows + branches + small_params[4] + small_params[5]
    grad_context = product_back(grad_rows, mixer_out).astype(jnp.bfloat16)
    grad_projected = attend_back(turned, logs, tables, begins, grad_context)
    half_in = 3 * local_width // 2
    leaves = lax.dynamic_slice_in_dim(grad_projected, (1 - core) * half_in, half_in, 1)
    leaves, slope = order(leaves, slope)
    other_projected = across(leaves)
    cores = core[None].astype(jnp.int32)
    rest_before, rest_bias = hidden_back(1 - cores, grad_rows, shrink_weight, slope)
    other_before = across(rest_before)
    own_before, own_bias = hidden_back(cores, grad_rows, shrink_weight, slope)
    grad_expand_bias = jnp.where(
        core == 0,
        jnp.concatenate([own_bias[0], rest_bias[0]]),
        jnp.concatenate([rest_bias[0], own_bias[0]]),
    )

    lefts = [
        full_one, other_one, context, other_context, full_two, other_two, hidden, other_hidden
    ]
    rights = [grad_projected, other_projected, grad_rows, other_grads, own_before, other_before]
    sums = weight_grads(grad_table, lefts, rights)
    grad_projected, own_before, rest_before, sums = order(
        grad_projected, own_before, rest_before, sums
    )
    near_a, far_a, kept_a, near_b, far_b, kept_b = sums
    came_a, came_b = along_x(far_a), along_y(far_b)

    partial, norm_grads = norm_grad(
        cores,
        grad_projected,
        mixer_in,
        own_before,
        rest_before,
        expand_weight,
        full_rows,
        centre,
        scale,
        jnp.stack([small_params[0], small_params[2]]),
    )
    bias_grad = jnp.sum(grad_rows.astype(jnp.float32), axis=0)
    small = (
        jnp.sum(grad_projected.astype(jnp.float32), axis=0),
        grad_expand_bias,
        bias_grad,
    )

    came_a, came_b, partial, norm_grads, small, near_a, near_b = lax.optimization_barrier(
        (came_a, came_b, partial, norm_grads, small, near_a, near_b)
    )
    near_a, near_b = along_x(near_a), along_y(near_b)
    line = line_hop(partial, here, 1, None)
    pass_a = (kept_a[2:] + came_a.astype(jnp.float32)).astype(jnp.bfloat16)
    pass_b = (kept_b[2:] + came_b.astype(jnp.float32)).astype(jnp.bfloat16)
    norm_grads = norm_grads + along_line(norm_grads, 1)
    near_a, near_b, pass_a, pass_b, line, norm_grads = lax.optimization_barrier(
        (near_a, near_b, pass_a, pass_b, line, norm_grads)
    )
    far_a, far_b = along_y(pass_a), along_x(pass_b)
    line = line_hop(partial, here, 2, line)
    norm_grads = norm_grads + along_line(norm_grads, 2)
    small = jnp.concatenate(
        [
            small[0],
            small[1],
            norm_grads.reshape(-1),
            small[2],
            small[2],
            jnp.zeros((8 * D - 3 * local_width - 7 * D,), jnp.float32),
        ]
    ).reshape(LANES, LANES)

    small = small + across(small)
    total_a = kept_a[:2] + near_a.astype(jnp.float32)
    total_b = kept_b[:2] + near_b.astype(jnp.float32)

    far_a, far_b, line, small, total_a, total_b = lax.optimization_barrier(
        (far_a, far_b, line, small, total_a, total_b)
    )
    total_a = total_a + far_a.astype(jnp.float32)
    total_b = total_b + far_b.astype(jnp.float32)
    pieces = [total_a[0], total_b[0], across(total_a[1]), across(total_b[1])]
    small = small + along_x(small)
    small = small + along_y(small)
    line = line_hop(partial, here, 3, line)
    step_value = step_count[0].astype(jnp.float32)
    scalars = jnp.stack(
        [
            1.0 - jnp.power(beta_one, step_value),
            1.0 - jnp.power(beta_two, step_value),
            weight_decay[0],
            ema_decay[0],
        ]
    )
    state = [v.reshape(FLAT, LANES) for v in (master, moment_one, moment_two, average)]
    table = jnp.stack([buckets[0], core.astype(jnp.int32)])
    results = adam(table, scalars, rates, pieces, small, state)
    line, results = order(line, results)
    scaled = line_block(partial, here) + (
        line[0].astype(jnp.float32) + line[1].astype(jnp.float32)
    )
    grad_own = cotangent[0].astype(jnp.float32)
    input_grad = grad_own + own_scale * (
        scaled
        - jnp.mean(scaled, axis=-1, keepdims=True)
        - own_unit * jnp.mean(scaled * own_unit, axis=-1, keepdims=True)
    )
    return (output[None], input_grad[None], *[v.reshape(master.shape) for v in results])


def solution(mesh):
    placed = (
        P(("dp", "chip"), "tensor", None),
        P(("dp", "chip"), "tensor", None),
        P(("dp", "chip"), None),
        P(),
        P(),
        P(),
        P(),
        P(),
        P("tensor", ("dp", "chip"), None),
        P("tensor", ("dp", "chip"), None),
        P("tensor", ("dp", "chip"), None),
        P("tensor", ("dp", "chip"), None),
    )
    return jax.shard_map(
        device_program(mesh),
        mesh=mesh,
        in_specs=placed,
        out_specs=(
            P(("dp", "chip"), "tensor", None),
            P(("dp", "chip"), "tensor", None),
            P("tensor", ("dp", "chip"), None),
            P("tensor", ("dp", "chip"), None),
            P("tensor", ("dp", "chip"), None),
            P("tensor", ("dp", "chip"), None),
            P("tensor", ("dp", "chip"), None),
        ),
        check_vma=False,
    )
```

```python
import functools
import math

import jax
import jax.numpy as jnp
from jax import lax
from jax.experimental import pallas as pl
from jax.experimental.pallas import tpu as pltpu
from jax.sharding import PartitionSpec as P

D = 2048
H = 16
HD = 128
FF = 8192
ROT = 32


norm_epsilon = 1e-05
adam_epsilon = 1e-08
beta_one = 0.5
beta_two = 0.5
rope_base = 10000.0
masked_score = -1e30


def matmul(left, right):
    return jnp.dot(left, right, preferred_element_type=jnp.float32)


def product_rows(left, right):
    return lax.dot_general(
        left, right, (((0,), (0,)), ((), ())), preferred_element_type=jnp.float32
    )


def product_back(left, right):
    return lax.dot_general(
        left, right, (((1,), (1,)), ((), ())), preferred_element_type=jnp.float32
    )


def bound_list(local_width, local_ff):
    widths = [
        D * 3 * local_width,
        local_width * D,
        D * local_ff,
        local_ff * D,
        3 * local_width,
        local_ff,
        6 * D,
    ]
    bounds = [0]
    for part_width in widths:
        bounds.append(bounds[-1] + part_width)
    return bounds


def group_layout(seq_lengths, group_rows):
    order = jnp.arange(seq_lengths.shape[0], dtype=jnp.int32)
    seq_ends = jnp.sum(
        jnp.where(order[None, :] <= order[:, None], seq_lengths[None, :], 0), axis=1
    )
    starts = seq_ends - seq_lengths
    token_index = jnp.arange(group_rows, dtype=jnp.int32)
    segment = jnp.sum((token_index[:, None] >= seq_ends[None, :]).astype(jnp.int32), axis=1)
    chosen = (
        segment[:, None] == jnp.arange(seq_lengths.shape[0], dtype=jnp.int32)[None, :]
    ).astype(jnp.int32)
    places = token_index - jnp.sum(chosen * starts[None, :], axis=1)
    return (segment, places.astype(jnp.float32))


def rotary_tables(places):
    half_rot = ROT // 2
    frequency = rope_base ** (-2.0 * jnp.arange(half_rot, dtype=jnp.float32) / ROT)
    angles = places[:, None] * frequency[None, :]
    return (jnp.cos(angles)[:, None, :], jnp.sin(angles)[:, None, :])


def rotate(values, cosine, sines):
    half_rot = ROT // 2
    first = values[..., :half_rot]
    second = values[..., half_rot:ROT]
    return jnp.concatenate(
        [first * cosine - second * sines, second * cosine + first * sines, values[..., ROT:]],
        axis=-1,
    )


def norm_stats(inputs):
    center = inputs - jnp.mean(inputs, axis=-1, keepdims=True)
    scale = lax.rsqrt(jnp.mean(center * center, axis=-1, keepdims=True) + norm_epsilon)
    return (center * scale, scale)


def norm_back(grad_norm, gain, unit_rows, scale):
    scaled = grad_norm * gain
    return scale * (
        scaled
        - jnp.mean(scaled, axis=-1, keepdims=True)
        - unit_rows * jnp.mean(scaled * unit_rows, axis=-1, keepdims=True)
    )


def adam_update(
    weights, first, second, moving, gradient, step_rate, step_value, decay_rate, ema_keep
):
    bias_one = 1.0 - jnp.power(beta_one, step_value)
    bias_two = 1.0 - jnp.power(beta_two, step_value)
    new_first = beta_one * first + (1.0 - beta_one) * gradient
    new_second = beta_two * second + (1.0 - beta_two) * gradient * gradient
    ratio = new_first / bias_one / (jnp.sqrt(new_second / bias_two) + adam_epsilon)
    new_weights = weights - step_rate * (ratio + decay_rate * weights)
    new_moving = ema_keep * moving + (1.0 - ema_keep) * new_weights
    return (new_weights, new_first, new_second, new_moving)


def on_device(
    residual,
    cotangent,
    lengths,
    owners,
    step_count,
    rates,
    weight_decay,
    ema_decay,
    master,
    moment_one,
    moment_two,
    average,
):
    tensor_count = lax.axis_size("tensor")
    group_count = lax.axis_size(("dp", "chip"))
    local_heads = H // tensor_count
    local_width = local_heads * HD
    local_ff = FF // tensor_count
    rows_here = residual.shape[1]
    group_rows = rows_here * tensor_count
    bucket_size = master.shape[2]
    bounds = bound_list(local_width, local_ff)
    slots = jnp.arange(group_count, dtype=jnp.int32)
    inverse = jnp.sum(
        slots[None, :] * (owners[None, :] == slots[:, None]).astype(jnp.int32), axis=1
    )
    gathered = lax.all_gather(master.astype(jnp.bfloat16), ("dp", "chip"), axis=1, tiled=True)
    flat_params = jnp.take(gathered[0], owners, axis=0).reshape(-1)
    mixer_in = flat_params[bounds[0] : bounds[1]].reshape(D, 3 * local_width)
    mixer_out = flat_params[bounds[1] : bounds[2]].reshape(local_width, D)
    expand_weight = flat_params[bounds[2] : bounds[3]].reshape(D, local_ff)
    shrink_weight = flat_params[bounds[3] : bounds[4]].reshape(local_ff, D)
    mixer_bias = flat_params[bounds[4] : bounds[5]].astype(jnp.float32)
    expand_bias = flat_params[bounds[5] : bounds[6]].astype(jnp.float32)
    small_params = flat_params[bounds[6] : bounds[7]].reshape(6, D).astype(jnp.float32)
    own_rows = residual[0].astype(jnp.float32)
    segment, places = group_layout(lengths[0], group_rows)
    cosine, sines = rotary_tables(places)
    own_unit, own_scale = norm_stats(own_rows)
    normed_one = (own_unit * small_params[0] + small_params[1]).astype(jnp.bfloat16)
    normed_two = (own_unit * small_params[2] + small_params[3]).astype(jnp.bfloat16)
    full_one, full_two = (
        lax.all_gather(normed_one, "tensor", axis=0, tiled=True),
        lax.all_gather(normed_two, "tensor", axis=0, tiled=True),
    )
    projected = matmul(full_one, mixer_in) + mixer_bias
    head_shape = (group_rows, local_heads, HD)
    queries = rotate(projected[:, :local_width].reshape(head_shape), cosine, sines).astype(
        jnp.bfloat16
    )
    keys = rotate(
        projected[:, local_width : 2 * local_width].reshape(head_shape), cosine, sines
    ).astype(jnp.bfloat16)
    values = projected[:, 2 * local_width :].reshape(head_shape).astype(jnp.bfloat16)
    block_rows = min(512, group_rows)
    block_count = group_rows // block_rows
    score_scale = 1.0 / math.sqrt(HD)
    key_index = jnp.arange(group_rows, dtype=jnp.int32)

    def block_scores(start):
        query_block = lax.dynamic_slice_in_dim(queries, start, block_rows, 0)
        scores = (
            jnp.einsum("qhd,khd->hqk", query_block, keys, preferred_element_type=jnp.float32)
            * score_scale
        )
        row_index = start + jnp.arange(block_rows, dtype=jnp.int32)
        row_segment = lax.dynamic_slice_in_dim(segment, start, block_rows, 0)
        allowed = (row_segment[:, None] == segment[None, :]) & (
            key_index[None, :] <= row_index[:, None]
        )
        return (query_block, jnp.where(allowed[None], scores, masked_score))

    def attend_block(index):
        query_block, scores = block_scores(index * block_rows)
        row_top = jnp.max(scores, axis=-1, keepdims=True)
        raised = jnp.exp(scores - row_top)
        totals = jnp.sum(raised, axis=-1, keepdims=True)
        soft_weights = (raised / totals).astype(jnp.bfloat16)
        mixed = jnp.einsum("hqk,khd->qhd", soft_weights, values, preferred_element_type=jnp.float32)
        return (mixed.reshape(block_rows, local_width), (row_top + jnp.log(totals))[..., 0])

    context_blocks, log_blocks = lax.map(attend_block, jnp.arange(block_count, dtype=jnp.int32))
    context = context_blocks.reshape(group_rows, local_width).astype(jnp.bfloat16)
    before = matmul(full_two, expand_weight) + expand_bias
    hidden = jax.nn.gelu(before, approximate=False).astype(jnp.bfloat16)
    branches = lax.psum_scatter(
        matmul(context, mixer_out) + matmul(hidden, shrink_weight),
        "tensor",
        scatter_dimension=0,
        tiled=True,
    )
    output = own_rows + branches + small_params[4] + small_params[5]
    grad_own = cotangent[0].astype(jnp.float32)
    grad_rows = lax.all_gather(cotangent[0], "tensor", axis=0, tiled=True)
    grad_mixer_out = product_rows(context, grad_rows)
    grad_shrink = product_rows(hidden, grad_rows)
    grad_context = product_back(grad_rows, mixer_out).astype(jnp.bfloat16)
    grad_hidden = product_back(grad_rows, shrink_weight)
    gelu_pull = jax.vjp(lambda inner: jax.nn.gelu(inner, approximate=False), before)[1]
    grad_before = gelu_pull(grad_hidden)[0].astype(jnp.bfloat16)
    grad_expand = product_rows(full_two, grad_before)
    grad_expand_bias = jnp.sum(grad_before.astype(jnp.float32), axis=0)
    partial_two = product_back(grad_before, expand_weight)

    def attention_back(carry, index):
        grad_keys, grad_values = carry
        start = index * block_rows
        query_block, scores = block_scores(start)
        log_rows = lax.dynamic_index_in_dim(log_blocks, index, 0, keepdims=False)
        soft_weights = jnp.exp(scores - log_rows[..., None])
        grad_block = lax.dynamic_slice_in_dim(grad_context, start, block_rows, 0).reshape(
            block_rows, local_heads, HD
        )
        grad_weights = jnp.einsum(
            "qhd,khd->hqk", grad_block, values, preferred_element_type=jnp.float32
        )
        delta = jnp.sum(soft_weights * grad_weights, axis=-1, keepdims=True)
        grad_scores = (soft_weights * (grad_weights - delta)).astype(jnp.bfloat16)
        grad_query = (
            jnp.einsum("hqk,khd->qhd", grad_scores, keys, preferred_element_type=jnp.float32)
            * score_scale
        )
        grad_keys = (
            grad_keys
            + jnp.einsum(
                "hqk,qhd->khd", grad_scores, query_block, preferred_element_type=jnp.float32
            )
            * score_scale
        )
        grad_values = grad_values + jnp.einsum(
            "hqk,qhd->khd",
            soft_weights.astype(jnp.bfloat16),
            grad_block,
            preferred_element_type=jnp.float32,
        )
        return ((grad_keys, grad_values), grad_query)

    zero_heads = jnp.zeros(head_shape, jnp.float32)
    (grad_keys, grad_values), grad_query = lax.scan(
        attention_back, (zero_heads, zero_heads), jnp.arange(block_count, dtype=jnp.int32)
    )
    grad_query = grad_query.reshape(head_shape)
    grad_projected = jnp.concatenate(
        [
            rotate(grad_query, cosine, -sines).reshape(group_rows, local_width),
            rotate(grad_keys, cosine, -sines).reshape(group_rows, local_width),
            grad_values.reshape(group_rows, local_width),
        ],
        axis=1,
    ).astype(jnp.bfloat16)
    grad_mixer_in = product_rows(full_one, grad_projected)
    grad_mixer_bias = jnp.sum(grad_projected.astype(jnp.float32), axis=0)
    partial_one = product_back(grad_projected, mixer_in)
    bias_grad = jnp.sum(grad_own, axis=0)
    grad_one, grad_two = (
        lax.psum_scatter(partial_one, "tensor", scatter_dimension=0, tiled=True),
        lax.psum_scatter(partial_two, "tensor", scatter_dimension=0, tiled=True),
    )
    norm_grads = [
        jnp.sum(grad_one * own_unit, axis=0),
        jnp.sum(grad_one, axis=0),
        jnp.sum(grad_two * own_unit, axis=0),
        jnp.sum(grad_two, axis=0),
    ]
    input_grad = (
        grad_own
        + norm_back(grad_one, small_params[0], own_unit, own_scale)
        + norm_back(grad_two, small_params[2], own_unit, own_scale)
    )
    small_grad = jnp.stack(norm_grads + [bias_grad, bias_grad])
    small_grad = lax.psum(small_grad, "tensor")
    flat_grad = jnp.concatenate(
        [
            grad_mixer_in.reshape(-1),
            grad_mixer_out.reshape(-1),
            grad_expand.reshape(-1),
            grad_shrink.reshape(-1),
            grad_mixer_bias,
            grad_expand_bias,
            small_grad.reshape(-1),
            jnp.zeros((group_count * bucket_size - bounds[7],), jnp.float32),
        ]
    )
    stored_grad = jnp.take(flat_grad.reshape(group_count, bucket_size), inverse, axis=0)
    reduced = lax.psum_scatter(stored_grad, ("dp", "chip"), scatter_dimension=0, tiled=True)[0]
    my_bucket = inverse[lax.axis_index(("dp", "chip"))]
    position = my_bucket * bucket_size + jnp.arange(bucket_size, dtype=jnp.int32)
    step_rate = jnp.zeros((bucket_size,), jnp.float32) + rates[0]
    for kind_index in range(1, 8):
        step_rate = jnp.where(position >= bounds[kind_index], rates[kind_index], step_rate)
    step_value = step_count[0].astype(jnp.float32)
    new_weights, new_first, new_second, new_moving = adam_update(
        master[0, 0],
        moment_one[0, 0],
        moment_two[0, 0],
        average[0, 0],
        reduced,
        step_rate,
        step_value,
        weight_decay[0],
        ema_decay[0],
    )
    return (
        output[None],
        input_grad[None],
        new_weights[None, None],
        new_first[None, None],
        new_second[None, None],
        new_moving[None, None],
        reduced[None, None],
    )


LANES = 128
TROWS = 16


def fits(mesh):
    return mesh.shape["dp"] == 4 and mesh.shape["chip"] == 2 and mesh.shape["tensor"] == 4


def device_program(mesh):
    return on_device_fast if fits(mesh) else on_device


CHUNKS = 4
BROWS = 768
QROWS = 1024
FRONT = 128
BACK = 256
FLAT = 12304
HBM = pltpu.HBM


LIGHT = pl.CostEstimate(flops=1, bytes_accessed=1, transcendentals=0)


def params(limit_mb, **more):
    return pltpu.CompilerParams(vmem_limit_bytes=limit_mb * 1024 * 1024, **more)


def part_row(part):
    rows = (16 // CHUNKS) * BROWS
    return (0, rows + 16 * TROWS, 0, rows)[part]


def pack_kernel(bucket_ref, flat_ref, *refs):
    outs, padded, sem = refs[:2], refs[2], refs[3]
    bucket = bucket_ref[0]
    load = pltpu.make_async_copy(flat_ref, padded.at[pl.ds(FRONT, FLAT)], sem)
    load.start()
    padded[pl.ds(0, FRONT)] = jnp.zeros((FRONT, LANES), jnp.float32)
    padded[pl.ds(FRONT + FLAT, BACK)] = jnp.zeros((BACK, LANES), jnp.float32)
    load.wait()
    wide, narrow = 16 // CHUNKS, 12 // CHUNKS

    def take(start, stride):
        return padded[pl.ds(start, 16, stride=stride), :].astype(jnp.bfloat16)

    @pl.when(bucket >= 2)
    def _():
        def step(tile, carry):
            row = pl.multiple_of(tile * 16, 16)
            for panel in range(16):
                part = panel // wide
                at = part_row(part) + (panel % wide) * BROWS
                outs[part // 2][pl.ds(at + row, 16), :] = take(
                    (row - bucket) * 16 + panel + FRONT, 16
                )
            return carry

        lax.fori_loop(0, BROWS // 16, step, 0)

    @pl.when(bucket < 2)
    def _():
        def step(tile, carry):
            row = pl.multiple_of(tile * 16, 16)
            for panel in range(12):
                part = panel // narrow
                at = part_row(part) + (panel % narrow) * QROWS
                outs[part // 2][pl.ds(at + row, 16), :] = take(
                    row * 12 + panel - 16 * bucket + FRONT, 12
                )
            return carry

        lax.fori_loop(0, QROWS // 16, step, 0)

    tails = wide * BROWS

    @pl.when(bucket >= 1)
    def _():
        for panel in range(16):
            outs[0][pl.ds(tails + panel * TROWS, TROWS), :] = take(
                (BROWS - bucket) * 16 + panel + FRONT, 16
            )

    @pl.when(bucket == 0)
    def _():
        for panel in range(16):
            outs[0][pl.ds(tails + panel * TROWS, TROWS), :] = take(
                QROWS * 12 + min(panel, 11) + FRONT, 12
            )


def chunk_rows():
    return (16 // CHUNKS) * (BROWS + TROWS)


def pack(bucket, flat):
    rows = (32 // CHUNKS) * BROWS
    return pl.pallas_call(
        pack_kernel,
        out_shape=[
            jax.ShapeDtypeStruct((rows + 16 * TROWS, LANES), jnp.bfloat16),
            jax.ShapeDtypeStruct((rows, LANES), jnp.bfloat16),
        ],
        in_specs=[pl.BlockSpec(memory_space=pltpu.SMEM), pl.BlockSpec(memory_space=HBM)],
        out_specs=[pl.BlockSpec(memory_space=pltpu.VMEM)] * 2,
        scratch_shapes=[
            pltpu.VMEM((FRONT + FLAT + BACK, LANES), jnp.float32),
            pltpu.SemaphoreType.DMA,
        ],
        compiler_params=params(24),
        cost_estimate=LIGHT,
        name="pack_params",
    )(bucket, flat)


PLACES = {
    0: (("in", 0, 1024, 0),),
    1: (("in", 1024, 1024, 0),),
    2: (("out", 0, 512, 0), ("up", 0, 256, 512)),
    3: (("up", 256, 768, 0),),
    4: (("up", 1024, 768, 0),),
    5: (("up", 1792, 256, 0), ("down", 0, 512, 256)),
    6: (("down", 512, 768, 0),),
    7: (("down", 1280, 768, 0),),
}
NAMES = ("in", "out", "up", "down", "bias")


def panels_of(bucket):
    return (12 if bucket < 2 else 16) // CHUNKS


MATRICES = {
    "in": (2048, 1536),
    "out": (512, 2048),
    "up": (2048, 2048),
    "down": (2048, 2048),
    "bias": (TROWS, 2048),
}


def head_of(bucket):
    if bucket == 8:
        return ("bias", 0)
    name, first, _, _ = PLACES[bucket][0]
    return (name, first)


def columns(panel):
    return pl.ds(panel * LANES, LANES)


def unpack_kernel(part, bucket_ref, *refs):
    sources = refs[:8]
    staged, tails, load_sems, tail_sem, store_sems = refs[-5:]
    matrices = refs[-11:-5] if part == 0 else refs[-9:-5]
    outs = dict(zip(NAMES[: len(matrices)], matrices, strict=False))
    main = (16 // CHUNKS) * BROWS
    loads = [
        pltpu.make_async_copy(
            sources[k].at[pl.ds(0 if k % 4 == 3 else part_row(part), main)],
            staged.at[bucket_ref[k]],
            load_sems.at[k],
        )
        for k in range(8)
    ]
    if part == 0:
        for k in range(8):
            pltpu.make_async_copy(
                sources[k].at[pl.ds(main, 16 * TROWS)], tails.at[bucket_ref[k]], tail_sem
            ).start()
        take_tails = pltpu.make_async_copy(tails, tails, tail_sem)
    else:
        take_tails = pltpu.make_async_copy(refs[8], tails, tail_sem)
        take_tails.start()
    for load in loads:
        load.start()
    take_tails.wait()
    for load in loads:
        load.wait()
    stores = []

    def store(source, target):
        stores.append(pltpu.make_async_copy(source, target, store_sems.at[len(stores)]))
        stores[-1].start()

    if part == 0:
        store(tails, matrices[5])
        for panel in range(16):
            store(
                tails.at[7, pl.ds(panel * TROWS, TROWS)],
                outs["bias"].at[pl.ds(0, TROWS), columns(panel)],
            )
    for bucket in range(8):
        span = QROWS if bucket < 2 else BROWS
        wide = panels_of(bucket)
        for panel in range(wide):
            if bucket:
                head = pl.ds(panel * span, TROWS)
                tail = pl.ds((part * wide + panel) * TROWS, TROWS)
                staged[bucket, head, :] = staged[bucket, head, :] + tails[bucket - 1, tail, :]
            for name, first, rows, offset in PLACES[bucket]:
                store(
                    staged.at[bucket, pl.ds(panel * span + offset, rows)],
                    outs[name].at[pl.ds(first, rows), columns(part * wide + panel)],
                )
    for put in stores:
        put.wait()


def unpack(part, buckets, sources, before):
    copies = sum(len(PLACES[b]) * panels_of(b) for b in range(8)) + (0 if part else 17)
    names = NAMES[:4] if part else NAMES
    tails = jax.ShapeDtypeStruct((8, 16 * TROWS, LANES), jnp.bfloat16)
    shapes = [jax.ShapeDtypeStruct(MATRICES[name], jnp.bfloat16) for name in names]
    results = pl.pallas_call(
        functools.partial(unpack_kernel, part),
        out_shape=shapes if part else [*shapes, tails],
        in_specs=[pl.BlockSpec(memory_space=pltpu.SMEM)]
        + [pl.BlockSpec(memory_space=HBM)] * (8 + (5 if part else 0)),
        out_specs=[pl.BlockSpec(memory_space=HBM)] * (4 if part else 6),
        input_output_aliases={10 + at: at for at in range(4)} if part else {},
        scratch_shapes=[
            pltpu.VMEM((8, (16 // CHUNKS) * BROWS, LANES), jnp.bfloat16),
            pltpu.VMEM(tails.shape, tails.dtype),
            pltpu.SemaphoreType.DMA((8,)),
            pltpu.SemaphoreType.DMA,
            pltpu.SemaphoreType.DMA((copies,)),
        ],
        compiler_params=params(60),
        cost_estimate=LIGHT,
        name="unpack_params",
    )(buckets, *sources, *((before[5], *before[:4]) if part else ()))
    return [*results, *before[4:]] if part else results


GRAD_ROWS = 256
PAIR = 2 * GRAD_ROWS
IN_STEPS, OUT_STEPS, UP_STEPS, DOWN_STEPS = 4, 1, 4, 4
GRAD_EDGES = (0, 4, 5, 9, 13)
GRAD_STEPS = 13
KEPT, NEAR, FAR = 0, 1, 2


def weight_grad_kernel(table, *refs):
    lefts, projected, late, outs = refs[:8], refs[8:10], refs[10:14], refs[14:20]
    wide32, wide16, tail32, tail16, held, sems, tail_sem, late_sem = refs[20:]
    step = pl.program_id(0)
    core = table[0]
    main = (16 // CHUNKS) * BROWS

    def bucket_of(block):
        return jnp.where(block < 2 * IN_STEPS, block // 4, (block - 2) // 3)

    def kind_of(part, bucket):
        return table[1 + 16 * part + bucket], table[9 + 16 * part + bucket]

    def targets(part, kind, place):
        return [
            (kind == NEAR, True, outs[2 * part].at[jnp.minimum(place, 1)]),
            (kind == FAR, True, outs[2 * part + 1].at[jnp.minimum(place, 1)]),
            (jnp.logical_and(kind == KEPT, place >= 2), False, outs[4].at[part, jnp.clip(place - 2, 0, 1)]),
            (jnp.logical_and(kind == KEPT, place < 2), False, outs[5].at[part, jnp.minimum(place, 1)]),
        ]

    def wait(at):
        slot = lax.rem(at, 2)
        for panels, mine in ((3, at < IN_STEPS), (4, at >= IN_STEPS)):

            @pl.when(mine)
            def _(panels=panels):
                rows = pl.ds(0, panels * GRAD_ROWS)
                for half in range(2):
                    bucket = bucket_of(2 * at + half)
                    for part in range(2):
                        kind, _ = kind_of(part, bucket)
                        sem = sems.at[slot, part, half]

                        @pl.when(kind == KEPT)
                        def _(part=part, sem=sem):
                            place = outs[5].at[part, 0, rows]
                            pltpu.make_async_copy(place, place, sem).wait()

                        @pl.when(kind != KEPT)
                        def _(part=part, sem=sem):
                            place = outs[2 * part].at[0, rows]
                            pltpu.make_async_copy(place, place, sem).wait()

    @pl.when(step >= 2)
    def _():
        wait(step - 2)

    late_copies = []
    for at, source in enumerate(late):
        width = held.shape[2]
        if source.shape[1] > width:
            source = source.at[:, pl.ds(pl.multiple_of(core * width, width), width)]
        late_copies.append(pltpu.make_async_copy(source, held.at[at], late_sem.at[at]))

    @pl.when(step == 0)
    def _():
        for copy in late_copies:
            copy.start()
        tail32[...] = jnp.zeros_like(tail32)
        tail16[...] = jnp.zeros_like(tail16)

    @pl.when(step == GRAD_EDGES[1])
    def _():
        for copy in late_copies[:2]:
            copy.wait()

    @pl.when(step == GRAD_EDGES[2])
    def _():
        for copy in late_copies[2:]:
            copy.wait()

    def multiply(pair, right, panels, span):
        slot = lax.rem(step, 2)
        if right == 0:
            own, other = projected[0][...], projected[1][...]
        else:
            own, other = held[2 * right - 2], held[2 * right - 1]
        wide32[slot, :, pl.ds(0, 2 * panels * LANES)] = product_rows(
            lefts[2 * pair][...], own
        ) + product_rows(lefts[2 * pair + 1][...], other)
        for half in range(2):
            block = 2 * step + half
            bucket = bucket_of(block)
            before = jnp.maximum(bucket - 1, 0)
            if pair == 0:
                first, offset = block == 4, lax.rem(block, 4)
            else:
                offset = lax.rem(block - 2, 3)
                first = offset == 0
            offset = pl.multiple_of(offset * GRAD_ROWS, GRAD_ROWS)
            for part in range(2):
                kind, place = kind_of(part, bucket)

                @pl.when(kind != KEPT)
                def _(half=half, part=part):
                    for panel in range(panels):
                        tile = wide32[
                            slot, pl.ds(half * GRAD_ROWS, GRAD_ROWS), columns(part * panels + panel)
                        ]
                        rows = pl.ds(panel * GRAD_ROWS, GRAD_ROWS)
                        wide16[slot, part, half, rows, :] = tile.astype(jnp.bfloat16)

                for is_it, short, target in targets(part, kind, place):

                    @pl.when(is_it)
                    def _(half=half, part=part, short=short, target=target, offset=offset):
                        for panel in range(panels):
                            if short:
                                rows = pl.ds(panel * GRAD_ROWS, GRAD_ROWS)
                                source = wide16.at[slot, part, half, rows]
                            else:
                                rows = pl.ds(half * GRAD_ROWS, GRAD_ROWS)
                                source = wide32.at[slot, rows, columns(part * panels + panel)]
                            pltpu.make_async_copy(
                                source,
                                target.at[pl.ds(panel * span + offset, GRAD_ROWS)],
                                sems.at[slot, part, half],
                            ).start()

            @pl.when(first)
            def _(half=half, before=before):
                for part in range(2):
                    for panel in range(panels):
                        tile = wide32[
                            slot, pl.ds(half * GRAD_ROWS, TROWS), columns(part * panels + panel)
                        ]
                        rows = pl.ds(panel * TROWS, TROWS)
                        tail32[part, before, rows, :] = tile
                        tail16[part, before, rows, :] = tile.astype(jnp.bfloat16)

    for pair, right in enumerate((0, 1, 2, 1)):

        @pl.when(jnp.logical_and(step >= GRAD_EDGES[pair], step < GRAD_EDGES[pair + 1]))
        def _(pair=pair, right=right):
            multiply(pair, right, *((3, QROWS) if pair == 0 else (4, BROWS)))

    @pl.when(step == GRAD_STEPS - 1)
    def _():
        def tails(act):
            for part in range(2):
                for bucket in range(8):
                    for is_it, short, place in targets(part, *kind_of(part, bucket)):

                        @pl.when(is_it)
                        def _(part=part, bucket=bucket, short=short, place=place):
                            stage = tail16 if short else tail32
                            act(
                                pltpu.make_async_copy(
                                    stage.at[part, bucket],
                                    place.at[pl.ds(main, stage.shape[2])],
                                    tail_sem.at[part, bucket],
                                )
                            )

        tails(lambda copy: copy.start())
        wait(step - 1)
        wait(step)
        tails(lambda copy: copy.wait())


def weight_grads(table, lefts, rights):
    tokens = lefts[0].shape[0]

    def columns_at(first, count):
        return pl.BlockSpec(
            (tokens, PAIR), lambda i, table: (0, jnp.clip(i - first, 0, count - 1))
        )

    left_specs = [
        columns_at(first, last - first)
        for first, last in zip(GRAD_EDGES, GRAD_EDGES[1:], strict=False)
        for _ in range(2)
    ]
    projected = rights[1].shape
    right_specs = [
        pl.BlockSpec(projected, lambda i, table: (0, table[0])),
        pl.BlockSpec(projected, lambda i, table: (0, 0)),
    ]
    rows = chunk_rows()
    short = jax.ShapeDtypeStruct((2, rows, LANES), jnp.bfloat16)
    wide = jax.ShapeDtypeStruct((2, 2, rows, LANES), jnp.float32)
    return pl.pallas_call(
        weight_grad_kernel,
        out_shape=[short] * 4 + [wide] * 2,
        grid_spec=pltpu.PrefetchScalarGridSpec(
            num_scalar_prefetch=1,
            grid=(GRAD_STEPS,),
            in_specs=left_specs + right_specs + [pl.BlockSpec(memory_space=HBM)] * 4,
            out_specs=[pl.BlockSpec(memory_space=HBM)] * 6,
            scratch_shapes=[
                pltpu.VMEM((2, PAIR, 8 * LANES), jnp.float32),
                pltpu.VMEM((2, 2, 2, 4 * GRAD_ROWS, LANES), jnp.bfloat16),
                pltpu.VMEM((2, 8, 4 * TROWS, LANES), jnp.float32),
                pltpu.VMEM((2, 8, 4 * TROWS, LANES), jnp.bfloat16),
                pltpu.VMEM((4, tokens, 8 * LANES), jnp.bfloat16),
                pltpu.SemaphoreType.DMA((2, 2, 2)),
                pltpu.SemaphoreType.DMA((2, 8)),
                pltpu.SemaphoreType.DMA((4,)),
            ],
        ),
        compiler_params=params(60),
        cost_estimate=LIGHT,
        name="weight_grads",
    )(table, *lefts, *rights)


NORM_COLUMNS = 512


def norm_grad_kernel(
    core, grad_projected, mixer_in, own_before, own_up, rest_before, rest_up, rows, centre, scale,
    gains, partial, sums,
):
    one = product_back(grad_projected[...], mixer_in[...])
    two = product_back(own_before[...], own_up[...]) + product_back(rest_before[...], rest_up[...])
    unit = (rows[...].astype(jnp.float32) - centre[...]) * scale[...]
    partial[...] = one * gains[0:1, :] + two * gains[1:2, :]
    for at, value in enumerate((one * unit, one, two * unit, two)):
        sums[at : at + 1, :] = jnp.sum(value, axis=0, keepdims=True)


def norm_grad(core, grad_projected, mixer_in, own_before, rest_before, up, rows, centre, scale, gains):
    tokens = rows.shape[0]
    half = up.shape[1] // 2

    def whole(value):
        return pl.BlockSpec(value.shape, lambda i, core: (0, 0))

    block = pl.BlockSpec((tokens, NORM_COLUMNS), lambda i, core: (0, i))
    return pl.pallas_call(
        norm_grad_kernel,
        out_shape=[
            jax.ShapeDtypeStruct((tokens, D), jnp.float32),
            jax.ShapeDtypeStruct((4, D), jnp.float32),
        ],
        grid_spec=pltpu.PrefetchScalarGridSpec(
            num_scalar_prefetch=1,
            grid=(D // NORM_COLUMNS,),
            in_specs=[
                whole(grad_projected),
                pl.BlockSpec((NORM_COLUMNS, mixer_in.shape[1]), lambda i, core: (i, 0)),
                whole(own_before),
                pl.BlockSpec((NORM_COLUMNS, half), lambda i, core: (i, core[0])),
                whole(rest_before),
                pl.BlockSpec((NORM_COLUMNS, half), lambda i, core: (i, 1 - core[0])),
                block,
                whole(centre),
                whole(scale),
                pl.BlockSpec((2, NORM_COLUMNS), lambda i, core: (0, i)),
            ],
            out_specs=[block, pl.BlockSpec((4, NORM_COLUMNS), lambda i, core: (0, i))],
        ),
        compiler_params=params(60),
        cost_estimate=LIGHT,
        name="norm_grad",
    )(core, grad_projected, mixer_in, own_before, up, rest_before, up, rows, centre, scale, gains)


ADAM_ROWS = 1024


def adam_kernel(table, scalar_ref, rate_ref, *refs):
    stays, near, far, small = refs[:2], refs[2:6], refs[6:10], refs[10]
    weights, first, second, moving = refs[11:15]
    new_weights, new_first, new_second, new_moving, reduced = refs[15:20]
    held32, held16, flat, sems = refs[20:]
    bucket, core = table[0], table[1]
    wide, narrow = 16 // CHUNKS, 12 // CHUNKS
    main = wide * BROWS
    turn_at = pl.program_id(0)

    def put(part, row, start, stride):
        rows = pl.ds(row, 16)
        value = held32[part, rows, :] + (
            held16[0, part, rows, :].astype(jnp.float32) + held16[1, part, rows, :].astype(jnp.float32)
        )
        flat[pl.ds(start, 16, stride=stride), :] = value

    @pl.when(turn_at == 0)
    def _():
        loads = []
        for at in range(4):
            place = 2 * (core if at < 2 else 1 - core) + at % 2
            source = stays[at // 2].at[at % 2, at // 2]
            loads.append(pltpu.make_async_copy(source, held32.at[place], sems.at[0, at]))
            for which, came in enumerate((near, far)):
                loads.append(
                    pltpu.make_async_copy(
                        came[at].at[at // 2], held16.at[which, place], sems.at[1 + which, at]
                    )
                )
        for load in loads:
            load.start()
        for load in loads:
            load.wait()

        @pl.when(bucket >= 1)
        def _():
            for panel in range(16):
                put(
                    panel // wide,
                    main + (panel % wide) * TROWS,
                    (BROWS - bucket) * 16 + panel + FRONT,
                    16,
                )

        @pl.when(bucket == 0)
        def _():
            for panel in range(12):
                put(
                    panel // narrow,
                    main + (panel % narrow) * TROWS,
                    QROWS * 12 + panel + FRONT,
                    12,
                )

        @pl.when(bucket == 7)
        def _():
            flat[pl.ds(FRONT + FLAT - LANES, LANES), :] = small[...]

    @pl.when(bucket >= 2)
    def _():
        def reach(at):
            return jnp.clip(at * (ADAM_ROWS // 256) + jnp.where(at > 0, 1, 0), 0, BROWS // 16)

        def step(tile, carry):
            row = pl.multiple_of(tile * 16, 16)
            for panel in range(16):
                put(
                    panel // wide,
                    (panel % wide) * BROWS + row,
                    (row - bucket) * 16 + panel + FRONT,
                    16,
                )
            return carry

        lax.fori_loop(reach(turn_at), reach(turn_at + 1), step, 0)

    @pl.when(bucket < 2)
    def _():
        def reach(at):
            tiles = (at * ADAM_ROWS + 16) // 192 + 1
            return jnp.clip(jnp.where(at > 0, tiles, 0), 0, QROWS // 16)

        def step(tile, carry):
            row = pl.multiple_of(tile * 16, 16)
            for panel in range(12):
                put(
                    panel // narrow,
                    (panel % narrow) * QROWS + row,
                    row * 12 + panel - 16 * bucket + FRONT,
                    12,
                )
            return carry

        lax.fori_loop(reach(turn_at), reach(turn_at + 1), step, 0)

    start = turn_at * ADAM_ROWS
    gradient = flat[pl.ds(pl.multiple_of(FRONT + start, 8), ADAM_ROWS), :]
    reduced[...] = gradient
    scale_one, scale_two, decay, keep = (scalar_ref[at] for at in range(4))
    one = beta_one * first[...] + (1.0 - beta_one) * gradient
    two = beta_two * second[...] + (1.0 - beta_two) * gradient * gradient
    new_first[...] = one
    new_second[...] = two
    old = weights[...]
    change = (one * scale_one) / (jnp.sqrt(two * scale_two) + adam_epsilon) + decay * old

    def write(rate):
        fresh = old - rate * change
        new_weights[...] = fresh
        new_moving[...] = keep * moving[...] + (1.0 - keep) * fresh

    first_row = bucket * FLAT + start
    bounds = [bound // LANES for bound in bound_list(512, 2048)[1:]]
    kinds = [sum(jnp.where(at >= bound, 1, 0) for bound in bounds) for at in (first_row, first_row + ADAM_ROWS - 1)]

    @pl.when(kinds[0] == kinds[1])
    def _():
        write(rate_ref[kinds[0]])

    @pl.when(kinds[0] != kinds[1])
    def _():
        row = first_row + lax.broadcasted_iota(jnp.int32, (ADAM_ROWS, LANES), 0)
        rate = jnp.full((ADAM_ROWS, LANES), rate_ref[0], jnp.float32)
        for kind, bound in enumerate(bounds):
            rate = jnp.where(row >= bound, rate_ref[kind + 1], rate)
        write(rate)


def adam(table, scalars, rates, stays, near, far, small, state):
    steps = -(-FLAT // ADAM_ROWS)
    block = pl.BlockSpec((ADAM_ROWS, LANES), lambda i: (i, 0))
    return pl.pallas_call(
        adam_kernel,
        grid=(steps,),
        out_shape=[jax.ShapeDtypeStruct((FLAT, LANES), jnp.float32)] * 5,
        in_specs=[pl.BlockSpec(memory_space=pltpu.SMEM)] * 3
        + [pl.BlockSpec(memory_space=HBM)] * 10
        + [pl.BlockSpec(memory_space=pltpu.VMEM)]
        + [block] * 4,
        out_specs=[block] * 5,
        scratch_shapes=[
            pltpu.VMEM((4, chunk_rows(), LANES), jnp.float32),
            pltpu.VMEM((2, 4, chunk_rows(), LANES), jnp.bfloat16),
            pltpu.VMEM((FRONT + steps * ADAM_ROWS, LANES), jnp.float32),
            pltpu.SemaphoreType.DMA((3, 4)),
        ],
        compiler_params=params(48),
        cost_estimate=LIGHT,
        name="adam",
    )(table, scalars, rates, *stays, *near, *far, small, *state)


def finish_kernel(index, partial, up, down, rows, grads, out):
    scaled = partial[...] + (up[...].astype(jnp.float32) + down[...].astype(jnp.float32))
    unit, scale = norm_stats(rows[...].astype(jnp.float32))
    out[...] = grads[...].astype(jnp.float32) + scale * (
        scaled
        - jnp.mean(scaled, axis=-1, keepdims=True)
        - unit * jnp.mean(scaled * unit, axis=-1, keepdims=True)
    )


def finish(index, partial, line, rows, grads):
    count, width = rows.shape
    steps = 4
    block = pl.BlockSpec((count // steps, width), lambda i, index: (i, 0))
    return pl.pallas_call(
        finish_kernel,
        out_shape=jax.ShapeDtypeStruct((count, width), jnp.float32),
        grid_spec=pltpu.PrefetchScalarGridSpec(
            num_scalar_prefetch=1,
            grid=(steps,),
            in_specs=[
                pl.BlockSpec((count // steps, width), lambda i, index: (index[0] * steps + i, 0)),
                block,
                block,
                block,
                block,
            ],
            out_specs=block,
        ),
        compiler_params=params(24),
        cost_estimate=LIGHT,
        name="finish",
    )(index, partial, *line, rows, grads)


FF_BLOCK = 256


def hidden_kernel(normed, up, up_bias, *refs):
    hidden, slope = refs[-2:]
    before = matmul(normed[...], up[...]) + up_bias[...]
    half = 0.5 + 0.5 * lax.erf(before * math.sqrt(0.5))
    hidden[...] = (before * half).astype(jnp.bfloat16)
    slope[...] = half + before * jnp.exp(-0.5 * before * before) * (1.0 / math.sqrt(2.0 * math.pi))


def hidden_layer(half, normed, up, up_bias, before):
    rows, units = normed.shape[0], up.shape[1]
    steps = units // FF_BLOCK // 2
    block = pl.BlockSpec((rows, FF_BLOCK), lambda i: (0, i + half * steps))
    return pl.pallas_call(
        hidden_kernel,
        grid=(steps,),
        out_shape=[
            jax.ShapeDtypeStruct((rows, units), jnp.bfloat16),
            jax.ShapeDtypeStruct((rows, units), jnp.float32),
        ],
        in_specs=[
            pl.BlockSpec(memory_space=pltpu.VMEM),
            pl.BlockSpec((D, FF_BLOCK), lambda i: (0, i + half * steps)),
            pl.BlockSpec((1, FF_BLOCK), lambda i: (0, i + half * steps)),
        ]
        + [pl.BlockSpec(memory_space=HBM)] * len(before),
        out_specs=[block, block],
        input_output_aliases={3 + at: at for at in range(len(before))},
        compiler_params=params(60),
        cost_estimate=LIGHT,
        name="hidden_layer",
    )(normed, up, up_bias, *before)


def hidden_back_kernel(half, grads, down, slope, grad_before, grad_bias):
    rounded = (slope[...] * product_back(grads[...], down[...])).astype(jnp.bfloat16)
    grad_before[...] = rounded
    grad_bias[...] = jnp.sum(rounded.astype(jnp.float32), axis=0, keepdims=True)


def hidden_back(half, grads, down, slope):
    rows, units = slope.shape
    steps = units // FF_BLOCK // 2
    return pl.pallas_call(
        hidden_back_kernel,
        out_shape=[
            jax.ShapeDtypeStruct((rows, units // 2), jnp.bfloat16),
            jax.ShapeDtypeStruct((1, units // 2), jnp.float32),
        ],
        grid_spec=pltpu.PrefetchScalarGridSpec(
            num_scalar_prefetch=1,
            grid=(steps,),
            in_specs=[
                pl.BlockSpec((rows, D), lambda i, half: (0, 0)),
                pl.BlockSpec((FF_BLOCK, D), lambda i, half: (half[0] * steps + i, 0)),
                pl.BlockSpec((rows, FF_BLOCK), lambda i, half: (0, half[0] * steps + i)),
            ],
            out_specs=[
                pl.BlockSpec((rows, FF_BLOCK), lambda i, half: (0, i)),
                pl.BlockSpec((1, FF_BLOCK), lambda i, half: (0, i)),
            ],
        ),
        compiler_params=params(60),
        cost_estimate=LIGHT,
        name="hidden_back",
    )(half, grads, down, slope)


def product_kernel(back, *refs):
    total = None
    for left, right in zip(refs[:-1:2], refs[1:-1:2], strict=True):
        value = (product_back if back else matmul)(left[...], right[...])
        total = value if total is None else total + value
    refs[-1][...] = total.astype(refs[-1].dtype)


def product(pairs, width, dtype, back=False):
    rows = pairs[0][0].shape[0]
    count = pairs[0][1].shape[0 if back else 1]
    specs = []
    for left, right in pairs:
        specs.append(pl.BlockSpec(memory_space=pltpu.VMEM))
        if back:
            specs.append(pl.BlockSpec((width, right.shape[1]), lambda i: (i, 0)))
        else:
            specs.append(pl.BlockSpec((right.shape[0], width), lambda i: (0, i)))
    return pl.pallas_call(
        functools.partial(product_kernel, back),
        grid=(count // width,),
        out_shape=jax.ShapeDtypeStruct((rows, count), dtype),
        in_specs=specs,
        out_specs=pl.BlockSpec((rows, width), lambda i: (0, i)),
        compiler_params=params(60),
        cost_estimate=LIGHT,
        name="product",
    )(*[value for pair in pairs for value in pair])


def norm_kernel(rows, gains, one, two, centre, scale):
    values = rows[...].astype(jnp.float32)
    middle = jnp.mean(values, axis=-1, keepdims=True)
    values = values - middle
    factor = lax.rsqrt(jnp.mean(values * values, axis=-1, keepdims=True) + norm_epsilon)
    unit = values * factor
    one[...] = (unit * gains[0:1, :] + gains[1:2, :]).astype(jnp.bfloat16)
    two[...] = (unit * gains[2:3, :] + gains[3:4, :]).astype(jnp.bfloat16)
    centre[...] = middle
    scale[...] = factor


def norms(rows, small_params):
    count, width = rows.shape
    height = 128
    block = pl.BlockSpec((height, width), lambda i: (i, 0))
    column = pl.BlockSpec((height, 1), lambda i: (i, 0))
    return pl.pallas_call(
        norm_kernel,
        grid=(count // height,),
        out_shape=[jax.ShapeDtypeStruct((count, width), jnp.bfloat16)] * 2
        + [jax.ShapeDtypeStruct((count, 1), jnp.float32)] * 2,
        in_specs=[block, pl.BlockSpec(memory_space=pltpu.VMEM)],
        out_specs=[block, block, column, column],
        compiler_params=params(60),
        cost_estimate=LIGHT,
        name="norms",
    )(rows, small_params)


QUERY_BLOCK = 256


def turn(values, tables, sign):
    plain, lower, upper = tables
    half_rot = ROT // 2
    return (
        values * plain
        + pltpu.roll(values, HD - half_rot, 1) * (sign * lower)
        + pltpu.roll(values, half_rot, 1) * (sign * upper)
    )


def block_scores(query, keys, begins, first, first_key):
    scores = product_back(query, keys) * (1.0 / math.sqrt(HD))
    row_index = first + lax.broadcasted_iota(jnp.int32, scores.shape, 0)
    key_index = first_key + lax.broadcasted_iota(jnp.int32, scores.shape, 1)
    allowed = (key_index <= row_index) & (key_index >= begins)
    return jnp.where(allowed, scores, masked_score)


def head_columns(width, head):
    return [pl.ds(pl.multiple_of(part * width + head * HD, HD), HD) for part in range(3)]


def attend_kernel(projected, bias, plain, lower, upper, begins, context, turned, logs):
    rows, width = context.shape

    def one_head(head, carry):
        cols = head_columns(width, head)
        tables = (plain[...], lower[...], upper[...])
        raw = [projected[:, col] + bias[:, col] for col in cols]
        queries = turn(raw[0], tables, 1.0).astype(jnp.bfloat16)
        keys = turn(raw[1], tables, 1.0).astype(jnp.bfloat16)
        values = raw[2].astype(jnp.bfloat16)
        for col, value in zip(cols, (queries, keys, values), strict=True):
            turned[:, col] = value
        for first in range(0, rows, QUERY_BLOCK):
            last = first + QUERY_BLOCK
            mine = slice(first, last)
            seen = slice(max(0, first - rows // 2), last)
            scores = block_scores(queries[mine], keys[seen], begins[mine, :], first, seen.start)
            top = jnp.max(scores, axis=-1, keepdims=True)
            raised = jnp.exp(scores - top)
            total = jnp.sum(raised, axis=-1, keepdims=True)
            rounded = (raised / total).astype(jnp.bfloat16)
            context[mine, cols[0]] = matmul(rounded, values[seen]).astype(jnp.bfloat16)
            logs[head, mine, :] = top + jnp.log(total)
        return carry

    lax.fori_loop(0, width // HD, one_head, 0)


def attend(projected, bias, tables, begins):
    rows, width = projected.shape[0], projected.shape[1] // 3
    whole = pl.BlockSpec(memory_space=pltpu.VMEM)
    return pl.pallas_call(
        attend_kernel,
        out_shape=[
            jax.ShapeDtypeStruct((rows, width), jnp.bfloat16),
            jax.ShapeDtypeStruct((rows, 3 * width), jnp.bfloat16),
            jax.ShapeDtypeStruct((width // HD, rows, 1), jnp.float32),
        ],
        in_specs=[whole] * 6,
        out_specs=[whole] * 3,
        compiler_params=params(60),
        cost_estimate=LIGHT,
        name="attend",
    )(projected, bias, *tables, begins)


def attend_back_kernel(
    turned, logs, plain, lower, upper, begins, grad_context, grad_projected, key_sum, value_sum
):
    rows, width = grad_context.shape
    score_scale = 1.0 / math.sqrt(HD)

    def one_head(head, carry):
        cols = head_columns(width, head)
        queries, keys, values = (turned[:, col] for col in cols)
        key_sum[...] = jnp.zeros_like(key_sum)
        value_sum[...] = jnp.zeros_like(value_sum)
        for first in range(0, rows, QUERY_BLOCK):
            last = first + QUERY_BLOCK
            mine = slice(first, last)
            query = queries[mine]
            seen = slice(max(0, first - rows // 2), last)
            scores = block_scores(query, keys[seen], begins[mine, :], first, seen.start)
            soft = jnp.exp(scores - logs[head, mine, :])
            grad_mine = grad_context[mine, cols[0]]
            grad_soft = product_back(grad_mine, values[seen])
            delta = jnp.sum(soft * grad_soft, axis=-1, keepdims=True)
            grad_scores = (soft * (grad_soft - delta)).astype(jnp.bfloat16)
            grad_query = matmul(grad_scores, keys[seen]) * score_scale
            tables = (plain[mine, :], lower[mine, :], upper[mine, :])
            grad_projected[mine, cols[0]] = turn(grad_query, tables, -1.0).astype(jnp.bfloat16)
            key_sum[seen, :] += product_rows(grad_scores, query)
            value_sum[seen, :] += product_rows(soft.astype(jnp.bfloat16), grad_mine)
        tables = (plain[...], lower[...], upper[...])
        grad_projected[:, cols[1]] = turn(key_sum[...] * score_scale, tables, -1.0).astype(
            jnp.bfloat16
        )
        grad_projected[:, cols[2]] = value_sum[...].astype(jnp.bfloat16)
        return carry

    lax.fori_loop(0, width // HD, one_head, 0)


def attend_back(turned, logs, tables, begins, grad_context):
    rows, width = grad_context.shape
    whole = pl.BlockSpec(memory_space=pltpu.VMEM)
    return pl.pallas_call(
        attend_back_kernel,
        out_shape=jax.ShapeDtypeStruct((rows, 3 * width), jnp.bfloat16),
        in_specs=[whole] * 7,
        out_specs=whole,
        scratch_shapes=[pltpu.VMEM((rows, HD), jnp.float32)] * 2,
        compiler_params=params(60),
        cost_estimate=LIGHT,
        name="attend_back",
    )(turned, logs, *tables, begins, grad_context)


def rope_tables(places):
    half_rot = ROT // 2
    frequency = rope_base ** (-2.0 * jnp.arange(half_rot, dtype=jnp.float32) / ROT)
    angles = places[:, None] * frequency[None, :]
    cosine, sines = jnp.cos(angles), jnp.sin(angles)
    rest = jnp.zeros((places.shape[0], HD - ROT), jnp.float32)
    none = jnp.zeros_like(sines)
    return (
        jnp.concatenate([cosine, cosine, rest + 1.0], axis=1),
        jnp.concatenate([-sines, none, rest], axis=1),
        jnp.concatenate([none, sines, rest], axis=1),
    )


def along_x(value):
    return lax.ppermute(value, "dp", [(i, i ^ 1) for i in range(4)])


def along_y(value):
    return lax.ppermute(value, "dp", [(i, i ^ 2) for i in range(4)])


def along_line(value, bit):
    return lax.ppermute(value, "tensor", [(i, i ^ bit) for i in range(4)])


def along(bit, value):
    return lax.ppermute(
        value, ("dp", "chip"), [(i, (i // 2 ^ bit) * 2 + (i % 2 ^ 1)) for i in range(8)]
    )


def across(value):
    return lax.ppermute(value, "chip", [(0, 1), (1, 0)])


def line_block(partial, index):
    rows = partial.shape[0] // 4
    return lax.dynamic_slice_in_dim(partial, jnp.clip(index, 0, 3) * rows, rows, 0)


def line_leaving(partial, here, hop, came):
    up, down = line_block(partial, here + 4 - hop), line_block(partial, here - 4 + hop)
    if came is not None:
        up = up + came[0].astype(jnp.float32)
        down = down + came[1].astype(jnp.float32)
    return up.astype(jnp.bfloat16), down.astype(jnp.bfloat16)


def line_hop(leaving, hop):
    ups, downs = [(i, i + 1) for i in range(hop)], [(i, i - 1) for i in range(4 - hop, 4)]
    return lax.ppermute(leaving[0], "tensor", ups), lax.ppermute(leaving[1], "tensor", downs)


def on_device_fast(
    residual,
    cotangent,
    lengths,
    owners,
    step_count,
    rates,
    weight_decay,
    ema_decay,
    master,
    moment_one,
    moment_two,
    average,
):
    local_width = HD * H // lax.axis_size("tensor")
    group_rows = residual.shape[1] * lax.axis_size("tensor")
    slots = jnp.arange(8, dtype=jnp.int32)
    inverse = jnp.sum(
        slots[None, :] * (owners[None, :] == slots[:, None]).astype(jnp.int32), axis=1
    )
    data_index, core, here = lax.axis_index("dp"), lax.axis_index("chip"), lax.axis_index("tensor")
    partners = jnp.stack([(data_index ^ j) * 2 + (core ^ c) for c in range(2) for j in range(4)])
    buckets = jnp.sum(
        jnp.where(partners[:, None] == slots[None, :], inverse[None, :], 0), axis=1
    ).astype(jnp.int32)
    partner_of = jnp.sum(
        jnp.where(buckets[None, :] == slots[:, None], slots[None, :], 0), axis=1
    )
    hop, other = partner_of % 4, partner_of // 4
    grad_table = [core[None]]
    for first, second in ((hop % 2, hop // 2), (hop // 2, hop % 2)):
        grad_table.append(first * (1 + second))
        grad_table.append(other + 2 * second * (1 - first))
    grad_table = jnp.concatenate(grad_table).astype(jnp.int32)

    full_rows = lax.all_gather(residual[0], "tensor", axis=0, tiled=True)
    grad_rows = lax.all_gather(cotangent[0], "tensor", axis=0, tiled=True)
    own_rows = residual[0].astype(jnp.float32)

    def order(*values):
        return lax.optimization_barrier(values)

    one, two = pack(buckets[:1], master.reshape(FLAT, LANES))
    one_x, one_y, one_own = order(along_x(one), along_y(one), across(one))

    def from_far(first, second, from_x, from_y):
        rows = (16 // CHUNKS) * BROWS
        start = part_row(second)
        count = start if first == 0 else rows
        return [along_x(from_y[:count]), along_y(from_x[start : start + rows])]

    far = from_far(0, 1, one_x, one_y)
    near_x, near_y, two_own = across(one_x), across(one_y), across(two)
    far, near_x, near_y, two_own, two = order(far, near_x, near_y, two_own, two)

    two_x, two_y = along_x(two), along_y(two)
    far_other = [across(value) for value in far]
    weights = []
    for part in range(2):
        sources = [one, one_x, one_y, far[part], one_own, near_x, near_y, far_other[part]]
        weights = unpack(part, buckets, sources, weights)
    weights, full_rows = order(weights, full_rows)
    flat_bias = weights[4][:8].reshape(-1).astype(jnp.float32)
    mixer_bias = flat_bias[: 3 * local_width]
    expand_bias = flat_bias[3 * local_width : 3 * local_width + D]
    small_params = flat_bias[3 * local_width + D : 3 * local_width + 7 * D].reshape(6, D)
    full_one, full_two, centre, scale = norms(full_rows, small_params)
    two_x, two_y, full_rows, full_one, full_two, weights = order(
        two_x, two_y, full_rows, full_one, full_two, weights
    )
    other_rows = across(full_rows)

    far = from_far(2, 3, two_x, two_y)
    near_x, near_y = across(two_x), across(two_y)
    hidden_half = hidden_layer(0, full_two, weights[2], expand_bias[None], ())
    other_one, other_two, _, _ = norms(other_rows, small_params)
    far, near_x, near_y, hidden_half, weights, other_one, other_two = order(
        far, near_x, near_y, hidden_half, weights, other_one, other_two
    )

    far_other = [across(value) for value in far]
    for part in range(2):
        sources = [two, two_x, two_y, far[part], two_own, near_x, near_y, far_other[part]]
        weights = unpack(2 + part, buckets, sources, weights)
    mixer_in, mixer_out, expand_weight, shrink_weight = weights[:4]

    half_width = D // 2
    other_grads = across(lax.dynamic_slice_in_dim(grad_rows, (1 - core) * half_width, half_width, 1))

    rank = jnp.arange(lengths.shape[1], dtype=jnp.int32)
    seq_ends = jnp.sum(jnp.where(rank[None, :] <= rank[:, None], lengths[0][None, :], 0), axis=1)
    token_index = jnp.arange(group_rows, dtype=jnp.int32)
    passed = (token_index[:, None] >= seq_ends[None, :]).astype(jnp.int32)
    begins = jnp.sum(passed * lengths[0][None, :], axis=1)
    tables = rope_tables((token_index - begins).astype(jnp.float32))
    begins = begins[:, None]

    projected = product([(full_one, mixer_in)], 256, jnp.float32)
    context, turned, logs = attend(projected, mixer_bias[None], tables, begins)
    hidden, slope = hidden_layer(1, full_two, expand_weight, expand_bias[None], hidden_half)
    other_context, other_hidden = across(context), across(hidden)
    branches = product([(context, mixer_out), (hidden, shrink_weight)], 256, jnp.float32)
    branches, turned = order(branches, turned)
    branches = lax.psum_scatter(branches, "tensor", scatter_dimension=0, tiled=True)
    output = own_rows + branches + small_params[4] + small_params[5]
    grad_context = product([(grad_rows, mixer_out)], 256, jnp.bfloat16, back=True)
    grad_projected = attend_back(turned, logs, tables, begins, grad_context)
    half_in = 3 * local_width // 2
    leaves = lax.dynamic_slice_in_dim(grad_projected, (1 - core) * half_in, half_in, 1)
    leaves, slope = order(leaves, slope)
    other_projected = across(leaves)
    cores = core[None].astype(jnp.int32)
    rest_before, rest_bias = hidden_back(1 - cores, grad_rows, shrink_weight, slope)
    other_before = across(rest_before)
    own_before, own_bias = hidden_back(cores, grad_rows, shrink_weight, slope)
    grad_expand_bias = jnp.where(
        core == 0,
        jnp.concatenate([own_bias[0], rest_bias[0]]),
        jnp.concatenate([rest_bias[0], own_bias[0]]),
    )

    lefts = [
        full_one, other_one, context, other_context, full_two, other_two, hidden, other_hidden
    ]
    rights = [grad_projected, other_projected, grad_rows, other_grads, own_before, other_before]
    sums = weight_grads(grad_table, lefts, rights)
    grad_projected, own_before, rest_before, sums = order(
        grad_projected, own_before, rest_before, sums
    )
    near_a, far_a, near_b, far_b, passed, stays = sums
    came_a, came_b, other_stays = along_x(far_a), along_y(far_b), across(stays)

    partial, norm_grads = norm_grad(
        cores,
        grad_projected,
        mixer_in,
        own_before,
        rest_before,
        expand_weight,
        full_rows,
        centre,
        scale,
        jnp.stack([small_params[0], small_params[2]]),
    )
    bias_grad = jnp.sum(grad_rows.astype(jnp.float32), axis=0)
    small = (
        jnp.sum(grad_projected.astype(jnp.float32), axis=0),
        grad_expand_bias,
        bias_grad,
    )

    norm_grads = norm_grads + along_line(norm_grads, 1)
    leaving = line_leaving(partial, here, 1, None)
    came_a, came_b, other_stays, partial, leaving, norm_grads, small, near_a, near_b = order(
        came_a, came_b, other_stays, partial, leaving, norm_grads, small, near_a, near_b
    )
    near_a, near_b = along_x(near_a), along_y(near_b)
    line = line_hop(leaving, 1)
    pass_a = (passed[0] + came_a.astype(jnp.float32)).astype(jnp.bfloat16)
    pass_b = (passed[1] + came_b.astype(jnp.float32)).astype(jnp.bfloat16)
    norm_grads = norm_grads + along_line(norm_grads, 2)
    leaving = line_leaving(partial, here, 2, line)
    small = jnp.concatenate(
        [
            small[0],
            small[1],
            norm_grads.reshape(-1),
            small[2],
            small[2],
            jnp.zeros((8 * D - 3 * local_width - 7 * D,), jnp.float32),
        ]
    ).reshape(LANES, LANES)
    near_a, near_b, pass_a, pass_b, leaving, small, output = order(
        near_a, near_b, pass_a, pass_b, leaving, small, output
    )
    small = small + across(small)
    far_a, far_b = along_y(pass_a), along_x(pass_b)
    line = line_hop(leaving, 2)
    near = [near_a, near_b, across(near_a), across(near_b)]
    leaving = line_leaving(partial, here, 3, line)

    far_a, far_b, near, leaving, small = order(far_a, far_b, near, leaving, small)
    small = small + along_x(small)
    small = small + along_y(small)
    far = [far_a, far_b, across(far_a), across(far_b)]
    line = line_hop(leaving, 3)

    step_value = step_count[0].astype(jnp.float32)
    scalars = jnp.stack(
        [
            1.0 / (1.0 - jnp.power(beta_one, step_value)),
            1.0 / (1.0 - jnp.power(beta_two, step_value)),
            weight_decay[0],
            ema_decay[0],
        ]
    )
    state = [v.reshape(FLAT, LANES) for v in (master, moment_one, moment_two, average)]
    table = jnp.stack([buckets[0], core.astype(jnp.int32)])
    results = adam(table, scalars, rates, [stays, other_stays], near, far, small, state)
    line, results = order(line, results)
    input_grad = finish(here[None].astype(jnp.int32), partial, line, residual[0], cotangent[0])
    return (output[None], input_grad[None], *[v.reshape(master.shape) for v in results])


def solution(mesh):
    placed = (
        P(("dp", "chip"), "tensor", None),
        P(("dp", "chip"), "tensor", None),
        P(("dp", "chip"), None),
        P(),
        P(),
        P(),
        P(),
        P(),
        P("tensor", ("dp", "chip"), None),
        P("tensor", ("dp", "chip"), None),
        P("tensor", ("dp", "chip"), None),
        P("tensor", ("dp", "chip"), None),
    )
    return jax.shard_map(
        device_program(mesh),
        mesh=mesh,
        in_specs=placed,
        out_specs=(
            P(("dp", "chip"), "tensor", None),
            P(("dp", "chip"), "tensor", None),
            P("tensor", ("dp", "chip"), None),
            P("tensor", ("dp", "chip"), None),
            P("tensor", ("dp", "chip"), None),
            P("tensor", ("dp", "chip"), None),
            P("tensor", ("dp", "chip"), None),
        ),
        check_vma=False,
    )
```

```python
import functools
import math

import jax
import jax.numpy as jnp
from jax import lax
from jax.experimental import pallas as pl
from jax.experimental.pallas import tpu as pltpu
from jax.sharding import PartitionSpec as P

D = 2048
H = 16
HD = 128
FF = 8192
ROT = 32


norm_epsilon = 1e-05
adam_epsilon = 1e-08
beta_one = 0.5
beta_two = 0.5
rope_base = 10000.0
masked_score = -1e30


def matmul(left, right):
    return jnp.dot(left, right, preferred_element_type=jnp.float32)


def product_rows(left, right):
    return lax.dot_general(
        left, right, (((0,), (0,)), ((), ())), preferred_element_type=jnp.float32
    )


def product_back(left, right):
    return lax.dot_general(
        left, right, (((1,), (1,)), ((), ())), preferred_element_type=jnp.float32
    )


def bound_list(local_width, local_ff):
    widths = [
        D * 3 * local_width,
        local_width * D,
        D * local_ff,
        local_ff * D,
        3 * local_width,
        local_ff,
        6 * D,
    ]
    bounds = [0]
    for part_width in widths:
        bounds.append(bounds[-1] + part_width)
    return bounds


def group_layout(seq_lengths, group_rows):
    order = jnp.arange(seq_lengths.shape[0], dtype=jnp.int32)
    seq_ends = jnp.sum(
        jnp.where(order[None, :] <= order[:, None], seq_lengths[None, :], 0), axis=1
    )
    starts = seq_ends - seq_lengths
    token_index = jnp.arange(group_rows, dtype=jnp.int32)
    segment = jnp.sum((token_index[:, None] >= seq_ends[None, :]).astype(jnp.int32), axis=1)
    chosen = (
        segment[:, None] == jnp.arange(seq_lengths.shape[0], dtype=jnp.int32)[None, :]
    ).astype(jnp.int32)
    places = token_index - jnp.sum(chosen * starts[None, :], axis=1)
    return (segment, places.astype(jnp.float32))


def rotary_tables(places):
    half_rot = ROT // 2
    frequency = rope_base ** (-2.0 * jnp.arange(half_rot, dtype=jnp.float32) / ROT)
    angles = places[:, None] * frequency[None, :]
    return (jnp.cos(angles)[:, None, :], jnp.sin(angles)[:, None, :])


def rotate(values, cosine, sines):
    half_rot = ROT // 2
    first = values[..., :half_rot]
    second = values[..., half_rot:ROT]
    return jnp.concatenate(
        [first * cosine - second * sines, second * cosine + first * sines, values[..., ROT:]],
        axis=-1,
    )


def norm_stats(inputs):
    center = inputs - jnp.mean(inputs, axis=-1, keepdims=True)
    scale = lax.rsqrt(jnp.mean(center * center, axis=-1, keepdims=True) + norm_epsilon)
    return (center * scale, scale)


def norm_back(grad_norm, gain, unit_rows, scale):
    scaled = grad_norm * gain
    return scale * (
        scaled
        - jnp.mean(scaled, axis=-1, keepdims=True)
        - unit_rows * jnp.mean(scaled * unit_rows, axis=-1, keepdims=True)
    )


def adam_update(
    weights, first, second, moving, gradient, step_rate, step_value, decay_rate, ema_keep
):
    bias_one = 1.0 - jnp.power(beta_one, step_value)
    bias_two = 1.0 - jnp.power(beta_two, step_value)
    new_first = beta_one * first + (1.0 - beta_one) * gradient
    new_second = beta_two * second + (1.0 - beta_two) * gradient * gradient
    ratio = new_first / bias_one / (jnp.sqrt(new_second / bias_two) + adam_epsilon)
    new_weights = weights - step_rate * (ratio + decay_rate * weights)
    new_moving = ema_keep * moving + (1.0 - ema_keep) * new_weights
    return (new_weights, new_first, new_second, new_moving)


def on_device(
    residual,
    cotangent,
    lengths,
    owners,
    step_count,
    rates,
    weight_decay,
    ema_decay,
    master,
    moment_one,
    moment_two,
    average,
):
    tensor_count = lax.axis_size("tensor")
    group_count = lax.axis_size(("dp", "chip"))
    local_heads = H // tensor_count
    local_width = local_heads * HD
    local_ff = FF // tensor_count
    rows_here = residual.shape[1]
    group_rows = rows_here * tensor_count
    bucket_size = master.shape[2]
    bounds = bound_list(local_width, local_ff)
    slots = jnp.arange(group_count, dtype=jnp.int32)
    inverse = jnp.sum(
        slots[None, :] * (owners[None, :] == slots[:, None]).astype(jnp.int32), axis=1
    )
    gathered = lax.all_gather(master.astype(jnp.bfloat16), ("dp", "chip"), axis=1, tiled=True)
    flat_params = jnp.take(gathered[0], owners, axis=0).reshape(-1)
    mixer_in = flat_params[bounds[0] : bounds[1]].reshape(D, 3 * local_width)
    mixer_out = flat_params[bounds[1] : bounds[2]].reshape(local_width, D)
    expand_weight = flat_params[bounds[2] : bounds[3]].reshape(D, local_ff)
    shrink_weight = flat_params[bounds[3] : bounds[4]].reshape(local_ff, D)
    mixer_bias = flat_params[bounds[4] : bounds[5]].astype(jnp.float32)
    expand_bias = flat_params[bounds[5] : bounds[6]].astype(jnp.float32)
    small_params = flat_params[bounds[6] : bounds[7]].reshape(6, D).astype(jnp.float32)
    own_rows = residual[0].astype(jnp.float32)
    segment, places = group_layout(lengths[0], group_rows)
    cosine, sines = rotary_tables(places)
    own_unit, own_scale = norm_stats(own_rows)
    normed_one = (own_unit * small_params[0] + small_params[1]).astype(jnp.bfloat16)
    normed_two = (own_unit * small_params[2] + small_params[3]).astype(jnp.bfloat16)
    full_one, full_two = (
        lax.all_gather(normed_one, "tensor", axis=0, tiled=True),
        lax.all_gather(normed_two, "tensor", axis=0, tiled=True),
    )
    projected = matmul(full_one, mixer_in) + mixer_bias
    head_shape = (group_rows, local_heads, HD)
    queries = rotate(projected[:, :local_width].reshape(head_shape), cosine, sines).astype(
        jnp.bfloat16
    )
    keys = rotate(
        projected[:, local_width : 2 * local_width].reshape(head_shape), cosine, sines
    ).astype(jnp.bfloat16)
    values = projected[:, 2 * local_width :].reshape(head_shape).astype(jnp.bfloat16)
    block_rows = min(512, group_rows)
    block_count = group_rows // block_rows
    score_scale = 1.0 / math.sqrt(HD)
    key_index = jnp.arange(group_rows, dtype=jnp.int32)

    def block_scores(start):
        query_block = lax.dynamic_slice_in_dim(queries, start, block_rows, 0)
        scores = (
            jnp.einsum("qhd,khd->hqk", query_block, keys, preferred_element_type=jnp.float32)
            * score_scale
        )
        row_index = start + jnp.arange(block_rows, dtype=jnp.int32)
        row_segment = lax.dynamic_slice_in_dim(segment, start, block_rows, 0)
        allowed = (row_segment[:, None] == segment[None, :]) & (
            key_index[None, :] <= row_index[:, None]
        )
        return (query_block, jnp.where(allowed[None], scores, masked_score))

    def attend_block(index):
        query_block, scores = block_scores(index * block_rows)
        row_top = jnp.max(scores, axis=-1, keepdims=True)
        raised = jnp.exp(scores - row_top)
        totals = jnp.sum(raised, axis=-1, keepdims=True)
        soft_weights = (raised / totals).astype(jnp.bfloat16)
        mixed = jnp.einsum("hqk,khd->qhd", soft_weights, values, preferred_element_type=jnp.float32)
        return (mixed.reshape(block_rows, local_width), (row_top + jnp.log(totals))[..., 0])

    context_blocks, log_blocks = lax.map(attend_block, jnp.arange(block_count, dtype=jnp.int32))
    context = context_blocks.reshape(group_rows, local_width).astype(jnp.bfloat16)
    before = matmul(full_two, expand_weight) + expand_bias
    hidden = jax.nn.gelu(before, approximate=False).astype(jnp.bfloat16)
    branches = lax.psum_scatter(
        matmul(context, mixer_out) + matmul(hidden, shrink_weight),
        "tensor",
        scatter_dimension=0,
        tiled=True,
    )
    output = own_rows + branches + small_params[4] + small_params[5]
    grad_own = cotangent[0].astype(jnp.float32)
    grad_rows = lax.all_gather(cotangent[0], "tensor", axis=0, tiled=True)
    grad_mixer_out = product_rows(context, grad_rows)
    grad_shrink = product_rows(hidden, grad_rows)
    grad_context = product_back(grad_rows, mixer_out).astype(jnp.bfloat16)
    grad_hidden = product_back(grad_rows, shrink_weight)
    gelu_pull = jax.vjp(lambda inner: jax.nn.gelu(inner, approximate=False), before)[1]
    grad_before = gelu_pull(grad_hidden)[0].astype(jnp.bfloat16)
    grad_expand = product_rows(full_two, grad_before)
    grad_expand_bias = jnp.sum(grad_before.astype(jnp.float32), axis=0)
    partial_two = product_back(grad_before, expand_weight)

    def attention_back(carry, index):
        grad_keys, grad_values = carry
        start = index * block_rows
        query_block, scores = block_scores(start)
        log_rows = lax.dynamic_index_in_dim(log_blocks, index, 0, keepdims=False)
        soft_weights = jnp.exp(scores - log_rows[..., None])
        grad_block = lax.dynamic_slice_in_dim(grad_context, start, block_rows, 0).reshape(
            block_rows, local_heads, HD
        )
        grad_weights = jnp.einsum(
            "qhd,khd->hqk", grad_block, values, preferred_element_type=jnp.float32
        )
        delta = jnp.sum(soft_weights * grad_weights, axis=-1, keepdims=True)
        grad_scores = (soft_weights * (grad_weights - delta)).astype(jnp.bfloat16)
        grad_query = (
            jnp.einsum("hqk,khd->qhd", grad_scores, keys, preferred_element_type=jnp.float32)
            * score_scale
        )
        grad_keys = (
            grad_keys
            + jnp.einsum(
                "hqk,qhd->khd", grad_scores, query_block, preferred_element_type=jnp.float32
            )
            * score_scale
        )
        grad_values = grad_values + jnp.einsum(
            "hqk,qhd->khd",
            soft_weights.astype(jnp.bfloat16),
            grad_block,
            preferred_element_type=jnp.float32,
        )
        return ((grad_keys, grad_values), grad_query)

    zero_heads = jnp.zeros(head_shape, jnp.float32)
    (grad_keys, grad_values), grad_query = lax.scan(
        attention_back, (zero_heads, zero_heads), jnp.arange(block_count, dtype=jnp.int32)
    )
    grad_query = grad_query.reshape(head_shape)
    grad_projected = jnp.concatenate(
        [
            rotate(grad_query, cosine, -sines).reshape(group_rows, local_width),
            rotate(grad_keys, cosine, -sines).reshape(group_rows, local_width),
            grad_values.reshape(group_rows, local_width),
        ],
        axis=1,
    ).astype(jnp.bfloat16)
    grad_mixer_in = product_rows(full_one, grad_projected)
    grad_mixer_bias = jnp.sum(grad_projected.astype(jnp.float32), axis=0)
    partial_one = product_back(grad_projected, mixer_in)
    bias_grad = jnp.sum(grad_own, axis=0)
    grad_one, grad_two = (
        lax.psum_scatter(partial_one, "tensor", scatter_dimension=0, tiled=True),
        lax.psum_scatter(partial_two, "tensor", scatter_dimension=0, tiled=True),
    )
    norm_grads = [
        jnp.sum(grad_one * own_unit, axis=0),
        jnp.sum(grad_one, axis=0),
        jnp.sum(grad_two * own_unit, axis=0),
        jnp.sum(grad_two, axis=0),
    ]
    input_grad = (
        grad_own
        + norm_back(grad_one, small_params[0], own_unit, own_scale)
        + norm_back(grad_two, small_params[2], own_unit, own_scale)
    )
    small_grad = jnp.stack(norm_grads + [bias_grad, bias_grad])
    small_grad = lax.psum(small_grad, "tensor")
    flat_grad = jnp.concatenate(
        [
            grad_mixer_in.reshape(-1),
            grad_mixer_out.reshape(-1),
            grad_expand.reshape(-1),
            grad_shrink.reshape(-1),
            grad_mixer_bias,
            grad_expand_bias,
            small_grad.reshape(-1),
            jnp.zeros((group_count * bucket_size - bounds[7],), jnp.float32),
        ]
    )
    stored_grad = jnp.take(flat_grad.reshape(group_count, bucket_size), inverse, axis=0)
    reduced = lax.psum_scatter(stored_grad, ("dp", "chip"), scatter_dimension=0, tiled=True)[0]
    my_bucket = inverse[lax.axis_index(("dp", "chip"))]
    position = my_bucket * bucket_size + jnp.arange(bucket_size, dtype=jnp.int32)
    step_rate = jnp.zeros((bucket_size,), jnp.float32) + rates[0]
    for kind_index in range(1, 8):
        step_rate = jnp.where(position >= bounds[kind_index], rates[kind_index], step_rate)
    step_value = step_count[0].astype(jnp.float32)
    new_weights, new_first, new_second, new_moving = adam_update(
        master[0, 0],
        moment_one[0, 0],
        moment_two[0, 0],
        average[0, 0],
        reduced,
        step_rate,
        step_value,
        weight_decay[0],
        ema_decay[0],
    )
    return (
        output[None],
        input_grad[None],
        new_weights[None, None],
        new_first[None, None],
        new_second[None, None],
        new_moving[None, None],
        reduced[None, None],
    )


LANES = 128
TROWS = 16


def fits(mesh):
    return mesh.shape["dp"] == 4 and mesh.shape["chip"] == 2 and mesh.shape["tensor"] == 4


def device_program(mesh):
    return on_device_fast if fits(mesh) else on_device


CHUNKS = 4
BROWS = 768
QROWS = 1024
FRONT = 128
BACK = 256
FLAT = 12304
HBM = pltpu.HBM


LIGHT = pl.CostEstimate(flops=1, bytes_accessed=1, transcendentals=0)


def params(limit_mb, **more):
    return pltpu.CompilerParams(vmem_limit_bytes=limit_mb * 1024 * 1024, **more)


def part_row(part):
    rows = (16 // CHUNKS) * BROWS
    return (0, rows + 16 * TROWS, 0, rows)[part]


def pack_kernel(bucket_ref, flat_ref, *refs):
    outs, padded, sem = refs[:2], refs[2], refs[3]
    bucket = bucket_ref[0]
    load = pltpu.make_async_copy(flat_ref, padded.at[pl.ds(FRONT, FLAT)], sem)
    load.start()
    padded[pl.ds(0, FRONT)] = jnp.zeros((FRONT, LANES), jnp.float32)
    padded[pl.ds(FRONT + FLAT, BACK)] = jnp.zeros((BACK, LANES), jnp.float32)
    load.wait()
    wide, narrow = 16 // CHUNKS, 12 // CHUNKS

    def take(start, stride):
        return padded[pl.ds(start, 16, stride=stride), :].astype(jnp.bfloat16)

    @pl.when(bucket >= 2)
    def _():
        def step(tile, carry):
            row = pl.multiple_of(tile * 16, 16)
            for panel in range(16):
                part = panel // wide
                at = part_row(part) + (panel % wide) * BROWS
                outs[part // 2][pl.ds(at + row, 16), :] = take(
                    (row - bucket) * 16 + panel + FRONT, 16
                )
            return carry

        lax.fori_loop(0, BROWS // 16, step, 0)

    @pl.when(bucket < 2)
    def _():
        def step(tile, carry):
            row = pl.multiple_of(tile * 16, 16)
            for panel in range(12):
                part = panel // narrow
                at = part_row(part) + (panel % narrow) * QROWS
                outs[part // 2][pl.ds(at + row, 16), :] = take(
                    row * 12 + panel - 16 * bucket + FRONT, 12
                )
            return carry

        lax.fori_loop(0, QROWS // 16, step, 0)

    tails = wide * BROWS

    @pl.when(bucket >= 1)
    def _():
        for panel in range(16):
            outs[0][pl.ds(tails + panel * TROWS, TROWS), :] = take(
                (BROWS - bucket) * 16 + panel + FRONT, 16
            )

    @pl.when(bucket == 0)
    def _():
        for panel in range(16):
            outs[0][pl.ds(tails + panel * TROWS, TROWS), :] = take(
                QROWS * 12 + min(panel, 11) + FRONT, 12
            )


def chunk_rows():
    return (16 // CHUNKS) * (BROWS + TROWS)


def pack(bucket, flat):
    rows = (32 // CHUNKS) * BROWS
    return pl.pallas_call(
        pack_kernel,
        out_shape=[
            jax.ShapeDtypeStruct((rows + 16 * TROWS, LANES), jnp.bfloat16),
            jax.ShapeDtypeStruct((rows, LANES), jnp.bfloat16),
        ],
        in_specs=[pl.BlockSpec(memory_space=pltpu.SMEM), pl.BlockSpec(memory_space=HBM)],
        out_specs=[pl.BlockSpec(memory_space=pltpu.VMEM)] * 2,
        scratch_shapes=[
            pltpu.VMEM((FRONT + FLAT + BACK, LANES), jnp.float32),
            pltpu.SemaphoreType.DMA,
        ],
        compiler_params=params(24),
        cost_estimate=LIGHT,
        name="pack_params",
    )(bucket, flat)


PLACES = {
    0: (("in", 0, 1024, 0),),
    1: (("in", 1024, 1024, 0),),
    2: (("mix", 0, 512, 0), ("up", 0, 256, 512)),
    3: (("up", 256, 768, 0),),
    4: (("up", 1024, 768, 0),),
    5: (("up", 1792, 256, 0), ("mix", 512, 512, 256)),
    6: (("mix", 1024, 768, 0),),
    7: (("mix", 1792, 768, 0),),
}
NAMES = ("in", "mix", "up", "bias")


def panels_of(bucket):
    return (12 if bucket < 2 else 16) // CHUNKS


MATRICES = {
    "in": (2048, 1536),
    "mix": (2560, 2048),
    "up": (2048, 2048),
    "bias": (TROWS, 2048),
}


def columns(panel):
    return pl.ds(panel * LANES, LANES)


def unpack_kernel(parts, bucket_ref, *refs):
    sources = refs[:16]
    staged, tails, load_sems, tail_sem, store_sems = refs[-5:]
    matrices = refs[-10:-5] if parts[0] == 0 else refs[-8:-5]
    outs = dict(zip(NAMES[: len(matrices)], matrices, strict=False))
    main = (16 // CHUNKS) * BROWS
    if parts[0] == 0:
        for k in range(8):
            pltpu.make_async_copy(
                sources[k].at[pl.ds(main, 16 * TROWS)], tails.at[bucket_ref[k]], tail_sem
            ).start()
        take_tails = pltpu.make_async_copy(tails, tails, tail_sem)
    else:
        take_tails = pltpu.make_async_copy(refs[16], tails, tail_sem)
        take_tails.start()
    for at in range(2):
        for k in range(8):
            pltpu.make_async_copy(
                sources[8 * at + k].at[pl.ds(0 if k % 4 == 3 else part_row(parts[at]), main)],
                staged.at[at, bucket_ref[k]],
                load_sems.at[at, bucket_ref[k]],
            ).start()
    take_tails.wait()
    stores = []

    def store(source, target):
        stores.append(pltpu.make_async_copy(source, target, store_sems.at[len(stores)]))
        stores[-1].start()

    if parts[0] == 0:
        store(tails, matrices[4])
        for panel in range(16):
            store(
                tails.at[7, pl.ds(panel * TROWS, TROWS)],
                outs["bias"].at[pl.ds(0, TROWS), columns(panel)],
            )
    for at, part in enumerate(parts):
        for bucket in range(8):
            held = staged.at[at, bucket]
            pltpu.make_async_copy(held, held, load_sems.at[at, bucket]).wait()
            span = QROWS if bucket < 2 else BROWS
            wide = panels_of(bucket)
            for panel in range(wide):
                if bucket:
                    head = pl.ds(panel * span, TROWS)
                    tail = pl.ds((part * wide + panel) * TROWS, TROWS)
                    staged[at, bucket, head, :] = (
                        staged[at, bucket, head, :] + tails[bucket - 1, tail, :]
                    )
                for name, first, rows, offset in PLACES[bucket]:
                    store(
                        staged.at[at, bucket, pl.ds(panel * span + offset, rows)],
                        outs[name].at[pl.ds(first, rows), columns(part * wide + panel)],
                    )
    for put in stores:
        put.wait()


def unpack(parts, buckets, sources, before):
    first = parts[0] == 0
    copies = 2 * sum(len(PLACES[b]) * panels_of(b) for b in range(8)) + (17 if first else 0)
    names = NAMES if first else NAMES[:3]
    tails = jax.ShapeDtypeStruct((8, 16 * TROWS, LANES), jnp.bfloat16)
    shapes = [jax.ShapeDtypeStruct(MATRICES[name], jnp.bfloat16) for name in names]
    results = pl.pallas_call(
        functools.partial(unpack_kernel, parts),
        out_shape=[*shapes, tails] if first else shapes,
        in_specs=[pl.BlockSpec(memory_space=pltpu.SMEM)]
        + [pl.BlockSpec(memory_space=HBM)] * (16 + (0 if first else 4)),
        out_specs=[pl.BlockSpec(memory_space=HBM)] * (5 if first else 3),
        input_output_aliases={} if first else {18 + at: at for at in range(3)},
        scratch_shapes=[
            pltpu.VMEM((2, 8, (16 // CHUNKS) * BROWS, LANES), jnp.bfloat16),
            pltpu.VMEM(tails.shape, tails.dtype),
            pltpu.SemaphoreType.DMA((2, 8)),
            pltpu.SemaphoreType.DMA,
            pltpu.SemaphoreType.DMA((copies,)),
        ],
        compiler_params=params(60),
        cost_estimate=LIGHT,
        name="unpack_params",
    )(buckets, *sources, *(() if first else (before[4], *before[:3])))
    return results if first else [*results, *before[3:]]


GRAD_ROWS = 256
PAIR = 2 * GRAD_ROWS
IN_STEPS, OUT_STEPS, UP_STEPS, DOWN_STEPS = 4, 1, 4, 4
GRAD_EDGES = (0, 4, 5, 9, 13)
GRAD_STEPS = 13
KEPT, NEAR, FAR = 0, 1, 2


def weight_grad_kernel(table, *refs):
    lefts, projected, late, outs = refs[:8], refs[8:10], refs[10:14], refs[14:20]
    wide32, wide16, tail32, tail16, held, sems, tail_sem, late_sem = refs[20:]
    step = pl.program_id(0)
    core = table[0]
    main = (16 // CHUNKS) * BROWS

    def bucket_of(block):
        return jnp.where(block < 2 * IN_STEPS, block // 4, (block - 2) // 3)

    def kind_of(part, bucket):
        return table[1 + 16 * part + bucket], table[9 + 16 * part + bucket]

    def targets(part, kind, place):
        return [
            (kind == NEAR, True, outs[2 * part].at[jnp.minimum(place, 1)]),
            (kind == FAR, True, outs[2 * part + 1].at[jnp.minimum(place, 1)]),
            (jnp.logical_and(kind == KEPT, place >= 2), False, outs[4].at[part, jnp.clip(place - 2, 0, 1)]),
            (jnp.logical_and(kind == KEPT, place < 2), False, outs[5].at[part, jnp.minimum(place, 1)]),
        ]

    def wait(at):
        slot = lax.rem(at, 2)
        for panels, mine in ((3, at < IN_STEPS), (4, at >= IN_STEPS)):

            @pl.when(mine)
            def _(panels=panels):
                rows = pl.ds(0, panels * GRAD_ROWS)
                for half in range(2):
                    bucket = bucket_of(2 * at + half)
                    for part in range(2):
                        kind, _ = kind_of(part, bucket)
                        sem = sems.at[slot, part, half]

                        @pl.when(kind == KEPT)
                        def _(part=part, sem=sem):
                            place = outs[5].at[part, 0, rows]
                            pltpu.make_async_copy(place, place, sem).wait()

                        @pl.when(kind != KEPT)
                        def _(part=part, sem=sem):
                            place = outs[2 * part].at[0, rows]
                            pltpu.make_async_copy(place, place, sem).wait()

    @pl.when(step >= 2)
    def _():
        wait(step - 2)

    late_copies = []
    for at, source in enumerate(late):
        width = held.shape[2]
        if source.shape[1] > width:
            source = source.at[:, pl.ds(pl.multiple_of(core * width, width), width)]
        late_copies.append(pltpu.make_async_copy(source, held.at[at], late_sem.at[at]))

    @pl.when(step == 0)
    def _():
        for copy in late_copies:
            copy.start()
        tail32[...] = jnp.zeros_like(tail32)
        tail16[...] = jnp.zeros_like(tail16)

    @pl.when(step == GRAD_EDGES[1])
    def _():
        for copy in late_copies[:2]:
            copy.wait()

    @pl.when(step == GRAD_EDGES[2])
    def _():
        for copy in late_copies[2:]:
            copy.wait()

    def multiply(pair, right, panels, span):
        slot = lax.rem(step, 2)
        if right == 0:
            own, other = projected[0][...], projected[1][...]
        else:
            own, other = held[2 * right - 2], held[2 * right - 1]
        wide32[slot, :, pl.ds(0, 2 * panels * LANES)] = product_rows(
            lefts[2 * pair][...], own
        ) + product_rows(lefts[2 * pair + 1][...], other)
        for half in range(2):
            block = 2 * step + half
            bucket = bucket_of(block)
            before = jnp.maximum(bucket - 1, 0)
            if pair == 0:
                first, offset = block == 4, lax.rem(block, 4)
            else:
                offset = lax.rem(block - 2, 3)
                first = offset == 0
            offset = pl.multiple_of(offset * GRAD_ROWS, GRAD_ROWS)
            for part in range(2):
                kind, place = kind_of(part, bucket)

                @pl.when(kind != KEPT)
                def _(half=half, part=part):
                    for panel in range(panels):
                        tile = wide32[
                            slot, pl.ds(half * GRAD_ROWS, GRAD_ROWS), columns(part * panels + panel)
                        ]
                        rows = pl.ds(panel * GRAD_ROWS, GRAD_ROWS)
                        wide16[slot, part, half, rows, :] = tile.astype(jnp.bfloat16)

                for is_it, short, target in targets(part, kind, place):

                    @pl.when(is_it)
                    def _(half=half, part=part, short=short, target=target, offset=offset):
                        for panel in range(panels):
                            if short:
                                rows = pl.ds(panel * GRAD_ROWS, GRAD_ROWS)
                                source = wide16.at[slot, part, half, rows]
                            else:
                                rows = pl.ds(half * GRAD_ROWS, GRAD_ROWS)
                                source = wide32.at[slot, rows, columns(part * panels + panel)]
                            pltpu.make_async_copy(
                                source,
                                target.at[pl.ds(panel * span + offset, GRAD_ROWS)],
                                sems.at[slot, part, half],
                            ).start()

            @pl.when(first)
            def _(half=half, before=before):
                for part in range(2):
                    for panel in range(panels):
                        tile = wide32[
                            slot, pl.ds(half * GRAD_ROWS, TROWS), columns(part * panels + panel)
                        ]
                        rows = pl.ds(panel * TROWS, TROWS)
                        tail32[part, before, rows, :] = tile
                        tail16[part, before, rows, :] = tile.astype(jnp.bfloat16)

    for pair, right in enumerate((0, 1, 2, 1)):

        @pl.when(jnp.logical_and(step >= GRAD_EDGES[pair], step < GRAD_EDGES[pair + 1]))
        def _(pair=pair, right=right):
            multiply(pair, right, *((3, QROWS) if pair == 0 else (4, BROWS)))

    @pl.when(step == GRAD_STEPS - 1)
    def _():
        def tails(act):
            for part in range(2):
                for bucket in range(8):
                    for is_it, short, place in targets(part, *kind_of(part, bucket)):

                        @pl.when(is_it)
                        def _(part=part, bucket=bucket, short=short, place=place):
                            stage = tail16 if short else tail32
                            act(
                                pltpu.make_async_copy(
                                    stage.at[part, bucket],
                                    place.at[pl.ds(main, stage.shape[2])],
                                    tail_sem.at[part, bucket],
                                )
                            )

        tails(lambda copy: copy.start())
        wait(step - 1)
        wait(step)
        tails(lambda copy: copy.wait())


def weight_grads(table, lefts, rights):
    tokens = lefts[0].shape[0]

    def columns_at(first, count, ahead):
        return pl.BlockSpec(
            (tokens, PAIR), lambda i, table: (0, ahead + jnp.clip(i - first, 0, count - 1))
        )

    left_specs = [
        columns_at(first, last - first, ahead)
        for first, last, ahead in zip(GRAD_EDGES, GRAD_EDGES[1:], (0, 0, 0, 1), strict=False)
        for _ in range(2)
    ]
    half = (tokens, rights[0].shape[1] // 2)
    right_specs = [pl.BlockSpec(half, lambda i, table: (0, table[0]))] * 2
    rows = chunk_rows()
    short = jax.ShapeDtypeStruct((2, rows, LANES), jnp.bfloat16)
    wide = jax.ShapeDtypeStruct((2, 2, rows, LANES), jnp.float32)
    return pl.pallas_call(
        weight_grad_kernel,
        out_shape=[short] * 4 + [wide] * 2,
        grid_spec=pltpu.PrefetchScalarGridSpec(
            num_scalar_prefetch=1,
            grid=(GRAD_STEPS,),
            in_specs=left_specs + right_specs + [pl.BlockSpec(memory_space=HBM)] * 4,
            out_specs=[pl.BlockSpec(memory_space=HBM)] * 6,
            scratch_shapes=[
                pltpu.VMEM((2, PAIR, 8 * LANES), jnp.float32),
                pltpu.VMEM((2, 2, 2, 4 * GRAD_ROWS, LANES), jnp.bfloat16),
                pltpu.VMEM((2, 8, 4 * TROWS, LANES), jnp.float32),
                pltpu.VMEM((2, 8, 4 * TROWS, LANES), jnp.bfloat16),
                pltpu.VMEM((4, tokens, 8 * LANES), jnp.bfloat16),
                pltpu.SemaphoreType.DMA((2, 2, 2)),
                pltpu.SemaphoreType.DMA((2, 8)),
                pltpu.SemaphoreType.DMA((4,)),
            ],
        ),
        compiler_params=params(60),
        cost_estimate=LIGHT,
        name="weight_grads",
    )(table, *lefts, *rights)


NORM_COLUMNS = 512


def norm_grad_kernel(
    core, grad_projected, mixer_in, own_before, own_up, rest_before, rest_up, rows, centre, scale,
    gains, partial, sums,
):
    one = product_back(grad_projected[...], mixer_in[...])
    two = product_back(own_before[...], own_up[...]) + product_back(rest_before[...], rest_up[...])
    unit = (rows[...].astype(jnp.float32) - centre[...]) * scale[...]
    partial[...] = (one * gains[0:1, :] + two * gains[1:2, :]).astype(jnp.bfloat16)
    for at, value in enumerate((one * unit, one, two * unit, two)):
        sums[at : at + 1, :] = jnp.sum(value, axis=0, keepdims=True)


def norm_grad(core, grad_projected, mixer_in, own_before, rest_before, up, rows, centre, scale, gains):
    tokens = rows.shape[0]
    half = up.shape[1] // 2

    def whole(value):
        return pl.BlockSpec(value.shape, lambda i, core: (0, 0))

    block = pl.BlockSpec((tokens, NORM_COLUMNS), lambda i, core: (0, i))
    return pl.pallas_call(
        norm_grad_kernel,
        out_shape=[
            jax.ShapeDtypeStruct((tokens, D), jnp.bfloat16),
            jax.ShapeDtypeStruct((4, D), jnp.float32),
        ],
        grid_spec=pltpu.PrefetchScalarGridSpec(
            num_scalar_prefetch=1,
            grid=(D // NORM_COLUMNS,),
            in_specs=[
                whole(grad_projected),
                pl.BlockSpec((NORM_COLUMNS, mixer_in.shape[1]), lambda i, core: (i, 0)),
                whole(own_before),
                pl.BlockSpec((NORM_COLUMNS, half), lambda i, core: (i, core[0])),
                whole(rest_before),
                pl.BlockSpec((NORM_COLUMNS, half), lambda i, core: (i, 1 - core[0])),
                block,
                whole(centre),
                whole(scale),
                pl.BlockSpec((2, NORM_COLUMNS), lambda i, core: (0, i)),
            ],
            out_specs=[block, pl.BlockSpec((4, NORM_COLUMNS), lambda i, core: (0, i))],
        ),
        compiler_params=params(60),
        cost_estimate=LIGHT,
        name="norm_grad",
    )(core, grad_projected, mixer_in, own_before, up, rest_before, up, rows, centre, scale, gains)


ADAM_ROWS = 3080


def adam_kernel(table, scalar_ref, rate_ref, *refs):
    stays, near, far, small = refs[:2], refs[2:6], refs[6:10], refs[10]
    weights, first, second, moving = refs[11:15]
    new_weights, new_first, new_second, new_moving, reduced = refs[15:20]
    held32, held16, flat, sems = refs[20:]
    bucket, core = table[0], table[1]
    wide, narrow = 16 // CHUNKS, 12 // CHUNKS
    main = wide * BROWS
    turn_at = pl.program_id(0)

    def put(part, row, start, stride):
        rows = pl.ds(row, 16)
        value = held32[part, rows, :] + (
            held16[0, part, rows, :].astype(jnp.float32) + held16[1, part, rows, :].astype(jnp.float32)
        )
        flat[pl.ds(start, 16, stride=stride), :] = value

    @pl.when(turn_at == 0)
    def _():
        loads = []
        for at in range(4):
            place = 2 * (core if at < 2 else 1 - core) + at % 2
            source = stays[at // 2].at[at % 2, at // 2]
            loads.append(pltpu.make_async_copy(source, held32.at[place], sems.at[0, at]))
            for which, came in enumerate((near, far)):
                loads.append(
                    pltpu.make_async_copy(
                        came[at].at[at // 2], held16.at[which, place], sems.at[1 + which, at]
                    )
                )
        for load in loads:
            load.start()
        for load in loads:
            load.wait()

        @pl.when(bucket >= 1)
        def _():
            for panel in range(16):
                put(
                    panel // wide,
                    main + (panel % wide) * TROWS,
                    (BROWS - bucket) * 16 + panel + FRONT,
                    16,
                )

        @pl.when(bucket == 0)
        def _():
            for panel in range(12):
                put(
                    panel // narrow,
                    main + (panel % narrow) * TROWS,
                    QROWS * 12 + panel + FRONT,
                    12,
                )

        @pl.when(bucket == 7)
        def _():
            flat[pl.ds(FRONT + FLAT - LANES, LANES), :] = small[...]

    @pl.when(bucket >= 2)
    def _():
        def reach(at):
            tiles = (at * (ADAM_ROWS // 8) // 2 + 23) // 16
            return jnp.clip(jnp.where(at > 0, tiles, 0), 0, BROWS // 16)

        def step(tile, carry):
            row = pl.multiple_of(tile * 16, 16)
            for panel in range(16):
                put(
                    panel // wide,
                    (panel % wide) * BROWS + row,
                    (row - bucket) * 16 + panel + FRONT,
                    16,
                )
            return carry

        lax.fori_loop(reach(turn_at), reach(turn_at + 1), step, 0)

    @pl.when(bucket < 2)
    def _():
        def reach(at):
            tiles = (at * ADAM_ROWS + 16) // 192 + 1
            return jnp.clip(jnp.where(at > 0, tiles, 0), 0, QROWS // 16)

        def step(tile, carry):
            row = pl.multiple_of(tile * 16, 16)
            for panel in range(12):
                put(
                    panel // narrow,
                    (panel % narrow) * QROWS + row,
                    row * 12 + panel - 16 * bucket + FRONT,
                    12,
                )
            return carry

        lax.fori_loop(reach(turn_at), reach(turn_at + 1), step, 0)

    start = turn_at * ADAM_ROWS
    gradient = flat[pl.ds(pl.multiple_of(FRONT + start, 8), ADAM_ROWS), :]
    reduced[...] = gradient
    scale_one, scale_two, decay, keep = (scalar_ref[at] for at in range(4))
    one = beta_one * first[...] + (1.0 - beta_one) * gradient
    two = beta_two * second[...] + (1.0 - beta_two) * gradient * gradient
    new_first[...] = one
    new_second[...] = two
    old = weights[...]
    change = (one * scale_one) / (jnp.sqrt(two * scale_two) + adam_epsilon) + decay * old

    def write(rate):
        fresh = old - rate * change
        new_weights[...] = fresh
        new_moving[...] = keep * moving[...] + (1.0 - keep) * fresh

    first_row = bucket * FLAT + start
    bounds = [bound // LANES for bound in bound_list(512, 2048)[1:]]
    kinds = [sum(jnp.where(at >= bound, 1, 0) for bound in bounds) for at in (first_row, first_row + ADAM_ROWS - 1)]

    @pl.when(kinds[0] == kinds[1])
    def _():
        write(rate_ref[kinds[0]])

    @pl.when(kinds[0] != kinds[1])
    def _():
        row = first_row + lax.broadcasted_iota(jnp.int32, (ADAM_ROWS, LANES), 0)
        rate = jnp.full((ADAM_ROWS, LANES), rate_ref[0], jnp.float32)
        for kind, bound in enumerate(bounds):
            rate = jnp.where(row >= bound, rate_ref[kind + 1], rate)
        write(rate)


def adam(table, scalars, rates, stays, near, far, small, state):
    steps = -(-FLAT // ADAM_ROWS)
    block = pl.BlockSpec((ADAM_ROWS, LANES), lambda i: (i, 0))
    return pl.pallas_call(
        adam_kernel,
        grid=(steps,),
        out_shape=[jax.ShapeDtypeStruct((FLAT, LANES), jnp.float32)] * 5,
        in_specs=[pl.BlockSpec(memory_space=pltpu.SMEM)] * 3
        + [pl.BlockSpec(memory_space=HBM)] * 2
        + [pl.BlockSpec(memory_space=pl.ANY)] * 8
        + [pl.BlockSpec(memory_space=pltpu.VMEM)]
        + [block] * 4,
        out_specs=[block] * 5,
        scratch_shapes=[
            pltpu.VMEM((4, chunk_rows(), LANES), jnp.float32),
            pltpu.VMEM((2, 4, chunk_rows(), LANES), jnp.bfloat16),
            pltpu.VMEM((FRONT + max(steps * ADAM_ROWS, FLAT + BACK), LANES), jnp.float32),
            pltpu.SemaphoreType.DMA((3, 4)),
        ],
        compiler_params=params(60),
        cost_estimate=LIGHT,
        name="adam",
    )(table, scalars, rates, *stays, *near, *far, small, *state)


def finish_kernel(terms, rows, grads, out):
    scaled = terms[0].astype(jnp.float32)
    for at in range(1, terms.shape[0]):
        scaled = scaled + terms[at].astype(jnp.float32)
    unit, scale = norm_stats(rows[...].astype(jnp.float32))
    out[...] = grads[...].astype(jnp.float32) + scale * (
        scaled
        - jnp.mean(scaled, axis=-1, keepdims=True)
        - unit * jnp.mean(scaled * unit, axis=-1, keepdims=True)
    )


def finish(terms, rows, grads):
    count, width = rows.shape
    height = count // 4
    block = pl.BlockSpec((height, width), lambda i: (i, 0))
    return pl.pallas_call(
        finish_kernel,
        grid=(count // height,),
        out_shape=jax.ShapeDtypeStruct((count, width), jnp.float32),
        in_specs=[
            pl.BlockSpec((terms.shape[0], height, width), lambda i: (0, i, 0)),
            block,
            block,
        ],
        out_specs=block,
        compiler_params=params(60),
        cost_estimate=LIGHT,
        name="finish",
    )(terms, rows, grads)


FF_BLOCK = 256


def hidden_kernel(normed, up, up_bias, *refs):
    hidden, slope = refs[-2:]
    before = matmul(normed[...], up[...]) + up_bias[...]
    half = 0.5 + 0.5 * lax.erf(before * math.sqrt(0.5))
    hidden[...] = (before * half).astype(jnp.bfloat16)
    slope[...] = half + before * jnp.exp(-0.5 * before * before) * (1.0 / math.sqrt(2.0 * math.pi))


def hidden_layer(half, width, normed, up, up_bias, before):
    rows, units = normed.shape[0], up.shape[1]
    steps = units // FF_BLOCK // 2
    block = pl.BlockSpec((rows, FF_BLOCK), lambda i: (0, i + half * steps))
    return pl.pallas_call(
        hidden_kernel,
        grid=(steps,),
        out_shape=[
            jax.ShapeDtypeStruct((rows, width + units), jnp.bfloat16),
            jax.ShapeDtypeStruct((rows, units), jnp.float32),
        ],
        in_specs=[
            pl.BlockSpec(memory_space=pltpu.VMEM),
            pl.BlockSpec((D, FF_BLOCK), lambda i: (0, i + half * steps)),
            pl.BlockSpec((1, FF_BLOCK), lambda i: (0, i + half * steps)),
        ]
        + [pl.BlockSpec(memory_space=HBM)] * len(before),
        out_specs=[
            pl.BlockSpec((rows, FF_BLOCK), lambda i: (0, i + half * steps + width // FF_BLOCK)),
            block,
        ],
        input_output_aliases={3 + at: at for at in range(len(before))},
        compiler_params=params(60),
        cost_estimate=LIGHT,
        name="hidden_layer",
    )(normed, up, up_bias, *before)


def hidden_back_kernel(half, grads, down, slope, grad_before, grad_bias):
    rounded = (slope[...] * product_back(grads[...], down[...])).astype(jnp.bfloat16)
    grad_before[...] = rounded
    grad_bias[...] = jnp.sum(rounded.astype(jnp.float32), axis=0, keepdims=True)


def hidden_back(half, grads, mix, slope):
    rows, units = slope.shape
    first = (mix.shape[0] - units) // FF_BLOCK
    steps = units // FF_BLOCK // 2
    return pl.pallas_call(
        hidden_back_kernel,
        out_shape=[
            jax.ShapeDtypeStruct((rows, units // 2), jnp.bfloat16),
            jax.ShapeDtypeStruct((1, units // 2), jnp.float32),
        ],
        grid_spec=pltpu.PrefetchScalarGridSpec(
            num_scalar_prefetch=1,
            grid=(steps,),
            in_specs=[
                pl.BlockSpec((rows, D), lambda i, half: (0, 0)),
                pl.BlockSpec((FF_BLOCK, D), lambda i, half: (first + half[0] * steps + i, 0)),
                pl.BlockSpec((rows, FF_BLOCK), lambda i, half: (0, half[0] * steps + i)),
            ],
            out_specs=[
                pl.BlockSpec((rows, FF_BLOCK), lambda i, half: (0, i)),
                pl.BlockSpec((1, FF_BLOCK), lambda i, half: (0, i)),
            ],
        ),
        compiler_params=params(60),
        cost_estimate=LIGHT,
        name="hidden_back",
    )(half, grads, mix, slope)


def norm_kernel(rows, gains, one, two, centre, scale):
    values = rows[...].astype(jnp.float32)
    middle = jnp.mean(values, axis=-1, keepdims=True)
    values = values - middle
    factor = lax.rsqrt(jnp.mean(values * values, axis=-1, keepdims=True) + norm_epsilon)
    unit = values * factor
    one[...] = (unit * gains[0:1, :] + gains[1:2, :]).astype(jnp.bfloat16)
    two[...] = (unit * gains[2:3, :] + gains[3:4, :]).astype(jnp.bfloat16)
    centre[...] = middle
    scale[...] = factor


def norms(rows, small_params):
    count, width = rows.shape
    height = 128
    block = pl.BlockSpec((height, width), lambda i: (i, 0))
    column = pl.BlockSpec((height, 1), lambda i: (i, 0))
    return pl.pallas_call(
        norm_kernel,
        grid=(count // height,),
        out_shape=[jax.ShapeDtypeStruct((count, width), jnp.bfloat16)] * 2
        + [jax.ShapeDtypeStruct((count, 1), jnp.float32)] * 2,
        in_specs=[block, pl.BlockSpec(memory_space=pltpu.VMEM)],
        out_specs=[block, block, column, column],
        compiler_params=params(60),
        cost_estimate=LIGHT,
        name="norms",
    )(rows, small_params)


QUERY_BLOCK = 256


def turn(values, tables, sign):
    plain, lower, upper = tables
    half_rot = ROT // 2
    return (
        values * plain
        + pltpu.roll(values, HD - half_rot, 1) * (sign * lower)
        + pltpu.roll(values, half_rot, 1) * (sign * upper)
    )


def block_scores(query, keys, begins, first, first_key):
    scores = product_back(query, keys) * (1.0 / math.sqrt(HD))
    row_index = first + lax.broadcasted_iota(jnp.int32, scores.shape, 0)
    key_index = first_key + lax.broadcasted_iota(jnp.int32, scores.shape, 1)
    allowed = (key_index <= row_index) & (key_index >= begins)
    return jnp.where(allowed, scores, masked_score)


HEAD_PAIR = 2 * HD


def attend_kernel(
    normed, queries_in, keys_in, values_in, bias, plain, lower, upper, begins, _, context, turned, logs
):
    rows = normed.shape[0]
    width = bias.shape[1] // 3
    first_column = pl.program_id(0) * HEAD_PAIR
    tables = (plain[...], lower[...], upper[...])
    for part, weights in enumerate((queries_in, keys_in, values_in)):
        projected = matmul(normed[...], weights[...])
        projected = projected + bias[
            :, pl.ds(pl.multiple_of(part * width + first_column, HEAD_PAIR), HEAD_PAIR)
        ]
        for head in range(2):
            value = projected[:, head * HD : (head + 1) * HD]
            if part < 2:
                value = turn(value, tables, 1.0)
            turned[part, :, head * HD : (head + 1) * HD] = value.astype(jnp.bfloat16)

    def one_head(head, carry):
        column = pl.ds(pl.multiple_of(head * HD, HD), HD)
        queries, keys, values = (turned[part, :, column] for part in range(3))
        for first in range(0, rows, QUERY_BLOCK):
            last = first + QUERY_BLOCK
            mine = slice(first, last)
            seen = slice(max(0, first - rows // 2), last)
            scores = block_scores(queries[mine], keys[seen], begins[mine, :], first, seen.start)
            top = jnp.max(scores, axis=-1, keepdims=True)
            raised = jnp.exp(scores - top)
            total = jnp.sum(raised, axis=-1, keepdims=True)
            rounded = (raised / total).astype(jnp.bfloat16)
            context[mine, column] = matmul(rounded, values[seen]).astype(jnp.bfloat16)
            logs[head, mine, :] = top + jnp.log(total)
        return carry

    lax.fori_loop(0, 2, one_head, 0)


def attend(normed, mixer_in, bias, tables, begins, mixed):
    rows, width = normed.shape[0], mixer_in.shape[1] // 3
    pairs = width // HEAD_PAIR
    whole = pl.BlockSpec(memory_space=pltpu.VMEM)

    def weights(part):
        return pl.BlockSpec((mixer_in.shape[0], HEAD_PAIR), lambda i: (0, part * pairs + i))

    return pl.pallas_call(
        attend_kernel,
        grid=(pairs,),
        out_shape=[
            jax.ShapeDtypeStruct(mixed.shape, mixed.dtype),
            jax.ShapeDtypeStruct((3, rows, width), jnp.bfloat16),
            jax.ShapeDtypeStruct((width // HD, rows, 1), jnp.float32),
        ],
        in_specs=[whole, weights(0), weights(1), weights(2)]
        + [whole] * 5
        + [pl.BlockSpec(memory_space=HBM)],
        out_specs=[
            pl.BlockSpec((rows, HEAD_PAIR), lambda i: (0, i)),
            pl.BlockSpec((3, rows, HEAD_PAIR), lambda i: (0, 0, i)),
            pl.BlockSpec((2, rows, 1), lambda i: (i, 0, 0)),
        ],
        input_output_aliases={9: 0},
        compiler_params=params(60),
        cost_estimate=LIGHT,
        name="attend",
    )(normed, mixer_in, mixer_in, mixer_in, bias, *tables, begins, mixed)


def attend_back_kernel(
    turned, logs, plain, lower, upper, begins, grad_context, grad_projected, key_sum, value_sum
):
    rows, width = grad_context.shape
    score_scale = 1.0 / math.sqrt(HD)

    def one_head(head, carry):
        cols = [pl.ds(pl.multiple_of(part * width + head * HD, HD), HD) for part in range(3)]
        queries, keys, values = (turned[part, :, cols[0]] for part in range(3))
        key_sum[...] = jnp.zeros_like(key_sum)
        value_sum[...] = jnp.zeros_like(value_sum)
        for first in range(0, rows, QUERY_BLOCK):
            last = first + QUERY_BLOCK
            mine = slice(first, last)
            query = queries[mine]
            seen = slice(max(0, first - rows // 2), last)
            scores = block_scores(query, keys[seen], begins[mine, :], first, seen.start)
            soft = jnp.exp(scores - logs[head, mine, :])
            grad_mine = grad_context[mine, cols[0]]
            grad_soft = product_back(grad_mine, values[seen])
            delta = jnp.sum(soft * grad_soft, axis=-1, keepdims=True)
            grad_scores = (soft * (grad_soft - delta)).astype(jnp.bfloat16)
            grad_query = matmul(grad_scores, keys[seen]) * score_scale
            tables = (plain[mine, :], lower[mine, :], upper[mine, :])
            grad_projected[mine, cols[0]] = turn(grad_query, tables, -1.0).astype(jnp.bfloat16)
            key_sum[seen, :] += product_rows(grad_scores, query)
            value_sum[seen, :] += product_rows(soft.astype(jnp.bfloat16), grad_mine)
        tables = (plain[...], lower[...], upper[...])
        grad_projected[:, cols[1]] = turn(key_sum[...] * score_scale, tables, -1.0).astype(
            jnp.bfloat16
        )
        grad_projected[:, cols[2]] = value_sum[...].astype(jnp.bfloat16)
        return carry

    lax.fori_loop(0, width // HD, one_head, 0)


def attend_back(turned, logs, tables, begins, grad_context):
    rows, width = grad_context.shape
    whole = pl.BlockSpec(memory_space=pltpu.VMEM)
    return pl.pallas_call(
        attend_back_kernel,
        out_shape=jax.ShapeDtypeStruct((rows, 3 * width), jnp.bfloat16),
        in_specs=[whole] * 7,
        out_specs=whole,
        scratch_shapes=[pltpu.VMEM((rows, HD), jnp.float32)] * 2,
        compiler_params=params(36),
        cost_estimate=LIGHT,
        name="attend_back",
    )(turned, logs, *tables, begins, grad_context)


def rope_tables(places):
    half_rot = ROT // 2
    frequency = rope_base ** (-2.0 * jnp.arange(half_rot, dtype=jnp.float32) / ROT)
    angles = places[:, None] * frequency[None, :]
    cosine, sines = jnp.cos(angles), jnp.sin(angles)
    rest = jnp.zeros((places.shape[0], HD - ROT), jnp.float32)
    none = jnp.zeros_like(sines)
    return (
        jnp.concatenate([cosine, cosine, rest + 1.0], axis=1),
        jnp.concatenate([-sines, none, rest], axis=1),
        jnp.concatenate([none, sines, rest], axis=1),
    )


def along_x(value):
    return lax.ppermute(value, "dp", [(i, i ^ 1) for i in range(4)])


def along_y(value):
    return lax.ppermute(value, "dp", [(i, i ^ 2) for i in range(4)])


def along_line(value, bit):
    return lax.ppermute(value, "tensor", [(i, i ^ bit) for i in range(4)])


def along(bit, value):
    return lax.ppermute(
        value, ("dp", "chip"), [(i, (i // 2 ^ bit) * 2 + (i % 2 ^ 1)) for i in range(8)]
    )


def across(value):
    return lax.ppermute(value, "chip", [(0, 1), (1, 0)])


def line_blocks(partial):
    count = lax.axis_size("tensor")
    rows = partial.shape[0] // count
    return lax.all_to_all(partial.reshape(count, rows, partial.shape[1]), "tensor", 0, 0)


def on_device_fast(
    residual,
    cotangent,
    lengths,
    owners,
    step_count,
    rates,
    weight_decay,
    ema_decay,
    master,
    moment_one,
    moment_two,
    average,
):
    local_width = HD * H // lax.axis_size("tensor")
    group_rows = residual.shape[1] * lax.axis_size("tensor")
    slots = jnp.arange(8, dtype=jnp.int32)
    inverse = jnp.sum(
        slots[None, :] * (owners[None, :] == slots[:, None]).astype(jnp.int32), axis=1
    )
    data_index, core, here = lax.axis_index("dp"), lax.axis_index("chip"), lax.axis_index("tensor")
    partners = jnp.stack([(data_index ^ j) * 2 + (core ^ c) for c in range(2) for j in range(4)])
    buckets = jnp.sum(
        jnp.where(partners[:, None] == slots[None, :], inverse[None, :], 0), axis=1
    ).astype(jnp.int32)
    partner_of = jnp.sum(
        jnp.where(buckets[None, :] == slots[:, None], slots[None, :], 0), axis=1
    )
    hop, other = partner_of % 4, partner_of // 4
    grad_table = [core[None]]
    for first, second in ((hop % 2, hop // 2), (hop // 2, hop % 2)):
        grad_table.append(first * (1 + second))
        grad_table.append(other + 2 * second * (1 - first))
    grad_table = jnp.concatenate(grad_table).astype(jnp.int32)

    full_rows = lax.all_gather(residual[0], "tensor", axis=0, tiled=True)
    grad_rows = lax.all_gather(cotangent[0], "tensor", axis=0, tiled=True)
    own_rows = residual[0].astype(jnp.float32)

    def order(*values):
        return lax.optimization_barrier(values)

    rank = jnp.arange(lengths.shape[1], dtype=jnp.int32)
    seq_ends = jnp.sum(jnp.where(rank[None, :] <= rank[:, None], lengths[0][None, :], 0), axis=1)
    token_index = jnp.arange(group_rows, dtype=jnp.int32)
    passed = (token_index[:, None] >= seq_ends[None, :]).astype(jnp.int32)
    begins = jnp.sum(passed * lengths[0][None, :], axis=1)
    tables = rope_tables((token_index - begins).astype(jnp.float32))
    begins = begins[:, None]

    one, two = pack(buckets[:1], master.reshape(FLAT, LANES))
    one_x, one_y, one_own = order(along_x(one), along_y(one), across(one))

    def from_far(first, second, from_x, from_y):
        rows = (16 // CHUNKS) * BROWS
        start = part_row(second)
        count = start if first == 0 else rows
        return [along_x(from_y[:count]), along_y(from_x[start : start + rows])]

    far = from_far(0, 1, one_x, one_y)
    near_x, near_y, two_own = across(one_x), across(one_y), across(two)
    far, near_x, near_y, two_own, two, tables, begins = order(
        far, near_x, near_y, two_own, two, tables, begins
    )

    two_x, two_y = along_x(two), along_y(two)
    far_other = [across(value) for value in far]
    sources = []
    for part in range(2):
        sources += [one, one_x, one_y, far[part], one_own, near_x, near_y, far_other[part]]
    weights = unpack((0, 1), buckets, sources, [])
    weights, full_rows = order(weights, full_rows)
    flat_bias = weights[3][:8].reshape(-1).astype(jnp.float32)
    mixer_bias = flat_bias[: 3 * local_width]
    expand_bias = flat_bias[3 * local_width : 3 * local_width + D]
    small_params = flat_bias[3 * local_width + D : 3 * local_width + 7 * D].reshape(6, D)
    full_one, full_two, centre, scale = norms(full_rows, small_params)
    hidden_half = hidden_layer(0, local_width, full_two, weights[2], expand_bias[None], ())
    two_x, two_y, full_rows, full_one, full_two, weights, hidden_half = order(
        two_x, two_y, full_rows, full_one, full_two, weights, hidden_half
    )
    other_rows = across(full_rows)

    far = from_far(2, 3, two_x, two_y)
    near_x, near_y = across(two_x), across(two_y)
    other_one, other_two, _, _ = norms(other_rows, small_params)
    far, near_x, near_y, hidden_half, weights, other_one, other_two = order(
        far, near_x, near_y, hidden_half, weights, other_one, other_two
    )

    far_other = [across(value) for value in far]
    sources = []
    for part in range(2):
        sources += [two, two_x, two_y, far[part], two_own, near_x, near_y, far_other[part]]
    weights = unpack((2, 3), buckets, sources, weights)
    mixer_in, mix_weight, expand_weight = weights[:3]

    mixed, slope = hidden_layer(1, local_width, full_two, expand_weight, expand_bias[None], hidden_half)
    mixed, turned, logs = attend(full_one, mixer_in, mixer_bias[None], tables, begins, mixed)
    other_mixed = across(mixed)
    branches = matmul(mixed, mix_weight)
    branches, turned, grad_rows = order(branches, turned, grad_rows)
    branches = lax.psum_scatter(branches, "tensor", scatter_dimension=0, tiled=True)
    other_grads = across(grad_rows)

    grad_context = product_back(grad_rows, mix_weight[:local_width]).astype(jnp.bfloat16)
    grad_projected = attend_back(turned, logs, tables, begins, grad_context)
    grad_projected, slope = order(grad_projected, slope)
    other_projected = across(grad_projected)
    cores = core[None].astype(jnp.int32)
    rest_before, rest_bias = hidden_back(1 - cores, grad_rows, mix_weight, slope)
    other_before = across(rest_before)
    own_before, own_bias = hidden_back(cores, grad_rows, mix_weight, slope)
    grad_expand_bias = jnp.where(
        core == 0,
        jnp.concatenate([own_bias[0], rest_bias[0]]),
        jnp.concatenate([rest_bias[0], own_bias[0]]),
    )

    lefts = [full_one, other_one, mixed, other_mixed, full_two, other_two, mixed, other_mixed]
    rights = [grad_projected, other_projected, grad_rows, other_grads, own_before, other_before]
    sums = weight_grads(grad_table, lefts, rights)
    grad_projected, own_before, rest_before, sums = order(
        grad_projected, own_before, rest_before, sums
    )
    near_a, far_a, near_b, far_b, passed, stays = sums
    came_a, came_b, other_stays = along_x(far_a), along_y(far_b), across(stays)

    partial, norm_grads = norm_grad(
        cores,
        grad_projected,
        mixer_in,
        own_before,
        rest_before,
        expand_weight,
        full_rows,
        centre,
        scale,
        jnp.stack([small_params[0], small_params[2]]),
    )
    bias_grad = jnp.sum(grad_rows.astype(jnp.float32), axis=0)
    small = (
        jnp.sum(grad_projected.astype(jnp.float32), axis=0),
        grad_expand_bias,
        bias_grad,
    )

    for bit in (1, 2):
        norm_grads = norm_grads + along_line(norm_grads, bit)
    came_a, came_b, other_stays, partial, norm_grads, small, near_a, near_b = order(
        came_a, came_b, other_stays, partial, norm_grads, small, near_a, near_b
    )
    near_a, near_b = along_x(near_a), along_y(near_b)
    terms = line_blocks(partial)
    pass_a = (passed[0] + came_a.astype(jnp.float32)).astype(jnp.bfloat16)
    pass_b = (passed[1] + came_b.astype(jnp.float32)).astype(jnp.bfloat16)
    small = jnp.concatenate(
        [
            small[0],
            small[1],
            norm_grads.reshape(-1),
            small[2],
            small[2],
            jnp.zeros((8 * D - 3 * local_width - 7 * D,), jnp.float32),
        ]
    ).reshape(LANES, LANES)
    small = small + across(small)
    small = small + along_x(small)
    near_a, near_b, pass_a, pass_b, small = order(near_a, near_b, pass_a, pass_b, small)
    output = residual[0].astype(jnp.float32) + branches + small_params[4] + small_params[5]
    far_a, far_b = along_y(pass_a), along_x(pass_b)
    near = [near_a, near_b, across(near_a), across(near_b)]
    far_a, far_b, near, small, output = order(far_a, far_b, near, small, output)
    far = [far_a, far_b, across(far_a), across(far_b)]
    small = small + along_y(small)

    step_value = step_count[0].astype(jnp.float32)
    scalars = jnp.stack(
        [
            1.0 / (1.0 - jnp.power(beta_one, step_value)),
            1.0 / (1.0 - jnp.power(beta_two, step_value)),
            weight_decay[0],
            ema_decay[0],
        ]
    )
    state = [v.reshape(FLAT, LANES) for v in (master, moment_one, moment_two, average)]
    table = jnp.stack([buckets[0], core.astype(jnp.int32)])
    results = adam(table, scalars, rates, [stays, other_stays], near, far, small, state)
    terms, results = order(terms, results)
    input_grad = finish(terms, residual[0], cotangent[0])
    return (output[None], input_grad[None], *[v.reshape(master.shape) for v in results])


def solution(mesh):
    placed = (
        P(("dp", "chip"), "tensor", None),
        P(("dp", "chip"), "tensor", None),
        P(("dp", "chip"), None),
        P(),
        P(),
        P(),
        P(),
        P(),
        P("tensor", ("dp", "chip"), None),
        P("tensor", ("dp", "chip"), None),
        P("tensor", ("dp", "chip"), None),
        P("tensor", ("dp", "chip"), None),
    )
    return jax.shard_map(
        device_program(mesh),
        mesh=mesh,
        in_specs=placed,
        out_specs=(
            P(("dp", "chip"), "tensor", None),
            P(("dp", "chip"), "tensor", None),
            P("tensor", ("dp", "chip"), None),
            P("tensor", ("dp", "chip"), None),
            P("tensor", ("dp", "chip"), None),
            P("tensor", ("dp", "chip"), None),
            P("tensor", ("dp", "chip"), None),
        ),
        check_vma=False,
    )
```

```python
import functools
import math

import jax
import jax.numpy as jnp
from jax import lax
from jax.experimental import pallas as pl
from jax.experimental.pallas import tpu as pltpu
from jax.sharding import PartitionSpec as P

D = 2048
H = 16
HD = 128
FF = 8192
ROT = 32


norm_epsilon = 1e-05
adam_epsilon = 1e-08
beta_one = 0.5
beta_two = 0.5
rope_base = 10000.0
masked_score = -1e30


def matmul(left, right):
    return jnp.dot(left, right, preferred_element_type=jnp.float32)


def product_rows(left, right):
    return lax.dot_general(
        left, right, (((0,), (0,)), ((), ())), preferred_element_type=jnp.float32
    )


def product_back(left, right):
    return lax.dot_general(
        left, right, (((1,), (1,)), ((), ())), preferred_element_type=jnp.float32
    )


def bound_list(local_width, local_ff):
    widths = [
        D * 3 * local_width,
        local_width * D,
        D * local_ff,
        local_ff * D,
        3 * local_width,
        local_ff,
        6 * D,
    ]
    bounds = [0]
    for part_width in widths:
        bounds.append(bounds[-1] + part_width)
    return bounds


def group_layout(seq_lengths, group_rows):
    order = jnp.arange(seq_lengths.shape[0], dtype=jnp.int32)
    seq_ends = jnp.sum(
        jnp.where(order[None, :] <= order[:, None], seq_lengths[None, :], 0), axis=1
    )
    starts = seq_ends - seq_lengths
    token_index = jnp.arange(group_rows, dtype=jnp.int32)
    segment = jnp.sum((token_index[:, None] >= seq_ends[None, :]).astype(jnp.int32), axis=1)
    chosen = (
        segment[:, None] == jnp.arange(seq_lengths.shape[0], dtype=jnp.int32)[None, :]
    ).astype(jnp.int32)
    places = token_index - jnp.sum(chosen * starts[None, :], axis=1)
    return (segment, places.astype(jnp.float32))


def rotary_tables(places):
    half_rot = ROT // 2
    frequency = rope_base ** (-2.0 * jnp.arange(half_rot, dtype=jnp.float32) / ROT)
    angles = places[:, None] * frequency[None, :]
    return (jnp.cos(angles)[:, None, :], jnp.sin(angles)[:, None, :])


def rotate(values, cosine, sines):
    half_rot = ROT // 2
    first = values[..., :half_rot]
    second = values[..., half_rot:ROT]
    return jnp.concatenate(
        [first * cosine - second * sines, second * cosine + first * sines, values[..., ROT:]],
        axis=-1,
    )


def norm_stats(inputs):
    center = inputs - jnp.mean(inputs, axis=-1, keepdims=True)
    scale = lax.rsqrt(jnp.mean(center * center, axis=-1, keepdims=True) + norm_epsilon)
    return (center * scale, scale)


def norm_back(grad_norm, gain, unit_rows, scale):
    scaled = grad_norm * gain
    return scale * (
        scaled
        - jnp.mean(scaled, axis=-1, keepdims=True)
        - unit_rows * jnp.mean(scaled * unit_rows, axis=-1, keepdims=True)
    )


def adam_update(
    weights, first, second, moving, gradient, step_rate, step_value, decay_rate, ema_keep
):
    bias_one = 1.0 - jnp.power(beta_one, step_value)
    bias_two = 1.0 - jnp.power(beta_two, step_value)
    new_first = beta_one * first + (1.0 - beta_one) * gradient
    new_second = beta_two * second + (1.0 - beta_two) * gradient * gradient
    ratio = new_first / bias_one / (jnp.sqrt(new_second / bias_two) + adam_epsilon)
    new_weights = weights - step_rate * (ratio + decay_rate * weights)
    new_moving = ema_keep * moving + (1.0 - ema_keep) * new_weights
    return (new_weights, new_first, new_second, new_moving)


def on_device(
    residual,
    cotangent,
    lengths,
    owners,
    step_count,
    rates,
    weight_decay,
    ema_decay,
    master,
    moment_one,
    moment_two,
    average,
):
    tensor_count = lax.axis_size("tensor")
    group_count = lax.axis_size(("dp", "chip"))
    local_heads = H // tensor_count
    local_width = local_heads * HD
    local_ff = FF // tensor_count
    rows_here = residual.shape[1]
    group_rows = rows_here * tensor_count
    bucket_size = master.shape[2]
    bounds = bound_list(local_width, local_ff)
    slots = jnp.arange(group_count, dtype=jnp.int32)
    inverse = jnp.sum(
        slots[None, :] * (owners[None, :] == slots[:, None]).astype(jnp.int32), axis=1
    )
    gathered = lax.all_gather(master.astype(jnp.bfloat16), ("dp", "chip"), axis=1, tiled=True)
    flat_params = jnp.take(gathered[0], owners, axis=0).reshape(-1)
    mixer_in = flat_params[bounds[0] : bounds[1]].reshape(D, 3 * local_width)
    mixer_out = flat_params[bounds[1] : bounds[2]].reshape(local_width, D)
    expand_weight = flat_params[bounds[2] : bounds[3]].reshape(D, local_ff)
    shrink_weight = flat_params[bounds[3] : bounds[4]].reshape(local_ff, D)
    mixer_bias = flat_params[bounds[4] : bounds[5]].astype(jnp.float32)
    expand_bias = flat_params[bounds[5] : bounds[6]].astype(jnp.float32)
    small_params = flat_params[bounds[6] : bounds[7]].reshape(6, D).astype(jnp.float32)
    own_rows = residual[0].astype(jnp.float32)
    segment, places = group_layout(lengths[0], group_rows)
    cosine, sines = rotary_tables(places)
    own_unit, own_scale = norm_stats(own_rows)
    normed_one = (own_unit * small_params[0] + small_params[1]).astype(jnp.bfloat16)
    normed_two = (own_unit * small_params[2] + small_params[3]).astype(jnp.bfloat16)
    full_one, full_two = (
        lax.all_gather(normed_one, "tensor", axis=0, tiled=True),
        lax.all_gather(normed_two, "tensor", axis=0, tiled=True),
    )
    projected = matmul(full_one, mixer_in) + mixer_bias
    head_shape = (group_rows, local_heads, HD)
    queries = rotate(projected[:, :local_width].reshape(head_shape), cosine, sines).astype(
        jnp.bfloat16
    )
    keys = rotate(
        projected[:, local_width : 2 * local_width].reshape(head_shape), cosine, sines
    ).astype(jnp.bfloat16)
    values = projected[:, 2 * local_width :].reshape(head_shape).astype(jnp.bfloat16)
    block_rows = min(512, group_rows)
    block_count = group_rows // block_rows
    score_scale = 1.0 / math.sqrt(HD)
    key_index = jnp.arange(group_rows, dtype=jnp.int32)

    def block_scores(start):
        query_block = lax.dynamic_slice_in_dim(queries, start, block_rows, 0)
        scores = (
            jnp.einsum("qhd,khd->hqk", query_block, keys, preferred_element_type=jnp.float32)
            * score_scale
        )
        row_index = start + jnp.arange(block_rows, dtype=jnp.int32)
        row_segment = lax.dynamic_slice_in_dim(segment, start, block_rows, 0)
        allowed = (row_segment[:, None] == segment[None, :]) & (
            key_index[None, :] <= row_index[:, None]
        )
        return (query_block, jnp.where(allowed[None], scores, masked_score))

    def attend_block(index):
        query_block, scores = block_scores(index * block_rows)
        row_top = jnp.max(scores, axis=-1, keepdims=True)
        raised = jnp.exp(scores - row_top)
        totals = jnp.sum(raised, axis=-1, keepdims=True)
        soft_weights = (raised / totals).astype(jnp.bfloat16)
        mixed = jnp.einsum("hqk,khd->qhd", soft_weights, values, preferred_element_type=jnp.float32)
        return (mixed.reshape(block_rows, local_width), (row_top + jnp.log(totals))[..., 0])

    context_blocks, log_blocks = lax.map(attend_block, jnp.arange(block_count, dtype=jnp.int32))
    context = context_blocks.reshape(group_rows, local_width).astype(jnp.bfloat16)
    before = matmul(full_two, expand_weight) + expand_bias
    hidden = jax.nn.gelu(before, approximate=False).astype(jnp.bfloat16)
    branches = lax.psum_scatter(
        matmul(context, mixer_out) + matmul(hidden, shrink_weight),
        "tensor",
        scatter_dimension=0,
        tiled=True,
    )
    output = own_rows + branches + small_params[4] + small_params[5]
    grad_own = cotangent[0].astype(jnp.float32)
    grad_rows = lax.all_gather(cotangent[0], "tensor", axis=0, tiled=True)
    grad_mixer_out = product_rows(context, grad_rows)
    grad_shrink = product_rows(hidden, grad_rows)
    grad_context = product_back(grad_rows, mixer_out).astype(jnp.bfloat16)
    grad_hidden = product_back(grad_rows, shrink_weight)
    gelu_pull = jax.vjp(lambda inner: jax.nn.gelu(inner, approximate=False), before)[1]
    grad_before = gelu_pull(grad_hidden)[0].astype(jnp.bfloat16)
    grad_expand = product_rows(full_two, grad_before)
    grad_expand_bias = jnp.sum(grad_before.astype(jnp.float32), axis=0)
    partial_two = product_back(grad_before, expand_weight)

    def attention_back(carry, index):
        grad_keys, grad_values = carry
        start = index * block_rows
        query_block, scores = block_scores(start)
        log_rows = lax.dynamic_index_in_dim(log_blocks, index, 0, keepdims=False)
        soft_weights = jnp.exp(scores - log_rows[..., None])
        grad_block = lax.dynamic_slice_in_dim(grad_context, start, block_rows, 0).reshape(
            block_rows, local_heads, HD
        )
        grad_weights = jnp.einsum(
            "qhd,khd->hqk", grad_block, values, preferred_element_type=jnp.float32
        )
        delta = jnp.sum(soft_weights * grad_weights, axis=-1, keepdims=True)
        grad_scores = (soft_weights * (grad_weights - delta)).astype(jnp.bfloat16)
        grad_query = (
            jnp.einsum("hqk,khd->qhd", grad_scores, keys, preferred_element_type=jnp.float32)
            * score_scale
        )
        grad_keys = (
            grad_keys
            + jnp.einsum(
                "hqk,qhd->khd", grad_scores, query_block, preferred_element_type=jnp.float32
            )
            * score_scale
        )
        grad_values = grad_values + jnp.einsum(
            "hqk,qhd->khd",
            soft_weights.astype(jnp.bfloat16),
            grad_block,
            preferred_element_type=jnp.float32,
        )
        return ((grad_keys, grad_values), grad_query)

    zero_heads = jnp.zeros(head_shape, jnp.float32)
    (grad_keys, grad_values), grad_query = lax.scan(
        attention_back, (zero_heads, zero_heads), jnp.arange(block_count, dtype=jnp.int32)
    )
    grad_query = grad_query.reshape(head_shape)
    grad_projected = jnp.concatenate(
        [
            rotate(grad_query, cosine, -sines).reshape(group_rows, local_width),
            rotate(grad_keys, cosine, -sines).reshape(group_rows, local_width),
            grad_values.reshape(group_rows, local_width),
        ],
        axis=1,
    ).astype(jnp.bfloat16)
    grad_mixer_in = product_rows(full_one, grad_projected)
    grad_mixer_bias = jnp.sum(grad_projected.astype(jnp.float32), axis=0)
    partial_one = product_back(grad_projected, mixer_in)
    bias_grad = jnp.sum(grad_own, axis=0)
    grad_one, grad_two = (
        lax.psum_scatter(partial_one, "tensor", scatter_dimension=0, tiled=True),
        lax.psum_scatter(partial_two, "tensor", scatter_dimension=0, tiled=True),
    )
    norm_grads = [
        jnp.sum(grad_one * own_unit, axis=0),
        jnp.sum(grad_one, axis=0),
        jnp.sum(grad_two * own_unit, axis=0),
        jnp.sum(grad_two, axis=0),
    ]
    input_grad = (
        grad_own
        + norm_back(grad_one, small_params[0], own_unit, own_scale)
        + norm_back(grad_two, small_params[2], own_unit, own_scale)
    )
    small_grad = jnp.stack(norm_grads + [bias_grad, bias_grad])
    small_grad = lax.psum(small_grad, "tensor")
    flat_grad = jnp.concatenate(
        [
            grad_mixer_in.reshape(-1),
            grad_mixer_out.reshape(-1),
            grad_expand.reshape(-1),
            grad_shrink.reshape(-1),
            grad_mixer_bias,
            grad_expand_bias,
            small_grad.reshape(-1),
            jnp.zeros((group_count * bucket_size - bounds[7],), jnp.float32),
        ]
    )
    stored_grad = jnp.take(flat_grad.reshape(group_count, bucket_size), inverse, axis=0)
    reduced = lax.psum_scatter(stored_grad, ("dp", "chip"), scatter_dimension=0, tiled=True)[0]
    my_bucket = inverse[lax.axis_index(("dp", "chip"))]
    position = my_bucket * bucket_size + jnp.arange(bucket_size, dtype=jnp.int32)
    step_rate = jnp.zeros((bucket_size,), jnp.float32) + rates[0]
    for kind_index in range(1, 8):
        step_rate = jnp.where(position >= bounds[kind_index], rates[kind_index], step_rate)
    step_value = step_count[0].astype(jnp.float32)
    new_weights, new_first, new_second, new_moving = adam_update(
        master[0, 0],
        moment_one[0, 0],
        moment_two[0, 0],
        average[0, 0],
        reduced,
        step_rate,
        step_value,
        weight_decay[0],
        ema_decay[0],
    )
    return (
        output[None],
        input_grad[None],
        new_weights[None, None],
        new_first[None, None],
        new_second[None, None],
        new_moving[None, None],
        reduced[None, None],
    )


LANES = 128
TROWS = 16


def fits(mesh):
    return mesh.shape["dp"] == 4 and mesh.shape["chip"] == 2 and mesh.shape["tensor"] == 4


def device_program(mesh):
    return on_device_fast if fits(mesh) else on_device


CHUNKS = 4
BROWS = 768
QROWS = 1024
FRONT = 128
BACK = 256
FLAT = 12304
HBM = pltpu.HBM


LIGHT = pl.CostEstimate(flops=1, bytes_accessed=1, transcendentals=0)


def params(limit_mb, **more):
    return pltpu.CompilerParams(vmem_limit_bytes=limit_mb * 1024 * 1024, **more)


def part_row(part):
    rows = (16 // CHUNKS) * BROWS
    return (0, rows + 16 * TROWS, 0, rows)[part]


def pack_kernel(bucket_ref, flat_ref, *refs):
    outs, padded, sem = refs[:2], refs[2], refs[3]
    bucket = bucket_ref[0]
    load = pltpu.make_async_copy(flat_ref, padded.at[pl.ds(FRONT, FLAT)], sem)
    load.start()
    padded[pl.ds(0, FRONT)] = jnp.zeros((FRONT, LANES), jnp.float32)
    padded[pl.ds(FRONT + FLAT, BACK)] = jnp.zeros((BACK, LANES), jnp.float32)
    load.wait()
    wide, narrow = 16 // CHUNKS, 12 // CHUNKS

    def take(start, stride):
        return padded[pl.ds(start, 16, stride=stride), :].astype(jnp.bfloat16)

    @pl.when(bucket >= 2)
    def _():
        def step(tile, carry):
            row = pl.multiple_of(tile * 16, 16)
            for panel in range(16):
                part = panel // wide
                at = part_row(part) + (panel % wide) * BROWS
                outs[part // 2][pl.ds(at + row, 16), :] = take(
                    (row - bucket) * 16 + panel + FRONT, 16
                )
            return carry

        lax.fori_loop(0, BROWS // 16, step, 0)

    @pl.when(bucket < 2)
    def _():
        def step(tile, carry):
            row = pl.multiple_of(tile * 16, 16)
            for panel in range(12):
                part = panel // narrow
                at = part_row(part) + (panel % narrow) * QROWS
                outs[part // 2][pl.ds(at + row, 16), :] = take(
                    row * 12 + panel - 16 * bucket + FRONT, 12
                )
            return carry

        lax.fori_loop(0, QROWS // 16, step, 0)

    tails = wide * BROWS

    @pl.when(bucket >= 1)
    def _():
        for panel in range(16):
            outs[0][pl.ds(tails + panel * TROWS, TROWS), :] = take(
                (BROWS - bucket) * 16 + panel + FRONT, 16
            )

    @pl.when(bucket == 0)
    def _():
        for panel in range(16):
            outs[0][pl.ds(tails + panel * TROWS, TROWS), :] = take(
                QROWS * 12 + min(panel, 11) + FRONT, 12
            )


def cut_kernel(starts, *refs):
    count = len(starts)
    copies = [
        pltpu.make_async_copy(
            refs[at].at[pl.ds(start, refs[count + at].shape[0])], refs[count + at], refs[-1].at[at]
        )
        for at, start in enumerate(starts)
    ]
    for copy in copies:
        copy.start()
    for copy in copies:
        copy.wait()


def cut(values, starts, counts):
    return pl.pallas_call(
        functools.partial(cut_kernel, starts),
        out_shape=[jax.ShapeDtypeStruct((count, LANES), jnp.bfloat16) for count in counts],
        in_specs=[pl.BlockSpec(memory_space=pl.ANY)] * len(values),
        out_specs=[pl.BlockSpec(memory_space=pltpu.VMEM)] * len(values),
        scratch_shapes=[pltpu.SemaphoreType.DMA((len(values),))],
        compiler_params=params(60),
        cost_estimate=LIGHT,
        name="cut",
    )(*values)


def chunk_rows():
    return (16 // CHUNKS) * (BROWS + TROWS)


def pack(bucket, flat):
    rows = (32 // CHUNKS) * BROWS
    return pl.pallas_call(
        pack_kernel,
        out_shape=[
            jax.ShapeDtypeStruct((rows + 16 * TROWS, LANES), jnp.bfloat16),
            jax.ShapeDtypeStruct((rows, LANES), jnp.bfloat16),
        ],
        in_specs=[pl.BlockSpec(memory_space=pltpu.SMEM), pl.BlockSpec(memory_space=HBM)],
        out_specs=[pl.BlockSpec(memory_space=pltpu.VMEM)] * 2,
        scratch_shapes=[
            pltpu.VMEM((FRONT + FLAT + BACK, LANES), jnp.float32),
            pltpu.SemaphoreType.DMA,
        ],
        compiler_params=params(24),
        cost_estimate=LIGHT,
        name="pack_params",
    )(bucket, flat)


PLACES = {
    0: (("in", 0, 1024, 0),),
    1: (("in", 1024, 1024, 0),),
    2: (("mix", 0, 512, 0), ("up", 0, 256, 512)),
    3: (("up", 256, 768, 0),),
    4: (("up", 1024, 768, 0),),
    5: (("up", 1792, 256, 0), ("mix", 512, 512, 256)),
    6: (("mix", 1024, 768, 0),),
    7: (("mix", 1792, 768, 0),),
}
NAMES = ("in", "mix", "up", "bias")


def panels_of(bucket):
    return (12 if bucket < 2 else 16) // CHUNKS


MATRICES = {
    "in": (2048, 1536),
    "mix": (2560, 2048),
    "up": (2048, 2048),
    "bias": (TROWS, 2048),
}


def columns(panel):
    return pl.ds(panel * LANES, LANES)


def place_parts(parts, bucket_ref, sources, tails_from, outs, tails_out, scratch):
    staged, tails, load_sems, tail_sem, store_sems = scratch
    main = (16 // CHUNKS) * BROWS
    if tails_from is None:
        for k in range(8):
            pltpu.make_async_copy(
                sources[k].at[pl.ds(main, 16 * TROWS)], tails.at[bucket_ref[k]], tail_sem
            ).start()
        take_tails = pltpu.make_async_copy(tails, tails, tail_sem)
    else:
        take_tails = pltpu.make_async_copy(tails_from, tails, tail_sem)
        take_tails.start()
    for at in range(2):
        for k in range(8):
            pltpu.make_async_copy(
                sources[8 * at + k].at[pl.ds(0 if k % 4 == 3 else part_row(parts[at]), main)],
                staged.at[at, bucket_ref[k]],
                load_sems.at[at, bucket_ref[k]],
            ).start()
    take_tails.wait()
    stores = []

    def store(source, target):
        stores.append(pltpu.make_async_copy(source, target, store_sems.at[len(stores)]))
        stores[-1].start()

    if tails_from is None:
        store(tails, tails_out)
        for panel in range(16):
            store(
                tails.at[7, pl.ds(panel * TROWS, TROWS)],
                outs["bias"].at[pl.ds(0, TROWS), columns(panel)],
            )
    for at, part in enumerate(parts):
        for bucket in range(8):
            held = staged.at[at, bucket]
            pltpu.make_async_copy(held, held, load_sems.at[at, bucket]).wait()
            span = QROWS if bucket < 2 else BROWS
            wide = panels_of(bucket)
            for panel in range(wide):
                if bucket:
                    head = pl.ds(panel * span, TROWS)
                    tail = pl.ds((part * wide + panel) * TROWS, TROWS)
                    staged[at, bucket, head, :] = (
                        staged[at, bucket, head, :] + tails[bucket - 1, tail, :]
                    )
                for name, first, rows, offset in PLACES[bucket]:
                    store(
                        staged.at[at, bucket, pl.ds(panel * span + offset, rows)],
                        outs[name].at[pl.ds(first, rows), columns(part * wide + panel)],
                    )
    return stores


def part_scratch(copies):
    return [
        pltpu.VMEM((2, 8, (16 // CHUNKS) * BROWS, LANES), jnp.bfloat16),
        pltpu.VMEM((8, 16 * TROWS, LANES), jnp.bfloat16),
        pltpu.SemaphoreType.DMA((2, 8)),
        pltpu.SemaphoreType.DMA,
        pltpu.SemaphoreType.DMA((copies,)),
    ]


def copies_of_parts():
    return 2 * sum(len(PLACES[b]) * panels_of(b) for b in range(8))


def unpack_kernel(bucket_ref, *refs):
    outs = dict(zip(NAMES, refs[16:20], strict=True))
    for put in place_parts((0, 1), bucket_ref, refs[:16], None, outs, refs[20], refs[21:]):
        put.wait()


def unpack(buckets, sources):
    shapes = [jax.ShapeDtypeStruct(MATRICES[name], jnp.bfloat16) for name in NAMES]
    tails = jax.ShapeDtypeStruct((8, 16 * TROWS, LANES), jnp.bfloat16)
    return pl.pallas_call(
        unpack_kernel,
        out_shape=[*shapes, tails],
        in_specs=[pl.BlockSpec(memory_space=pltpu.SMEM)] + [pl.BlockSpec(memory_space=HBM)] * 16,
        out_specs=[pl.BlockSpec(memory_space=HBM)] * 5,
        scratch_shapes=part_scratch(copies_of_parts() + 17),
        compiler_params=params(60),
        cost_estimate=LIGHT,
        name="unpack_params",
    )(buckets, *sources)


def unpack_hidden_kernel(width, bucket_ref, *refs):
    sources, tails_from, normed_from, up_bias = refs[:16], refs[16], refs[17], refs[18]
    outs = dict(zip(NAMES[:3], refs[24:27], strict=True))
    hidden_to, slope_to = refs[27:29]
    scratch, (normed, hidden, slope, normed_sem, out_sems) = refs[29:34], refs[34:]
    staged = scratch[0]
    load = pltpu.make_async_copy(normed_from, normed, normed_sem)
    load.start()
    stores = place_parts((2, 3), bucket_ref, sources, tails_from, outs, None, scratch)
    load.wait()
    rows_of_up = [
        (bucket, rows, offset)
        for bucket in range(8)
        for name, _, rows, offset in PLACES[bucket]
        if name == "up"
    ]
    half = up_bias.shape[1] // 2
    puts = []
    for block in range(half // FF_BLOCK):
        slot = block % 2
        if block >= 2:
            for put in puts[2 * block - 4 : 2 * block - 2]:
                put.wait()
        panels = []
        for panel in range(2 * block, 2 * block + 2):
            at, inner = panel // (16 // CHUNKS), panel % (16 // CHUNKS)
            pieces = [
                staged[at, bucket, pl.ds(inner * BROWS + offset, rows), :]
                for bucket, rows, offset in rows_of_up
            ]
            panels.append(jnp.concatenate(pieces, axis=0))
        first = half + block * FF_BLOCK
        gelu(
            matmul(normed[...], jnp.concatenate(panels, axis=1))
            + up_bias[:, first : first + FF_BLOCK],
            hidden.at[slot],
            slope.at[slot],
        )
        for which, (source, target, column) in enumerate(
            ((hidden, hidden_to, width + first), (slope, slope_to, first))
        ):
            puts.append(
                pltpu.make_async_copy(
                    source.at[slot],
                    target.at[:, pl.ds(column, FF_BLOCK)],
                    out_sems.at[slot, which],
                )
            )
            puts[-1].start()
    for put in [*puts[-4:], *stores]:
        put.wait()


def unpack_hidden(width, buckets, sources, before, normed, up_bias, halves):
    rows = normed.shape[0]
    hidden, slope = halves
    results = pl.pallas_call(
        functools.partial(unpack_hidden_kernel, width),
        out_shape=[jax.ShapeDtypeStruct(v.shape, v.dtype) for v in (*before[:3], hidden, slope)],
        in_specs=[pl.BlockSpec(memory_space=pltpu.SMEM)]
        + [pl.BlockSpec(memory_space=HBM)] * 18
        + [pl.BlockSpec(memory_space=pltpu.VMEM)]
        + [pl.BlockSpec(memory_space=HBM)] * 5,
        out_specs=[pl.BlockSpec(memory_space=HBM)] * 5,
        input_output_aliases={20 + at: at for at in range(5)},
        scratch_shapes=part_scratch(copies_of_parts())
        + [
            pltpu.VMEM(normed.shape, normed.dtype),
            pltpu.VMEM((2, rows, FF_BLOCK), jnp.bfloat16),
            pltpu.VMEM((2, rows, FF_BLOCK), jnp.float32),
            pltpu.SemaphoreType.DMA,
            pltpu.SemaphoreType.DMA((2, 2)),
        ],
        compiler_params=params(60),
        cost_estimate=LIGHT,
        name="unpack_hidden",
    )(buckets, *sources, before[4], normed, up_bias, *before[:3], hidden, slope)
    return results[:3], results[3], results[4]


GRAD_ROWS = 256
PAIR = 2 * GRAD_ROWS
IN_STEPS, OUT_STEPS, UP_STEPS, DOWN_STEPS = 4, 1, 4, 4
GRAD_EDGES = (0, 4, 5, 9, 13)
GRAD_STEPS = 13
KEPT, NEAR, FAR = 0, 1, 2


def weight_grad_kernel(table, *refs):
    lefts, projected, late, outs = refs[:8], refs[8:10], refs[10:14], refs[14:22]
    wide32, wide16, tail32, tail16, held, sems, tail_sem, late_sem = refs[22:]
    step = pl.program_id(0)
    core = table[0]
    main = (16 // CHUNKS) * BROWS

    def bucket_of(block):
        return jnp.where(block < 2 * IN_STEPS, block // 4, (block - 2) // 3)

    def kind_of(part, bucket):
        return table[1 + 16 * part + bucket], table[9 + 16 * part + bucket]

    def targets(part, kind, place):
        near = kind == NEAR
        return [
            (jnp.logical_and(near, place == 0), True, outs[3 * part]),
            (jnp.logical_and(near, place == 1), True, outs[3 * part + 1]),
            (kind == FAR, True, outs[3 * part + 2].at[jnp.minimum(place, 1)]),
            (jnp.logical_and(kind == KEPT, place >= 2), False, outs[6].at[part, jnp.clip(place - 2, 0, 1)]),
            (jnp.logical_and(kind == KEPT, place < 2), False, outs[7].at[part, jnp.minimum(place, 1)]),
        ]

    def wait(at):
        slot = lax.rem(at, 2)
        for panels, mine in ((3, at < IN_STEPS), (4, at >= IN_STEPS)):

            @pl.when(mine)
            def _(panels=panels):
                rows = pl.ds(0, panels * GRAD_ROWS)
                for half in range(2):
                    bucket = bucket_of(2 * at + half)
                    for part in range(2):
                        kind, _ = kind_of(part, bucket)
                        sem = sems.at[slot, part, half]

                        @pl.when(kind == KEPT)
                        def _(part=part, sem=sem):
                            place = outs[7].at[part, 0, rows]
                            pltpu.make_async_copy(place, place, sem).wait()

                        @pl.when(kind != KEPT)
                        def _(part=part, sem=sem):
                            place = outs[3 * part].at[rows]
                            pltpu.make_async_copy(place, place, sem).wait()

    @pl.when(step >= 2)
    def _():
        wait(step - 2)

    late_copies = []
    for at, source in enumerate(late):
        width = held.shape[2]
        if source.shape[1] > width:
            source = source.at[:, pl.ds(pl.multiple_of(core * width, width), width)]
        late_copies.append(pltpu.make_async_copy(source, held.at[at], late_sem.at[at]))

    @pl.when(step == 0)
    def _():
        for copy in late_copies:
            copy.start()
        tail32[...] = jnp.zeros_like(tail32)
        tail16[...] = jnp.zeros_like(tail16)

    @pl.when(step == GRAD_EDGES[1])
    def _():
        for copy in late_copies[:2]:
            copy.wait()

    @pl.when(step == GRAD_EDGES[2])
    def _():
        for copy in late_copies[2:]:
            copy.wait()

    def multiply(pair, right, panels, span):
        slot = lax.rem(step, 2)
        if right == 0:
            own, other = projected[0][...], projected[1][...]
        else:
            own, other = held[2 * right - 2], held[2 * right - 1]
        wide32[slot, :, pl.ds(0, 2 * panels * LANES)] = product_rows(
            lefts[2 * pair][...], own
        ) + product_rows(lefts[2 * pair + 1][...], other)
        for half in range(2):
            block = 2 * step + half
            bucket = bucket_of(block)
            before = jnp.maximum(bucket - 1, 0)
            if pair == 0:
                first, offset = block == 4, lax.rem(block, 4)
            else:
                offset = lax.rem(block - 2, 3)
                first = offset == 0
            offset = pl.multiple_of(offset * GRAD_ROWS, GRAD_ROWS)
            for part in range(2):
                kind, place = kind_of(part, bucket)

                @pl.when(kind != KEPT)
                def _(half=half, part=part):
                    for panel in range(panels):
                        tile = wide32[
                            slot, pl.ds(half * GRAD_ROWS, GRAD_ROWS), columns(part * panels + panel)
                        ]
                        rows = pl.ds(panel * GRAD_ROWS, GRAD_ROWS)
                        wide16[slot, part, half, rows, :] = tile.astype(jnp.bfloat16)

                for is_it, short, target in targets(part, kind, place):

                    @pl.when(is_it)
                    def _(half=half, part=part, short=short, target=target, offset=offset):
                        for panel in range(panels):
                            if short:
                                rows = pl.ds(panel * GRAD_ROWS, GRAD_ROWS)
                                source = wide16.at[slot, part, half, rows]
                            else:
                                rows = pl.ds(half * GRAD_ROWS, GRAD_ROWS)
                                source = wide32.at[slot, rows, columns(part * panels + panel)]
                            pltpu.make_async_copy(
                                source,
                                target.at[pl.ds(panel * span + offset, GRAD_ROWS)],
                                sems.at[slot, part, half],
                            ).start()

            @pl.when(first)
            def _(half=half, before=before):
                for part in range(2):
                    for panel in range(panels):
                        tile = wide32[
                            slot, pl.ds(half * GRAD_ROWS, TROWS), columns(part * panels + panel)
                        ]
                        rows = pl.ds(panel * TROWS, TROWS)
                        tail32[part, before, rows, :] = tile
                        tail16[part, before, rows, :] = tile.astype(jnp.bfloat16)

    for pair, right in enumerate((0, 1, 2, 1)):

        @pl.when(jnp.logical_and(step >= GRAD_EDGES[pair], step < GRAD_EDGES[pair + 1]))
        def _(pair=pair, right=right):
            multiply(pair, right, *((3, QROWS) if pair == 0 else (4, BROWS)))

    @pl.when(step == GRAD_STEPS - 1)
    def _():
        def tails(act):
            for part in range(2):
                for bucket in range(8):
                    for is_it, short, place in targets(part, *kind_of(part, bucket)):

                        @pl.when(is_it)
                        def _(part=part, bucket=bucket, short=short, place=place):
                            stage = tail16 if short else tail32
                            act(
                                pltpu.make_async_copy(
                                    stage.at[part, bucket],
                                    place.at[pl.ds(main, stage.shape[2])],
                                    tail_sem.at[part, bucket],
                                )
                            )

        tails(lambda copy: copy.start())
        wait(step - 1)
        wait(step)
        tails(lambda copy: copy.wait())


def weight_grads(table, lefts, rights):
    tokens = lefts[0].shape[0]

    def columns_at(first, count, ahead):
        return pl.BlockSpec(
            (tokens, PAIR), lambda i, table: (0, ahead + jnp.clip(i - first, 0, count - 1))
        )

    left_specs = [
        columns_at(first, last - first, ahead)
        for first, last, ahead in zip(GRAD_EDGES, GRAD_EDGES[1:], (0, 0, 0, 1), strict=False)
        for _ in range(2)
    ]
    half = (tokens, rights[0].shape[1] // 2)
    right_specs = [pl.BlockSpec(half, lambda i, table: (0, table[0]))] * 2
    rows = chunk_rows()
    near = jax.ShapeDtypeStruct((rows, LANES), jnp.bfloat16)
    short = jax.ShapeDtypeStruct((2, rows, LANES), jnp.bfloat16)
    wide = jax.ShapeDtypeStruct((2, 2, rows, LANES), jnp.float32)
    return pl.pallas_call(
        weight_grad_kernel,
        out_shape=[near, near, short] * 2 + [wide] * 2,
        grid_spec=pltpu.PrefetchScalarGridSpec(
            num_scalar_prefetch=1,
            grid=(GRAD_STEPS,),
            in_specs=left_specs + right_specs + [pl.BlockSpec(memory_space=HBM)] * 4,
            out_specs=[pl.BlockSpec(memory_space=HBM)] * 8,
            scratch_shapes=[
                pltpu.VMEM((2, PAIR, 8 * LANES), jnp.float32),
                pltpu.VMEM((2, 2, 2, 4 * GRAD_ROWS, LANES), jnp.bfloat16),
                pltpu.VMEM((2, 8, 4 * TROWS, LANES), jnp.float32),
                pltpu.VMEM((2, 8, 4 * TROWS, LANES), jnp.bfloat16),
                pltpu.VMEM((4, tokens, 8 * LANES), jnp.bfloat16),
                pltpu.SemaphoreType.DMA((2, 2, 2)),
                pltpu.SemaphoreType.DMA((2, 8)),
                pltpu.SemaphoreType.DMA((4,)),
            ],
        ),
        compiler_params=params(60),
        cost_estimate=LIGHT,
        name="weight_grads",
    )(table, *lefts, *rights)


NORM_COLUMNS = 512


def norm_grad_kernel(
    core, grad_projected, mixer_in, own_before, own_up, rest_before, rest_up, rows, centre, scale,
    gains, partial, sums,
):
    one = product_back(grad_projected[...], mixer_in[...])
    two = product_back(own_before[...], own_up[...]) + product_back(rest_before[...], rest_up[...])
    unit = (rows[...].astype(jnp.float32) - centre[...]) * scale[...]
    partial[...] = (one * gains[0:1, :] + two * gains[1:2, :]).astype(jnp.bfloat16)
    for at, value in enumerate((one * unit, one, two * unit, two)):
        sums[at : at + 1, :] = jnp.sum(value, axis=0, keepdims=True)


def norm_grad(core, grad_projected, mixer_in, own_before, rest_before, up, rows, centre, scale, gains):
    tokens = rows.shape[0]
    half = up.shape[1] // 2

    def whole(value):
        return pl.BlockSpec(value.shape, lambda i, core: (0, 0))

    block = pl.BlockSpec((tokens, NORM_COLUMNS), lambda i, core: (0, i))
    return pl.pallas_call(
        norm_grad_kernel,
        out_shape=[
            jax.ShapeDtypeStruct((tokens, D), jnp.bfloat16),
            jax.ShapeDtypeStruct((4, D), jnp.float32),
        ],
        grid_spec=pltpu.PrefetchScalarGridSpec(
            num_scalar_prefetch=1,
            grid=(D // NORM_COLUMNS,),
            in_specs=[
                whole(grad_projected),
                pl.BlockSpec((NORM_COLUMNS, mixer_in.shape[1]), lambda i, core: (i, 0)),
                whole(own_before),
                pl.BlockSpec((NORM_COLUMNS, half), lambda i, core: (i, core[0])),
                whole(rest_before),
                pl.BlockSpec((NORM_COLUMNS, half), lambda i, core: (i, 1 - core[0])),
                block,
                whole(centre),
                whole(scale),
                pl.BlockSpec((2, NORM_COLUMNS), lambda i, core: (0, i)),
            ],
            out_specs=[block, pl.BlockSpec((4, NORM_COLUMNS), lambda i, core: (0, i))],
        ),
        compiler_params=params(60),
        cost_estimate=LIGHT,
        name="norm_grad",
    )(core, grad_projected, mixer_in, own_before, up, rest_before, up, rows, centre, scale, gains)


ADAM_ROWS = 3080


def adam_kernel(table, scalar_ref, rate_ref, *refs):
    stays, near, far, small = refs[:2], refs[2:6], refs[6:10], refs[10]
    weights, first, second, moving = refs[11:15]
    new_weights, new_first, new_second, new_moving, reduced = refs[15:20]
    held32, held16, flat, sems = refs[20:]
    bucket, core = table[0], table[1]
    wide, narrow = 16 // CHUNKS, 12 // CHUNKS
    main = wide * BROWS
    turn_at = pl.program_id(0)

    def put(part, row, start, stride):
        rows = pl.ds(row, 16)
        value = held32[part, rows, :] + (
            held16[0, part, rows, :].astype(jnp.float32) + held16[1, part, rows, :].astype(jnp.float32)
        )
        flat[pl.ds(start, 16, stride=stride), :] = value

    @pl.when(turn_at == 0)
    def _():
        loads = []
        for at in range(4):
            place = 2 * (core if at < 2 else 1 - core) + at % 2
            source = stays[at // 2].at[at % 2, at // 2]
            loads.append(pltpu.make_async_copy(source, held32.at[place], sems.at[0, at]))
            for which, came in enumerate((near, far)):
                loads.append(
                    pltpu.make_async_copy(came[at], held16.at[which, place], sems.at[1 + which, at])
                )
        for load in loads:
            load.start()
        for load in loads:
            load.wait()

        @pl.when(bucket >= 1)
        def _():
            for panel in range(16):
                put(
                    panel // wide,
                    main + (panel % wide) * TROWS,
                    (BROWS - bucket) * 16 + panel + FRONT,
                    16,
                )

        @pl.when(bucket == 0)
        def _():
            for panel in range(12):
                put(
                    panel // narrow,
                    main + (panel % narrow) * TROWS,
                    QROWS * 12 + panel + FRONT,
                    12,
                )

        @pl.when(bucket == 7)
        def _():
            flat[pl.ds(FRONT + FLAT - LANES, LANES), :] = small[...]

    @pl.when(bucket >= 2)
    def _():
        def reach(at):
            tiles = (at * (ADAM_ROWS // 8) // 2 + 23) // 16
            return jnp.clip(jnp.where(at > 0, tiles, 0), 0, BROWS // 16)

        def step(tile, carry):
            row = pl.multiple_of(tile * 16, 16)
            for panel in range(16):
                put(
                    panel // wide,
                    (panel % wide) * BROWS + row,
                    (row - bucket) * 16 + panel + FRONT,
                    16,
                )
            return carry

        lax.fori_loop(reach(turn_at), reach(turn_at + 1), step, 0)

    @pl.when(bucket < 2)
    def _():
        def reach(at):
            tiles = (at * ADAM_ROWS + 16) // 192 + 1
            return jnp.clip(jnp.where(at > 0, tiles, 0), 0, QROWS // 16)

        def step(tile, carry):
            row = pl.multiple_of(tile * 16, 16)
            for panel in range(12):
                put(
                    panel // narrow,
                    (panel % narrow) * QROWS + row,
                    row * 12 + panel - 16 * bucket + FRONT,
                    12,
                )
            return carry

        lax.fori_loop(reach(turn_at), reach(turn_at + 1), step, 0)

    start = turn_at * ADAM_ROWS
    gradient = flat[pl.ds(pl.multiple_of(FRONT + start, 8), ADAM_ROWS), :]
    reduced[...] = gradient
    scale_one, scale_two, decay, keep = (scalar_ref[at] for at in range(4))
    one = beta_one * first[...] + (1.0 - beta_one) * gradient
    two = beta_two * second[...] + (1.0 - beta_two) * gradient * gradient
    new_first[...] = one
    new_second[...] = two
    old = weights[...]
    change = (one * scale_one) / (jnp.sqrt(two * scale_two) + adam_epsilon) + decay * old

    def write(rate):
        fresh = old - rate * change
        new_weights[...] = fresh
        new_moving[...] = keep * moving[...] + (1.0 - keep) * fresh

    first_row = bucket * FLAT + start
    bounds = [bound // LANES for bound in bound_list(512, 2048)[1:]]
    kinds = [sum(jnp.where(at >= bound, 1, 0) for bound in bounds) for at in (first_row, first_row + ADAM_ROWS - 1)]

    @pl.when(kinds[0] == kinds[1])
    def _():
        write(rate_ref[kinds[0]])

    @pl.when(kinds[0] != kinds[1])
    def _():
        row = first_row + lax.broadcasted_iota(jnp.int32, (ADAM_ROWS, LANES), 0)
        rate = jnp.full((ADAM_ROWS, LANES), rate_ref[0], jnp.float32)
        for kind, bound in enumerate(bounds):
            rate = jnp.where(row >= bound, rate_ref[kind + 1], rate)
        write(rate)


def adam(table, scalars, rates, stays, near, far, small, state):
    steps = -(-FLAT // ADAM_ROWS)
    block = pl.BlockSpec((ADAM_ROWS, LANES), lambda i: (i, 0))
    return pl.pallas_call(
        adam_kernel,
        grid=(steps,),
        out_shape=[jax.ShapeDtypeStruct((FLAT, LANES), jnp.float32)] * 5,
        in_specs=[pl.BlockSpec(memory_space=pltpu.SMEM)] * 3
        + [pl.BlockSpec(memory_space=HBM)] * 2
        + [pl.BlockSpec(memory_space=pl.ANY)] * 8
        + [pl.BlockSpec(memory_space=pltpu.VMEM)]
        + [block] * 4,
        out_specs=[block] * 5,
        scratch_shapes=[
            pltpu.VMEM((4, chunk_rows(), LANES), jnp.float32),
            pltpu.VMEM((2, 4, chunk_rows(), LANES), jnp.bfloat16),
            pltpu.VMEM((FRONT + max(steps * ADAM_ROWS, FLAT + BACK), LANES), jnp.float32),
            pltpu.SemaphoreType.DMA((3, 4)),
        ],
        compiler_params=params(60),
        cost_estimate=LIGHT,
        name="adam",
    )(table, scalars, rates, *stays, *near, *far, small, *state)


def finish_kernel(terms, rows, grads, out):
    scaled = terms[0].astype(jnp.float32)
    for at in range(1, terms.shape[0]):
        scaled = scaled + terms[at].astype(jnp.float32)
    unit, scale = norm_stats(rows[...].astype(jnp.float32))
    out[...] = grads[...].astype(jnp.float32) + scale * (
        scaled
        - jnp.mean(scaled, axis=-1, keepdims=True)
        - unit * jnp.mean(scaled * unit, axis=-1, keepdims=True)
    )


def finish(terms, rows, grads):
    count, width = rows.shape
    height = count // 4
    block = pl.BlockSpec((height, width), lambda i: (i, 0))
    return pl.pallas_call(
        finish_kernel,
        grid=(count // height,),
        out_shape=jax.ShapeDtypeStruct((count, width), jnp.float32),
        in_specs=[
            pl.BlockSpec((terms.shape[0], height, width), lambda i: (0, i, 0)),
            block,
            block,
        ],
        out_specs=block,
        compiler_params=params(60),
        cost_estimate=LIGHT,
        name="finish",
    )(terms, rows, grads)


FF_BLOCK = 256


def gelu(before, hidden, slope):
    half = 0.5 + 0.5 * lax.erf(before * math.sqrt(0.5))
    hidden[...] = (before * half).astype(jnp.bfloat16)
    slope[...] = half + before * jnp.exp(-0.5 * before * before) * (1.0 / math.sqrt(2.0 * math.pi))


def hidden_kernel(normed, up, up_bias, hidden, slope):
    gelu(matmul(normed[...], up[...]) + up_bias[...], hidden, slope)


def hidden_layer(width, normed, up, up_bias):
    rows, units = normed.shape[0], up.shape[1]
    block = pl.BlockSpec((rows, FF_BLOCK), lambda i: (0, i))
    return pl.pallas_call(
        hidden_kernel,
        grid=(units // FF_BLOCK // 2,),
        out_shape=[
            jax.ShapeDtypeStruct((rows, width + units), jnp.bfloat16),
            jax.ShapeDtypeStruct((rows, units), jnp.float32),
        ],
        in_specs=[
            pl.BlockSpec(memory_space=pltpu.VMEM),
            pl.BlockSpec((D, FF_BLOCK), lambda i: (0, i)),
            pl.BlockSpec((1, FF_BLOCK), lambda i: (0, i)),
        ],
        out_specs=[pl.BlockSpec((rows, FF_BLOCK), lambda i: (0, i + width // FF_BLOCK)), block],
        compiler_params=params(60),
        cost_estimate=LIGHT,
        name="hidden_layer",
    )(normed, up, up_bias)


def hidden_back_kernel(half, grads, down, slope, grad_before, grad_bias):
    rounded = (slope[...] * product_back(grads[...], down[...])).astype(jnp.bfloat16)
    grad_before[...] = rounded
    grad_bias[...] = jnp.sum(rounded.astype(jnp.float32), axis=0, keepdims=True)


def hidden_back(half, grads, mix, slope):
    rows, units = slope.shape
    first = (mix.shape[0] - units) // FF_BLOCK
    steps = units // FF_BLOCK // 2
    return pl.pallas_call(
        hidden_back_kernel,
        out_shape=[
            jax.ShapeDtypeStruct((rows, units // 2), jnp.bfloat16),
            jax.ShapeDtypeStruct((1, units // 2), jnp.float32),
        ],
        grid_spec=pltpu.PrefetchScalarGridSpec(
            num_scalar_prefetch=1,
            grid=(steps,),
            in_specs=[
                pl.BlockSpec((rows, D), lambda i, half: (0, 0)),
                pl.BlockSpec((FF_BLOCK, D), lambda i, half: (first + half[0] * steps + i, 0)),
                pl.BlockSpec((rows, FF_BLOCK), lambda i, half: (0, half[0] * steps + i)),
            ],
            out_specs=[
                pl.BlockSpec((rows, FF_BLOCK), lambda i, half: (0, i)),
                pl.BlockSpec((1, FF_BLOCK), lambda i, half: (0, i)),
            ],
        ),
        compiler_params=params(60),
        cost_estimate=LIGHT,
        name="hidden_back",
    )(half, grads, mix, slope)


def norm_kernel(rows, gains, one, two, centre, scale):
    values = rows[...].astype(jnp.float32)
    middle = jnp.mean(values, axis=-1, keepdims=True)
    values = values - middle
    factor = lax.rsqrt(jnp.mean(values * values, axis=-1, keepdims=True) + norm_epsilon)
    unit = values * factor
    one[...] = (unit * gains[0:1, :] + gains[1:2, :]).astype(jnp.bfloat16)
    two[...] = (unit * gains[2:3, :] + gains[3:4, :]).astype(jnp.bfloat16)
    centre[...] = middle
    scale[...] = factor


def norms(rows, small_params):
    count, width = rows.shape
    height = 128
    block = pl.BlockSpec((height, width), lambda i: (i, 0))
    column = pl.BlockSpec((height, 1), lambda i: (i, 0))
    return pl.pallas_call(
        norm_kernel,
        grid=(count // height,),
        out_shape=[jax.ShapeDtypeStruct((count, width), jnp.bfloat16)] * 2
        + [jax.ShapeDtypeStruct((count, 1), jnp.float32)] * 2,
        in_specs=[block, pl.BlockSpec(memory_space=pltpu.VMEM)],
        out_specs=[block, block, column, column],
        compiler_params=params(60),
        cost_estimate=LIGHT,
        name="norms",
    )(rows, small_params)


QUERY_BLOCK = 256


def turn(values, tables, sign):
    plain, lower, upper = tables
    half_rot = ROT // 2
    return (
        values * plain
        + pltpu.roll(values, HD - half_rot, 1) * (sign * lower)
        + pltpu.roll(values, half_rot, 1) * (sign * upper)
    )


def block_scores(query, keys, begins, first, first_key):
    scores = product_back(query, keys) * (1.0 / math.sqrt(HD))
    row_index = first + lax.broadcasted_iota(jnp.int32, scores.shape, 0)
    key_index = first_key + lax.broadcasted_iota(jnp.int32, scores.shape, 1)
    allowed = (key_index <= row_index) & (key_index >= begins)
    return jnp.where(allowed, scores, masked_score)


HEAD_PAIR = 2 * HD


def attend_kernel(
    normed, queries_in, keys_in, values_in, bias, plain, lower, upper, begins, _, context, turned, logs
):
    rows = normed.shape[0]
    width = bias.shape[1] // 3
    first_column = pl.program_id(0) * HEAD_PAIR
    tables = (plain[...], lower[...], upper[...])
    for part, weights in enumerate((queries_in, keys_in, values_in)):
        projected = matmul(normed[...], weights[...])
        projected = projected + bias[
            :, pl.ds(pl.multiple_of(part * width + first_column, HEAD_PAIR), HEAD_PAIR)
        ]
        for head in range(2):
            value = projected[:, head * HD : (head + 1) * HD]
            if part < 2:
                value = turn(value, tables, 1.0)
            turned[part, :, head * HD : (head + 1) * HD] = value.astype(jnp.bfloat16)

    def one_head(head, carry):
        column = pl.ds(pl.multiple_of(head * HD, HD), HD)
        queries, keys, values = (turned[part, :, column] for part in range(3))
        for first in range(0, rows, QUERY_BLOCK):
            last = first + QUERY_BLOCK
            mine = slice(first, last)
            seen = slice(max(0, first - rows // 2), last)
            scores = block_scores(queries[mine], keys[seen], begins[mine, :], first, seen.start)
            top = jnp.max(scores, axis=-1, keepdims=True)
            raised = jnp.exp(scores - top)
            total = jnp.sum(raised, axis=-1, keepdims=True)
            rounded = (raised / total).astype(jnp.bfloat16)
            context[mine, column] = matmul(rounded, values[seen]).astype(jnp.bfloat16)
            logs[head, mine, :] = top + jnp.log(total)
        return carry

    lax.fori_loop(0, 2, one_head, 0)


def attend(normed, mixer_in, bias, tables, begins, mixed):
    rows, width = normed.shape[0], mixer_in.shape[1] // 3
    pairs = width // HEAD_PAIR
    whole = pl.BlockSpec(memory_space=pltpu.VMEM)

    def weights(part):
        return pl.BlockSpec((mixer_in.shape[0], HEAD_PAIR), lambda i: (0, part * pairs + i))

    return pl.pallas_call(
        attend_kernel,
        grid=(pairs,),
        out_shape=[
            jax.ShapeDtypeStruct(mixed.shape, mixed.dtype),
            jax.ShapeDtypeStruct((3, rows, width), jnp.bfloat16),
            jax.ShapeDtypeStruct((width // HD, rows, 1), jnp.float32),
        ],
        in_specs=[whole, weights(0), weights(1), weights(2)]
        + [whole] * 5
        + [pl.BlockSpec(memory_space=HBM)],
        out_specs=[
            pl.BlockSpec((rows, HEAD_PAIR), lambda i: (0, i)),
            pl.BlockSpec((3, rows, HEAD_PAIR), lambda i: (0, 0, i)),
            pl.BlockSpec((2, rows, 1), lambda i: (i, 0, 0)),
        ],
        input_output_aliases={9: 0},
        compiler_params=params(60),
        cost_estimate=LIGHT,
        name="attend",
    )(normed, mixer_in, mixer_in, mixer_in, bias, *tables, begins, mixed)


def attend_back_kernel(
    turned, logs, plain, lower, upper, begins, grad_context, grad_projected, key_sum, value_sum
):
    rows, width = grad_context.shape
    score_scale = 1.0 / math.sqrt(HD)

    def one_head(head, carry):
        cols = [pl.ds(pl.multiple_of(part * width + head * HD, HD), HD) for part in range(3)]
        queries, keys, values = (turned[part, :, cols[0]] for part in range(3))
        key_sum[...] = jnp.zeros_like(key_sum)
        value_sum[...] = jnp.zeros_like(value_sum)
        for first in range(0, rows, QUERY_BLOCK):
            last = first + QUERY_BLOCK
            mine = slice(first, last)
            query = queries[mine]
            seen = slice(max(0, first - rows // 2), last)
            scores = block_scores(query, keys[seen], begins[mine, :], first, seen.start)
            soft = jnp.exp(scores - logs[head, mine, :])
            grad_mine = grad_context[mine, cols[0]]
            grad_soft = product_back(grad_mine, values[seen])
            delta = jnp.sum(soft * grad_soft, axis=-1, keepdims=True)
            grad_scores = (soft * (grad_soft - delta)).astype(jnp.bfloat16)
            grad_query = matmul(grad_scores, keys[seen]) * score_scale
            tables = (plain[mine, :], lower[mine, :], upper[mine, :])
            grad_projected[mine, cols[0]] = turn(grad_query, tables, -1.0).astype(jnp.bfloat16)
            key_sum[seen, :] += product_rows(grad_scores, query)
            value_sum[seen, :] += product_rows(soft.astype(jnp.bfloat16), grad_mine)
        tables = (plain[...], lower[...], upper[...])
        grad_projected[:, cols[1]] = turn(key_sum[...] * score_scale, tables, -1.0).astype(
            jnp.bfloat16
        )
        grad_projected[:, cols[2]] = value_sum[...].astype(jnp.bfloat16)
        return carry

    lax.fori_loop(0, width // HD, one_head, 0)


def attend_back(turned, logs, tables, begins, grad_context):
    rows, width = grad_context.shape
    whole = pl.BlockSpec(memory_space=pltpu.VMEM)
    return pl.pallas_call(
        attend_back_kernel,
        out_shape=jax.ShapeDtypeStruct((rows, 3 * width), jnp.bfloat16),
        in_specs=[whole] * 7,
        out_specs=whole,
        scratch_shapes=[pltpu.VMEM((rows, HD), jnp.float32)] * 2,
        compiler_params=params(36),
        cost_estimate=LIGHT,
        name="attend_back",
    )(turned, logs, *tables, begins, grad_context)


def rope_tables(places):
    half_rot = ROT // 2
    frequency = rope_base ** (-2.0 * jnp.arange(half_rot, dtype=jnp.float32) / ROT)
    angles = places[:, None] * frequency[None, :]
    cosine, sines = jnp.cos(angles), jnp.sin(angles)
    rest = jnp.zeros((places.shape[0], HD - ROT), jnp.float32)
    none = jnp.zeros_like(sines)
    return (
        jnp.concatenate([cosine, cosine, rest + 1.0], axis=1),
        jnp.concatenate([-sines, none, rest], axis=1),
        jnp.concatenate([none, sines, rest], axis=1),
    )


def along_x(value):
    return lax.ppermute(value, "dp", [(i, i ^ 1) for i in range(4)])


def along_y(value):
    return lax.ppermute(value, "dp", [(i, i ^ 2) for i in range(4)])


def along_line(value, bit):
    return lax.ppermute(value, "tensor", [(i, i ^ bit) for i in range(4)])


def along(bit, value):
    return lax.ppermute(
        value, ("dp", "chip"), [(i, (i // 2 ^ bit) * 2 + (i % 2 ^ 1)) for i in range(8)]
    )


def across(value):
    return lax.ppermute(value, "chip", [(0, 1), (1, 0)])


def line_blocks(partial):
    count = lax.axis_size("tensor")
    rows = partial.shape[0] // count
    return lax.all_to_all(partial.reshape(count, rows, partial.shape[1]), "tensor", 0, 0)


def on_device_fast(
    residual,
    cotangent,
    lengths,
    owners,
    step_count,
    rates,
    weight_decay,
    ema_decay,
    master,
    moment_one,
    moment_two,
    average,
):
    local_width = HD * H // lax.axis_size("tensor")
    group_rows = residual.shape[1] * lax.axis_size("tensor")
    slots = jnp.arange(8, dtype=jnp.int32)
    inverse = jnp.sum(
        slots[None, :] * (owners[None, :] == slots[:, None]).astype(jnp.int32), axis=1
    )
    data_index, core, here = lax.axis_index("dp"), lax.axis_index("chip"), lax.axis_index("tensor")
    partners = jnp.stack([(data_index ^ j) * 2 + (core ^ c) for c in range(2) for j in range(4)])
    buckets = jnp.sum(
        jnp.where(partners[:, None] == slots[None, :], inverse[None, :], 0), axis=1
    ).astype(jnp.int32)
    partner_of = jnp.sum(
        jnp.where(buckets[None, :] == slots[:, None], slots[None, :], 0), axis=1
    )
    hop, other = partner_of % 4, partner_of // 4
    grad_table = [core[None]]
    for first, second in ((hop % 2, hop // 2), (hop // 2, hop % 2)):
        grad_table.append(first * (1 + second))
        grad_table.append(other + 2 * second * (1 - first))
    grad_table = jnp.concatenate(grad_table).astype(jnp.int32)

    full_rows = lax.all_gather(residual[0], "tensor", axis=0, tiled=True)
    grad_rows = lax.all_gather(cotangent[0], "tensor", axis=0, tiled=True)
    own_rows = residual[0].astype(jnp.float32)

    def order(*values):
        return lax.optimization_barrier(values)

    rank = jnp.arange(lengths.shape[1], dtype=jnp.int32)
    seq_ends = jnp.sum(jnp.where(rank[None, :] <= rank[:, None], lengths[0][None, :], 0), axis=1)
    token_index = jnp.arange(group_rows, dtype=jnp.int32)
    passed = (token_index[:, None] >= seq_ends[None, :]).astype(jnp.int32)
    begins = jnp.sum(passed * lengths[0][None, :], axis=1)
    tables = rope_tables((token_index - begins).astype(jnp.float32))
    begins = begins[:, None]

    one, two = pack(buckets[:1], master.reshape(FLAT, LANES))
    one_x, one_y, one_own = order(along_x(one), along_y(one), across(one))

    def from_far(first, second, from_x, from_y):
        rows = (16 // CHUNKS) * BROWS
        start = part_row(second)
        count = start if first == 0 else rows
        if first == 0:
            from_y, from_x = from_y[:count], from_x[start : start + rows]
        else:
            from_y, from_x = cut([from_y, from_x], (0, start), (count, rows))
        return [along_x(from_y), along_y(from_x)]

    far = from_far(0, 1, one_x, one_y)
    near_x, near_y, two_own = across(one_x), across(one_y), across(two)
    far, near_x, near_y, two_own, two, tables, begins = order(
        far, near_x, near_y, two_own, two, tables, begins
    )

    two_x, two_y = along_x(two), along_y(two)
    far_other = [across(value) for value in far]
    sources = []
    for part in range(2):
        sources += [one, one_x, one_y, far[part], one_own, near_x, near_y, far_other[part]]
    weights = unpack(buckets, sources)
    weights, full_rows = order(weights, full_rows)
    flat_bias = weights[3][:8].reshape(-1).astype(jnp.float32)
    mixer_bias = flat_bias[: 3 * local_width]
    expand_bias = flat_bias[3 * local_width : 3 * local_width + D]
    small_params = flat_bias[3 * local_width + D : 3 * local_width + 7 * D].reshape(6, D)
    full_one, full_two, centre, scale = norms(full_rows, small_params)
    hidden_half = hidden_layer(local_width, full_two, weights[2], expand_bias[None])
    two_x, two_y, full_rows, full_one, full_two, weights, hidden_half = order(
        two_x, two_y, full_rows, full_one, full_two, weights, hidden_half
    )
    other_rows = across(full_rows)

    far = from_far(2, 3, two_x, two_y)
    near_x, near_y = across(two_x), across(two_y)
    other_one, other_two, _, _ = norms(other_rows, small_params)
    far, near_x, near_y, hidden_half, weights, other_one, other_two = order(
        far, near_x, near_y, hidden_half, weights, other_one, other_two
    )

    far_other = [across(value) for value in far]
    sources = []
    for part in range(2):
        sources += [two, two_x, two_y, far[part], two_own, near_x, near_y, far_other[part]]
    (mixer_in, mix_weight, expand_weight), mixed, slope = unpack_hidden(
        local_width, buckets, sources, weights, full_two, expand_bias[None], hidden_half
    )

    mixed, turned, logs = attend(full_one, mixer_in, mixer_bias[None], tables, begins, mixed)
    other_mixed = across(mixed)
    branches = matmul(mixed, mix_weight)
    branches, turned, grad_rows = order(branches, turned, grad_rows)
    branches = lax.psum_scatter(branches, "tensor", scatter_dimension=0, tiled=True)
    other_grads = across(grad_rows)

    grad_context = product_back(grad_rows, mix_weight[:local_width]).astype(jnp.bfloat16)
    grad_projected = attend_back(turned, logs, tables, begins, grad_context)
    grad_projected, slope = order(grad_projected, slope)
    other_projected = across(grad_projected)
    cores = core[None].astype(jnp.int32)
    rest_before, rest_bias = hidden_back(1 - cores, grad_rows, mix_weight, slope)
    other_before = across(rest_before)
    own_before, own_bias = hidden_back(cores, grad_rows, mix_weight, slope)
    grad_expand_bias = jnp.where(
        core == 0,
        jnp.concatenate([own_bias[0], rest_bias[0]]),
        jnp.concatenate([rest_bias[0], own_bias[0]]),
    )

    lefts = [full_one, other_one, mixed, other_mixed, full_two, other_two, mixed, other_mixed]
    rights = [grad_projected, other_projected, grad_rows, other_grads, own_before, other_before]
    sums = weight_grads(grad_table, lefts, rights)
    grad_projected, own_before, rest_before, sums = order(
        grad_projected, own_before, rest_before, sums
    )
    near_a, cross_a, far_a, near_b, cross_b, far_b, passed, stays = sums
    came_a, came_b, other_stays = along_x(far_a), along_y(far_b), across(stays)

    partial, norm_grads = norm_grad(
        cores,
        grad_projected,
        mixer_in,
        own_before,
        rest_before,
        expand_weight,
        full_rows,
        centre,
        scale,
        jnp.stack([small_params[0], small_params[2]]),
    )
    bias_grad = jnp.sum(grad_rows.astype(jnp.float32), axis=0)
    small = (
        jnp.sum(grad_projected.astype(jnp.float32), axis=0),
        grad_expand_bias,
        bias_grad,
    )

    norm_grads, other_stays = order(norm_grads, other_stays)
    one, two, three = (along_line(norm_grads, bit) for bit in (1, 2, 3))
    norm_grads = (norm_grads + one) + (two + three)
    near = [near_a, near_b, cross_a, cross_b]
    came_a, came_b, other_stays, partial, norm_grads, small, near = order(
        came_a, came_b, other_stays, partial, norm_grads, small, near
    )
    near = [along_x(near[0]), along_y(near[1]), along(1, near[2]), along(2, near[3])]
    terms = line_blocks(partial)
    pass_a = [(passed[0, at] + came_a[at].astype(jnp.float32)).astype(jnp.bfloat16) for at in range(2)]
    pass_b = [(passed[1, at] + came_b[at].astype(jnp.float32)).astype(jnp.bfloat16) for at in range(2)]
    small = jnp.concatenate(
        [
            small[0],
            small[1],
            norm_grads.reshape(-1),
            small[2],
            small[2],
            jnp.zeros((8 * D - 3 * local_width - 7 * D,), jnp.float32),
        ]
    ).reshape(LANES, LANES)
    small = small + across(small)
    small = small + along_x(small)
    output = residual[0].astype(jnp.float32) + branches + small_params[4] + small_params[5]
    near, pass_a, pass_b, small, output = order(near, pass_a, pass_b, small, output)
    far = [along_y(pass_a[0]), along_x(pass_b[0]), along(2, pass_a[1]), along(1, pass_b[1])]
    small = small + along_y(small)
    far, small = order(far, small)

    step_value = step_count[0].astype(jnp.float32)
    scalars = jnp.stack(
        [
            1.0 / (1.0 - jnp.power(beta_one, step_value)),
            1.0 / (1.0 - jnp.power(beta_two, step_value)),
            weight_decay[0],
            ema_decay[0],
        ]
    )
    state = [v.reshape(FLAT, LANES) for v in (master, moment_one, moment_two, average)]
    table = jnp.stack([buckets[0], core.astype(jnp.int32)])
    results = adam(table, scalars, rates, [stays, other_stays], near, far, small, state)
    terms, results = order(terms, results)
    input_grad = finish(terms, residual[0], cotangent[0])
    return (output[None], input_grad[None], *[v.reshape(master.shape) for v in results])


def solution(mesh):
    placed = (
        P(("dp", "chip"), "tensor", None),
        P(("dp", "chip"), "tensor", None),
        P(("dp", "chip"), None),
        P(),
        P(),
        P(),
        P(),
        P(),
        P("tensor", ("dp", "chip"), None),
        P("tensor", ("dp", "chip"), None),
        P("tensor", ("dp", "chip"), None),
        P("tensor", ("dp", "chip"), None),
    )
    return jax.shard_map(
        device_program(mesh),
        mesh=mesh,
        in_specs=placed,
        out_specs=(
            P(("dp", "chip"), "tensor", None),
            P(("dp", "chip"), "tensor", None),
            P("tensor", ("dp", "chip"), None),
            P("tensor", ("dp", "chip"), None),
            P("tensor", ("dp", "chip"), None),
            P("tensor", ("dp", "chip"), None),
            P("tensor", ("dp", "chip"), None),
        ),
        check_vma=False,
    )
```

```python
import functools
import math

import jax
import jax.numpy as jnp
from jax import lax
from jax.experimental import pallas as pl
from jax.experimental.pallas import tpu as pltpu
from jax.sharding import PartitionSpec as P

D = 2048
H = 16
HD = 128
FF = 8192
ROT = 32


norm_epsilon = 1e-05
adam_epsilon = 1e-08
beta_one = 0.5
beta_two = 0.5
rope_base = 10000.0
masked_score = -1e30


def matmul(left, right):
    return jnp.dot(left, right, preferred_element_type=jnp.float32)


def product_rows(left, right):
    return lax.dot_general(
        left, right, (((0,), (0,)), ((), ())), preferred_element_type=jnp.float32
    )


def product_back(left, right):
    return lax.dot_general(
        left, right, (((1,), (1,)), ((), ())), preferred_element_type=jnp.float32
    )


def bound_list(local_width, local_ff):
    widths = [
        D * 3 * local_width,
        local_width * D,
        D * local_ff,
        local_ff * D,
        3 * local_width,
        local_ff,
        6 * D,
    ]
    bounds = [0]
    for part_width in widths:
        bounds.append(bounds[-1] + part_width)
    return bounds


def group_layout(seq_lengths, group_rows):
    order = jnp.arange(seq_lengths.shape[0], dtype=jnp.int32)
    seq_ends = jnp.sum(
        jnp.where(order[None, :] <= order[:, None], seq_lengths[None, :], 0), axis=1
    )
    starts = seq_ends - seq_lengths
    token_index = jnp.arange(group_rows, dtype=jnp.int32)
    segment = jnp.sum((token_index[:, None] >= seq_ends[None, :]).astype(jnp.int32), axis=1)
    chosen = (
        segment[:, None] == jnp.arange(seq_lengths.shape[0], dtype=jnp.int32)[None, :]
    ).astype(jnp.int32)
    places = token_index - jnp.sum(chosen * starts[None, :], axis=1)
    return (segment, places.astype(jnp.float32))


def rotary_tables(places):
    half_rot = ROT // 2
    frequency = rope_base ** (-2.0 * jnp.arange(half_rot, dtype=jnp.float32) / ROT)
    angles = places[:, None] * frequency[None, :]
    return (jnp.cos(angles)[:, None, :], jnp.sin(angles)[:, None, :])


def rotate(values, cosine, sines):
    half_rot = ROT // 2
    first = values[..., :half_rot]
    second = values[..., half_rot:ROT]
    return jnp.concatenate(
        [first * cosine - second * sines, second * cosine + first * sines, values[..., ROT:]],
        axis=-1,
    )


def norm_stats(inputs):
    center = inputs - jnp.mean(inputs, axis=-1, keepdims=True)
    scale = lax.rsqrt(jnp.mean(center * center, axis=-1, keepdims=True) + norm_epsilon)
    return (center * scale, scale)


def norm_back(grad_norm, gain, unit_rows, scale):
    scaled = grad_norm * gain
    return scale * (
        scaled
        - jnp.mean(scaled, axis=-1, keepdims=True)
        - unit_rows * jnp.mean(scaled * unit_rows, axis=-1, keepdims=True)
    )


def adam_update(
    weights, first, second, moving, gradient, step_rate, step_value, decay_rate, ema_keep
):
    bias_one = 1.0 - jnp.power(beta_one, step_value)
    bias_two = 1.0 - jnp.power(beta_two, step_value)
    new_first = beta_one * first + (1.0 - beta_one) * gradient
    new_second = beta_two * second + (1.0 - beta_two) * gradient * gradient
    ratio = new_first / bias_one / (jnp.sqrt(new_second / bias_two) + adam_epsilon)
    new_weights = weights - step_rate * (ratio + decay_rate * weights)
    new_moving = ema_keep * moving + (1.0 - ema_keep) * new_weights
    return (new_weights, new_first, new_second, new_moving)


def on_device(
    residual,
    cotangent,
    lengths,
    owners,
    step_count,
    rates,
    weight_decay,
    ema_decay,
    master,
    moment_one,
    moment_two,
    average,
):
    tensor_count = lax.axis_size("tensor")
    group_count = lax.axis_size(("dp", "chip"))
    local_heads = H // tensor_count
    local_width = local_heads * HD
    local_ff = FF // tensor_count
    rows_here = residual.shape[1]
    group_rows = rows_here * tensor_count
    bucket_size = master.shape[2]
    bounds = bound_list(local_width, local_ff)
    slots = jnp.arange(group_count, dtype=jnp.int32)
    inverse = jnp.sum(
        slots[None, :] * (owners[None, :] == slots[:, None]).astype(jnp.int32), axis=1
    )
    gathered = lax.all_gather(master.astype(jnp.bfloat16), ("dp", "chip"), axis=1, tiled=True)
    flat_params = jnp.take(gathered[0], owners, axis=0).reshape(-1)
    mixer_in = flat_params[bounds[0] : bounds[1]].reshape(D, 3 * local_width)
    mixer_out = flat_params[bounds[1] : bounds[2]].reshape(local_width, D)
    expand_weight = flat_params[bounds[2] : bounds[3]].reshape(D, local_ff)
    shrink_weight = flat_params[bounds[3] : bounds[4]].reshape(local_ff, D)
    mixer_bias = flat_params[bounds[4] : bounds[5]].astype(jnp.float32)
    expand_bias = flat_params[bounds[5] : bounds[6]].astype(jnp.float32)
    small_params = flat_params[bounds[6] : bounds[7]].reshape(6, D).astype(jnp.float32)
    own_rows = residual[0].astype(jnp.float32)
    segment, places = group_layout(lengths[0], group_rows)
    cosine, sines = rotary_tables(places)
    own_unit, own_scale = norm_stats(own_rows)
    normed_one = (own_unit * small_params[0] + small_params[1]).astype(jnp.bfloat16)
    normed_two = (own_unit * small_params[2] + small_params[3]).astype(jnp.bfloat16)
    full_one, full_two = (
        lax.all_gather(normed_one, "tensor", axis=0, tiled=True),
        lax.all_gather(normed_two, "tensor", axis=0, tiled=True),
    )
    projected = matmul(full_one, mixer_in) + mixer_bias
    head_shape = (group_rows, local_heads, HD)
    queries = rotate(projected[:, :local_width].reshape(head_shape), cosine, sines).astype(
        jnp.bfloat16
    )
    keys = rotate(
        projected[:, local_width : 2 * local_width].reshape(head_shape), cosine, sines
    ).astype(jnp.bfloat16)
    values = projected[:, 2 * local_width :].reshape(head_shape).astype(jnp.bfloat16)
    block_rows = min(512, group_rows)
    block_count = group_rows // block_rows
    score_scale = 1.0 / math.sqrt(HD)
    key_index = jnp.arange(group_rows, dtype=jnp.int32)

    def block_scores(start):
        query_block = lax.dynamic_slice_in_dim(queries, start, block_rows, 0)
        scores = (
            jnp.einsum("qhd,khd->hqk", query_block, keys, preferred_element_type=jnp.float32)
            * score_scale
        )
        row_index = start + jnp.arange(block_rows, dtype=jnp.int32)
        row_segment = lax.dynamic_slice_in_dim(segment, start, block_rows, 0)
        allowed = (row_segment[:, None] == segment[None, :]) & (
            key_index[None, :] <= row_index[:, None]
        )
        return (query_block, jnp.where(allowed[None], scores, masked_score))

    def attend_block(index):
        query_block, scores = block_scores(index * block_rows)
        row_top = jnp.max(scores, axis=-1, keepdims=True)
        raised = jnp.exp(scores - row_top)
        totals = jnp.sum(raised, axis=-1, keepdims=True)
        soft_weights = (raised / totals).astype(jnp.bfloat16)
        mixed = jnp.einsum("hqk,khd->qhd", soft_weights, values, preferred_element_type=jnp.float32)
        return (mixed.reshape(block_rows, local_width), (row_top + jnp.log(totals))[..., 0])

    context_blocks, log_blocks = lax.map(attend_block, jnp.arange(block_count, dtype=jnp.int32))
    context = context_blocks.reshape(group_rows, local_width).astype(jnp.bfloat16)
    before = matmul(full_two, expand_weight) + expand_bias
    hidden = jax.nn.gelu(before, approximate=False).astype(jnp.bfloat16)
    branches = lax.psum_scatter(
        matmul(context, mixer_out) + matmul(hidden, shrink_weight),
        "tensor",
        scatter_dimension=0,
        tiled=True,
    )
    output = own_rows + branches + small_params[4] + small_params[5]
    grad_own = cotangent[0].astype(jnp.float32)
    grad_rows = lax.all_gather(cotangent[0], "tensor", axis=0, tiled=True)
    grad_mixer_out = product_rows(context, grad_rows)
    grad_shrink = product_rows(hidden, grad_rows)
    grad_context = product_back(grad_rows, mixer_out).astype(jnp.bfloat16)
    grad_hidden = product_back(grad_rows, shrink_weight)
    gelu_pull = jax.vjp(lambda inner: jax.nn.gelu(inner, approximate=False), before)[1]
    grad_before = gelu_pull(grad_hidden)[0].astype(jnp.bfloat16)
    grad_expand = product_rows(full_two, grad_before)
    grad_expand_bias = jnp.sum(grad_before.astype(jnp.float32), axis=0)
    partial_two = product_back(grad_before, expand_weight)

    def attention_back(carry, index):
        grad_keys, grad_values = carry
        start = index * block_rows
        query_block, scores = block_scores(start)
        log_rows = lax.dynamic_index_in_dim(log_blocks, index, 0, keepdims=False)
        soft_weights = jnp.exp(scores - log_rows[..., None])
        grad_block = lax.dynamic_slice_in_dim(grad_context, start, block_rows, 0).reshape(
            block_rows, local_heads, HD
        )
        grad_weights = jnp.einsum(
            "qhd,khd->hqk", grad_block, values, preferred_element_type=jnp.float32
        )
        delta = jnp.sum(soft_weights * grad_weights, axis=-1, keepdims=True)
        grad_scores = (soft_weights * (grad_weights - delta)).astype(jnp.bfloat16)
        grad_query = (
            jnp.einsum("hqk,khd->qhd", grad_scores, keys, preferred_element_type=jnp.float32)
            * score_scale
        )
        grad_keys = (
            grad_keys
            + jnp.einsum(
                "hqk,qhd->khd", grad_scores, query_block, preferred_element_type=jnp.float32
            )
            * score_scale
        )
        grad_values = grad_values + jnp.einsum(
            "hqk,qhd->khd",
            soft_weights.astype(jnp.bfloat16),
            grad_block,
            preferred_element_type=jnp.float32,
        )
        return ((grad_keys, grad_values), grad_query)

    zero_heads = jnp.zeros(head_shape, jnp.float32)
    (grad_keys, grad_values), grad_query = lax.scan(
        attention_back, (zero_heads, zero_heads), jnp.arange(block_count, dtype=jnp.int32)
    )
    grad_query = grad_query.reshape(head_shape)
    grad_projected = jnp.concatenate(
        [
            rotate(grad_query, cosine, -sines).reshape(group_rows, local_width),
            rotate(grad_keys, cosine, -sines).reshape(group_rows, local_width),
            grad_values.reshape(group_rows, local_width),
        ],
        axis=1,
    ).astype(jnp.bfloat16)
    grad_mixer_in = product_rows(full_one, grad_projected)
    grad_mixer_bias = jnp.sum(grad_projected.astype(jnp.float32), axis=0)
    partial_one = product_back(grad_projected, mixer_in)
    bias_grad = jnp.sum(grad_own, axis=0)
    grad_one, grad_two = (
        lax.psum_scatter(partial_one, "tensor", scatter_dimension=0, tiled=True),
        lax.psum_scatter(partial_two, "tensor", scatter_dimension=0, tiled=True),
    )
    norm_grads = [
        jnp.sum(grad_one * own_unit, axis=0),
        jnp.sum(grad_one, axis=0),
        jnp.sum(grad_two * own_unit, axis=0),
        jnp.sum(grad_two, axis=0),
    ]
    input_grad = (
        grad_own
        + norm_back(grad_one, small_params[0], own_unit, own_scale)
        + norm_back(grad_two, small_params[2], own_unit, own_scale)
    )
    small_grad = jnp.stack(norm_grads + [bias_grad, bias_grad])
    small_grad = lax.psum(small_grad, "tensor")
    flat_grad = jnp.concatenate(
        [
            grad_mixer_in.reshape(-1),
            grad_mixer_out.reshape(-1),
            grad_expand.reshape(-1),
            grad_shrink.reshape(-1),
            grad_mixer_bias,
            grad_expand_bias,
            small_grad.reshape(-1),
            jnp.zeros((group_count * bucket_size - bounds[7],), jnp.float32),
        ]
    )
    stored_grad = jnp.take(flat_grad.reshape(group_count, bucket_size), inverse, axis=0)
    reduced = lax.psum_scatter(stored_grad, ("dp", "chip"), scatter_dimension=0, tiled=True)[0]
    my_bucket = inverse[lax.axis_index(("dp", "chip"))]
    position = my_bucket * bucket_size + jnp.arange(bucket_size, dtype=jnp.int32)
    step_rate = jnp.zeros((bucket_size,), jnp.float32) + rates[0]
    for kind_index in range(1, 8):
        step_rate = jnp.where(position >= bounds[kind_index], rates[kind_index], step_rate)
    step_value = step_count[0].astype(jnp.float32)
    new_weights, new_first, new_second, new_moving = adam_update(
        master[0, 0],
        moment_one[0, 0],
        moment_two[0, 0],
        average[0, 0],
        reduced,
        step_rate,
        step_value,
        weight_decay[0],
        ema_decay[0],
    )
    return (
        output[None],
        input_grad[None],
        new_weights[None, None],
        new_first[None, None],
        new_second[None, None],
        new_moving[None, None],
        reduced[None, None],
    )


LANES = 128
TROWS = 16


def fits(mesh):
    return mesh.shape["dp"] == 4 and mesh.shape["chip"] == 2 and mesh.shape["tensor"] == 4


def device_program(mesh):
    return on_device_fast if fits(mesh) else on_device


CHUNKS = 4
BROWS = 768
QROWS = 1024
FRONT = 128
BACK = 256
FLAT = 12304
HBM = pltpu.HBM


LIGHT = pl.CostEstimate(flops=1, bytes_accessed=1, transcendentals=0)


def params(limit_mb, **more):
    return pltpu.CompilerParams(vmem_limit_bytes=limit_mb * 1024 * 1024, **more)


def part_row(part):
    rows = (16 // CHUNKS) * BROWS
    return (0, rows + 16 * TROWS, 0, rows)[part]


def pack_kernel(bucket_ref, flat_ref, *refs):
    outs, padded, sem = refs[:2], refs[2], refs[3]
    bucket = bucket_ref[0]
    load = pltpu.make_async_copy(flat_ref, padded.at[pl.ds(FRONT, FLAT)], sem)
    load.start()
    padded[pl.ds(0, FRONT)] = jnp.zeros((FRONT, LANES), jnp.float32)
    padded[pl.ds(FRONT + FLAT, BACK)] = jnp.zeros((BACK, LANES), jnp.float32)
    load.wait()
    wide, narrow = 16 // CHUNKS, 12 // CHUNKS

    def take(start, stride):
        return padded[pl.ds(start, 16, stride=stride), :].astype(jnp.bfloat16)

    @pl.when(bucket >= 2)
    def _():
        def step(tile, carry):
            row = pl.multiple_of(tile * 16, 16)
            for panel in range(16):
                part = panel // wide
                at = part_row(part) + (panel % wide) * BROWS
                outs[part // 2][pl.ds(at + row, 16), :] = take(
                    (row - bucket) * 16 + panel + FRONT, 16
                )
            return carry

        lax.fori_loop(0, BROWS // 16, step, 0)

    @pl.when(bucket < 2)
    def _():
        def step(tile, carry):
            row = pl.multiple_of(tile * 16, 16)
            for panel in range(12):
                part = panel // narrow
                at = part_row(part) + (panel % narrow) * QROWS
                outs[part // 2][pl.ds(at + row, 16), :] = take(
                    row * 12 + panel - 16 * bucket + FRONT, 12
                )
            return carry

        lax.fori_loop(0, QROWS // 16, step, 0)

    tails = wide * BROWS

    @pl.when(bucket >= 1)
    def _():
        for panel in range(16):
            outs[0][pl.ds(tails + panel * TROWS, TROWS), :] = take(
                (BROWS - bucket) * 16 + panel + FRONT, 16
            )

    @pl.when(bucket == 0)
    def _():
        for panel in range(16):
            outs[0][pl.ds(tails + panel * TROWS, TROWS), :] = take(
                QROWS * 12 + min(panel, 11) + FRONT, 12
            )


def cut_kernel(starts, *refs):
    count = len(starts)
    copies = [
        pltpu.make_async_copy(
            refs[at].at[pl.ds(start, refs[count + at].shape[0])], refs[count + at], refs[-1].at[at]
        )
        for at, start in enumerate(starts)
    ]
    for copy in copies:
        copy.start()
    for copy in copies:
        copy.wait()


def cut(values, starts, counts):
    return pl.pallas_call(
        functools.partial(cut_kernel, starts),
        out_shape=[jax.ShapeDtypeStruct((count, LANES), jnp.bfloat16) for count in counts],
        in_specs=[pl.BlockSpec(memory_space=pl.ANY)] * len(values),
        out_specs=[pl.BlockSpec(memory_space=pltpu.VMEM)] * len(values),
        scratch_shapes=[pltpu.SemaphoreType.DMA((len(values),))],
        compiler_params=params(60),
        cost_estimate=LIGHT,
        name="cut",
    )(*values)


def chunk_rows():
    return (16 // CHUNKS) * (BROWS + TROWS)


def pack(bucket, flat):
    rows = (32 // CHUNKS) * BROWS
    return pl.pallas_call(
        pack_kernel,
        out_shape=[
            jax.ShapeDtypeStruct((rows + 16 * TROWS, LANES), jnp.bfloat16),
            jax.ShapeDtypeStruct((rows, LANES), jnp.bfloat16),
        ],
        in_specs=[pl.BlockSpec(memory_space=pltpu.SMEM), pl.BlockSpec(memory_space=HBM)],
        out_specs=[pl.BlockSpec(memory_space=pltpu.VMEM)] * 2,
        scratch_shapes=[
            pltpu.VMEM((FRONT + FLAT + BACK, LANES), jnp.float32),
            pltpu.SemaphoreType.DMA,
        ],
        compiler_params=params(24),
        cost_estimate=LIGHT,
        name="pack_params",
    )(bucket, flat)


PLACES = {
    0: (("in", 0, 1024, 0),),
    1: (("in", 1024, 1024, 0),),
    2: (("mix", 0, 512, 0), ("up", 0, 256, 512)),
    3: (("up", 256, 768, 0),),
    4: (("up", 1024, 768, 0),),
    5: (("up", 1792, 256, 0), ("mix", 512, 512, 256)),
    6: (("mix", 1024, 768, 0),),
    7: (("mix", 1792, 768, 0),),
}
NAMES = ("in", "mix", "up", "bias")


def panels_of(bucket):
    return (12 if bucket < 2 else 16) // CHUNKS


MATRICES = {
    "in": (2048, 1536),
    "mix": (2560, 2048),
    "up": (2048, 2048),
    "bias": (TROWS, 2048),
}


def columns(panel):
    return pl.ds(panel * LANES, LANES)


def place_parts(parts, bucket_ref, sources, tails_from, outs, tails_out, scratch):
    staged, tails, load_sems, tail_sem, store_sems = scratch
    main = (16 // CHUNKS) * BROWS
    if tails_from is None:
        for k in range(8):
            pltpu.make_async_copy(
                sources[k].at[pl.ds(main, 16 * TROWS)], tails.at[bucket_ref[k]], tail_sem
            ).start()
        take_tails = pltpu.make_async_copy(tails, tails, tail_sem)
    else:
        take_tails = pltpu.make_async_copy(tails_from, tails, tail_sem)
        take_tails.start()
    for at in range(2):
        for k in range(8):
            pltpu.make_async_copy(
                sources[8 * at + k].at[pl.ds(0 if k % 4 == 3 else part_row(parts[at]), main)],
                staged.at[at, bucket_ref[k]],
                load_sems.at[at, bucket_ref[k]],
            ).start()
    take_tails.wait()
    stores = []

    def store(source, target):
        stores.append(pltpu.make_async_copy(source, target, store_sems.at[len(stores)]))
        stores[-1].start()

    if tails_from is None:
        store(tails, tails_out)
        for panel in range(16):
            store(
                tails.at[7, pl.ds(panel * TROWS, TROWS)],
                outs["bias"].at[pl.ds(0, TROWS), columns(panel)],
            )
    for at, part in enumerate(parts):
        for bucket in range(8):
            held = staged.at[at, bucket]
            pltpu.make_async_copy(held, held, load_sems.at[at, bucket]).wait()
            span = QROWS if bucket < 2 else BROWS
            wide = panels_of(bucket)
            for panel in range(wide):
                if bucket:
                    head = pl.ds(panel * span, TROWS)
                    tail = pl.ds((part * wide + panel) * TROWS, TROWS)
                    staged[at, bucket, head, :] = (
                        staged[at, bucket, head, :] + tails[bucket - 1, tail, :]
                    )
                for name, first, rows, offset in PLACES[bucket]:
                    store(
                        staged.at[at, bucket, pl.ds(panel * span + offset, rows)],
                        outs[name].at[pl.ds(first, rows), columns(part * wide + panel)],
                    )
    return stores


def part_scratch(copies):
    return [
        pltpu.VMEM((2, 8, (16 // CHUNKS) * BROWS, LANES), jnp.bfloat16),
        pltpu.VMEM((8, 16 * TROWS, LANES), jnp.bfloat16),
        pltpu.SemaphoreType.DMA((2, 8)),
        pltpu.SemaphoreType.DMA,
        pltpu.SemaphoreType.DMA((copies,)),
    ]


def copies_of_parts():
    return 2 * sum(len(PLACES[b]) * panels_of(b) for b in range(8))


def unpack_kernel(bucket_ref, *refs):
    outs = dict(zip(NAMES, refs[16:20], strict=True))
    for put in place_parts((0, 1), bucket_ref, refs[:16], None, outs, refs[20], refs[21:]):
        put.wait()


def unpack(buckets, sources):
    shapes = [jax.ShapeDtypeStruct(MATRICES[name], jnp.bfloat16) for name in NAMES]
    tails = jax.ShapeDtypeStruct((8, 16 * TROWS, LANES), jnp.bfloat16)
    return pl.pallas_call(
        unpack_kernel,
        out_shape=[*shapes, tails],
        in_specs=[pl.BlockSpec(memory_space=pltpu.SMEM)] + [pl.BlockSpec(memory_space=HBM)] * 16,
        out_specs=[pl.BlockSpec(memory_space=HBM)] * 5,
        scratch_shapes=part_scratch(copies_of_parts() + 17),
        compiler_params=params(60),
        cost_estimate=LIGHT,
        name="unpack_params",
    )(buckets, *sources)


def unpack_hidden_kernel(width, bucket_ref, *refs):
    sources, tails_from, normed_from, up_bias = refs[:16], refs[16], refs[17], refs[18]
    outs = dict(zip(NAMES[:3], refs[24:27], strict=True))
    hidden_to, slope_to = refs[27:29]
    scratch, (normed, hidden, slope, normed_sem, out_sems) = refs[29:34], refs[34:]
    staged = scratch[0]
    load = pltpu.make_async_copy(normed_from, normed, normed_sem)
    load.start()
    stores = place_parts((2, 3), bucket_ref, sources, tails_from, outs, None, scratch)
    load.wait()
    rows_of_up = [
        (bucket, rows, offset)
        for bucket in range(8)
        for name, _, rows, offset in PLACES[bucket]
        if name == "up"
    ]
    half = up_bias.shape[1] // 2
    puts = []
    for block in range(half // FF_BLOCK):
        slot = block % 2
        if block >= 2:
            for put in puts[2 * block - 4 : 2 * block - 2]:
                put.wait()
        panels = []
        for panel in range(2 * block, 2 * block + 2):
            at, inner = panel // (16 // CHUNKS), panel % (16 // CHUNKS)
            pieces = [
                staged[at, bucket, pl.ds(inner * BROWS + offset, rows), :]
                for bucket, rows, offset in rows_of_up
            ]
            panels.append(jnp.concatenate(pieces, axis=0))
        first = half + block * FF_BLOCK
        gelu(
            matmul(normed[...], jnp.concatenate(panels, axis=1))
            + up_bias[:, first : first + FF_BLOCK],
            hidden.at[slot],
            slope.at[slot],
        )
        for which, (source, target, column) in enumerate(
            ((hidden, hidden_to, width + first), (slope, slope_to, first))
        ):
            puts.append(
                pltpu.make_async_copy(
                    source.at[slot],
                    target.at[:, pl.ds(column, FF_BLOCK)],
                    out_sems.at[slot, which],
                )
            )
            puts[-1].start()
    for put in [*puts[-4:], *stores]:
        put.wait()


def unpack_hidden(width, buckets, sources, before, normed, up_bias, halves):
    rows = normed.shape[0]
    hidden, slope = halves
    results = pl.pallas_call(
        functools.partial(unpack_hidden_kernel, width),
        out_shape=[jax.ShapeDtypeStruct(v.shape, v.dtype) for v in (*before[:3], hidden, slope)],
        in_specs=[pl.BlockSpec(memory_space=pltpu.SMEM)]
        + [pl.BlockSpec(memory_space=HBM)] * 18
        + [pl.BlockSpec(memory_space=pltpu.VMEM)]
        + [pl.BlockSpec(memory_space=HBM)] * 5,
        out_specs=[pl.BlockSpec(memory_space=HBM)] * 5,
        input_output_aliases={20 + at: at for at in range(5)},
        scratch_shapes=part_scratch(copies_of_parts())
        + [
            pltpu.VMEM(normed.shape, normed.dtype),
            pltpu.VMEM((2, rows, FF_BLOCK), jnp.bfloat16),
            pltpu.VMEM((2, rows, FF_BLOCK), jnp.float32),
            pltpu.SemaphoreType.DMA,
            pltpu.SemaphoreType.DMA((2, 2)),
        ],
        compiler_params=params(60),
        cost_estimate=LIGHT,
        name="unpack_hidden",
    )(buckets, *sources, before[4], normed, up_bias, *before[:3], hidden, slope)
    return results[:3], results[3], results[4]


GRAD_ROWS = 256
PAIR = 2 * GRAD_ROWS
IN_STEPS, OUT_STEPS, UP_STEPS, DOWN_STEPS = 4, 1, 4, 4
GRAD_EDGES = (0, 4, 5, 9, 13)
GRAD_STEPS = 13
KEPT, NEAR, FAR = 0, 1, 2


def weight_grad_kernel(table, *refs):
    lefts, projected, late, outs = refs[:8], refs[8:10], refs[10:14], refs[14:22]
    wide32, wide16, tail32, tail16, held, sems, tail_sem, late_sem = refs[22:]
    step = pl.program_id(0)
    core = table[0]
    main = (16 // CHUNKS) * BROWS

    def bucket_of(block):
        return jnp.where(block < 2 * IN_STEPS, block // 4, (block - 2) // 3)

    def kind_of(part, bucket):
        return table[1 + 16 * part + bucket], table[9 + 16 * part + bucket]

    def targets(part, kind, place):
        near = kind == NEAR
        return [
            (jnp.logical_and(near, place == 0), True, outs[3 * part]),
            (jnp.logical_and(near, place == 1), True, outs[3 * part + 1]),
            (kind == FAR, True, outs[3 * part + 2].at[jnp.minimum(place, 1)]),
            (jnp.logical_and(kind == KEPT, place >= 2), False, outs[6].at[part, jnp.clip(place - 2, 0, 1)]),
            (jnp.logical_and(kind == KEPT, place < 2), False, outs[7].at[part, jnp.minimum(place, 1)]),
        ]

    def wait(at):
        slot = lax.rem(at, 2)
        for panels, mine in ((3, at < IN_STEPS), (4, at >= IN_STEPS)):

            @pl.when(mine)
            def _(panels=panels):
                rows = pl.ds(0, panels * GRAD_ROWS)
                for half in range(2):
                    bucket = bucket_of(2 * at + half)
                    for part in range(2):
                        kind, _ = kind_of(part, bucket)
                        sem = sems.at[slot, part, half]

                        @pl.when(kind == KEPT)
                        def _(part=part, sem=sem):
                            place = outs[7].at[part, 0, rows]
                            pltpu.make_async_copy(place, place, sem).wait()

                        @pl.when(kind != KEPT)
                        def _(part=part, sem=sem):
                            place = outs[3 * part].at[rows]
                            pltpu.make_async_copy(place, place, sem).wait()

    @pl.when(step >= 2)
    def _():
        wait(step - 2)

    late_copies = []
    for at, source in enumerate(late):
        width = held.shape[2]
        if source.shape[1] > width:
            source = source.at[:, pl.ds(pl.multiple_of(core * width, width), width)]
        late_copies.append(pltpu.make_async_copy(source, held.at[at], late_sem.at[at]))

    @pl.when(step == 0)
    def _():
        for copy in late_copies:
            copy.start()
        tail32[...] = jnp.zeros_like(tail32)
        tail16[...] = jnp.zeros_like(tail16)

    @pl.when(step == GRAD_EDGES[1])
    def _():
        for copy in late_copies[:2]:
            copy.wait()

    @pl.when(step == GRAD_EDGES[2])
    def _():
        for copy in late_copies[2:]:
            copy.wait()

    def multiply(pair, right, panels, span):
        slot = lax.rem(step, 2)
        if right == 0:
            own, other = projected[0][...], projected[1][...]
        else:
            own, other = held[2 * right - 2], held[2 * right - 1]
        wide32[slot, :, pl.ds(0, 2 * panels * LANES)] = product_rows(
            lefts[2 * pair][...], own
        ) + product_rows(lefts[2 * pair + 1][...], other)
        for half in range(2):
            block = 2 * step + half
            bucket = bucket_of(block)
            before = jnp.maximum(bucket - 1, 0)
            if pair == 0:
                first, offset = block == 4, lax.rem(block, 4)
            else:
                offset = lax.rem(block - 2, 3)
                first = offset == 0
            offset = pl.multiple_of(offset * GRAD_ROWS, GRAD_ROWS)
            for part in range(2):
                kind, place = kind_of(part, bucket)

                @pl.when(kind != KEPT)
                def _(half=half, part=part):
                    for panel in range(panels):
                        tile = wide32[
                            slot, pl.ds(half * GRAD_ROWS, GRAD_ROWS), columns(part * panels + panel)
                        ]
                        rows = pl.ds(panel * GRAD_ROWS, GRAD_ROWS)
                        wide16[slot, part, half, rows, :] = tile.astype(jnp.bfloat16)

                for is_it, short, target in targets(part, kind, place):

                    @pl.when(is_it)
                    def _(half=half, part=part, short=short, target=target, offset=offset):
                        for panel in range(panels):
                            if short:
                                rows = pl.ds(panel * GRAD_ROWS, GRAD_ROWS)
                                source = wide16.at[slot, part, half, rows]
                            else:
                                rows = pl.ds(half * GRAD_ROWS, GRAD_ROWS)
                                source = wide32.at[slot, rows, columns(part * panels + panel)]
                            pltpu.make_async_copy(
                                source,
                                target.at[pl.ds(panel * span + offset, GRAD_ROWS)],
                                sems.at[slot, part, half],
                            ).start()

            @pl.when(first)
            def _(half=half, before=before):
                for part in range(2):
                    for panel in range(panels):
                        tile = wide32[
                            slot, pl.ds(half * GRAD_ROWS, TROWS), columns(part * panels + panel)
                        ]
                        rows = pl.ds(panel * TROWS, TROWS)
                        tail32[part, before, rows, :] = tile
                        tail16[part, before, rows, :] = tile.astype(jnp.bfloat16)

    for pair, right in enumerate((0, 1, 2, 1)):

        @pl.when(jnp.logical_and(step >= GRAD_EDGES[pair], step < GRAD_EDGES[pair + 1]))
        def _(pair=pair, right=right):
            multiply(pair, right, *((3, QROWS) if pair == 0 else (4, BROWS)))

    @pl.when(step == GRAD_STEPS - 1)
    def _():
        def tails(act):
            for part in range(2):
                for bucket in range(8):
                    for is_it, short, place in targets(part, *kind_of(part, bucket)):

                        @pl.when(is_it)
                        def _(part=part, bucket=bucket, short=short, place=place):
                            stage = tail16 if short else tail32
                            act(
                                pltpu.make_async_copy(
                                    stage.at[part, bucket],
                                    place.at[pl.ds(main, stage.shape[2])],
                                    tail_sem.at[part, bucket],
                                )
                            )

        tails(lambda copy: copy.start())
        wait(step - 1)
        wait(step)
        tails(lambda copy: copy.wait())


def weight_grads(table, lefts, rights):
    tokens = lefts[0].shape[0]

    def columns_at(first, count, ahead):
        return pl.BlockSpec(
            (tokens, PAIR), lambda i, table: (0, ahead + jnp.clip(i - first, 0, count - 1))
        )

    left_specs = [
        columns_at(first, last - first, ahead)
        for first, last, ahead in zip(GRAD_EDGES, GRAD_EDGES[1:], (0, 0, 0, 1), strict=False)
        for _ in range(2)
    ]
    half = (tokens, rights[0].shape[1] // 2)
    right_specs = [pl.BlockSpec(half, lambda i, table: (0, table[0]))] * 2
    rows = chunk_rows()
    near = jax.ShapeDtypeStruct((rows, LANES), jnp.bfloat16)
    short = jax.ShapeDtypeStruct((2, rows, LANES), jnp.bfloat16)
    wide = jax.ShapeDtypeStruct((2, 2, rows, LANES), jnp.float32)
    return pl.pallas_call(
        weight_grad_kernel,
        out_shape=[near, near, short] * 2 + [wide] * 2,
        grid_spec=pltpu.PrefetchScalarGridSpec(
            num_scalar_prefetch=1,
            grid=(GRAD_STEPS,),
            in_specs=left_specs + right_specs + [pl.BlockSpec(memory_space=HBM)] * 4,
            out_specs=[pl.BlockSpec(memory_space=HBM)] * 8,
            scratch_shapes=[
                pltpu.VMEM((2, PAIR, 8 * LANES), jnp.float32),
                pltpu.VMEM((2, 2, 2, 4 * GRAD_ROWS, LANES), jnp.bfloat16),
                pltpu.VMEM((2, 8, 4 * TROWS, LANES), jnp.float32),
                pltpu.VMEM((2, 8, 4 * TROWS, LANES), jnp.bfloat16),
                pltpu.VMEM((4, tokens, 8 * LANES), jnp.bfloat16),
                pltpu.SemaphoreType.DMA((2, 2, 2)),
                pltpu.SemaphoreType.DMA((2, 8)),
                pltpu.SemaphoreType.DMA((4,)),
            ],
        ),
        compiler_params=params(60),
        cost_estimate=LIGHT,
        name="weight_grads",
    )(table, *lefts, *rights)


NORM_COLUMNS = 512


def norm_grad_kernel(
    core, grad_projected, mixer_in, own_before, own_up, rest_before, rest_up, rows, centre, scale,
    gains, partial, sums,
):
    one = product_back(grad_projected[...], mixer_in[...])
    two = product_back(own_before[...], own_up[...]) + product_back(rest_before[...], rest_up[...])
    unit = (rows[...].astype(jnp.float32) - centre[...]) * scale[...]
    partial[...] = (one * gains[0:1, :] + two * gains[1:2, :]).astype(jnp.bfloat16)
    for at, value in enumerate((one * unit, one, two * unit, two)):
        sums[at : at + 1, :] = jnp.sum(value, axis=0, keepdims=True)


def norm_grad(core, grad_projected, mixer_in, own_before, rest_before, up, rows, centre, scale, gains):
    tokens = rows.shape[0]
    half = up.shape[1] // 2

    def whole(value):
        return pl.BlockSpec(value.shape, lambda i, core: (0, 0))

    block = pl.BlockSpec((tokens, NORM_COLUMNS), lambda i, core: (0, i))
    return pl.pallas_call(
        norm_grad_kernel,
        out_shape=[
            jax.ShapeDtypeStruct((tokens, D), jnp.bfloat16),
            jax.ShapeDtypeStruct((4, D), jnp.float32),
        ],
        grid_spec=pltpu.PrefetchScalarGridSpec(
            num_scalar_prefetch=1,
            grid=(D // NORM_COLUMNS,),
            in_specs=[
                whole(grad_projected),
                pl.BlockSpec((NORM_COLUMNS, mixer_in.shape[1]), lambda i, core: (i, 0)),
                whole(own_before),
                pl.BlockSpec((NORM_COLUMNS, half), lambda i, core: (i, core[0])),
                whole(rest_before),
                pl.BlockSpec((NORM_COLUMNS, half), lambda i, core: (i, 1 - core[0])),
                block,
                whole(centre),
                whole(scale),
                pl.BlockSpec((2, NORM_COLUMNS), lambda i, core: (0, i)),
            ],
            out_specs=[block, pl.BlockSpec((4, NORM_COLUMNS), lambda i, core: (0, i))],
        ),
        compiler_params=params(60),
        cost_estimate=LIGHT,
        name="norm_grad",
    )(core, grad_projected, mixer_in, own_before, up, rest_before, up, rows, centre, scale, gains)


ADAM_ROWS = 3080


def adam_kernel(table, scalar_ref, rate_ref, *refs):
    stays, near, far, small = refs[:2], refs[2:6], refs[6:10], refs[10]
    weights, first, second, moving = refs[11:15]
    new_weights, new_first, new_second, new_moving, reduced = refs[15:20]
    held32, held16, flat, sems = refs[20:]
    bucket, core = table[0], table[1]
    wide, narrow = 16 // CHUNKS, 12 // CHUNKS
    main = wide * BROWS
    turn_at = pl.program_id(0)

    def put(part, row, start, stride):
        rows = pl.ds(row, 16)
        value = held32[part, rows, :] + (
            held16[0, part, rows, :].astype(jnp.float32) + held16[1, part, rows, :].astype(jnp.float32)
        )
        flat[pl.ds(start, 16, stride=stride), :] = value

    @pl.when(turn_at == 0)
    def _():
        loads = []
        for at in range(4):
            place = 2 * (core if at < 2 else 1 - core) + at % 2
            source = stays[at // 2].at[at % 2, at // 2]
            loads.append(pltpu.make_async_copy(source, held32.at[place], sems.at[0, at]))
            for which, came in enumerate((near, far)):
                loads.append(
                    pltpu.make_async_copy(came[at], held16.at[which, place], sems.at[1 + which, at])
                )
        for load in loads:
            load.start()
        for load in loads:
            load.wait()

        @pl.when(bucket >= 1)
        def _():
            for panel in range(16):
                put(
                    panel // wide,
                    main + (panel % wide) * TROWS,
                    (BROWS - bucket) * 16 + panel + FRONT,
                    16,
                )

        @pl.when(bucket == 0)
        def _():
            for panel in range(12):
                put(
                    panel // narrow,
                    main + (panel % narrow) * TROWS,
                    QROWS * 12 + panel + FRONT,
                    12,
                )

        @pl.when(bucket == 7)
        def _():
            flat[pl.ds(FRONT + FLAT - LANES, LANES), :] = small[...]

    @pl.when(bucket >= 2)
    def _():
        def reach(at):
            tiles = (at * (ADAM_ROWS // 8) // 2 + 23) // 16
            return jnp.clip(jnp.where(at > 0, tiles, 0), 0, BROWS // 16)

        def step(tile, carry):
            row = pl.multiple_of(tile * 16, 16)
            for panel in range(16):
                put(
                    panel // wide,
                    (panel % wide) * BROWS + row,
                    (row - bucket) * 16 + panel + FRONT,
                    16,
                )
            return carry

        lax.fori_loop(reach(turn_at), reach(turn_at + 1), step, 0)

    @pl.when(bucket < 2)
    def _():
        def reach(at):
            tiles = (at * ADAM_ROWS + 16) // 192 + 1
            return jnp.clip(jnp.where(at > 0, tiles, 0), 0, QROWS // 16)

        def step(tile, carry):
            row = pl.multiple_of(tile * 16, 16)
            for panel in range(12):
                put(
                    panel // narrow,
                    (panel % narrow) * QROWS + row,
                    row * 12 + panel - 16 * bucket + FRONT,
                    12,
                )
            return carry

        lax.fori_loop(reach(turn_at), reach(turn_at + 1), step, 0)

    start = turn_at * ADAM_ROWS
    gradient = flat[pl.ds(pl.multiple_of(FRONT + start, 8), ADAM_ROWS), :]
    reduced[...] = gradient
    scale_one, scale_two, decay, keep = (scalar_ref[at] for at in range(4))
    one = beta_one * first[...] + (1.0 - beta_one) * gradient
    two = beta_two * second[...] + (1.0 - beta_two) * gradient * gradient
    new_first[...] = one
    new_second[...] = two
    old = weights[...]
    change = (one * scale_one) / (jnp.sqrt(two * scale_two) + adam_epsilon) + decay * old

    def write(rate):
        fresh = old - rate * change
        new_weights[...] = fresh
        new_moving[...] = keep * moving[...] + (1.0 - keep) * fresh

    first_row = bucket * FLAT + start
    bounds = [bound // LANES for bound in bound_list(512, 2048)[1:]]
    kinds = [sum(jnp.where(at >= bound, 1, 0) for bound in bounds) for at in (first_row, first_row + ADAM_ROWS - 1)]

    @pl.when(kinds[0] == kinds[1])
    def _():
        write(rate_ref[kinds[0]])

    @pl.when(kinds[0] != kinds[1])
    def _():
        row = first_row + lax.broadcasted_iota(jnp.int32, (ADAM_ROWS, LANES), 0)
        rate = jnp.full((ADAM_ROWS, LANES), rate_ref[0], jnp.float32)
        for kind, bound in enumerate(bounds):
            rate = jnp.where(row >= bound, rate_ref[kind + 1], rate)
        write(rate)


def adam(table, scalars, rates, stays, near, far, small, state):
    steps = -(-FLAT // ADAM_ROWS)
    block = pl.BlockSpec((ADAM_ROWS, LANES), lambda i: (i, 0))
    return pl.pallas_call(
        adam_kernel,
        grid=(steps,),
        out_shape=[jax.ShapeDtypeStruct((FLAT, LANES), jnp.float32)] * 5,
        in_specs=[pl.BlockSpec(memory_space=pltpu.SMEM)] * 3
        + [pl.BlockSpec(memory_space=HBM)] * 2
        + [pl.BlockSpec(memory_space=pl.ANY)] * 8
        + [pl.BlockSpec(memory_space=pltpu.VMEM)]
        + [block] * 4,
        out_specs=[block] * 5,
        scratch_shapes=[
            pltpu.VMEM((4, chunk_rows(), LANES), jnp.float32),
            pltpu.VMEM((2, 4, chunk_rows(), LANES), jnp.bfloat16),
            pltpu.VMEM((FRONT + max(steps * ADAM_ROWS, FLAT + BACK), LANES), jnp.float32),
            pltpu.SemaphoreType.DMA((3, 4)),
        ],
        compiler_params=params(60),
        cost_estimate=LIGHT,
        name="adam",
    )(table, scalars, rates, *stays, *near, *far, small, *state)


def finish_kernel(terms, rows, grads, out):
    scaled = terms[0].astype(jnp.float32)
    for at in range(1, terms.shape[0]):
        scaled = scaled + terms[at].astype(jnp.float32)
    unit, scale = norm_stats(rows[...].astype(jnp.float32))
    out[...] = grads[...].astype(jnp.float32) + scale * (
        scaled
        - jnp.mean(scaled, axis=-1, keepdims=True)
        - unit * jnp.mean(scaled * unit, axis=-1, keepdims=True)
    )


def finish(terms, rows, grads):
    count, width = rows.shape
    height = count // 4
    block = pl.BlockSpec((height, width), lambda i: (i, 0))
    return pl.pallas_call(
        finish_kernel,
        grid=(count // height,),
        out_shape=jax.ShapeDtypeStruct((count, width), jnp.float32),
        in_specs=[
            pl.BlockSpec((terms.shape[0], height, width), lambda i: (0, i, 0)),
            block,
            block,
        ],
        out_specs=block,
        compiler_params=params(60),
        cost_estimate=LIGHT,
        name="finish",
    )(terms, rows, grads)


FF_BLOCK = 256


def gelu(before, hidden, slope):
    half = 0.5 + 0.5 * lax.erf(before * math.sqrt(0.5))
    hidden[...] = (before * half).astype(jnp.bfloat16)
    slope[...] = half + before * jnp.exp(-0.5 * before * before) * (1.0 / math.sqrt(2.0 * math.pi))


def hidden_kernel(normed, up, up_bias, hidden, slope):
    gelu(matmul(normed[...], up[...]) + up_bias[...], hidden, slope)


def hidden_layer(width, normed, up, up_bias):
    rows, units = normed.shape[0], up.shape[1]
    block = pl.BlockSpec((rows, FF_BLOCK), lambda i: (0, i))
    return pl.pallas_call(
        hidden_kernel,
        grid=(units // FF_BLOCK // 2,),
        out_shape=[
            jax.ShapeDtypeStruct((rows, width + units), jnp.bfloat16),
            jax.ShapeDtypeStruct((rows, units), jnp.float32),
        ],
        in_specs=[
            pl.BlockSpec(memory_space=pltpu.VMEM),
            pl.BlockSpec((D, FF_BLOCK), lambda i: (0, i)),
            pl.BlockSpec((1, FF_BLOCK), lambda i: (0, i)),
        ],
        out_specs=[pl.BlockSpec((rows, FF_BLOCK), lambda i: (0, i + width // FF_BLOCK)), block],
        compiler_params=params(60),
        cost_estimate=LIGHT,
        name="hidden_layer",
    )(normed, up, up_bias)


def hidden_back_kernel(half, grads, down, slope, grad_before, grad_bias):
    rounded = (slope[...] * product_back(grads[...], down[...])).astype(jnp.bfloat16)
    grad_before[...] = rounded
    grad_bias[...] = jnp.sum(rounded.astype(jnp.float32), axis=0, keepdims=True)


def hidden_back(half, grads, mix, slope):
    rows, units = slope.shape
    first = (mix.shape[0] - units) // FF_BLOCK
    steps = units // FF_BLOCK // 2
    return pl.pallas_call(
        hidden_back_kernel,
        out_shape=[
            jax.ShapeDtypeStruct((rows, units // 2), jnp.bfloat16),
            jax.ShapeDtypeStruct((1, units // 2), jnp.float32),
        ],
        grid_spec=pltpu.PrefetchScalarGridSpec(
            num_scalar_prefetch=1,
            grid=(steps,),
            in_specs=[
                pl.BlockSpec((rows, D), lambda i, half: (0, 0)),
                pl.BlockSpec((FF_BLOCK, D), lambda i, half: (first + half[0] * steps + i, 0)),
                pl.BlockSpec((rows, FF_BLOCK), lambda i, half: (0, half[0] * steps + i)),
            ],
            out_specs=[
                pl.BlockSpec((rows, FF_BLOCK), lambda i, half: (0, i)),
                pl.BlockSpec((1, FF_BLOCK), lambda i, half: (0, i)),
            ],
        ),
        compiler_params=params(60),
        cost_estimate=LIGHT,
        name="hidden_back",
    )(half, grads, mix, slope)


def norm_kernel(rows, gains, one, two, centre, scale):
    values = rows[...].astype(jnp.float32)
    middle = jnp.mean(values, axis=-1, keepdims=True)
    values = values - middle
    factor = lax.rsqrt(jnp.mean(values * values, axis=-1, keepdims=True) + norm_epsilon)
    unit = values * factor
    one[...] = (unit * gains[0:1, :] + gains[1:2, :]).astype(jnp.bfloat16)
    two[...] = (unit * gains[2:3, :] + gains[3:4, :]).astype(jnp.bfloat16)
    centre[...] = middle
    scale[...] = factor


def norms(rows, small_params):
    count, width = rows.shape
    height = 128
    block = pl.BlockSpec((height, width), lambda i: (i, 0))
    column = pl.BlockSpec((height, 1), lambda i: (i, 0))
    return pl.pallas_call(
        norm_kernel,
        grid=(count // height,),
        out_shape=[jax.ShapeDtypeStruct((count, width), jnp.bfloat16)] * 2
        + [jax.ShapeDtypeStruct((count, 1), jnp.float32)] * 2,
        in_specs=[block, pl.BlockSpec(memory_space=pltpu.VMEM)],
        out_specs=[block, block, column, column],
        compiler_params=params(60),
        cost_estimate=LIGHT,
        name="norms",
    )(rows, small_params)


QUERY_BLOCK = 256


def turn(values, tables, sign):
    plain, lower, upper = tables
    half_rot = ROT // 2
    return (
        values * plain
        + pltpu.roll(values, HD - half_rot, 1) * (sign * lower)
        + pltpu.roll(values, half_rot, 1) * (sign * upper)
    )


def block_scores(query, keys, begins, first, first_key):
    scores = product_back(query, keys) * (1.0 / math.sqrt(HD))
    row_index = first + lax.broadcasted_iota(jnp.int32, scores.shape, 0)
    key_index = first_key + lax.broadcasted_iota(jnp.int32, scores.shape, 1)
    allowed = (key_index <= row_index) & (key_index >= begins)
    return jnp.where(allowed, scores, masked_score)


HEAD_PAIR = 2 * HD


def attend_kernel(
    normed, queries_in, keys_in, values_in, bias, plain, lower, upper, begins, _, context, turned, logs
):
    rows = normed.shape[0]
    width = bias.shape[1] // 3
    first_column = pl.program_id(0) * HEAD_PAIR
    tables = (plain[...], lower[...], upper[...])
    for part, weights in enumerate((queries_in, keys_in, values_in)):
        projected = matmul(normed[...], weights[...])
        projected = projected + bias[
            :, pl.ds(pl.multiple_of(part * width + first_column, HEAD_PAIR), HEAD_PAIR)
        ]
        for head in range(2):
            value = projected[:, head * HD : (head + 1) * HD]
            if part < 2:
                value = turn(value, tables, 1.0)
            turned[part, :, head * HD : (head + 1) * HD] = value.astype(jnp.bfloat16)

    def one_head(head, carry):
        column = pl.ds(pl.multiple_of(head * HD, HD), HD)
        queries, keys, values = (turned[part, :, column] for part in range(3))
        for first in range(0, rows, QUERY_BLOCK):
            last = first + QUERY_BLOCK
            mine = slice(first, last)
            seen = slice(max(0, first - rows // 2), last)
            scores = block_scores(queries[mine], keys[seen], begins[mine, :], first, seen.start)
            top = jnp.max(scores, axis=-1, keepdims=True)
            raised = jnp.exp(scores - top)
            total = jnp.sum(raised, axis=-1, keepdims=True)
            rounded = (raised / total).astype(jnp.bfloat16)
            context[mine, column] = matmul(rounded, values[seen]).astype(jnp.bfloat16)
            logs[head, mine, :] = top + jnp.log(total)
        return carry

    lax.fori_loop(0, 2, one_head, 0)


def attend(normed, mixer_in, bias, tables, begins, mixed):
    rows, width = normed.shape[0], mixer_in.shape[1] // 3
    pairs = width // HEAD_PAIR
    whole = pl.BlockSpec(memory_space=pltpu.VMEM)

    def weights(part):
        return pl.BlockSpec((mixer_in.shape[0], HEAD_PAIR), lambda i: (0, part * pairs + i))

    return pl.pallas_call(
        attend_kernel,
        grid=(pairs,),
        out_shape=[
            jax.ShapeDtypeStruct(mixed.shape, mixed.dtype),
            jax.ShapeDtypeStruct((3, rows, width), jnp.bfloat16),
            jax.ShapeDtypeStruct((width // HD, rows, 1), jnp.float32),
        ],
        in_specs=[whole, weights(0), weights(1), weights(2)]
        + [whole] * 5
        + [pl.BlockSpec(memory_space=HBM)],
        out_specs=[
            pl.BlockSpec((rows, HEAD_PAIR), lambda i: (0, i)),
            pl.BlockSpec((3, rows, HEAD_PAIR), lambda i: (0, 0, i)),
            pl.BlockSpec((2, rows, 1), lambda i: (i, 0, 0)),
        ],
        input_output_aliases={9: 0},
        compiler_params=params(60),
        cost_estimate=LIGHT,
        name="attend",
    )(normed, mixer_in, mixer_in, mixer_in, bias, *tables, begins, mixed)


def attend_back_kernel(
    turned, logs, plain, lower, upper, begins, grad_context, grad_projected, key_sum, value_sum
):
    rows, width = grad_context.shape
    score_scale = 1.0 / math.sqrt(HD)

    def one_head(head, carry):
        cols = [pl.ds(pl.multiple_of(part * width + head * HD, HD), HD) for part in range(3)]
        queries, keys, values = (turned[part, :, cols[0]] for part in range(3))
        key_sum[...] = jnp.zeros_like(key_sum)
        value_sum[...] = jnp.zeros_like(value_sum)
        for first in range(0, rows, QUERY_BLOCK):
            last = first + QUERY_BLOCK
            mine = slice(first, last)
            query = queries[mine]
            seen = slice(max(0, first - rows // 2), last)
            scores = block_scores(query, keys[seen], begins[mine, :], first, seen.start)
            soft = jnp.exp(scores - logs[head, mine, :])
            grad_mine = grad_context[mine, cols[0]]
            grad_soft = product_back(grad_mine, values[seen])
            delta = jnp.sum(soft * grad_soft, axis=-1, keepdims=True)
            grad_scores = (soft * (grad_soft - delta)).astype(jnp.bfloat16)
            grad_query = matmul(grad_scores, keys[seen]) * score_scale
            tables = (plain[mine, :], lower[mine, :], upper[mine, :])
            grad_projected[mine, cols[0]] = turn(grad_query, tables, -1.0).astype(jnp.bfloat16)
            key_sum[seen, :] += product_rows(grad_scores, query)
            value_sum[seen, :] += product_rows(soft.astype(jnp.bfloat16), grad_mine)
        tables = (plain[...], lower[...], upper[...])
        grad_projected[:, cols[1]] = turn(key_sum[...] * score_scale, tables, -1.0).astype(
            jnp.bfloat16
        )
        grad_projected[:, cols[2]] = value_sum[...].astype(jnp.bfloat16)
        return carry

    lax.fori_loop(0, width // HD, one_head, 0)


def attend_back(turned, logs, tables, begins, grad_context):
    rows, width = grad_context.shape
    whole = pl.BlockSpec(memory_space=pltpu.VMEM)
    return pl.pallas_call(
        attend_back_kernel,
        out_shape=jax.ShapeDtypeStruct((rows, 3 * width), jnp.bfloat16),
        in_specs=[whole] * 7,
        out_specs=whole,
        scratch_shapes=[pltpu.VMEM((rows, HD), jnp.float32)] * 2,
        compiler_params=params(36),
        cost_estimate=LIGHT,
        name="attend_back",
    )(turned, logs, *tables, begins, grad_context)


def rope_tables(places):
    half_rot = ROT // 2
    frequency = rope_base ** (-2.0 * jnp.arange(half_rot, dtype=jnp.float32) / ROT)
    angles = places[:, None] * frequency[None, :]
    cosine, sines = jnp.cos(angles), jnp.sin(angles)
    rest = jnp.zeros((places.shape[0], HD - ROT), jnp.float32)
    none = jnp.zeros_like(sines)
    return (
        jnp.concatenate([cosine, cosine, rest + 1.0], axis=1),
        jnp.concatenate([-sines, none, rest], axis=1),
        jnp.concatenate([none, sines, rest], axis=1),
    )


def along_x(value):
    return lax.ppermute(value, "dp", [(i, i ^ 1) for i in range(4)])


def along_y(value):
    return lax.ppermute(value, "dp", [(i, i ^ 2) for i in range(4)])


def along_line(value, bit):
    return lax.ppermute(value, "tensor", [(i, i ^ bit) for i in range(4)])


def along(bit, value):
    return lax.ppermute(
        value, ("dp", "chip"), [(i, (i // 2 ^ bit) * 2 + (i % 2 ^ 1)) for i in range(8)]
    )


def across(value):
    return lax.ppermute(value, "chip", [(0, 1), (1, 0)])


def line_blocks(partial):
    count = lax.axis_size("tensor")
    rows = partial.shape[0] // count
    return lax.all_to_all(partial.reshape(count, rows, partial.shape[1]), "tensor", 0, 0)


def on_device_fast(
    residual,
    cotangent,
    lengths,
    owners,
    step_count,
    rates,
    weight_decay,
    ema_decay,
    master,
    moment_one,
    moment_two,
    average,
):
    local_width = HD * H // lax.axis_size("tensor")
    group_rows = residual.shape[1] * lax.axis_size("tensor")
    slots = jnp.arange(8, dtype=jnp.int32)
    inverse = jnp.sum(
        slots[None, :] * (owners[None, :] == slots[:, None]).astype(jnp.int32), axis=1
    )
    data_index, core, here = lax.axis_index("dp"), lax.axis_index("chip"), lax.axis_index("tensor")
    partners = jnp.stack([(data_index ^ j) * 2 + (core ^ c) for c in range(2) for j in range(4)])
    buckets = jnp.sum(
        jnp.where(partners[:, None] == slots[None, :], inverse[None, :], 0), axis=1
    ).astype(jnp.int32)
    partner_of = jnp.sum(
        jnp.where(buckets[None, :] == slots[:, None], slots[None, :], 0), axis=1
    )
    hop, other = partner_of % 4, partner_of // 4
    grad_table = [core[None]]
    for first, second in ((hop % 2, hop // 2), (hop // 2, hop % 2)):
        grad_table.append(first * (1 + second))
        grad_table.append(other + 2 * second * (1 - first))
    grad_table = jnp.concatenate(grad_table).astype(jnp.int32)

    full_rows = lax.all_gather(residual[0], "tensor", axis=0, tiled=True)
    grad_rows = lax.all_gather(cotangent[0], "tensor", axis=0, tiled=True)
    own_rows = residual[0].astype(jnp.float32)

    def order(*values):
        return lax.optimization_barrier(values)

    rank = jnp.arange(lengths.shape[1], dtype=jnp.int32)
    seq_ends = jnp.sum(jnp.where(rank[None, :] <= rank[:, None], lengths[0][None, :], 0), axis=1)
    token_index = jnp.arange(group_rows, dtype=jnp.int32)
    passed = (token_index[:, None] >= seq_ends[None, :]).astype(jnp.int32)
    begins = jnp.sum(passed * lengths[0][None, :], axis=1)
    tables = rope_tables((token_index - begins).astype(jnp.float32))
    begins = begins[:, None]

    one, two = pack(buckets[:1], master.reshape(FLAT, LANES))
    one_x, one_y, one_own = order(along_x(one), along_y(one), across(one))

    def from_far(first, second, from_x, from_y):
        rows = (16 // CHUNKS) * BROWS
        start = part_row(second)
        count = start if first == 0 else rows
        if first == 0:
            from_y, from_x = from_y[:count], from_x[start : start + rows]
        else:
            from_y, from_x = cut([from_y, from_x], (0, start), (count, rows))
        return [along_x(from_y), along_y(from_x)]

    far = from_far(0, 1, one_x, one_y)
    near_x, near_y, two_own = across(one_x), across(one_y), across(two)
    far, near_x, near_y, two_own, two, tables, begins = order(
        far, near_x, near_y, two_own, two, tables, begins
    )

    two_x, two_y = along_x(two), along_y(two)
    far_other = [across(value) for value in far]
    sources = []
    for part in range(2):
        sources += [one, one_x, one_y, far[part], one_own, near_x, near_y, far_other[part]]
    weights = unpack(buckets, sources)
    weights, full_rows = order(weights, full_rows)
    flat_bias = weights[3][:8].reshape(-1).astype(jnp.float32)
    mixer_bias = flat_bias[: 3 * local_width]
    expand_bias = flat_bias[3 * local_width : 3 * local_width + D]
    small_params = flat_bias[3 * local_width + D : 3 * local_width + 7 * D].reshape(6, D)
    full_one, full_two, centre, scale = norms(full_rows, small_params)
    hidden_half = hidden_layer(local_width, full_two, weights[2], expand_bias[None])
    two_x, two_y, full_rows, full_one, full_two, weights, hidden_half = order(
        two_x, two_y, full_rows, full_one, full_two, weights, hidden_half
    )
    other_rows = across(full_rows)

    far = from_far(2, 3, two_x, two_y)
    near_x, near_y = across(two_x), across(two_y)
    other_one, other_two, _, _ = norms(other_rows, small_params)
    far, near_x, near_y, hidden_half, weights, other_one, other_two = order(
        far, near_x, near_y, hidden_half, weights, other_one, other_two
    )

    far_other = [across(value) for value in far]
    sources = []
    for part in range(2):
        sources += [two, two_x, two_y, far[part], two_own, near_x, near_y, far_other[part]]
    (mixer_in, mix_weight, expand_weight), mixed, slope = unpack_hidden(
        local_width, buckets, sources, weights, full_two, expand_bias[None], hidden_half
    )

    mixed, turned, logs = attend(full_one, mixer_in, mixer_bias[None], tables, begins, mixed)
    other_mixed = across(mixed)
    branches = matmul(mixed, mix_weight)
    branches, turned, grad_rows = order(branches, turned, grad_rows)
    branches = lax.psum_scatter(branches, "tensor", scatter_dimension=0, tiled=True)
    other_grads = across(grad_rows)

    grad_context = product_back(grad_rows, mix_weight[:local_width]).astype(jnp.bfloat16)
    grad_projected = attend_back(turned, logs, tables, begins, grad_context)
    grad_projected, slope = order(grad_projected, slope)
    other_projected = across(grad_projected)
    cores = core[None].astype(jnp.int32)
    rest_before, rest_bias = hidden_back(1 - cores, grad_rows, mix_weight, slope)
    other_before = across(rest_before)
    own_before, own_bias = hidden_back(cores, grad_rows, mix_weight, slope)
    grad_expand_bias = jnp.where(
        core == 0,
        jnp.concatenate([own_bias[0], rest_bias[0]]),
        jnp.concatenate([rest_bias[0], own_bias[0]]),
    )

    lefts = [full_one, other_one, mixed, other_mixed, full_two, other_two, mixed, other_mixed]
    rights = [grad_projected, other_projected, grad_rows, other_grads, own_before, other_before]
    sums = weight_grads(grad_table, lefts, rights)
    grad_projected, own_before, rest_before, sums = order(
        grad_projected, own_before, rest_before, sums
    )
    near_a, cross_a, far_a, near_b, cross_b, far_b, passed, stays = sums
    came_a, came_b, other_stays = along_x(far_a), along_y(far_b), across(stays)

    partial, norm_grads = norm_grad(
        cores,
        grad_projected,
        mixer_in,
        own_before,
        rest_before,
        expand_weight,
        full_rows,
        centre,
        scale,
        jnp.stack([small_params[0], small_params[2]]),
    )
    bias_grad = jnp.sum(grad_rows.astype(jnp.float32), axis=0)
    small = (
        jnp.sum(grad_projected.astype(jnp.float32), axis=0),
        grad_expand_bias,
        bias_grad,
    )

    norm_grads, other_stays = order(norm_grads, other_stays)
    one, two, three = (along_line(norm_grads, bit) for bit in (1, 2, 3))
    norm_grads = (norm_grads + one) + (two + three)
    near = [near_a, near_b, cross_a, cross_b]
    came_a, came_b, other_stays, partial, norm_grads, small, near = order(
        came_a, came_b, other_stays, partial, norm_grads, small, near
    )
    near = [along_x(near[0]), along_y(near[1]), along(1, near[2]), along(2, near[3])]
    terms = line_blocks(partial)
    pass_a = [(passed[0, at] + came_a[at].astype(jnp.float32)).astype(jnp.bfloat16) for at in range(2)]
    pass_b = [(passed[1, at] + came_b[at].astype(jnp.float32)).astype(jnp.bfloat16) for at in range(2)]
    small = jnp.concatenate(
        [
            small[0],
            small[1],
            norm_grads.reshape(-1),
            small[2],
            small[2],
            jnp.zeros((8 * D - 3 * local_width - 7 * D,), jnp.float32),
        ]
    ).reshape(LANES, LANES)
    small = small + across(small)
    small = small + along_x(small)
    near, pass_a, pass_b, small = order(near, pass_a, pass_b, small)
    output = residual[0].astype(jnp.float32) + branches + small_params[4] + small_params[5]
    far = [along_y(pass_a[0]), along_x(pass_b[0]), along(2, pass_a[1]), along(1, pass_b[1])]
    output, small = order(output, small)
    small = small + along_y(small)
    far, output, small = order(far, output, small)

    step_value = step_count[0].astype(jnp.float32)
    scalars = jnp.stack(
        [
            1.0 / (1.0 - jnp.power(beta_one, step_value)),
            1.0 / (1.0 - jnp.power(beta_two, step_value)),
            weight_decay[0],
            ema_decay[0],
        ]
    )
    state = [v.reshape(FLAT, LANES) for v in (master, moment_one, moment_two, average)]
    table = jnp.stack([buckets[0], core.astype(jnp.int32)])
    results = adam(table, scalars, rates, [stays, other_stays], near, far, small, state)
    terms, results = order(terms, results)
    input_grad = finish(terms, residual[0], cotangent[0])
    return (output[None], input_grad[None], *[v.reshape(master.shape) for v in results])


def solution(mesh):
    placed = (
        P(("dp", "chip"), "tensor", None),
        P(("dp", "chip"), "tensor", None),
        P(("dp", "chip"), None),
        P(),
        P(),
        P(),
        P(),
        P(),
        P("tensor", ("dp", "chip"), None),
        P("tensor", ("dp", "chip"), None),
        P("tensor", ("dp", "chip"), None),
        P("tensor", ("dp", "chip"), None),
    )
    return jax.shard_map(
        device_program(mesh),
        mesh=mesh,
        in_specs=placed,
        out_specs=(
            P(("dp", "chip"), "tensor", None),
            P(("dp", "chip"), "tensor", None),
            P("tensor", ("dp", "chip"), None),
            P("tensor", ("dp", "chip"), None),
            P("tensor", ("dp", "chip"), None),
            P("tensor", ("dp", "chip"), None),
            P("tensor", ("dp", "chip"), None),
        ),
        check_vma=False,
    )
```

```python
import functools
import math

import jax
import jax.numpy as jnp
from jax import lax
from jax.experimental import pallas as pl
from jax.experimental.pallas import tpu as pltpu
from jax.sharding import PartitionSpec as P

D = 2048
H = 16
HD = 128
FF = 8192
ROT = 32


norm_epsilon = 1e-05
adam_epsilon = 1e-08
beta_one = 0.5
beta_two = 0.5
rope_base = 10000.0
masked_score = -1e30


def matmul(left, right):
    return jnp.dot(left, right, preferred_element_type=jnp.float32)


def product_rows(left, right):
    return lax.dot_general(
        left, right, (((0,), (0,)), ((), ())), preferred_element_type=jnp.float32
    )


def product_back(left, right):
    return lax.dot_general(
        left, right, (((1,), (1,)), ((), ())), preferred_element_type=jnp.float32
    )


def bound_list(local_width, local_ff):
    widths = [
        D * 3 * local_width,
        local_width * D,
        D * local_ff,
        local_ff * D,
        3 * local_width,
        local_ff,
        6 * D,
    ]
    bounds = [0]
    for part_width in widths:
        bounds.append(bounds[-1] + part_width)
    return bounds


def group_layout(seq_lengths, group_rows):
    order = jnp.arange(seq_lengths.shape[0], dtype=jnp.int32)
    seq_ends = jnp.sum(
        jnp.where(order[None, :] <= order[:, None], seq_lengths[None, :], 0), axis=1
    )
    starts = seq_ends - seq_lengths
    token_index = jnp.arange(group_rows, dtype=jnp.int32)
    segment = jnp.sum((token_index[:, None] >= seq_ends[None, :]).astype(jnp.int32), axis=1)
    chosen = (
        segment[:, None] == jnp.arange(seq_lengths.shape[0], dtype=jnp.int32)[None, :]
    ).astype(jnp.int32)
    places = token_index - jnp.sum(chosen * starts[None, :], axis=1)
    return (segment, places.astype(jnp.float32))


def rotary_tables(places):
    half_rot = ROT // 2
    frequency = rope_base ** (-2.0 * jnp.arange(half_rot, dtype=jnp.float32) / ROT)
    angles = places[:, None] * frequency[None, :]
    return (jnp.cos(angles)[:, None, :], jnp.sin(angles)[:, None, :])


def rotate(values, cosine, sines):
    half_rot = ROT // 2
    first = values[..., :half_rot]
    second = values[..., half_rot:ROT]
    return jnp.concatenate(
        [first * cosine - second * sines, second * cosine + first * sines, values[..., ROT:]],
        axis=-1,
    )


def norm_stats(inputs):
    center = inputs - jnp.mean(inputs, axis=-1, keepdims=True)
    scale = lax.rsqrt(jnp.mean(center * center, axis=-1, keepdims=True) + norm_epsilon)
    return (center * scale, scale)


def norm_back(grad_norm, gain, unit_rows, scale):
    scaled = grad_norm * gain
    return scale * (
        scaled
        - jnp.mean(scaled, axis=-1, keepdims=True)
        - unit_rows * jnp.mean(scaled * unit_rows, axis=-1, keepdims=True)
    )


def adam_update(
    weights, first, second, moving, gradient, step_rate, step_value, decay_rate, ema_keep
):
    bias_one = 1.0 - jnp.power(beta_one, step_value)
    bias_two = 1.0 - jnp.power(beta_two, step_value)
    new_first = beta_one * first + (1.0 - beta_one) * gradient
    new_second = beta_two * second + (1.0 - beta_two) * gradient * gradient
    ratio = new_first / bias_one / (jnp.sqrt(new_second / bias_two) + adam_epsilon)
    new_weights = weights - step_rate * (ratio + decay_rate * weights)
    new_moving = ema_keep * moving + (1.0 - ema_keep) * new_weights
    return (new_weights, new_first, new_second, new_moving)


def on_device(
    residual,
    cotangent,
    lengths,
    owners,
    step_count,
    rates,
    weight_decay,
    ema_decay,
    master,
    moment_one,
    moment_two,
    average,
):
    tensor_count = lax.axis_size("tensor")
    group_count = lax.axis_size(("dp", "chip"))
    local_heads = H // tensor_count
    local_width = local_heads * HD
    local_ff = FF // tensor_count
    rows_here = residual.shape[1]
    group_rows = rows_here * tensor_count
    bucket_size = master.shape[2]
    bounds = bound_list(local_width, local_ff)
    slots = jnp.arange(group_count, dtype=jnp.int32)
    inverse = jnp.sum(
        slots[None, :] * (owners[None, :] == slots[:, None]).astype(jnp.int32), axis=1
    )
    gathered = lax.all_gather(master.astype(jnp.bfloat16), ("dp", "chip"), axis=1, tiled=True)
    flat_params = jnp.take(gathered[0], owners, axis=0).reshape(-1)
    mixer_in = flat_params[bounds[0] : bounds[1]].reshape(D, 3 * local_width)
    mixer_out = flat_params[bounds[1] : bounds[2]].reshape(local_width, D)
    expand_weight = flat_params[bounds[2] : bounds[3]].reshape(D, local_ff)
    shrink_weight = flat_params[bounds[3] : bounds[4]].reshape(local_ff, D)
    mixer_bias = flat_params[bounds[4] : bounds[5]].astype(jnp.float32)
    expand_bias = flat_params[bounds[5] : bounds[6]].astype(jnp.float32)
    small_params = flat_params[bounds[6] : bounds[7]].reshape(6, D).astype(jnp.float32)
    own_rows = residual[0].astype(jnp.float32)
    segment, places = group_layout(lengths[0], group_rows)
    cosine, sines = rotary_tables(places)
    own_unit, own_scale = norm_stats(own_rows)
    normed_one = (own_unit * small_params[0] + small_params[1]).astype(jnp.bfloat16)
    normed_two = (own_unit * small_params[2] + small_params[3]).astype(jnp.bfloat16)
    full_one, full_two = (
        lax.all_gather(normed_one, "tensor", axis=0, tiled=True),
        lax.all_gather(normed_two, "tensor", axis=0, tiled=True),
    )
    projected = matmul(full_one, mixer_in) + mixer_bias
    head_shape = (group_rows, local_heads, HD)
    queries = rotate(projected[:, :local_width].reshape(head_shape), cosine, sines).astype(
        jnp.bfloat16
    )
    keys = rotate(
        projected[:, local_width : 2 * local_width].reshape(head_shape), cosine, sines
    ).astype(jnp.bfloat16)
    values = projected[:, 2 * local_width :].reshape(head_shape).astype(jnp.bfloat16)
    block_rows = min(512, group_rows)
    block_count = group_rows // block_rows
    score_scale = 1.0 / math.sqrt(HD)
    key_index = jnp.arange(group_rows, dtype=jnp.int32)

    def block_scores(start):
        query_block = lax.dynamic_slice_in_dim(queries, start, block_rows, 0)
        scores = (
            jnp.einsum("qhd,khd->hqk", query_block, keys, preferred_element_type=jnp.float32)
            * score_scale
        )
        row_index = start + jnp.arange(block_rows, dtype=jnp.int32)
        row_segment = lax.dynamic_slice_in_dim(segment, start, block_rows, 0)
        allowed = (row_segment[:, None] == segment[None, :]) & (
            key_index[None, :] <= row_index[:, None]
        )
        return (query_block, jnp.where(allowed[None], scores, masked_score))

    def attend_block(index):
        query_block, scores = block_scores(index * block_rows)
        row_top = jnp.max(scores, axis=-1, keepdims=True)
        raised = jnp.exp(scores - row_top)
        totals = jnp.sum(raised, axis=-1, keepdims=True)
        soft_weights = (raised / totals).astype(jnp.bfloat16)
        mixed = jnp.einsum("hqk,khd->qhd", soft_weights, values, preferred_element_type=jnp.float32)
        return (mixed.reshape(block_rows, local_width), (row_top + jnp.log(totals))[..., 0])

    context_blocks, log_blocks = lax.map(attend_block, jnp.arange(block_count, dtype=jnp.int32))
    context = context_blocks.reshape(group_rows, local_width).astype(jnp.bfloat16)
    before = matmul(full_two, expand_weight) + expand_bias
    hidden = jax.nn.gelu(before, approximate=False).astype(jnp.bfloat16)
    branches = lax.psum_scatter(
        matmul(context, mixer_out) + matmul(hidden, shrink_weight),
        "tensor",
        scatter_dimension=0,
        tiled=True,
    )
    output = own_rows + branches + small_params[4] + small_params[5]
    grad_own = cotangent[0].astype(jnp.float32)
    grad_rows = lax.all_gather(cotangent[0], "tensor", axis=0, tiled=True)
    grad_mixer_out = product_rows(context, grad_rows)
    grad_shrink = product_rows(hidden, grad_rows)
    grad_context = product_back(grad_rows, mixer_out).astype(jnp.bfloat16)
    grad_hidden = product_back(grad_rows, shrink_weight)
    gelu_pull = jax.vjp(lambda inner: jax.nn.gelu(inner, approximate=False), before)[1]
    grad_before = gelu_pull(grad_hidden)[0].astype(jnp.bfloat16)
    grad_expand = product_rows(full_two, grad_before)
    grad_expand_bias = jnp.sum(grad_before.astype(jnp.float32), axis=0)
    partial_two = product_back(grad_before, expand_weight)

    def attention_back(carry, index):
        grad_keys, grad_values = carry
        start = index * block_rows
        query_block, scores = block_scores(start)
        log_rows = lax.dynamic_index_in_dim(log_blocks, index, 0, keepdims=False)
        soft_weights = jnp.exp(scores - log_rows[..., None])
        grad_block = lax.dynamic_slice_in_dim(grad_context, start, block_rows, 0).reshape(
            block_rows, local_heads, HD
        )
        grad_weights = jnp.einsum(
            "qhd,khd->hqk", grad_block, values, preferred_element_type=jnp.float32
        )
        delta = jnp.sum(soft_weights * grad_weights, axis=-1, keepdims=True)
        grad_scores = (soft_weights * (grad_weights - delta)).astype(jnp.bfloat16)
        grad_query = (
            jnp.einsum("hqk,khd->qhd", grad_scores, keys, preferred_element_type=jnp.float32)
            * score_scale
        )
        grad_keys = (
            grad_keys
            + jnp.einsum(
                "hqk,qhd->khd", grad_scores, query_block, preferred_element_type=jnp.float32
            )
            * score_scale
        )
        grad_values = grad_values + jnp.einsum(
            "hqk,qhd->khd",
            soft_weights.astype(jnp.bfloat16),
            grad_block,
            preferred_element_type=jnp.float32,
        )
        return ((grad_keys, grad_values), grad_query)

    zero_heads = jnp.zeros(head_shape, jnp.float32)
    (grad_keys, grad_values), grad_query = lax.scan(
        attention_back, (zero_heads, zero_heads), jnp.arange(block_count, dtype=jnp.int32)
    )
    grad_query = grad_query.reshape(head_shape)
    grad_projected = jnp.concatenate(
        [
            rotate(grad_query, cosine, -sines).reshape(group_rows, local_width),
            rotate(grad_keys, cosine, -sines).reshape(group_rows, local_width),
            grad_values.reshape(group_rows, local_width),
        ],
        axis=1,
    ).astype(jnp.bfloat16)
    grad_mixer_in = product_rows(full_one, grad_projected)
    grad_mixer_bias = jnp.sum(grad_projected.astype(jnp.float32), axis=0)
    partial_one = product_back(grad_projected, mixer_in)
    bias_grad = jnp.sum(grad_own, axis=0)
    grad_one, grad_two = (
        lax.psum_scatter(partial_one, "tensor", scatter_dimension=0, tiled=True),
        lax.psum_scatter(partial_two, "tensor", scatter_dimension=0, tiled=True),
    )
    norm_grads = [
        jnp.sum(grad_one * own_unit, axis=0),
        jnp.sum(grad_one, axis=0),
        jnp.sum(grad_two * own_unit, axis=0),
        jnp.sum(grad_two, axis=0),
    ]
    input_grad = (
        grad_own
        + norm_back(grad_one, small_params[0], own_unit, own_scale)
        + norm_back(grad_two, small_params[2], own_unit, own_scale)
    )
    small_grad = jnp.stack(norm_grads + [bias_grad, bias_grad])
    small_grad = lax.psum(small_grad, "tensor")
    flat_grad = jnp.concatenate(
        [
            grad_mixer_in.reshape(-1),
            grad_mixer_out.reshape(-1),
            grad_expand.reshape(-1),
            grad_shrink.reshape(-1),
            grad_mixer_bias,
            grad_expand_bias,
            small_grad.reshape(-1),
            jnp.zeros((group_count * bucket_size - bounds[7],), jnp.float32),
        ]
    )
    stored_grad = jnp.take(flat_grad.reshape(group_count, bucket_size), inverse, axis=0)
    reduced = lax.psum_scatter(stored_grad, ("dp", "chip"), scatter_dimension=0, tiled=True)[0]
    my_bucket = inverse[lax.axis_index(("dp", "chip"))]
    position = my_bucket * bucket_size + jnp.arange(bucket_size, dtype=jnp.int32)
    step_rate = jnp.zeros((bucket_size,), jnp.float32) + rates[0]
    for kind_index in range(1, 8):
        step_rate = jnp.where(position >= bounds[kind_index], rates[kind_index], step_rate)
    step_value = step_count[0].astype(jnp.float32)
    new_weights, new_first, new_second, new_moving = adam_update(
        master[0, 0],
        moment_one[0, 0],
        moment_two[0, 0],
        average[0, 0],
        reduced,
        step_rate,
        step_value,
        weight_decay[0],
        ema_decay[0],
    )
    return (
        output[None],
        input_grad[None],
        new_weights[None, None],
        new_first[None, None],
        new_second[None, None],
        new_moving[None, None],
        reduced[None, None],
    )


LANES = 128
TROWS = 16


def fits(mesh):
    return mesh.shape["dp"] == 4 and mesh.shape["chip"] == 2 and mesh.shape["tensor"] == 4


def device_program(mesh):
    return on_device_fast if fits(mesh) else on_device


CHUNKS = 4
BROWS = 768
QROWS = 1024
FRONT = 128
BACK = 256
FLAT = 12304
HBM = pltpu.HBM


LIGHT = pl.CostEstimate(flops=1, bytes_accessed=1, transcendentals=0)


def params(limit_mb, **more):
    return pltpu.CompilerParams(vmem_limit_bytes=limit_mb * 1024 * 1024, **more)


def part_row(part):
    rows = (16 // CHUNKS) * BROWS
    return (0, rows + 16 * TROWS, 0, rows)[part]


def pack_kernel(bucket_ref, flat_ref, *refs):
    outs, padded, sem = refs[:2], refs[2], refs[3]
    bucket = bucket_ref[0]
    load = pltpu.make_async_copy(flat_ref, padded.at[pl.ds(FRONT, FLAT)], sem)
    load.start()
    padded[pl.ds(0, FRONT)] = jnp.zeros((FRONT, LANES), jnp.float32)
    padded[pl.ds(FRONT + FLAT, BACK)] = jnp.zeros((BACK, LANES), jnp.float32)
    load.wait()
    wide, narrow = 16 // CHUNKS, 12 // CHUNKS

    def take(start, stride):
        return padded[pl.ds(start, 16, stride=stride), :].astype(jnp.bfloat16)

    @pl.when(bucket >= 2)
    def _():
        def step(tile, carry):
            row = pl.multiple_of(tile * 16, 16)
            for panel in range(16):
                part = panel // wide
                at = part_row(part) + (panel % wide) * BROWS
                outs[part // 2][pl.ds(at + row, 16), :] = take(
                    (row - bucket) * 16 + panel + FRONT, 16
                )
            return carry

        lax.fori_loop(0, BROWS // 16, step, 0)

    @pl.when(bucket < 2)
    def _():
        def step(tile, carry):
            row = pl.multiple_of(tile * 16, 16)
            for panel in range(12):
                part = panel // narrow
                at = part_row(part) + (panel % narrow) * QROWS
                outs[part // 2][pl.ds(at + row, 16), :] = take(
                    row * 12 + panel - 16 * bucket + FRONT, 12
                )
            return carry

        lax.fori_loop(0, QROWS // 16, step, 0)

    tails = wide * BROWS

    @pl.when(bucket >= 1)
    def _():
        for panel in range(16):
            outs[0][pl.ds(tails + panel * TROWS, TROWS), :] = take(
                (BROWS - bucket) * 16 + panel + FRONT, 16
            )

    @pl.when(bucket == 0)
    def _():
        for panel in range(16):
            outs[0][pl.ds(tails + panel * TROWS, TROWS), :] = take(
                QROWS * 12 + min(panel, 11) + FRONT, 12
            )


def cut_kernel(starts, *refs):
    count = len(starts)
    copies = [
        pltpu.make_async_copy(
            refs[at].at[pl.ds(start, refs[count + at].shape[0])], refs[count + at], refs[-1].at[at]
        )
        for at, start in enumerate(starts)
    ]
    for copy in copies:
        copy.start()
    for copy in copies:
        copy.wait()


def cut(values, starts, counts):
    return pl.pallas_call(
        functools.partial(cut_kernel, starts),
        out_shape=[jax.ShapeDtypeStruct((count, LANES), jnp.bfloat16) for count in counts],
        in_specs=[pl.BlockSpec(memory_space=pl.ANY)] * len(values),
        out_specs=[pl.BlockSpec(memory_space=pltpu.VMEM)] * len(values),
        scratch_shapes=[pltpu.SemaphoreType.DMA((len(values),))],
        compiler_params=params(60),
        cost_estimate=LIGHT,
        name="cut",
    )(*values)


def chunk_rows():
    return (16 // CHUNKS) * (BROWS + TROWS)


def pack(bucket, flat):
    rows = (32 // CHUNKS) * BROWS
    return pl.pallas_call(
        pack_kernel,
        out_shape=[
            jax.ShapeDtypeStruct((rows + 16 * TROWS, LANES), jnp.bfloat16),
            jax.ShapeDtypeStruct((rows, LANES), jnp.bfloat16),
        ],
        in_specs=[pl.BlockSpec(memory_space=pltpu.SMEM), pl.BlockSpec(memory_space=HBM)],
        out_specs=[pl.BlockSpec(memory_space=pltpu.VMEM)] * 2,
        scratch_shapes=[
            pltpu.VMEM((FRONT + FLAT + BACK, LANES), jnp.float32),
            pltpu.SemaphoreType.DMA,
        ],
        compiler_params=params(24),
        cost_estimate=LIGHT,
        name="pack_params",
    )(bucket, flat)


PLACES = {
    0: (("in", 0, 1024, 0),),
    1: (("in", 1024, 1024, 0),),
    2: (("mix", 0, 512, 0), ("up", 0, 256, 512)),
    3: (("up", 256, 768, 0),),
    4: (("up", 1024, 768, 0),),
    5: (("up", 1792, 256, 0), ("mix", 512, 512, 256)),
    6: (("mix", 1024, 768, 0),),
    7: (("mix", 1792, 768, 0),),
}
NAMES = ("in", "mix", "up", "bias")


def panels_of(bucket):
    return (12 if bucket < 2 else 16) // CHUNKS


MATRICES = {
    "in": (2048, 1536),
    "mix": (2560, 2048),
    "up": (2048, 2048),
    "bias": (TROWS, 2048),
}


def columns(panel):
    return pl.ds(panel * LANES, LANES)


def place_parts(parts, bucket_ref, sources, tails_from, outs, tails_out, scratch):
    staged, tails, load_sems, tail_sem, store_sems = scratch
    main = (16 // CHUNKS) * BROWS
    if tails_from is None:
        for k in range(8):
            pltpu.make_async_copy(
                sources[k].at[pl.ds(main, 16 * TROWS)], tails.at[bucket_ref[k]], tail_sem
            ).start()
        take_tails = pltpu.make_async_copy(tails, tails, tail_sem)
    else:
        take_tails = pltpu.make_async_copy(tails_from, tails, tail_sem)
        take_tails.start()
    for at in range(2):
        for k in range(8):
            pltpu.make_async_copy(
                sources[8 * at + k].at[pl.ds(0 if k % 4 == 3 else part_row(parts[at]), main)],
                staged.at[at, bucket_ref[k]],
                load_sems.at[at, bucket_ref[k]],
            ).start()
    take_tails.wait()
    stores = []

    def store(source, target):
        stores.append(pltpu.make_async_copy(source, target, store_sems.at[len(stores)]))
        stores[-1].start()

    if tails_from is None:
        store(tails, tails_out)
        for panel in range(16):
            store(
                tails.at[7, pl.ds(panel * TROWS, TROWS)],
                outs["bias"].at[pl.ds(0, TROWS), columns(panel)],
            )
    for at, part in enumerate(parts):
        for bucket in range(8):
            held = staged.at[at, bucket]
            pltpu.make_async_copy(held, held, load_sems.at[at, bucket]).wait()
            span = QROWS if bucket < 2 else BROWS
            wide = panels_of(bucket)
            for panel in range(wide):
                if bucket:
                    head = pl.ds(panel * span, TROWS)
                    tail = pl.ds((part * wide + panel) * TROWS, TROWS)
                    staged[at, bucket, head, :] = (
                        staged[at, bucket, head, :] + tails[bucket - 1, tail, :]
                    )
                for name, first, rows, offset in PLACES[bucket]:
                    store(
                        staged.at[at, bucket, pl.ds(panel * span + offset, rows)],
                        outs[name].at[pl.ds(first, rows), columns(part * wide + panel)],
                    )
    return stores


def part_scratch(copies):
    return [
        pltpu.VMEM((2, 8, (16 // CHUNKS) * BROWS, LANES), jnp.bfloat16),
        pltpu.VMEM((8, 16 * TROWS, LANES), jnp.bfloat16),
        pltpu.SemaphoreType.DMA((2, 8)),
        pltpu.SemaphoreType.DMA,
        pltpu.SemaphoreType.DMA((copies,)),
    ]


def copies_of_parts():
    return 2 * sum(len(PLACES[b]) * panels_of(b) for b in range(8))


def unpack_kernel(bucket_ref, *refs):
    outs = dict(zip(NAMES, refs[16:20], strict=True))
    for put in place_parts((0, 1), bucket_ref, refs[:16], None, outs, refs[20], refs[21:]):
        put.wait()


def unpack(buckets, sources):
    shapes = [jax.ShapeDtypeStruct(MATRICES[name], jnp.bfloat16) for name in NAMES]
    tails = jax.ShapeDtypeStruct((8, 16 * TROWS, LANES), jnp.bfloat16)
    return pl.pallas_call(
        unpack_kernel,
        out_shape=[*shapes, tails],
        in_specs=[pl.BlockSpec(memory_space=pltpu.SMEM)] + [pl.BlockSpec(memory_space=HBM)] * 16,
        out_specs=[pl.BlockSpec(memory_space=HBM)] * 5,
        scratch_shapes=part_scratch(copies_of_parts() + 17),
        compiler_params=params(60),
        cost_estimate=LIGHT,
        name="unpack_params",
    )(buckets, *sources)


def unpack_hidden_kernel(width, bucket_ref, *refs):
    sources, tails_from, normed_from, up_bias = refs[:16], refs[16], refs[17], refs[18]
    outs = dict(zip(NAMES[:3], refs[24:27], strict=True))
    hidden_to, slope_to = refs[27:29]
    scratch, (normed, hidden, slope, normed_sem, out_sems) = refs[29:34], refs[34:]
    staged = scratch[0]
    load = pltpu.make_async_copy(normed_from, normed, normed_sem)
    load.start()
    stores = place_parts((2, 3), bucket_ref, sources, tails_from, outs, None, scratch)
    load.wait()
    rows_of_up = [
        (bucket, rows, offset)
        for bucket in range(8)
        for name, _, rows, offset in PLACES[bucket]
        if name == "up"
    ]
    half = up_bias.shape[1] // 2
    puts = []
    for block in range(half // FF_BLOCK):
        slot = block % 2
        if block >= 2:
            for put in puts[2 * block - 4 : 2 * block - 2]:
                put.wait()
        panels = []
        for panel in range(2 * block, 2 * block + 2):
            at, inner = panel // (16 // CHUNKS), panel % (16 // CHUNKS)
            pieces = [
                staged[at, bucket, pl.ds(inner * BROWS + offset, rows), :]
                for bucket, rows, offset in rows_of_up
            ]
            panels.append(jnp.concatenate(pieces, axis=0))
        first = half + block * FF_BLOCK
        gelu(
            matmul(normed[...], jnp.concatenate(panels, axis=1))
            + up_bias[:, first : first + FF_BLOCK],
            hidden.at[slot],
            slope.at[slot],
        )
        for which, (source, target, column) in enumerate(
            ((hidden, hidden_to, width + first), (slope, slope_to, first))
        ):
            puts.append(
                pltpu.make_async_copy(
                    source.at[slot],
                    target.at[:, pl.ds(column, FF_BLOCK)],
                    out_sems.at[slot, which],
                )
            )
            puts[-1].start()
    for put in [*puts[-4:], *stores]:
        put.wait()


def unpack_hidden(width, buckets, sources, before, normed, up_bias, halves):
    rows = normed.shape[0]
    hidden, slope = halves
    results = pl.pallas_call(
        functools.partial(unpack_hidden_kernel, width),
        out_shape=[jax.ShapeDtypeStruct(v.shape, v.dtype) for v in (*before[:3], hidden, slope)],
        in_specs=[pl.BlockSpec(memory_space=pltpu.SMEM)]
        + [pl.BlockSpec(memory_space=HBM)] * 18
        + [pl.BlockSpec(memory_space=pltpu.VMEM)]
        + [pl.BlockSpec(memory_space=HBM)] * 5,
        out_specs=[pl.BlockSpec(memory_space=HBM)] * 5,
        input_output_aliases={20 + at: at for at in range(5)},
        scratch_shapes=part_scratch(copies_of_parts())
        + [
            pltpu.VMEM(normed.shape, normed.dtype),
            pltpu.VMEM((2, rows, FF_BLOCK), jnp.bfloat16),
            pltpu.VMEM((2, rows, FF_BLOCK), jnp.float32),
            pltpu.SemaphoreType.DMA,
            pltpu.SemaphoreType.DMA((2, 2)),
        ],
        compiler_params=params(60),
        cost_estimate=LIGHT,
        name="unpack_hidden",
    )(buckets, *sources, before[4], normed, up_bias, *before[:3], hidden, slope)
    return results[:3], results[3], results[4]


GRAD_ROWS = 256
PAIR = 2 * GRAD_ROWS
IN_STEPS, OUT_STEPS, UP_STEPS, DOWN_STEPS = 4, 1, 4, 4
GRAD_EDGES = (0, 4, 5, 9, 13)
GRAD_STEPS = 13
KEPT, NEAR, FAR = 0, 1, 2


def weight_grad_kernel(table, *refs):
    lefts, projected, late, outs = refs[:8], refs[8:10], refs[10:14], refs[14:22]
    wide32, wide16, tail32, tail16, held, sems, tail_sem, late_sem = refs[22:]
    step = pl.program_id(0)
    core = table[0]
    main = (16 // CHUNKS) * BROWS

    def bucket_of(block):
        return jnp.where(block < 2 * IN_STEPS, block // 4, (block - 2) // 3)

    def kind_of(part, bucket):
        return table[1 + 16 * part + bucket], table[9 + 16 * part + bucket]

    def targets(part, kind, place):
        near = kind == NEAR
        return [
            (jnp.logical_and(near, place == 0), True, outs[3 * part]),
            (jnp.logical_and(near, place == 1), True, outs[3 * part + 1]),
            (kind == FAR, True, outs[3 * part + 2].at[jnp.minimum(place, 1)]),
            (jnp.logical_and(kind == KEPT, place >= 2), False, outs[6].at[part, jnp.clip(place - 2, 0, 1)]),
            (jnp.logical_and(kind == KEPT, place < 2), False, outs[7].at[part, jnp.minimum(place, 1)]),
        ]

    def wait(at):
        slot = lax.rem(at, 2)
        for panels, mine in ((3, at < IN_STEPS), (4, at >= IN_STEPS)):

            @pl.when(mine)
            def _(panels=panels):
                rows = pl.ds(0, panels * GRAD_ROWS)
                for half in range(2):
                    bucket = bucket_of(2 * at + half)
                    for part in range(2):
                        kind, _ = kind_of(part, bucket)
                        sem = sems.at[slot, part, half]

                        @pl.when(kind == KEPT)
                        def _(part=part, sem=sem):
                            place = outs[7].at[part, 0, rows]
                            pltpu.make_async_copy(place, place, sem).wait()

                        @pl.when(kind != KEPT)
                        def _(part=part, sem=sem):
                            place = outs[3 * part].at[rows]
                            pltpu.make_async_copy(place, place, sem).wait()

    @pl.when(step >= 2)
    def _():
        wait(step - 2)

    late_copies = []
    for at, source in enumerate(late):
        width = held.shape[2]
        if source.shape[1] > width:
            source = source.at[:, pl.ds(pl.multiple_of(core * width, width), width)]
        late_copies.append(pltpu.make_async_copy(source, held.at[at], late_sem.at[at]))

    @pl.when(step == 0)
    def _():
        for copy in late_copies:
            copy.start()
        tail32[...] = jnp.zeros_like(tail32)
        tail16[...] = jnp.zeros_like(tail16)

    @pl.when(step == GRAD_EDGES[1])
    def _():
        for copy in late_copies[:2]:
            copy.wait()

    @pl.when(step == GRAD_EDGES[2])
    def _():
        for copy in late_copies[2:]:
            copy.wait()

    def multiply(pair, right, panels, span):
        slot = lax.rem(step, 2)
        if right == 0:
            own, other = projected[0][...], projected[1][...]
        else:
            own, other = held[2 * right - 2], held[2 * right - 1]
        wide32[slot, :, pl.ds(0, 2 * panels * LANES)] = product_rows(
            lefts[2 * pair][...], own
        ) + product_rows(lefts[2 * pair + 1][...], other)
        for half in range(2):
            block = 2 * step + half
            bucket = bucket_of(block)
            before = jnp.maximum(bucket - 1, 0)
            if pair == 0:
                first, offset = block == 4, lax.rem(block, 4)
            else:
                offset = lax.rem(block - 2, 3)
                first = offset == 0
            offset = pl.multiple_of(offset * GRAD_ROWS, GRAD_ROWS)
            for part in range(2):
                kind, place = kind_of(part, bucket)

                @pl.when(kind != KEPT)
                def _(half=half, part=part):
                    for panel in range(panels):
                        tile = wide32[
                            slot, pl.ds(half * GRAD_ROWS, GRAD_ROWS), columns(part * panels + panel)
                        ]
                        rows = pl.ds(panel * GRAD_ROWS, GRAD_ROWS)
                        wide16[slot, part, half, rows, :] = tile.astype(jnp.bfloat16)

                for is_it, short, target in targets(part, kind, place):

                    @pl.when(is_it)
                    def _(half=half, part=part, short=short, target=target, offset=offset):
                        for panel in range(panels):
                            if short:
                                rows = pl.ds(panel * GRAD_ROWS, GRAD_ROWS)
                                source = wide16.at[slot, part, half, rows]
                            else:
                                rows = pl.ds(half * GRAD_ROWS, GRAD_ROWS)
                                source = wide32.at[slot, rows, columns(part * panels + panel)]
                            pltpu.make_async_copy(
                                source,
                                target.at[pl.ds(panel * span + offset, GRAD_ROWS)],
                                sems.at[slot, part, half],
                            ).start()

            @pl.when(first)
            def _(half=half, before=before):
                for part in range(2):
                    for panel in range(panels):
                        tile = wide32[
                            slot, pl.ds(half * GRAD_ROWS, TROWS), columns(part * panels + panel)
                        ]
                        rows = pl.ds(panel * TROWS, TROWS)
                        tail32[part, before, rows, :] = tile
                        tail16[part, before, rows, :] = tile.astype(jnp.bfloat16)

    for pair, right in enumerate((0, 1, 2, 1)):

        @pl.when(jnp.logical_and(step >= GRAD_EDGES[pair], step < GRAD_EDGES[pair + 1]))
        def _(pair=pair, right=right):
            multiply(pair, right, *((3, QROWS) if pair == 0 else (4, BROWS)))

    @pl.when(step == GRAD_STEPS - 1)
    def _():
        def tails(act):
            for part in range(2):
                for bucket in range(8):
                    for is_it, short, place in targets(part, *kind_of(part, bucket)):

                        @pl.when(is_it)
                        def _(part=part, bucket=bucket, short=short, place=place):
                            stage = tail16 if short else tail32
                            act(
                                pltpu.make_async_copy(
                                    stage.at[part, bucket],
                                    place.at[pl.ds(main, stage.shape[2])],
                                    tail_sem.at[part, bucket],
                                )
                            )

        tails(lambda copy: copy.start())
        wait(step - 1)
        wait(step)
        tails(lambda copy: copy.wait())


def weight_grads(table, lefts, rights):
    tokens = lefts[0].shape[0]

    def columns_at(first, count, ahead):
        return pl.BlockSpec(
            (tokens, PAIR), lambda i, table: (0, ahead + jnp.clip(i - first, 0, count - 1))
        )

    left_specs = [
        columns_at(first, last - first, ahead)
        for first, last, ahead in zip(GRAD_EDGES, GRAD_EDGES[1:], (0, 0, 0, 1), strict=False)
        for _ in range(2)
    ]
    half = (tokens, rights[0].shape[1] // 2)
    right_specs = [pl.BlockSpec(half, lambda i, table: (0, table[0]))] * 2
    rows = chunk_rows()
    near = jax.ShapeDtypeStruct((rows, LANES), jnp.bfloat16)
    short = jax.ShapeDtypeStruct((2, rows, LANES), jnp.bfloat16)
    wide = jax.ShapeDtypeStruct((2, 2, rows, LANES), jnp.float32)
    return pl.pallas_call(
        weight_grad_kernel,
        out_shape=[near, near, short] * 2 + [wide] * 2,
        grid_spec=pltpu.PrefetchScalarGridSpec(
            num_scalar_prefetch=1,
            grid=(GRAD_STEPS,),
            in_specs=left_specs + right_specs + [pl.BlockSpec(memory_space=HBM)] * 4,
            out_specs=[pl.BlockSpec(memory_space=HBM)] * 8,
            scratch_shapes=[
                pltpu.VMEM((2, PAIR, 8 * LANES), jnp.float32),
                pltpu.VMEM((2, 2, 2, 4 * GRAD_ROWS, LANES), jnp.bfloat16),
                pltpu.VMEM((2, 8, 4 * TROWS, LANES), jnp.float32),
                pltpu.VMEM((2, 8, 4 * TROWS, LANES), jnp.bfloat16),
                pltpu.VMEM((4, tokens, 8 * LANES), jnp.bfloat16),
                pltpu.SemaphoreType.DMA((2, 2, 2)),
                pltpu.SemaphoreType.DMA((2, 8)),
                pltpu.SemaphoreType.DMA((4,)),
            ],
        ),
        compiler_params=params(60),
        cost_estimate=LIGHT,
        name="weight_grads",
    )(table, *lefts, *rights)


NORM_COLUMNS = 512


def norm_grad_kernel(
    core, grad_projected, mixer_in, own_before, own_up, rest_before, rest_up, rows, centre, scale,
    gains, partial, sums,
):
    one = product_back(grad_projected[...], mixer_in[...])
    two = product_back(own_before[...], own_up[...]) + product_back(rest_before[...], rest_up[...])
    unit = (rows[...].astype(jnp.float32) - centre[...]) * scale[...]
    partial[...] = (one * gains[0:1, :] + two * gains[1:2, :]).astype(jnp.bfloat16)
    for at, value in enumerate((one * unit, one, two * unit, two)):
        sums[at : at + 1, :] = jnp.sum(value, axis=0, keepdims=True)


def norm_grad(core, grad_projected, mixer_in, own_before, rest_before, up, rows, centre, scale, gains):
    tokens = rows.shape[0]
    half = up.shape[1] // 2

    def whole(value):
        return pl.BlockSpec(value.shape, lambda i, core: (0, 0))

    block = pl.BlockSpec((tokens, NORM_COLUMNS), lambda i, core: (0, i))
    return pl.pallas_call(
        norm_grad_kernel,
        out_shape=[
            jax.ShapeDtypeStruct((tokens, D), jnp.bfloat16),
            jax.ShapeDtypeStruct((4, D), jnp.float32),
        ],
        grid_spec=pltpu.PrefetchScalarGridSpec(
            num_scalar_prefetch=1,
            grid=(D // NORM_COLUMNS,),
            in_specs=[
                whole(grad_projected),
                pl.BlockSpec((NORM_COLUMNS, mixer_in.shape[1]), lambda i, core: (i, 0)),
                whole(own_before),
                pl.BlockSpec((NORM_COLUMNS, half), lambda i, core: (i, core[0])),
                whole(rest_before),
                pl.BlockSpec((NORM_COLUMNS, half), lambda i, core: (i, 1 - core[0])),
                block,
                whole(centre),
                whole(scale),
                pl.BlockSpec((2, NORM_COLUMNS), lambda i, core: (0, i)),
            ],
            out_specs=[block, pl.BlockSpec((4, NORM_COLUMNS), lambda i, core: (0, i))],
        ),
        compiler_params=params(60),
        cost_estimate=LIGHT,
        name="norm_grad",
    )(core, grad_projected, mixer_in, own_before, up, rest_before, up, rows, centre, scale, gains)


ADAM_ROWS = 3080


def adam_kernel(table, scalar_ref, rate_ref, *refs):
    stays, near, far, small = refs[:2], refs[2:6], refs[6:10], refs[10]
    weights, first, second, moving = refs[11:15]
    new_weights, new_first, new_second, new_moving, reduced = refs[15:20]
    held32, held16, flat, sems = refs[20:]
    bucket, core = table[0], table[1]
    wide, narrow = 16 // CHUNKS, 12 // CHUNKS
    main = wide * BROWS
    turn_at = pl.program_id(0)

    def put(part, row, start, stride):
        rows = pl.ds(row, 16)
        value = held32[part, rows, :] + (
            held16[0, part, rows, :].astype(jnp.float32) + held16[1, part, rows, :].astype(jnp.float32)
        )
        flat[pl.ds(start, 16, stride=stride), :] = value

    @pl.when(turn_at == 0)
    def _():
        loads = []
        for at in range(4):
            place = 2 * (core if at < 2 else 1 - core) + at % 2
            source = stays[at // 2].at[at % 2, at // 2]
            loads.append(pltpu.make_async_copy(source, held32.at[place], sems.at[0, at]))
            for which, came in enumerate((near, far)):
                loads.append(
                    pltpu.make_async_copy(came[at], held16.at[which, place], sems.at[1 + which, at])
                )
        for load in loads:
            load.start()
        for load in loads:
            load.wait()

        @pl.when(bucket >= 1)
        def _():
            for panel in range(16):
                put(
                    panel // wide,
                    main + (panel % wide) * TROWS,
                    (BROWS - bucket) * 16 + panel + FRONT,
                    16,
                )

        @pl.when(bucket == 0)
        def _():
            for panel in range(12):
                put(
                    panel // narrow,
                    main + (panel % narrow) * TROWS,
                    QROWS * 12 + panel + FRONT,
                    12,
                )

        @pl.when(bucket == 7)
        def _():
            flat[pl.ds(FRONT + FLAT - LANES, LANES), :] = small[...]

    @pl.when(bucket >= 2)
    def _():
        def reach(at):
            tiles = (at * (ADAM_ROWS // 8) // 2 + 23) // 16
            return jnp.clip(jnp.where(at > 0, tiles, 0), 0, BROWS // 16)

        def step(tile, carry):
            row = pl.multiple_of(tile * 16, 16)
            for panel in range(16):
                put(
                    panel // wide,
                    (panel % wide) * BROWS + row,
                    (row - bucket) * 16 + panel + FRONT,
                    16,
                )
            return carry

        lax.fori_loop(reach(turn_at), reach(turn_at + 1), step, 0)

    @pl.when(bucket < 2)
    def _():
        def reach(at):
            tiles = (at * ADAM_ROWS + 16) // 192 + 1
            return jnp.clip(jnp.where(at > 0, tiles, 0), 0, QROWS // 16)

        def step(tile, carry):
            row = pl.multiple_of(tile * 16, 16)
            for panel in range(12):
                put(
                    panel // narrow,
                    (panel % narrow) * QROWS + row,
                    row * 12 + panel - 16 * bucket + FRONT,
                    12,
                )
            return carry

        lax.fori_loop(reach(turn_at), reach(turn_at + 1), step, 0)

    start = turn_at * ADAM_ROWS
    gradient = flat[pl.ds(pl.multiple_of(FRONT + start, 8), ADAM_ROWS), :]
    reduced[...] = gradient
    scale_one, scale_two, decay, keep = (scalar_ref[at] for at in range(4))
    one = beta_one * first[...] + (1.0 - beta_one) * gradient
    two = beta_two * second[...] + (1.0 - beta_two) * gradient * gradient
    new_first[...] = one
    new_second[...] = two
    old = weights[...]
    change = (one * scale_one) / (jnp.sqrt(two * scale_two) + adam_epsilon) + decay * old

    def write(rate):
        fresh = old - rate * change
        new_weights[...] = fresh
        new_moving[...] = keep * moving[...] + (1.0 - keep) * fresh

    first_row = bucket * FLAT + start
    bounds = [bound // LANES for bound in bound_list(512, 2048)[1:]]
    kinds = [sum(jnp.where(at >= bound, 1, 0) for bound in bounds) for at in (first_row, first_row + ADAM_ROWS - 1)]

    @pl.when(kinds[0] == kinds[1])
    def _():
        write(rate_ref[kinds[0]])

    @pl.when(kinds[0] != kinds[1])
    def _():
        row = first_row + lax.broadcasted_iota(jnp.int32, (ADAM_ROWS, LANES), 0)
        rate = jnp.full((ADAM_ROWS, LANES), rate_ref[0], jnp.float32)
        for kind, bound in enumerate(bounds):
            rate = jnp.where(row >= bound, rate_ref[kind + 1], rate)
        write(rate)


def adam(table, scalars, rates, stays, near, far, small, state):
    steps = -(-FLAT // ADAM_ROWS)
    block = pl.BlockSpec((ADAM_ROWS, LANES), lambda i: (i, 0))
    return pl.pallas_call(
        adam_kernel,
        grid=(steps,),
        out_shape=[jax.ShapeDtypeStruct((FLAT, LANES), jnp.float32)] * 5,
        in_specs=[pl.BlockSpec(memory_space=pltpu.SMEM)] * 3
        + [pl.BlockSpec(memory_space=HBM)] * 2
        + [pl.BlockSpec(memory_space=pl.ANY)] * 8
        + [pl.BlockSpec(memory_space=pltpu.VMEM)]
        + [block] * 4,
        out_specs=[block] * 5,
        scratch_shapes=[
            pltpu.VMEM((4, chunk_rows(), LANES), jnp.float32),
            pltpu.VMEM((2, 4, chunk_rows(), LANES), jnp.bfloat16),
            pltpu.VMEM((FRONT + max(steps * ADAM_ROWS, FLAT + BACK), LANES), jnp.float32),
            pltpu.SemaphoreType.DMA((3, 4)),
        ],
        compiler_params=params(60),
        cost_estimate=LIGHT,
        name="adam",
    )(table, scalars, rates, *stays, *near, *far, small, *state)


def finish_kernel(terms, rows, grads, out):
    scaled = terms[0].astype(jnp.float32)
    for at in range(1, terms.shape[0]):
        scaled = scaled + terms[at].astype(jnp.float32)
    unit, scale = norm_stats(rows[...].astype(jnp.float32))
    out[...] = grads[...].astype(jnp.float32) + scale * (
        scaled
        - jnp.mean(scaled, axis=-1, keepdims=True)
        - unit * jnp.mean(scaled * unit, axis=-1, keepdims=True)
    )


def finish(terms, rows, grads):
    count, width = rows.shape
    height = count // 2
    block = pl.BlockSpec((height, width), lambda i: (i, 0))
    return pl.pallas_call(
        finish_kernel,
        grid=(count // height,),
        out_shape=jax.ShapeDtypeStruct((count, width), jnp.float32),
        in_specs=[
            pl.BlockSpec((terms.shape[0], height, width), lambda i: (0, i, 0)),
            block,
            block,
        ],
        out_specs=block,
        compiler_params=params(60),
        cost_estimate=LIGHT,
        name="finish",
    )(terms, rows, grads)


FF_BLOCK = 256


def gelu(before, hidden, slope):
    half = 0.5 + 0.5 * lax.erf(before * math.sqrt(0.5))
    hidden[...] = (before * half).astype(jnp.bfloat16)
    slope[...] = half + before * jnp.exp(-0.5 * before * before) * (1.0 / math.sqrt(2.0 * math.pi))


def hidden_kernel(normed, up, up_bias, hidden, slope):
    gelu(matmul(normed[...], up[...]) + up_bias[...], hidden, slope)


def hidden_layer(width, normed, up, up_bias):
    rows, units = normed.shape[0], up.shape[1]
    block = pl.BlockSpec((rows, FF_BLOCK), lambda i: (0, i))
    return pl.pallas_call(
        hidden_kernel,
        grid=(units // FF_BLOCK // 2,),
        out_shape=[
            jax.ShapeDtypeStruct((rows, width + units), jnp.bfloat16),
            jax.ShapeDtypeStruct((rows, units), jnp.float32),
        ],
        in_specs=[
            pl.BlockSpec(memory_space=pltpu.VMEM),
            pl.BlockSpec((D, FF_BLOCK), lambda i: (0, i)),
            pl.BlockSpec((1, FF_BLOCK), lambda i: (0, i)),
        ],
        out_specs=[pl.BlockSpec((rows, FF_BLOCK), lambda i: (0, i + width // FF_BLOCK)), block],
        compiler_params=params(60),
        cost_estimate=LIGHT,
        name="hidden_layer",
    )(normed, up, up_bias)


def hidden_back_kernel(half, grads, down, slope, grad_before, grad_bias):
    rounded = (slope[...] * product_back(grads[...], down[...])).astype(jnp.bfloat16)
    grad_before[...] = rounded
    grad_bias[...] = jnp.sum(rounded.astype(jnp.float32), axis=0, keepdims=True)


def hidden_back(half, grads, mix, slope):
    rows, units = slope.shape
    first = (mix.shape[0] - units) // FF_BLOCK
    steps = units // FF_BLOCK // 2
    return pl.pallas_call(
        hidden_back_kernel,
        out_shape=[
            jax.ShapeDtypeStruct((rows, units // 2), jnp.bfloat16),
            jax.ShapeDtypeStruct((1, units // 2), jnp.float32),
        ],
        grid_spec=pltpu.PrefetchScalarGridSpec(
            num_scalar_prefetch=1,
            grid=(steps,),
            in_specs=[
                pl.BlockSpec((rows, D), lambda i, half: (0, 0)),
                pl.BlockSpec((FF_BLOCK, D), lambda i, half: (first + half[0] * steps + i, 0)),
                pl.BlockSpec((rows, FF_BLOCK), lambda i, half: (0, half[0] * steps + i)),
            ],
            out_specs=[
                pl.BlockSpec((rows, FF_BLOCK), lambda i, half: (0, i)),
                pl.BlockSpec((1, FF_BLOCK), lambda i, half: (0, i)),
            ],
        ),
        compiler_params=params(60),
        cost_estimate=LIGHT,
        name="hidden_back",
    )(half, grads, mix, slope)


def norm_kernel(rows, gains, one, two, centre, scale):
    values = rows[...].astype(jnp.float32)
    middle = jnp.mean(values, axis=-1, keepdims=True)
    values = values - middle
    factor = lax.rsqrt(jnp.mean(values * values, axis=-1, keepdims=True) + norm_epsilon)
    unit = values * factor
    one[...] = (unit * gains[0:1, :] + gains[1:2, :]).astype(jnp.bfloat16)
    two[...] = (unit * gains[2:3, :] + gains[3:4, :]).astype(jnp.bfloat16)
    centre[...] = middle
    scale[...] = factor


def norms(rows, small_params):
    count, width = rows.shape
    height = 128
    block = pl.BlockSpec((height, width), lambda i: (i, 0))
    column = pl.BlockSpec((height, 1), lambda i: (i, 0))
    return pl.pallas_call(
        norm_kernel,
        grid=(count // height,),
        out_shape=[jax.ShapeDtypeStruct((count, width), jnp.bfloat16)] * 2
        + [jax.ShapeDtypeStruct((count, 1), jnp.float32)] * 2,
        in_specs=[block, pl.BlockSpec(memory_space=pltpu.VMEM)],
        out_specs=[block, block, column, column],
        compiler_params=params(60),
        cost_estimate=LIGHT,
        name="norms",
    )(rows, small_params)


QUERY_BLOCK = 256


def turn(values, tables, sign):
    plain, lower, upper = tables
    half_rot = ROT // 2
    return (
        values * plain
        + pltpu.roll(values, HD - half_rot, 1) * (sign * lower)
        + pltpu.roll(values, half_rot, 1) * (sign * upper)
    )


def block_scores(query, keys, begins, first, first_key):
    scores = product_back(query, keys) * (1.0 / math.sqrt(HD))
    row_index = first + lax.broadcasted_iota(jnp.int32, scores.shape, 0)
    key_index = first_key + lax.broadcasted_iota(jnp.int32, scores.shape, 1)
    allowed = (key_index <= row_index) & (key_index >= begins)
    return jnp.where(allowed, scores, masked_score)


HEAD_PAIR = 2 * HD


def attend_kernel(
    normed, queries_in, keys_in, values_in, bias, plain, lower, upper, begins, _, context, turned, logs
):
    rows = normed.shape[0]
    width = bias.shape[1] // 3
    first_column = pl.program_id(0) * HEAD_PAIR
    tables = (plain[...], lower[...], upper[...])
    for part, weights in enumerate((queries_in, keys_in, values_in)):
        projected = matmul(normed[...], weights[...])
        projected = projected + bias[
            :, pl.ds(pl.multiple_of(part * width + first_column, HEAD_PAIR), HEAD_PAIR)
        ]
        for head in range(2):
            value = projected[:, head * HD : (head + 1) * HD]
            if part < 2:
                value = turn(value, tables, 1.0)
            turned[part, :, head * HD : (head + 1) * HD] = value.astype(jnp.bfloat16)

    def one_head(head, carry):
        column = pl.ds(pl.multiple_of(head * HD, HD), HD)
        queries, keys, values = (turned[part, :, column] for part in range(3))
        for first in range(0, rows, QUERY_BLOCK):
            last = first + QUERY_BLOCK
            mine = slice(first, last)
            seen = slice(max(0, first - rows // 2), last)
            scores = block_scores(queries[mine], keys[seen], begins[mine, :], first, seen.start)
            top = jnp.max(scores, axis=-1, keepdims=True)
            raised = jnp.exp(scores - top)
            total = jnp.sum(raised, axis=-1, keepdims=True)
            rounded = (raised / total).astype(jnp.bfloat16)
            context[mine, column] = matmul(rounded, values[seen]).astype(jnp.bfloat16)
            logs[head, mine, :] = top + jnp.log(total)
        return carry

    lax.fori_loop(0, 2, one_head, 0)


def attend(normed, mixer_in, bias, tables, begins, mixed):
    rows, width = normed.shape[0], mixer_in.shape[1] // 3
    pairs = width // HEAD_PAIR
    whole = pl.BlockSpec(memory_space=pltpu.VMEM)

    def weights(part):
        return pl.BlockSpec((mixer_in.shape[0], HEAD_PAIR), lambda i: (0, part * pairs + i))

    return pl.pallas_call(
        attend_kernel,
        grid=(pairs,),
        out_shape=[
            jax.ShapeDtypeStruct(mixed.shape, mixed.dtype),
            jax.ShapeDtypeStruct((3, rows, width), jnp.bfloat16),
            jax.ShapeDtypeStruct((width // HD, rows, 1), jnp.float32),
        ],
        in_specs=[whole, weights(0), weights(1), weights(2)]
        + [whole] * 5
        + [pl.BlockSpec(memory_space=HBM)],
        out_specs=[
            pl.BlockSpec((rows, HEAD_PAIR), lambda i: (0, i)),
            pl.BlockSpec((3, rows, HEAD_PAIR), lambda i: (0, 0, i)),
            pl.BlockSpec((2, rows, 1), lambda i: (i, 0, 0)),
        ],
        input_output_aliases={9: 0},
        compiler_params=params(40),
        cost_estimate=LIGHT,
        name="attend",
    )(normed, mixer_in, mixer_in, mixer_in, bias, *tables, begins, mixed)


def attend_back_kernel(
    turned, logs, plain, lower, upper, begins, grad_context, grad_projected, key_sum, value_sum
):
    rows, width = grad_context.shape
    score_scale = 1.0 / math.sqrt(HD)

    def one_head(head, carry):
        cols = [pl.ds(pl.multiple_of(part * width + head * HD, HD), HD) for part in range(3)]
        queries, keys, values = (turned[part, :, cols[0]] for part in range(3))
        key_sum[...] = jnp.zeros_like(key_sum)
        value_sum[...] = jnp.zeros_like(value_sum)
        for first in range(0, rows, QUERY_BLOCK):
            last = first + QUERY_BLOCK
            mine = slice(first, last)
            query = queries[mine]
            seen = slice(max(0, first - rows // 2), last)
            scores = block_scores(query, keys[seen], begins[mine, :], first, seen.start)
            soft = jnp.exp(scores - logs[head, mine, :])
            grad_mine = grad_context[mine, cols[0]]
            grad_soft = product_back(grad_mine, values[seen])
            delta = jnp.sum(soft * grad_soft, axis=-1, keepdims=True)
            grad_scores = (soft * (grad_soft - delta)).astype(jnp.bfloat16)
            grad_query = matmul(grad_scores, keys[seen]) * score_scale
            tables = (plain[mine, :], lower[mine, :], upper[mine, :])
            grad_projected[mine, cols[0]] = turn(grad_query, tables, -1.0).astype(jnp.bfloat16)
            key_sum[seen, :] += product_rows(grad_scores, query)
            value_sum[seen, :] += product_rows(soft.astype(jnp.bfloat16), grad_mine)
        tables = (plain[...], lower[...], upper[...])
        grad_projected[:, cols[1]] = turn(key_sum[...] * score_scale, tables, -1.0).astype(
            jnp.bfloat16
        )
        grad_projected[:, cols[2]] = value_sum[...].astype(jnp.bfloat16)
        return carry

    lax.fori_loop(0, width // HD, one_head, 0)


def attend_back(turned, logs, tables, begins, grad_context):
    rows, width = grad_context.shape
    whole = pl.BlockSpec(memory_space=pltpu.VMEM)
    return pl.pallas_call(
        attend_back_kernel,
        out_shape=jax.ShapeDtypeStruct((rows, 3 * width), jnp.bfloat16),
        in_specs=[whole] * 7,
        out_specs=whole,
        scratch_shapes=[pltpu.VMEM((rows, HD), jnp.float32)] * 2,
        compiler_params=params(36),
        cost_estimate=LIGHT,
        name="attend_back",
    )(turned, logs, *tables, begins, grad_context)


def rope_tables(places):
    half_rot = ROT // 2
    frequency = rope_base ** (-2.0 * jnp.arange(half_rot, dtype=jnp.float32) / ROT)
    angles = places[:, None] * frequency[None, :]
    cosine, sines = jnp.cos(angles), jnp.sin(angles)
    rest = jnp.zeros((places.shape[0], HD - ROT), jnp.float32)
    none = jnp.zeros_like(sines)
    return (
        jnp.concatenate([cosine, cosine, rest + 1.0], axis=1),
        jnp.concatenate([-sines, none, rest], axis=1),
        jnp.concatenate([none, sines, rest], axis=1),
    )


def along_x(value):
    return lax.ppermute(value, "dp", [(i, i ^ 1) for i in range(4)])


def along_y(value):
    return lax.ppermute(value, "dp", [(i, i ^ 2) for i in range(4)])


def along_line(value, bit):
    return lax.ppermute(value, "tensor", [(i, i ^ bit) for i in range(4)])


def along(bit, value):
    return lax.ppermute(
        value, ("dp", "chip"), [(i, (i // 2 ^ bit) * 2 + (i % 2 ^ 1)) for i in range(8)]
    )


def across(value):
    return lax.ppermute(value, "chip", [(0, 1), (1, 0)])


def line_blocks(partial):
    count = lax.axis_size("tensor")
    rows = partial.shape[0] // count
    return lax.all_to_all(partial.reshape(count, rows, partial.shape[1]), "tensor", 0, 0)


def on_device_fast(
    residual,
    cotangent,
    lengths,
    owners,
    step_count,
    rates,
    weight_decay,
    ema_decay,
    master,
    moment_one,
    moment_two,
    average,
):
    local_width = HD * H // lax.axis_size("tensor")
    group_rows = residual.shape[1] * lax.axis_size("tensor")
    slots = jnp.arange(8, dtype=jnp.int32)
    inverse = jnp.sum(
        slots[None, :] * (owners[None, :] == slots[:, None]).astype(jnp.int32), axis=1
    )
    data_index, core, here = lax.axis_index("dp"), lax.axis_index("chip"), lax.axis_index("tensor")
    partners = jnp.stack([(data_index ^ j) * 2 + (core ^ c) for c in range(2) for j in range(4)])
    buckets = jnp.sum(
        jnp.where(partners[:, None] == slots[None, :], inverse[None, :], 0), axis=1
    ).astype(jnp.int32)
    partner_of = jnp.sum(
        jnp.where(buckets[None, :] == slots[:, None], slots[None, :], 0), axis=1
    )
    hop, other = partner_of % 4, partner_of // 4
    grad_table = [core[None]]
    for first, second in ((hop % 2, hop // 2), (hop // 2, hop % 2)):
        grad_table.append(first * (1 + second))
        grad_table.append(other + 2 * second * (1 - first))
    grad_table = jnp.concatenate(grad_table).astype(jnp.int32)

    full_rows = lax.all_gather(residual[0], "tensor", axis=0, tiled=True)
    grad_rows = lax.all_gather(cotangent[0], "tensor", axis=0, tiled=True)
    own_rows = residual[0].astype(jnp.float32)

    def order(*values):
        return lax.optimization_barrier(values)

    rank = jnp.arange(lengths.shape[1], dtype=jnp.int32)
    seq_ends = jnp.sum(jnp.where(rank[None, :] <= rank[:, None], lengths[0][None, :], 0), axis=1)
    token_index = jnp.arange(group_rows, dtype=jnp.int32)
    passed = (token_index[:, None] >= seq_ends[None, :]).astype(jnp.int32)
    begins = jnp.sum(passed * lengths[0][None, :], axis=1)
    tables = rope_tables((token_index - begins).astype(jnp.float32))
    begins = begins[:, None]

    one, two = pack(buckets[:1], master.reshape(FLAT, LANES))
    one_x, one_y, one_own = order(along_x(one), along_y(one), across(one))

    def from_far(first, second, from_x, from_y):
        rows = (16 // CHUNKS) * BROWS
        start = part_row(second)
        count = start if first == 0 else rows
        if first == 0:
            from_y, from_x = from_y[:count], from_x[start : start + rows]
        else:
            from_y, from_x = cut([from_y, from_x], (0, start), (count, rows))
        return [along_x(from_y), along_y(from_x)]

    far = from_far(0, 1, one_x, one_y)
    near_x, near_y, two_own = across(one_x), across(one_y), across(two)
    far, near_x, near_y, two_own, two, tables, begins = order(
        far, near_x, near_y, two_own, two, tables, begins
    )

    two_x, two_y = along_x(two), along_y(two)
    far_other = [across(value) for value in far]
    sources = []
    for part in range(2):
        sources += [one, one_x, one_y, far[part], one_own, near_x, near_y, far_other[part]]
    weights = unpack(buckets, sources)
    weights, full_rows = order(weights, full_rows)
    flat_bias = weights[3][:8].reshape(-1).astype(jnp.float32)
    mixer_bias = flat_bias[: 3 * local_width]
    expand_bias = flat_bias[3 * local_width : 3 * local_width + D]
    small_params = flat_bias[3 * local_width + D : 3 * local_width + 7 * D].reshape(6, D)
    full_one, full_two, centre, scale = norms(full_rows, small_params)
    hidden_half = hidden_layer(local_width, full_two, weights[2], expand_bias[None])
    two_x, two_y, full_rows, full_one, full_two, weights, hidden_half = order(
        two_x, two_y, full_rows, full_one, full_two, weights, hidden_half
    )
    other_rows = across(full_rows)

    far = from_far(2, 3, two_x, two_y)
    near_x, near_y = across(two_x), across(two_y)
    other_one, other_two, _, _ = norms(other_rows, small_params)
    far, near_x, near_y, hidden_half, weights, other_one, other_two = order(
        far, near_x, near_y, hidden_half, weights, other_one, other_two
    )

    far_other = [across(value) for value in far]
    sources = []
    for part in range(2):
        sources += [two, two_x, two_y, far[part], two_own, near_x, near_y, far_other[part]]
    (mixer_in, mix_weight, expand_weight), mixed, slope = unpack_hidden(
        local_width, buckets, sources, weights, full_two, expand_bias[None], hidden_half
    )

    mixed, turned, logs = attend(full_one, mixer_in, mixer_bias[None], tables, begins, mixed)
    other_mixed = across(mixed)
    branches = matmul(mixed, mix_weight)
    branches, turned, grad_rows = order(branches, turned, grad_rows)
    branches = lax.psum_scatter(branches, "tensor", scatter_dimension=0, tiled=True)
    other_grads = across(grad_rows)

    grad_context = product_back(grad_rows, mix_weight[:local_width]).astype(jnp.bfloat16)
    grad_projected = attend_back(turned, logs, tables, begins, grad_context)
    grad_projected, slope = order(grad_projected, slope)
    other_projected = across(grad_projected)
    cores = core[None].astype(jnp.int32)
    rest_before, rest_bias = hidden_back(1 - cores, grad_rows, mix_weight, slope)
    other_before = across(rest_before)
    own_before, own_bias = hidden_back(cores, grad_rows, mix_weight, slope)
    grad_expand_bias = jnp.where(
        core == 0,
        jnp.concatenate([own_bias[0], rest_bias[0]]),
        jnp.concatenate([rest_bias[0], own_bias[0]]),
    )

    lefts = [full_one, other_one, mixed, other_mixed, full_two, other_two, mixed, other_mixed]
    rights = [grad_projected, other_projected, grad_rows, other_grads, own_before, other_before]
    sums = weight_grads(grad_table, lefts, rights)
    grad_projected, own_before, rest_before, sums = order(
        grad_projected, own_before, rest_before, sums
    )
    near_a, cross_a, far_a, near_b, cross_b, far_b, passed, stays = sums
    came_a, came_b, other_stays = along_x(far_a), along_y(far_b), across(stays)

    partial, norm_grads = norm_grad(
        cores,
        grad_projected,
        mixer_in,
        own_before,
        rest_before,
        expand_weight,
        full_rows,
        centre,
        scale,
        jnp.stack([small_params[0], small_params[2]]),
    )
    bias_grad = jnp.sum(grad_rows.astype(jnp.float32), axis=0)
    small = (
        jnp.sum(grad_projected.astype(jnp.float32), axis=0),
        grad_expand_bias,
        bias_grad,
    )

    norm_grads, other_stays = order(norm_grads, other_stays)
    one, two, three = (along_line(norm_grads, bit) for bit in (1, 2, 3))
    norm_grads = (norm_grads + one) + (two + three)
    near = [near_a, near_b, cross_a, cross_b]
    came_a, came_b, other_stays, partial, norm_grads, small, near = order(
        came_a, came_b, other_stays, partial, norm_grads, small, near
    )
    near = [along_x(near[0]), along_y(near[1]), along(1, near[2]), along(2, near[3])]
    terms = line_blocks(partial)
    pass_a = [(passed[0, at] + came_a[at].astype(jnp.float32)).astype(jnp.bfloat16) for at in range(2)]
    pass_b = [(passed[1, at] + came_b[at].astype(jnp.float32)).astype(jnp.bfloat16) for at in range(2)]
    small = jnp.concatenate(
        [
            small[0],
            small[1],
            norm_grads.reshape(-1),
            small[2],
            small[2],
            jnp.zeros((8 * D - 3 * local_width - 7 * D,), jnp.float32),
        ]
    ).reshape(LANES, LANES)
    small = small + across(small)
    small = small + along_x(small)
    near, pass_a, pass_b, small = order(near, pass_a, pass_b, small)
    output = residual[0].astype(jnp.float32) + branches + small_params[4] + small_params[5]
    far = [along_y(pass_a[0]), along_x(pass_b[0]), along(2, pass_a[1]), along(1, pass_b[1])]
    output, small = order(output, small)
    small = small + along_y(small)
    far, output, small = order(far, output, small)

    step_value = step_count[0].astype(jnp.float32)
    scalars = jnp.stack(
        [
            1.0 / (1.0 - jnp.power(beta_one, step_value)),
            1.0 / (1.0 - jnp.power(beta_two, step_value)),
            weight_decay[0],
            ema_decay[0],
        ]
    )
    state = [v.reshape(FLAT, LANES) for v in (master, moment_one, moment_two, average)]
    table = jnp.stack([buckets[0], core.astype(jnp.int32)])
    results = adam(table, scalars, rates, [stays, other_stays], near, far, small, state)
    terms, results = order(terms, results)
    input_grad = finish(terms, residual[0], cotangent[0])
    return (output[None], input_grad[None], *[v.reshape(master.shape) for v in results])


def solution(mesh):
    placed = (
        P(("dp", "chip"), "tensor", None),
        P(("dp", "chip"), "tensor", None),
        P(("dp", "chip"), None),
        P(),
        P(),
        P(),
        P(),
        P(),
        P("tensor", ("dp", "chip"), None),
        P("tensor", ("dp", "chip"), None),
        P("tensor", ("dp", "chip"), None),
        P("tensor", ("dp", "chip"), None),
    )
    return jax.shard_map(
        device_program(mesh),
        mesh=mesh,
        in_specs=placed,
        out_specs=(
            P(("dp", "chip"), "tensor", None),
            P(("dp", "chip"), "tensor", None),
            P("tensor", ("dp", "chip"), None),
            P("tensor", ("dp", "chip"), None),
            P("tensor", ("dp", "chip"), None),
            P("tensor", ("dp", "chip"), None),
            P("tensor", ("dp", "chip"), None),
        ),
        check_vma=False,
    )
```
